32 devices in a mesh: pert: 2 (over y), band: 16 (over z, x, core).
Axes of the slice: x: 2, y: 2, z: 4, core: 2. Of those that a mesh axis runs over, the one named last changes fastest.
Arguments:
- response: bfloat16 [1024, 12288], P('pert', 'band'), parts along dimension 0, may hold values from -6 to 6
- orbitals: bfloat16 [512, 12288], P(None, 'band'), may hold values from -6 to 6
- projectors: bfloat16 [2048, 12288], P(None, 'band'), may hold values from -6 to 6
- potential: float32 [12288], P('band'), may hold values from -1 to 1
- perturbing: float32 [24576], P(('pert', 'band')), parts along dimension 0, may hold values from -6 to 6
- energies: float32 [512], replicated, may hold values from -1 to -0.2
- window_start: int32 [512], replicated, may hold values from 0 to 31, as said below
- block_count: int32 [512], replicated, may hold values from 1 to 9, as said below
Outputs:
- updated_response: bfloat16 [1024, 12288], P('pert', 'band'), parts along dimension 0
- residual: bfloat16 [1024, 12288], P('pert', 'band'), parts along dimension 0
The draws below stay inside these ranges and needn't reach their ends.
There are 2 independent parts, one for each index of `pert`. The reference program is written for one: setup_inputs(seed, part) draws one part's arguments, and reference() takes and returns one part's arrays. A program takes and returns all parts, laid end to end along the dimension named above; an argument that names none is the same for every part. Nothing has to cross between parts.
Inputs may be any that keep to these rules, and one draw needn't show every extreme that they name: `window_start`: band n lies in block n // 16. Each band's window contains its own block and starts at most 4 blocks below it. `block_count`: each band's window ends at most 4 blocks above its own block and never past block 31.
All inputs are finite; a program needn't handle non-finite values.
Results may differ from the reference program's by a relative error of at most 0.0041.
Values may be sent and summed in bfloat16 or wider, within the bound.
No kernel may reach another device: no remote copies, remote signals or barrier semaphores. Data moves between devices by JAX's collectives and lax.ppermute only.
A program may use at most 128 MiB of HBM per device.

```python
import math
import jax
import jax.numpy as jnp

GY = 8
GZ = 16
NOCC = 2048
NBW = 512
NBLK = 32
REACH = 4
GX = 96
CELLS = 12288
BLK = 16


def window_parts(key):
    base_key = jax.random.fold_in(key, 11)
    lower_reach = jax.random.randint(jax.random.fold_in(base_key, 1), (NBW,), 0, REACH + 1)
    upper_reach = jax.random.randint(jax.random.fold_in(base_key, 2), (NBW,), 0, REACH + 1)
    band_index = jnp.arange(NBW, dtype=jnp.int32)
    own_block = band_index // BLK
    widest = band_index == NBLK // 2 * BLK
    lower_reach = jnp.where(widest, REACH, lower_reach)
    upper_reach = jnp.where(widest, REACH, upper_reach)
    final_band = band_index == NBW - 1
    lower_reach = jnp.where(final_band, 0, lower_reach)
    first_block = jnp.maximum(own_block - lower_reach, 0)
    last_block = jnp.minimum(own_block + upper_reach, NBLK - 1)
    return (first_block.astype(jnp.int32), (last_block - first_block + 1).astype(jnp.int32))


def draw_window_start(key, part):
    return window_parts(key)[0]


def draw_block_count(key, part):
    return window_parts(key)[1]


def level_of(stream_key, extent, cuts, smallest, largest):
    def one(dim, blocks):
        draws = jax.random.uniform(jax.random.fold_in(jax.random.fold_in(stream_key, 6), dim), (blocks,), jnp.float32, smallest / len(cuts), largest / len(cuts))
        return jnp.repeat(jnp.exp(draws), extent[dim] // blocks).reshape((-1,) + (1,) * (len(extent) - dim - 1))

    gain = one(*cuts[0])
    for cut in cuts[1:]:
        gain = gain * one(*cut)
    return gain


def centred(key, dims, deviation, limit, shards=(), held_as=jnp.bfloat16):
    array = deviation * jax.random.normal(key, dims, jnp.float32)
    if shards:
        array = array * level_of(key, dims, shards, -0.22, 0.18)
    return jnp.clip(array, -limit, limit).astype(held_as)


def setup_inputs(seed: int = 0, part: int = 0) -> dict:
    splits = jax.random.split(jax.random.key(seed), 9)
    part_splits = jax.random.split(jax.random.fold_in(splits[8], part), 9)
    return {
        "response": centred(part_splits[0], (NBW, CELLS), 1.0, 6.0, ((1, 16),)),
        "orbitals": centred(splits[1], (NBW, CELLS), 1.0, 6.0, ((1, 16),)),
        "projectors": centred(splits[2], (NOCC, CELLS), 1.0, 6.0, ((1, 16),)),
        "potential": jnp.clip(jax.random.uniform(splits[3], (CELLS,), jnp.float32, -1.0, 1.0) * level_of(splits[3], (CELLS,), ((0, 16),), -0.4, 0.0), -1.0, 1.0),
        "perturbing": centred(part_splits[4], (CELLS,), 1.0, 6.0, ((0, 16),), jnp.float32),
        "energies": jnp.clip(jax.random.uniform(splits[5], (NBW,), jnp.float32, -1.0, -0.2), -1.0, -0.2),
        "window_start": draw_window_start(jax.random.fold_in(splits[8], 71), part),
        "block_count": draw_block_count(jax.random.fold_in(splits[8], 71), part),
    }


COEFFS = (-5369.0 / 1800.0, 12.0 / 7.0, -15.0 / 56.0, 10.0 / 189.0, -1.0 / 112.0, 2.0 / 1925.0, -1.0 / 16632.0)
KINETIC = 0.125
STEP_SIZE = 0.3

def laplacian(grid_field):
    result = 3.0 * COEFFS[0] * grid_field
    for axis_number in (1, 2, 3):
        for offset in range(1, 7):
            result = result + COEFFS[offset] * (jnp.roll(grid_field, offset, axis_number) + jnp.roll(grid_field, -offset, axis_number))
    return result

def reference(response, orbitals, projectors, potential, perturbing, energies, window_start, block_count):
    cells = GX * GY * GZ
    ace_scale = 1.0 / math.sqrt(cells * NOCC)
    window_scale = 1.0 / math.sqrt(cells * NBW)
    response_wide = response.astype(jnp.float32)
    kinetic = -KINETIC * laplacian(response_wide.reshape(NBW, GX, GY, GZ)).reshape(NBW, cells)
    ace_intersection = (jnp.dot(response, projectors.T, preferred_element_type=jnp.float32) * ace_scale).astype(jnp.bfloat16)
    ace_term = -jnp.dot(ace_intersection, projectors, preferred_element_type=jnp.float32)
    applied = kinetic + potential[None, :] * response_wide + ace_term - energies[:, None] * response_wide
    orbitals_wide = orbitals.astype(jnp.float32)
    unprojected = -(perturbing[None, :] * orbitals_wide) - applied
    unprojected_low = unprojected.astype(jnp.bfloat16)
    intersections = (jnp.dot(unprojected_low, orbitals.T, preferred_element_type=jnp.float32) * window_scale).astype(jnp.bfloat16)
    block_ids = jnp.arange(NBW, dtype=jnp.int32) // (NBW // NBLK)
    lowest = window_start[:, None]
    highest = window_start[:, None] + block_count[:, None] - 1
    inside = (block_ids[None, :] >= lowest) & (block_ids[None, :] <= highest)
    intersections = jnp.where(inside, intersections, jnp.zeros_like(intersections))
    residual_wide = unprojected - jnp.dot(intersections, orbitals, preferred_element_type=jnp.float32)
    updated_response = (response_wide + STEP_SIZE * residual_wide).astype(jnp.bfloat16)
    return (updated_response, residual_wide.astype(jnp.bfloat16))
```

```python
import functools
import math

import jax
import jax.numpy as jnp
import ml_dtypes
import numpy as np
from jax import lax
from jax.experimental import pallas as pl
from jax.experimental.pallas import tpu as pltpu
from jax.sharding import PartitionSpec as P

GY = 8
GZ = 16
NBLK = 32
REACH = 4
GROUP_BLOCKS = 8
COEFFS = (
    -5369.0 / 1800.0,
    12.0 / 7.0,
    -15.0 / 56.0,
    10.0 / 189.0,
    -1.0 / 112.0,
    2.0 / 1925.0,
    -1.0 / 16632.0,
)
KINETIC = 0.125
STEP_SIZE = 0.3
CHUNKS = 2
VMEM_BYTES = 40 * 1024 * 1024
BF16 = jnp.bfloat16
F32 = jnp.float32
NT = (((1,), (1,)), ((), ()))


def levels_of(count):
    chips = count // 2
    across = 2 ** (int(math.log2(chips)) // 3)
    return (2, 1), (across, 2), (chips // across, 2 * across)


def position(level):
    size, stride = level
    return lax.rem(lax.div(lax.axis_index("band"), jnp.int32(stride)), jnp.int32(size))


def shifted(array, count, level, step):
    size, stride = level
    pairs = []
    for device in range(count):
        place = device // stride % size
        pairs.append((device, device + ((place + step) % size - place) * stride))
    return lax.ppermute(array, "band", pairs)


def plane_matrix():
    plane = GY * GZ
    matrix = 3.0 * COEFFS[0] * np.eye(plane)
    cells = np.arange(plane)
    y, z = cells // GZ, cells % GZ
    for offset in range(1, 7):
        for sign in (1, -1):
            np.add.at(matrix, ((y + sign * offset) % GY * GZ + z, cells), COEFFS[offset])
            np.add.at(matrix, (y * GZ + (z + sign * offset) % GZ, cells), COEFFS[offset])
    matrix = KINETIC * matrix
    high = matrix.astype(ml_dtypes.bfloat16)
    low = (matrix - high.astype(np.float64)).astype(ml_dtypes.bfloat16)
    return np.stack([high, low])


def whole():
    return pl.BlockSpec(memory_space=pltpu.VMEM)


def params():
    return pltpu.CompilerParams(vmem_limit_bytes=VMEM_BYTES)


def cost(flops, *arrays):
    moved = sum(math.prod(a.shape) * jnp.dtype(a.dtype).itemsize for a in arrays)
    return pl.CostEstimate(flops=int(flops), bytes_accessed=int(moved), transcendentals=0)


def local_call(body, outs, args, flops=0, scratch=()):
    return pl.pallas_call(
        body,
        out_shape=outs,
        in_specs=[whole() for _ in args],
        out_specs=jax.tree.map(lambda _: whole(), outs),
        scratch_shapes=scratch,
        compiler_params=params(),
        cost_estimate=cost(flops, *args, *jax.tree.leaves(outs)),
    )(*args)


def struct(shape, dtype):
    return jax.ShapeDtypeStruct(shape, dtype)


def partial_body(core, other, r_ref, p_ref, out_ref):
    half = out_ref.shape[0]
    c = position(core)
    row = pl.multiple_of((1 - c if other else c) * half, half)
    out_ref[...] = lax.dot_general(
        r_ref[pl.ds(row, half), :], p_ref[...], NT, preferred_element_type=F32
    ).astype(out_ref.dtype)


def partial_intersections(response, projectors, chunk, rows, core, other):
    cells = response.shape[1]
    count = projectors.shape[0]
    tile = min(512, count)
    out = struct((rows // 2, count), BF16 if other else F32)
    return pl.pallas_call(
        functools.partial(partial_body, core, other),
        grid=(count // tile,),
        out_shape=out,
        in_specs=[
            pl.BlockSpec((rows, cells), lambda i: (chunk, 0)),
            pl.BlockSpec((tile, cells), lambda i: (i, 0)),
        ],
        out_specs=pl.BlockSpec((rows // 2, tile), lambda i: (0, i)),
        compiler_params=params(),
        cost_estimate=cost(2 * rows // 2 * cells * count, projectors, out),
    )(response, projectors)


def split_body(received, level, along, *refs):
    keep_ref, taken, (own_ref, *sends) = refs[0], refs[1 : 1 + received], refs[1 + received :]
    size, _ = level
    me = position(level)
    width = own_ref.shape[along]
    for step, out in enumerate((own_ref, *sends)):
        at = pl.multiple_of(lax.rem(me + step, jnp.int32(size)) * width, width)
        part = (pl.ds(at, width), slice(None)) if along == 0 else (slice(None), pl.ds(at, width))
        total = keep_ref[part]
        for ref in taken:
            total = total + ref[part].astype(F32)
        out[...] = total.astype(out.dtype)


def split(keep, taken, level, along):
    size, _ = level
    shape = list(keep.shape)
    shape[along] //= size
    outs = [struct(shape, F32)] + [struct(shape, BF16)] * (size - 1)
    return local_call(
        functools.partial(split_body, len(taken), level, along), outs, [keep, *taken]
    )


def finish_body(scale, keep_ref, *refs):
    *taken, out_ref = refs
    total = keep_ref[...]
    for ref in taken:
        total = total + ref[...].astype(F32)
    out_ref[...] = (total * scale).astype(out_ref.dtype)


def finish(keep, taken, scale):
    return local_call(
        functools.partial(finish_body, scale), struct(keep.shape, BF16), [keep, *taken]
    )


def place_body(level, *refs):
    *parts, out_ref = refs
    size, _ = level
    me = position(level)
    width = parts[0].shape[1]
    for step, ref in enumerate(parts):
        at = pl.multiple_of(lax.rem(me - step + size, jnp.int32(size)) * width, width)
        out_ref[:, pl.ds(at, width)] = ref[...]


def place(parts, level):
    rows, width = parts[0].shape
    return local_call(
        functools.partial(place_body, level), struct((rows, width * level[0]), BF16), parts
    )


def local_body(depth, r_ref, l_ref, h_ref, o_ref, m_ref, pot_ref, v_ref, e_ref, out_ref):
    plane = GY * GZ
    reach = 6

    def plane_at(j):
        if j < 0:
            ref, k = l_ref, j + reach
        elif j < depth:
            ref, k = r_ref, j
        else:
            ref, k = h_ref, j - depth
        return ref[:, k * plane : (k + 1) * plane]

    for j in range(depth):
        cols = slice(j * plane, (j + 1) * plane)
        low = plane_at(j)
        centre = low.astype(F32)
        total = jnp.dot(low, m_ref[0], preferred_element_type=F32)
        total = total + jnp.dot(low, m_ref[1], preferred_element_type=F32)
        for offset in range(1, 7):
            pair = plane_at(j + offset).astype(F32) + plane_at(j - offset).astype(F32)
            total = total + (KINETIC * COEFFS[offset]) * pair
        total = total + (e_ref[...] - pot_ref[:, cols]) * centre
        out_ref[:, cols] = total - v_ref[:, cols] * o_ref[:, cols].astype(F32)


def local_part(response, low, high, orbitals, matrix, potential, perturbing, energies, chunk, rows):
    cells = response.shape[1]
    halo = low.shape[1]
    depth = cells // (GY * GZ)
    tile = 128
    per = rows // tile
    out = struct((rows, cells), F32)
    here = pl.BlockSpec((tile, cells), lambda i: (chunk * per + i, 0))
    side = pl.BlockSpec((tile, halo), lambda i: (i, 0))
    line = pl.BlockSpec((1, cells), lambda i: (0, 0))
    return pl.pallas_call(
        functools.partial(local_body, depth),
        grid=(per,),
        out_shape=out,
        in_specs=[
            here,
            side,
            side,
            here,
            pl.BlockSpec(matrix.shape, lambda i: (0, 0, 0)),
            line,
            line,
            pl.BlockSpec((tile, 1), lambda i: (chunk * per + i, 0)),
        ],
        out_specs=pl.BlockSpec((tile, cells), lambda i: (i, 0)),
        compiler_params=params(),
        cost_estimate=cost(2 * rows * cells * 300, low, high, low, low, out),
    )(response, low, high, orbitals, matrix, potential, perturbing, energies)


def first_orbital(group, group_rows, width, bands, blk):
    return max(0, min(group * group_rows - REACH * blk, bands - width))


def apply_body(chunk, core, across, group_rows, width, blk, *refs):
    size = across[0]
    blocks = refs[: 2 * size]
    p_ref, base_ref, o_ref, u_ref, send_ref, keep_ref, c_ref, s_ref = refs[2 * size :]
    rows, cells = u_ref.shape
    bands = o_ref.shape[0]
    c, x = position(core), position(across)
    share = blocks[0].shape[0]
    half = rows // 2
    for k, ref in enumerate(blocks):
        side, step = divmod(k, size)
        at = (c if side == 0 else 1 - c) * half
        at = at + lax.rem(x - step + size, jnp.int32(size)) * share
        c_ref[pl.ds(pl.multiple_of(at, share), share), :] = ref[...]
    tile = 256 if cells % 256 == 0 else 128
    for t in range(cells // tile):
        cols = slice(t * tile, (t + 1) * tile)
        u_ref[:, cols] = base_ref[:, cols] + jnp.dot(
            c_ref[...], p_ref[:, cols], preferred_element_type=F32
        )
    for g in range(rows // group_rows):
        start = first_orbital(chunk * (rows // group_rows) + g, group_rows, width, bands, blk)
        mine = slice(g * group_rows, (g + 1) * group_rows)
        s_ref[mine, :] = lax.dot_general(
            u_ref[mine, :].astype(BF16),
            o_ref[start : start + width, :],
            NT,
            preferred_element_type=F32,
        )
    send_ref[...] = s_ref[pl.ds(pl.multiple_of((1 - c) * half, half), half), :].astype(BF16)
    keep_ref[...] = s_ref[pl.ds(pl.multiple_of(c * half, half), half), :]


def sum_body(keep_ref, *refs):
    *taken, total_ref, low_ref = refs
    total = keep_ref[...]
    for ref in taken:
        total = total + ref[...].astype(F32)
    total_ref[...] = total
    low_ref[...] = total.astype(BF16)


def add_up(keep, taken):
    outs = [struct(keep.shape, F32), struct(keep.shape, BF16)]
    return local_call(sum_body, outs, [keep, *taken])


def project_body(chunk, core, group_rows, width, blk, *refs):
    own_ref, other_ref, o_ref, u_ref, r_ref, first_ref, many_ref = refs[:7]
    updated_ref, residual_ref, w_ref = refs[-3:]
    rows = u_ref.shape[0]
    bands = o_ref.shape[0]
    half = rows // 2
    c = position(core)
    w_ref[pl.ds(pl.multiple_of(c * half, half), half), :] = own_ref[...]
    w_ref[pl.ds(pl.multiple_of((1 - c) * half, half), half), :] = other_ref[...]
    for g in range(rows // group_rows):
        start = first_orbital(chunk * (rows // group_rows) + g, group_rows, width, bands, blk)
        mine = slice(g * group_rows, (g + 1) * group_rows)
        block = (lax.broadcasted_iota(jnp.int32, (group_rows, width), 1) + start) // blk
        lowest = first_ref[mine, :]
        inside = (block >= lowest) & (block < lowest + many_ref[mine, :])
        weights = jnp.where(inside, w_ref[mine, :].astype(F32), 0.0).astype(BF16)
        residual = u_ref[mine, :] - jnp.dot(
            weights, o_ref[start : start + width, :], preferred_element_type=F32
        )
        residual_ref[mine, :] = residual.astype(BF16)
        updated_ref[mine, :] = (r_ref[mine, :].astype(F32) + STEP_SIZE * residual).astype(BF16)


def project(own, other, orbitals, unprojected, response, first, many, before, chunk, core, sizes):
    rows, cells = unprojected.shape
    group_rows, width, blk = sizes
    out = struct(response.shape, BF16)
    here = pl.BlockSpec((rows, cells), lambda i: (chunk, 0))
    column = pl.BlockSpec((rows, 1), lambda i: (chunk, 0))

    def full(a):
        return pl.BlockSpec(a.shape, lambda i: (0, 0))

    args = [own, other, orbitals, unprojected, response, first, many, *before]
    specs = [full(own), full(other), full(orbitals), full(unprojected), here, column, column]
    specs += [pl.BlockSpec(memory_space=pl.ANY)] * len(before)
    return pl.pallas_call(
        functools.partial(project_body, chunk, core, group_rows, width, blk),
        grid=(1,),
        out_shape=[out, out],
        in_specs=specs,
        out_specs=[here, here],
        scratch_shapes=[pltpu.VMEM((rows, width), BF16)],
        input_output_aliases={7: 0, 8: 1} if before else {},
        compiler_params=params(),
        cost_estimate=cost(2 * rows * width * cells, orbitals, unprojected, unprojected),
    )(*args)


def shards(
    count, response, orbitals, projectors, potential, perturbing, energies, window_start, block_count
):
    bands, local_cells = response.shape
    cells = local_cells * count
    plane = GY * GZ
    halo = 6 * plane
    core, across, along = levels_of(count)
    ring = (count, 1)
    ace_scale = 1.0 / math.sqrt(cells * projectors.shape[0])
    window_scale = 1.0 / math.sqrt(cells * bands)
    blk = bands // NBLK
    group_rows = GROUP_BLOCKS * blk
    width = (GROUP_BLOCKS + 2 * REACH) * blk
    rows = bands // CHUNKS
    matrix = jnp.asarray(plane_matrix())
    potential, perturbing = potential[None, :], perturbing[None, :]
    energies, window_start, block_count = (
        a[:, None] for a in (energies, window_start, block_count)
    )

    sides = []
    keeps = []
    sent = []
    for chunk in range(CHUNKS):
        mine = slice(chunk * rows, (chunk + 1) * rows)
        sent.append(
            shifted(
                partial_intersections(response, projectors, chunk, rows, core, True), count, core, 1
            )
        )
        keeps.append(partial_intersections(response, projectors, chunk, rows, core, False))
        sides.append(
            (
                shifted(response[mine, local_cells - halo :], count, ring, 1),
                shifted(response[mine, :halo], count, ring, -1),
            )
        )

    outs = ()
    for chunk in range(CHUNKS):
        keep, *parts = split(keeps[chunk], [sent[chunk]], across, 0)
        taken = [shifted(part, count, across, k + 1) for k, part in enumerate(parts)]
        keep, *parts = split(keep, taken, along, 1)
        taken = [shifted(part, count, along, k + 1) for k, part in enumerate(parts)]
        share = finish(keep, taken, ace_scale)
        pieces = [share] + [shifted(share, count, along, k) for k in range(1, along[0])]
        own = place(pieces, along)
        blocks = [own] + [shifted(own, count, across, k) for k in range(1, across[0])]
        blocks += [shifted(block, count, core, 1) for block in blocks]
        low, high = sides[chunk]
        base = local_part(
            response, low, high, orbitals, matrix, potential, perturbing, energies, chunk, rows
        )
        unprojected, send, keep = local_call(
            functools.partial(apply_body, chunk, core, across, group_rows, width, blk),
            [
                struct((rows, local_cells), F32),
                struct((rows // 2, width), BF16),
                struct((rows // 2, width), F32),
            ],
            [*blocks, projectors, base, orbitals],
            flops=2 * rows * local_cells * (projectors.shape[0] + width),
            scratch=[
                pltpu.VMEM((rows, projectors.shape[0]), BF16),
                pltpu.VMEM((rows, width), F32),
            ],
        )
        total, low = add_up(keep, [shifted(send, count, core, 1)])
        total, low = add_up(total, [shifted(low, count, across, k) for k in range(1, across[0])])
        weights = finish(
            total, [shifted(low, count, along, k) for k in range(1, along[0])], window_scale
        )
        outs = project(
            weights,
            shifted(weights, count, core, 1),
            orbitals,
            unprojected,
            response,
            window_start,
            block_count,
            outs,
            chunk,
            core,
            (group_rows, width, blk),
        )
    return tuple(outs)


def solution(mesh):
    in_specs = (
        P("pert", "band"),
        P(None, "band"),
        P(None, "band"),
        P("band"),
        P(("pert", "band")),
        P(),
        P(),
        P(),
    )
    out_specs = (P("pert", "band"), P("pert", "band"))
    body = functools.partial(shards, mesh.shape["band"])
    return jax.shard_map(body, mesh=mesh, in_specs=in_specs, out_specs=out_specs, check_vma=False)
```

```python
import functools
import math

import jax
import jax.numpy as jnp
import ml_dtypes
import numpy as np
from jax import lax
from jax.experimental import pallas as pl
from jax.experimental.pallas import tpu as pltpu
from jax.sharding import PartitionSpec as P

GY = 8
GZ = 16
NBLK = 32
REACH = 4
GROUP_BLOCKS = 8
COEFFS = (
    -5369.0 / 1800.0,
    12.0 / 7.0,
    -15.0 / 56.0,
    10.0 / 189.0,
    -1.0 / 112.0,
    2.0 / 1925.0,
    -1.0 / 16632.0,
)
KINETIC = 0.125
STEP_SIZE = 0.3
VMEM_BYTES = 40 * 1024 * 1024
BF16 = jnp.bfloat16
F32 = jnp.float32
NT = (((1,), (1,)), ((), ()))


def levels_of(count):
    chips = count // 2
    across = 2 ** (int(math.log2(chips)) // 3)
    return (2, 1), (across, 2), (chips // across, 2 * across)


def position(level):
    size, stride = level
    return lax.rem(lax.div(lax.axis_index("band"), jnp.int32(stride)), jnp.int32(size))


def shifted(array, count, level, step):
    size, stride = level
    pairs = []
    for device in range(count):
        place = device // stride % size
        pairs.append((device, device + ((place + step) % size - place) * stride))
    return lax.ppermute(array, "band", pairs)


def plane_matrix():
    plane = GY * GZ
    matrix = 3.0 * COEFFS[0] * np.eye(plane)
    cells = np.arange(plane)
    y, z = cells // GZ, cells % GZ
    for offset in range(1, 7):
        for sign in (1, -1):
            np.add.at(matrix, ((y + sign * offset) % GY * GZ + z, cells), COEFFS[offset])
            np.add.at(matrix, (y * GZ + (z + sign * offset) % GZ, cells), COEFFS[offset])
    matrix = KINETIC * matrix
    high = matrix.astype(ml_dtypes.bfloat16)
    low = (matrix - high.astype(np.float64)).astype(ml_dtypes.bfloat16)
    return np.stack([high, low])


def whole():
    return pl.BlockSpec(memory_space=pltpu.VMEM)


def params():
    return pltpu.CompilerParams(vmem_limit_bytes=VMEM_BYTES)


def cost(flops, *arrays):
    moved = sum(math.prod(a.shape) * jnp.dtype(a.dtype).itemsize for a in arrays)
    return pl.CostEstimate(flops=int(flops), bytes_accessed=int(moved), transcendentals=0)


def local_call(body, outs, args, flops=0, scratch=()):
    return pl.pallas_call(
        body,
        out_shape=outs,
        in_specs=[whole() for _ in args],
        out_specs=jax.tree.map(lambda _: whole(), outs),
        scratch_shapes=scratch,
        compiler_params=params(),
        cost_estimate=cost(flops, *args, *jax.tree.leaves(outs)),
    )(*args)


def struct(shape, dtype):
    return jax.ShapeDtypeStruct(shape, dtype)


def partial_body(core, bands, parts, r_ref, p_ref, *outs):
    c = position(core)
    for (other, first, rows), out_ref in zip(parts, outs):
        row = pl.multiple_of((1 - c if other else c) * (bands // 2) + first, 16)
        out_ref[...] = lax.dot_general(
            r_ref[pl.ds(row, rows), :], p_ref[...], NT, preferred_element_type=F32
        ).astype(out_ref.dtype)


def partial_intersections(response, projectors, core, parts):
    bands, cells = response.shape
    count = projectors.shape[0]
    tile = min(512, count)
    outs = [struct((rows, count), BF16 if other else F32) for other, _, rows in parts]
    done = sum(rows for _, _, rows in parts)
    return pl.pallas_call(
        functools.partial(partial_body, core, bands, parts),
        grid=(count // tile,),
        out_shape=outs,
        in_specs=[
            pl.BlockSpec((bands, cells), lambda i: (0, 0)),
            pl.BlockSpec((tile, cells), lambda i: (i, 0)),
        ],
        out_specs=[pl.BlockSpec((rows, tile), lambda i: (0, i)) for _, _, rows in parts],
        compiler_params=params(),
        cost_estimate=cost(2 * done * cells * count, projectors, *outs),
    )(response, projectors)


def split_body(received, level, along, *refs):
    keep_ref, taken, (own_ref, *sends) = refs[0], refs[1 : 1 + received], refs[1 + received :]
    size, _ = level
    me = position(level)
    width = own_ref.shape[along]
    for step, out in enumerate((own_ref, *sends)):
        at = pl.multiple_of(lax.rem(me + step, jnp.int32(size)) * width, width)
        part = (pl.ds(at, width), slice(None)) if along == 0 else (slice(None), pl.ds(at, width))
        total = keep_ref[part]
        for ref in taken:
            total = total + ref[part].astype(F32)
        out[...] = total.astype(out.dtype)


def split(keep, taken, level, along):
    size, _ = level
    shape = list(keep.shape)
    shape[along] //= size
    outs = [struct(shape, F32)] + [struct(shape, BF16)] * (size - 1)
    return local_call(
        functools.partial(split_body, len(taken), level, along), outs, [keep, *taken]
    )


def finish_body(scale, keep_ref, *refs):
    *taken, out_ref = refs
    total = keep_ref[...]
    for ref in taken:
        total = total + ref[...].astype(F32)
    out_ref[...] = (total * scale).astype(out_ref.dtype)


def finish(keep, taken, scale):
    return local_call(
        functools.partial(finish_body, scale), struct(keep.shape, BF16), [keep, *taken]
    )


def place_body(level, along, *refs):
    *parts, out_ref = refs
    size, _ = level
    me = position(level)
    width = parts[0].shape[along]
    for step, ref in enumerate(parts):
        at = pl.multiple_of(lax.rem(me - step + size, jnp.int32(size)) * width, width)
        if along == 0:
            out_ref[pl.ds(at, width), :] = ref[...]
        else:
            out_ref[:, pl.ds(at, width)] = ref[...]


def place(parts, level, along):
    shape = list(parts[0].shape)
    shape[along] *= level[0]
    return local_call(functools.partial(place_body, level, along), struct(shape, BF16), parts)


def local_body(depth, r_ref, l_ref, h_ref, o_ref, m_ref, pot_ref, v_ref, e_ref, out_ref):
    plane = GY * GZ
    reach = 6

    def plane_at(j):
        if j < 0:
            ref, k = l_ref, j + reach
        elif j < depth:
            ref, k = r_ref, j
        else:
            ref, k = h_ref, j - depth
        return ref[:, k * plane : (k + 1) * plane]

    for j in range(depth):
        cols = slice(j * plane, (j + 1) * plane)
        low = plane_at(j)
        centre = low.astype(F32)
        total = jnp.dot(low, m_ref[0], preferred_element_type=F32)
        total = total + jnp.dot(low, m_ref[1], preferred_element_type=F32)
        for offset in range(1, 7):
            pair = plane_at(j + offset).astype(F32) + plane_at(j - offset).astype(F32)
            total = total + (KINETIC * COEFFS[offset]) * pair
        total = total + (e_ref[...] - pot_ref[:, cols]) * centre
        out_ref[:, cols] = total - v_ref[:, cols] * o_ref[:, cols].astype(F32)


def local_part(response, low, high, orbitals, matrix, potential, perturbing, energies):
    bands, cells = response.shape
    depth = cells // (GY * GZ)
    tile = 128
    out = struct((bands, cells), F32)
    here = pl.BlockSpec((tile, cells), lambda i: (i, 0))
    side = pl.BlockSpec((tile, low.shape[1]), lambda i: (i, 0))
    line = pl.BlockSpec((1, cells), lambda i: (0, 0))
    return pl.pallas_call(
        functools.partial(local_body, depth),
        grid=(bands // tile,),
        out_shape=out,
        in_specs=[
            here,
            side,
            side,
            here,
            pl.BlockSpec(matrix.shape, lambda i: (0, 0, 0)),
            line,
            line,
            pl.BlockSpec((tile, 1), lambda i: (i, 0)),
        ],
        out_specs=here,
        compiler_params=params(),
        cost_estimate=cost(2 * bands * cells * 300, low, high, low, low, out),
    )(response, low, high, orbitals, matrix, potential, perturbing, energies)


def first_orbital(group, group_rows, width, bands, blk):
    return max(0, min(group * group_rows - REACH * blk, bands - width))


def apply_body(core, across, rows_x, group_rows, width, blk, *refs):
    size = across[0]
    blocks = refs[: 2 * (size + 1)]
    p_ref, base_ref, o_ref, u_ref, send_ref, keep_ref, c_ref, s_ref = refs[2 * (size + 1) :]
    bands, cells = u_ref.shape
    c, x = position(core), position(across)
    half = bands // 2
    share = rows_x // size
    for k, ref in enumerate(blocks):
        side, step = divmod(k, size + 1)
        at = (c if side == 0 else 1 - c) * half
        if step < size:
            at = at + lax.rem(x - step + size, jnp.int32(size)) * share
        else:
            at = at + rows_x
        c_ref[pl.ds(pl.multiple_of(at, 16), ref.shape[0]), :] = ref[...]
    tile = 256 if cells % 256 == 0 else 128
    for t in range(cells // tile):
        cols = slice(t * tile, (t + 1) * tile)
        u_ref[:, cols] = base_ref[:, cols] + jnp.dot(
            c_ref[...], p_ref[:, cols], preferred_element_type=F32
        )
    for g in range(bands // group_rows):
        start = first_orbital(g, group_rows, width, bands, blk)
        mine = slice(g * group_rows, (g + 1) * group_rows)
        s_ref[mine, :] = lax.dot_general(
            u_ref[mine, :].astype(BF16),
            o_ref[start : start + width, :],
            NT,
            preferred_element_type=F32,
        )
    send_ref[...] = s_ref[pl.ds(pl.multiple_of((1 - c) * half, half), half), :].astype(BF16)
    keep_ref[...] = s_ref[pl.ds(pl.multiple_of(c * half, half), half), :]


def sum_body(keep_ref, *refs):
    *taken, total_ref, low_ref = refs
    total = keep_ref[...]
    for ref in taken:
        total = total + ref[...].astype(F32)
    total_ref[...] = total
    low_ref[...] = total.astype(BF16)


def add_up(keep, taken):
    outs = [struct(keep.shape, F32), struct(keep.shape, BF16)]
    return local_call(sum_body, outs, [keep, *taken])


def project_body(core, across, group_rows, width, blk, *refs):
    size = across[0]
    blocks = refs[: 2 * size]
    o_ref, u_ref, r_ref, first_ref, many_ref, updated_ref, residual_ref, w_ref = refs[2 * size :]
    bands = o_ref.shape[0]
    half = bands // 2
    c, x = position(core), position(across)
    for k, ref in enumerate(blocks):
        side, step = divmod(k, size)
        at = (c if side == 0 else 1 - c) * half
        at = at + lax.rem(x - step + size, jnp.int32(size)) * ref.shape[0]
        w_ref[pl.ds(pl.multiple_of(at, 16), ref.shape[0]), :] = ref[...]
    for g in range(bands // group_rows):
        start = first_orbital(g, group_rows, width, bands, blk)
        mine = slice(g * group_rows, (g + 1) * group_rows)
        block = (lax.broadcasted_iota(jnp.int32, (group_rows, width), 1) + start) // blk
        lowest = first_ref[mine, :]
        inside = (block >= lowest) & (block < lowest + many_ref[mine, :])
        weights = jnp.where(inside, w_ref[mine, :].astype(F32), 0.0).astype(BF16)
        residual = u_ref[mine, :] - jnp.dot(
            weights, o_ref[start : start + width, :], preferred_element_type=F32
        )
        residual_ref[mine, :] = residual.astype(BF16)
        updated_ref[mine, :] = (r_ref[mine, :].astype(F32) + STEP_SIZE * residual).astype(BF16)


def shards(
    count, response, orbitals, projectors, potential, perturbing, energies, window_start, block_count
):
    bands, local_cells = response.shape
    cells = local_cells * count
    projections = projectors.shape[0]
    halo = 6 * GY * GZ
    core, across, along = levels_of(count)
    ring = (count, 1)
    ace_scale = 1.0 / math.sqrt(cells * projections)
    window_scale = 1.0 / math.sqrt(cells * bands)
    blk = bands // NBLK
    group_rows = GROUP_BLOCKS * blk
    width = (GROUP_BLOCKS + 2 * REACH) * blk
    half = bands // 2
    rows_x = half // 2
    rows_z = half - rows_x
    matrix = jnp.asarray(plane_matrix())
    potential, perturbing = potential[None, :], perturbing[None, :]
    energies, window_start, block_count = (
        a[:, None] for a in (energies, window_start, block_count)
    )

    def to(array, level):
        return [shifted(array, count, level, k) for k in range(1, level[0])]

    def parts_to(parts, level):
        return [shifted(part, count, level, k + 1) for k, part in enumerate(parts)]

    low = shifted(response[:, local_cells - halo :], count, ring, 1)
    high = shifted(response[:, :halo], count, ring, -1)

    (sent_z,) = partial_intersections(response, projectors, core, [(True, rows_x, rows_z)])
    sent_z = shifted(sent_z, count, core, 1)
    (sent_x,) = partial_intersections(response, projectors, core, [(True, 0, rows_x)])
    sent_x = shifted(sent_x, count, core, 1)
    keep_z, keep_x = partial_intersections(
        response, projectors, core, [(False, rows_x, rows_z), (False, 0, rows_x)]
    )
    keep_z, *parts = split(keep_z, [sent_z], along, 1)
    taken_z = parts_to(parts, along)
    keep_x, *parts = split(keep_x, [sent_x], across, 0)
    taken_x = parts_to(parts, across)
    keep_x, *parts = split(keep_x, taken_x, along, 1)
    taken_x = parts_to(parts, along)
    keep_z, *parts = split(keep_z, taken_z, across, 0)
    taken_z = parts_to(parts, across)
    share_z = finish(keep_z, taken_z, ace_scale)
    share_x = finish(keep_x, taken_x, ace_scale)

    block_z = place([share_z, *to(share_z, across)], across, 0)
    block_x = place([share_x, *to(share_x, along)], along, 1)
    base = local_part(
        response, low, high, orbitals, matrix, potential, perturbing, energies
    )
    blocks_x = [block_x, *to(block_x, across)]
    block_z = place([block_z, *to(block_z, along)], along, 1)
    blocks = [*blocks_x, block_z]
    blocks += [shifted(block, count, core, 1) for block in blocks]

    unprojected, send, keep = local_call(
        functools.partial(apply_body, core, across, rows_x, group_rows, width, blk),
        [
            struct((bands, local_cells), F32),
            struct((half, width), BF16),
            struct((half, width), F32),
        ],
        [*blocks, projectors, base, orbitals],
        flops=2 * bands * local_cells * (projections + width),
        scratch=[pltpu.VMEM((bands, projections), BF16), pltpu.VMEM((bands, width), F32)],
    )
    keep, *parts = split(keep, to(send, core), across, 0)
    total, low = add_up(keep, parts_to(parts, across))
    weights = finish(total, to(low, along), window_scale)
    weights = [weights, *to(weights, across)]
    weights += [shifted(block, count, core, 1) for block in weights]
    out = struct((bands, local_cells), BF16)
    return local_call(
        functools.partial(project_body, core, across, group_rows, width, blk),
        (out, out),
        [*weights, orbitals, unprojected, response, window_start, block_count],
        flops=2 * bands * width * local_cells,
        scratch=[pltpu.VMEM((bands, width), BF16)],
    )


def solution(mesh):
    in_specs = (
        P("pert", "band"),
        P(None, "band"),
        P(None, "band"),
        P("band"),
        P(("pert", "band")),
        P(),
        P(),
        P(),
    )
    out_specs = (P("pert", "band"), P("pert", "band"))
    body = functools.partial(shards, mesh.shape["band"])
    return jax.shard_map(body, mesh=mesh, in_specs=in_specs, out_specs=out_specs, check_vma=False)
```

```python
import functools
import math

import jax
import jax.numpy as jnp
import ml_dtypes
import numpy as np
from jax import lax
from jax.experimental import pallas as pl
from jax.experimental.pallas import tpu as pltpu
from jax.sharding import PartitionSpec as P

GY = 8
GZ = 16
NBLK = 32
REACH = 4
GROUP_BLOCKS = 8
COEFFS = (
    -5369.0 / 1800.0,
    12.0 / 7.0,
    -15.0 / 56.0,
    10.0 / 189.0,
    -1.0 / 112.0,
    2.0 / 1925.0,
    -1.0 / 16632.0,
)
KINETIC = 0.125
STEP_SIZE = 0.3
VMEM_BYTES = 40 * 1024 * 1024
BF16 = jnp.bfloat16
F32 = jnp.float32
NT = (((1,), (1,)), ((), ()))


def levels_of(count):
    chips = count // 2
    across = 2 ** (int(math.log2(chips)) // 3)
    return (2, 1), (across, 2), (chips // across, 2 * across)


def position(level):
    size, stride = level
    return lax.rem(lax.div(lax.axis_index("band"), jnp.int32(stride)), jnp.int32(size))


def shifted(array, count, level, step):
    size, stride = level
    pairs = []
    for device in range(count):
        place = device // stride % size
        pairs.append((device, device + ((place + step) % size - place) * stride))
    return lax.ppermute(array, "band", pairs)


def plane_matrix():
    plane = GY * GZ
    matrix = 3.0 * COEFFS[0] * np.eye(plane)
    cells = np.arange(plane)
    y, z = cells // GZ, cells % GZ
    for offset in range(1, 7):
        for sign in (1, -1):
            np.add.at(matrix, ((y + sign * offset) % GY * GZ + z, cells), COEFFS[offset])
            np.add.at(matrix, (y * GZ + (z + sign * offset) % GZ, cells), COEFFS[offset])
    matrix = KINETIC * matrix
    high = matrix.astype(ml_dtypes.bfloat16)
    low = (matrix - high.astype(np.float64)).astype(ml_dtypes.bfloat16)
    return np.stack([high, low])


def whole():
    return pl.BlockSpec(memory_space=pltpu.VMEM)


def params():
    return pltpu.CompilerParams(vmem_limit_bytes=VMEM_BYTES)


def cost(flops, *arrays):
    moved = sum(math.prod(a.shape) * jnp.dtype(a.dtype).itemsize for a in arrays)
    return pl.CostEstimate(flops=int(flops), bytes_accessed=int(moved), transcendentals=0)


def local_call(body, outs, args, flops=0, scratch=()):
    return pl.pallas_call(
        body,
        out_shape=outs,
        in_specs=[whole() for _ in args],
        out_specs=jax.tree.map(lambda _: whole(), outs),
        scratch_shapes=scratch,
        compiler_params=params(),
        cost_estimate=cost(flops, *args, *jax.tree.leaves(outs)),
    )(*args)


def struct(shape, dtype):
    return jax.ShapeDtypeStruct(shape, dtype)


def partial_body(core, bands, parts, r_ref, p_ref, *outs):
    c = position(core)
    for (other, first, rows), out_ref in zip(parts, outs):
        row = pl.multiple_of((1 - c if other else c) * (bands // 2) + first, 16)
        out_ref[...] = lax.dot_general(
            r_ref[pl.ds(row, rows), :], p_ref[...], NT, preferred_element_type=F32
        ).astype(out_ref.dtype)


def partial_intersections(response, projectors, core, parts):
    bands, cells = response.shape
    count = projectors.shape[0]
    tile = min(512, count)
    outs = [struct((rows, count), BF16 if other else F32) for other, _, rows in parts]
    done = sum(rows for _, _, rows in parts)
    return pl.pallas_call(
        functools.partial(partial_body, core, bands, parts),
        grid=(count // tile,),
        out_shape=outs,
        in_specs=[
            pl.BlockSpec((bands, cells), lambda i: (0, 0)),
            pl.BlockSpec((tile, cells), lambda i: (i, 0)),
        ],
        out_specs=[pl.BlockSpec((rows, tile), lambda i: (0, i)) for _, _, rows in parts],
        compiler_params=params(),
        cost_estimate=cost(2 * done * cells * count, projectors, *outs),
    )(response, projectors)


def add_core_body(across, along, keep_ref, taken_ref, out_ref):
    _, rows, width = out_ref.shape
    for k in range(along[0]):
        for i in range(across[0]):
            part = (slice(i * rows, (i + 1) * rows), slice(k * width, (k + 1) * width))
            total = keep_ref[part] + taken_ref[part].astype(F32)
            out_ref[k * across[0] + i] = total.astype(BF16)


def finish_body(scale, taken_ref, out_ref):
    total = taken_ref[0].astype(F32)
    for k in range(1, taken_ref.shape[0]):
        total = total + taken_ref[k].astype(F32)
    low = (total * scale).astype(BF16)
    for k in range(out_ref.shape[0]):
        out_ref[k] = low


def local_body(depth, r_ref, l_ref, h_ref, o_ref, m_ref, pot_ref, v_ref, e_ref, out_ref):
    plane = GY * GZ
    reach = 6

    def plane_at(j):
        if j < 0:
            ref, k = l_ref, j + reach
        elif j < depth:
            ref, k = r_ref, j
        else:
            ref, k = h_ref, j - depth
        return ref[:, k * plane : (k + 1) * plane]

    for j in range(depth):
        cols = slice(j * plane, (j + 1) * plane)
        low = plane_at(j)
        centre = low.astype(F32)
        total = jnp.dot(low, m_ref[0], preferred_element_type=F32)
        total = total + jnp.dot(low, m_ref[1], preferred_element_type=F32)
        for offset in range(1, 7):
            pair = plane_at(j + offset).astype(F32) + plane_at(j - offset).astype(F32)
            total = total + (KINETIC * COEFFS[offset]) * pair
        total = total + (e_ref[...] - pot_ref[:, cols]) * centre
        out_ref[:, cols] = total - v_ref[:, cols] * o_ref[:, cols].astype(F32)


def local_part(response, low, high, orbitals, matrix, potential, perturbing, energies):
    bands, cells = response.shape
    depth = cells // (GY * GZ)
    tile = 128
    out = struct((bands, cells), F32)
    here = pl.BlockSpec((tile, cells), lambda i: (i, 0))
    side = pl.BlockSpec((tile, low.shape[1]), lambda i: (i, 0))
    line = pl.BlockSpec((1, cells), lambda i: (0, 0))
    return pl.pallas_call(
        functools.partial(local_body, depth),
        grid=(bands // tile,),
        out_shape=out,
        in_specs=[
            here,
            side,
            side,
            here,
            pl.BlockSpec(matrix.shape, lambda i: (0, 0, 0)),
            line,
            line,
            pl.BlockSpec((tile, 1), lambda i: (i, 0)),
        ],
        out_specs=here,
        compiler_params=params(),
        cost_estimate=cost(2 * bands * cells * 300, low, high, low, low, out),
    )(response, low, high, orbitals, matrix, potential, perturbing, energies)


def first_orbital(group, group_rows, width, bands, blk):
    return max(0, min(group * group_rows - REACH * blk, bands - width))


def apply_body(core, across, group_rows, width, blk, *refs):
    own_ref, other_ref, p_ref, base_ref, o_ref, u_ref, s_out_ref, c_ref = refs
    bands, cells = u_ref.shape
    c = position(core)
    half = bands // 2
    _, rows, share = own_ref.shape
    for side, ref in enumerate((own_ref, other_ref)):
        first = (c if side == 0 else 1 - c) * half
        for chip in range(ref.shape[0]):
            k, i = divmod(chip, across[0])
            at = pl.multiple_of(first + i * rows, 16)
            c_ref[pl.ds(at, rows), k * share : (k + 1) * share] = ref[chip]
    tile = 256 if cells % 256 == 0 else 128
    for t in range(cells // tile):
        cols = slice(t * tile, (t + 1) * tile)
        u_ref[:, cols] = base_ref[:, cols] + jnp.dot(
            c_ref[...], p_ref[:, cols], preferred_element_type=F32
        )
    for g in range(bands // group_rows):
        start = first_orbital(g, group_rows, width, bands, blk)
        mine = slice(g * group_rows, (g + 1) * group_rows)
        s_out_ref[mine, :] = lax.dot_general(
            u_ref[mine, :].astype(BF16),
            o_ref[start : start + width, :],
            NT,
            preferred_element_type=F32,
        ).astype(BF16)


def project_body(group_rows, width, blk, *refs):
    w_ref, o_ref, u_ref, r_ref, first_ref, many_ref, updated_ref, residual_ref = refs
    bands = o_ref.shape[0]
    for g in range(bands // group_rows):
        start = first_orbital(g, group_rows, width, bands, blk)
        mine = slice(g * group_rows, (g + 1) * group_rows)
        block = (lax.broadcasted_iota(jnp.int32, (group_rows, width), 1) + start) // blk
        lowest = first_ref[mine, :]
        inside = (block >= lowest) & (block < lowest + many_ref[mine, :])
        weights = jnp.where(inside, w_ref[mine, :].astype(F32), 0.0).astype(BF16)
        residual = u_ref[mine, :] - jnp.dot(
            weights, o_ref[start : start + width, :], preferred_element_type=F32
        )
        residual_ref[mine, :] = residual.astype(BF16)
        updated_ref[mine, :] = (r_ref[mine, :].astype(F32) + STEP_SIZE * residual).astype(BF16)


def shards(
    count, response, orbitals, projectors, potential, perturbing, energies, window_start, block_count
):
    bands, local_cells = response.shape
    cells = local_cells * count
    projections = projectors.shape[0]
    halo = 6 * GY * GZ
    core, across, along = levels_of(count)
    chips = count // 2
    ring = (count, 1)
    ace_scale = 1.0 / math.sqrt(cells * projections)
    window_scale = 1.0 / math.sqrt(cells * bands)
    blk = bands // NBLK
    group_rows = GROUP_BLOCKS * blk
    width = (GROUP_BLOCKS + 2 * REACH) * blk
    half = bands // 2
    same_core = [[2 * chip + side for chip in range(chips)] for side in range(2)]
    matrix = jnp.asarray(plane_matrix())
    potential, perturbing = potential[None, :], perturbing[None, :]
    energies, window_start, block_count = (
        a[:, None] for a in (energies, window_start, block_count)
    )

    low = shifted(response[:, local_cells - halo :], count, ring, 1)
    high = shifted(response[:, :halo], count, ring, -1)

    (sent,) = partial_intersections(response, projectors, core, [(True, 0, half)])
    sent = shifted(sent, count, core, 1)
    (keep,) = partial_intersections(response, projectors, core, [(False, 0, half)])
    shares = struct((chips, half // across[0], projections // along[0]), BF16)
    parts = local_call(
        functools.partial(add_core_body, across, along), shares, [keep, sent]
    )
    parts = lax.all_to_all(parts, "band", 0, 0, axis_index_groups=same_core)
    low, high, parts = lax.optimization_barrier((low, high, parts))
    base = local_part(
        response, low, high, orbitals, matrix, potential, perturbing, energies
    )
    parts, base = lax.optimization_barrier((parts, base))
    parts = local_call(functools.partial(finish_body, ace_scale), shares, [parts])
    own = lax.all_to_all(parts, "band", 0, 0, axis_index_groups=same_core)
    other = shifted(own, count, core, 1)

    unprojected, sums = local_call(
        functools.partial(apply_body, core, across, group_rows, width, blk),
        [struct((bands, local_cells), F32), struct((bands, width), BF16)],
        [own, other, projectors, base, orbitals],
        flops=2 * bands * local_cells * (projections + width),
        scratch=[pltpu.VMEM((bands, projections), BF16)],
    )
    shares = struct((count, bands // count, width), BF16)
    sums = lax.all_to_all(sums.reshape(shares.shape), "band", 0, 0)
    weights = local_call(functools.partial(finish_body, window_scale), shares, [sums])
    weights = lax.all_to_all(weights, "band", 0, 0).reshape(bands, width)
    out = struct((bands, local_cells), BF16)
    return local_call(
        functools.partial(project_body, group_rows, width, blk),
        (out, out),
        [weights, orbitals, unprojected, response, window_start, block_count],
        flops=2 * bands * width * local_cells,
    )


def solution(mesh):
    in_specs = (
        P("pert", "band"),
        P(None, "band"),
        P(None, "band"),
        P("band"),
        P(("pert", "band")),
        P(),
        P(),
        P(),
    )
    out_specs = (P("pert", "band"), P("pert", "band"))
    body = functools.partial(shards, mesh.shape["band"])
    return jax.shard_map(body, mesh=mesh, in_specs=in_specs, out_specs=out_specs, check_vma=False)
```

```python
import functools
import math

import jax
import jax.numpy as jnp
import ml_dtypes
import numpy as np
from jax import lax
from jax.experimental import pallas as pl
from jax.experimental.pallas import tpu as pltpu
from jax.sharding import PartitionSpec as P

GY = 8
GZ = 16
NBLK = 32
REACH = 4
GROUP_BLOCKS = 8
COEFFS = (
    -5369.0 / 1800.0,
    12.0 / 7.0,
    -15.0 / 56.0,
    10.0 / 189.0,
    -1.0 / 112.0,
    2.0 / 1925.0,
    -1.0 / 16632.0,
)
KINETIC = 0.125
STEP_SIZE = 0.3
VMEM_BYTES = 40 * 1024 * 1024
BF16 = jnp.bfloat16
F32 = jnp.float32
NT = (((1,), (1,)), ((), ()))


def levels_of(count):
    chips = count // 2
    across = 2 ** (int(math.log2(chips)) // 3)
    return (2, 1), (across, 2), (chips // across, 2 * across)


def position(level):
    size, stride = level
    return lax.rem(lax.div(lax.axis_index("band"), jnp.int32(stride)), jnp.int32(size))


def shifted(array, count, level, step):
    size, stride = level
    pairs = []
    for device in range(count):
        place = device // stride % size
        pairs.append((device, device + ((place + step) % size - place) * stride))
    return lax.ppermute(array, "band", pairs)


def plane_matrix():
    plane = GY * GZ
    matrix = 3.0 * COEFFS[0] * np.eye(plane)
    cells = np.arange(plane)
    y, z = cells // GZ, cells % GZ
    for offset in range(1, 7):
        for sign in (1, -1):
            np.add.at(matrix, ((y + sign * offset) % GY * GZ + z, cells), COEFFS[offset])
            np.add.at(matrix, (y * GZ + (z + sign * offset) % GZ, cells), COEFFS[offset])
    matrix = KINETIC * matrix
    high = matrix.astype(ml_dtypes.bfloat16)
    low = (matrix - high.astype(np.float64)).astype(ml_dtypes.bfloat16)
    return np.stack([high, low])


def whole():
    return pl.BlockSpec(memory_space=pltpu.VMEM)


def params():
    return pltpu.CompilerParams(vmem_limit_bytes=VMEM_BYTES)


def cost(flops, *arrays):
    moved = sum(math.prod(a.shape) * jnp.dtype(a.dtype).itemsize for a in arrays)
    return pl.CostEstimate(flops=int(flops), bytes_accessed=int(moved), transcendentals=0)


def local_call(body, outs, args, flops=0, scratch=()):
    return pl.pallas_call(
        body,
        out_shape=outs,
        in_specs=[whole() for _ in args],
        out_specs=jax.tree.map(lambda _: whole(), outs),
        scratch_shapes=scratch,
        compiler_params=params(),
        cost_estimate=cost(flops, *args, *jax.tree.leaves(outs)),
    )(*args)


def struct(shape, dtype):
    return jax.ShapeDtypeStruct(shape, dtype)


def partial_body(core, bands, parts, r_ref, p_ref, *outs):
    c = position(core)
    for (other, first, rows), out_ref in zip(parts, outs):
        row = pl.multiple_of((1 - c if other else c) * (bands // 2) + first, 16)
        out_ref[...] = lax.dot_general(
            r_ref[pl.ds(row, rows), :], p_ref[...], NT, preferred_element_type=F32
        ).astype(out_ref.dtype)


def partial_intersections(response, projectors, core, parts):
    bands, cells = response.shape
    count = projectors.shape[0]
    tile = min(512, count)
    outs = [struct((rows, count), BF16 if other else F32) for other, _, rows in parts]
    done = sum(rows for _, _, rows in parts)
    return pl.pallas_call(
        functools.partial(partial_body, core, bands, parts),
        grid=(count // tile,),
        out_shape=outs,
        in_specs=[
            pl.BlockSpec((bands, cells), lambda i: (0, 0)),
            pl.BlockSpec((tile, cells), lambda i: (i, 0)),
        ],
        out_specs=[pl.BlockSpec((rows, tile), lambda i: (0, i)) for _, _, rows in parts],
        compiler_params=params(),
        cost_estimate=cost(2 * done * cells * count, projectors, *outs),
    )(response, projectors)


def split_body(received, level, along, first, *refs):
    keep_ref, taken, (own_ref, *sends) = refs[0], refs[1 : 1 + received], refs[1 + received :]
    size, _ = level
    me = position(level)
    rows, width = own_ref.shape
    for step, out in enumerate((own_ref, *sends)):
        place = lax.rem(me + step, jnp.int32(size))
        if along == 0:
            at = pl.multiple_of(place * rows, 16)
            part = (pl.ds(at, rows), slice(None))
            theirs = (pl.ds(pl.multiple_of(at + first, 16), rows), slice(None))
        else:
            part = (slice(None), pl.ds(pl.multiple_of(place * width, width), width))
            theirs = (slice(first, first + rows), part[1])
        total = keep_ref[part]
        for ref in taken:
            total = total + ref[theirs].astype(F32)
        out[...] = total.astype(out.dtype)


def split(keep, taken, level, along, first=0):
    size, _ = level
    shape = list(keep.shape)
    shape[along] //= size
    outs = [struct(shape, F32)] + [struct(shape, BF16)] * (size - 1)
    return local_call(
        functools.partial(split_body, len(taken), level, along, first), outs, [keep, *taken]
    )


def finish_body(scale, keep_ref, *refs):
    *taken, out_ref = refs
    total = keep_ref[...]
    for ref in taken:
        total = total + ref[...].astype(F32)
    out_ref[...] = (total * scale).astype(out_ref.dtype)


def finish(keep, taken, scale):
    return local_call(
        functools.partial(finish_body, scale), struct(keep.shape, BF16), [keep, *taken]
    )


def place_body(level, along, *refs):
    *parts, out_ref = refs
    size, _ = level
    me = position(level)
    width = parts[0].shape[along]
    for step, ref in enumerate(parts):
        at = pl.multiple_of(lax.rem(me - step + size, jnp.int32(size)) * width, width)
        if along == 0:
            out_ref[pl.ds(at, width), :] = ref[...]
        else:
            out_ref[:, pl.ds(at, width)] = ref[...]


def place(parts, level, along):
    shape = list(parts[0].shape)
    shape[along] *= level[0]
    return local_call(functools.partial(place_body, level, along), struct(shape, BF16), parts)


def local_body(depth, sizes, *refs):
    r_ref, l_ref, o_ref, m_ref, pot_ref, v_ref, e_ref, first_ref, many_ref, out_ref, mask_ref = refs
    plane = GY * GZ
    reach = 6
    for j in range(depth):
        cols = slice(j * plane, (j + 1) * plane)
        low = r_ref[:, cols]
        total = jnp.dot(low, m_ref[0], preferred_element_type=F32)
        total = total + jnp.dot(low, m_ref[1], preferred_element_type=F32)
        for offset in range(1, 7):
            pair = 0.0
            for k in (j - offset, j + offset):
                if 0 <= k < depth:
                    pair = pair + r_ref[:, k * plane : (k + 1) * plane].astype(F32)
                elif k < 0:
                    k = k + reach
                    pair = pair + l_ref[:, k * plane : (k + 1) * plane].astype(F32)
            total = total + (KINETIC * COEFFS[offset]) * pair
        total = total + (e_ref[...] - pot_ref[:, cols]) * low.astype(F32)
        out_ref[:, cols] = total - v_ref[:, cols] * o_ref[:, cols].astype(F32)
    group_rows, width, blk, bands = sizes
    start = jnp.clip(pl.program_id(0) * group_rows - REACH * blk, 0, bands - width)
    block = (lax.broadcasted_iota(jnp.int32, mask_ref.shape, 1) + start) // blk
    lowest = first_ref[...]
    inside = (block >= lowest) & (block < lowest + many_ref[...])
    mask_ref[...] = jnp.where(inside, 1.0, 0.0).astype(BF16)


def local_part(response, low, orbitals, matrix, lines, columns, group_rows, width, blk):
    bands, cells = response.shape
    depth = cells // (GY * GZ)
    outs = [struct((bands, cells), F32), struct((bands, width), BF16)]
    here = pl.BlockSpec((group_rows, cells), lambda i: (i, 0))
    side = pl.BlockSpec((group_rows, low.shape[1]), lambda i: (i, 0))
    line = pl.BlockSpec((1, cells), lambda i: (0, 0))
    column = pl.BlockSpec((group_rows, 1), lambda i: (i, 0))
    return pl.pallas_call(
        functools.partial(local_body, depth, (group_rows, width, blk, bands)),
        grid=(bands // group_rows,),
        out_shape=outs,
        in_specs=[
            here,
            side,
            here,
            pl.BlockSpec(matrix.shape, lambda i: (0, 0, 0)),
            line,
            line,
            column,
            column,
            column,
        ],
        out_specs=[here, pl.BlockSpec((group_rows, width), lambda i: (i, 0))],
        compiler_params=params(),
        cost_estimate=cost(2 * bands * cells * 300, low, low, low, *outs),
    )(response, low, orbitals, matrix, *lines, *columns)


def next_body(depth, h_ref, base_ref, out_ref):
    plane = GY * GZ
    for j in range(depth):
        cols = slice(j * plane, (j + 1) * plane)
        total = base_ref[:, cols]
        for k in range(depth, j + 7):
            at = k - depth
            far = h_ref[:, at * plane : (at + 1) * plane].astype(F32)
            total = total + (KINETIC * COEFFS[k - j]) * far
        out_ref[:, cols] = total


def add_next(base, high, group_rows):
    bands, cells = base.shape
    out = struct(base.shape, F32)
    here = pl.BlockSpec((group_rows, cells), lambda i: (i, 0))
    return pl.pallas_call(
        functools.partial(next_body, cells // (GY * GZ)),
        grid=(bands // group_rows,),
        out_shape=out,
        in_specs=[pl.BlockSpec((group_rows, high.shape[1]), lambda i: (i, 0)), here],
        out_specs=here,
        compiler_params=params(),
        cost_estimate=cost(bands * cells * 14, high, base, out),
    )(high, base)


def first_orbital(group, group_rows, width, bands, blk):
    return max(0, min(group * group_rows - REACH * blk, bands - width))


def apply_body(core, across, rows_x, group_rows, width, blk, *refs):
    size = across[0]
    blocks = refs[: 2 * (size + 1)]
    p_ref, base_ref, o_ref, u_ref, send_ref, keep_ref, c_ref, s_ref = refs[2 * (size + 1) :]
    bands, cells = u_ref.shape
    c, x = position(core), position(across)
    half = bands // 2
    share = rows_x // size
    for k, ref in enumerate(blocks):
        side, step = divmod(k, size + 1)
        at = (c if side == 0 else 1 - c) * half
        if step < size:
            at = at + lax.rem(x - step + size, jnp.int32(size)) * share
        else:
            at = at + rows_x
        c_ref[pl.ds(pl.multiple_of(at, 16), ref.shape[0]), :] = ref[...]
    tile = 256 if cells % 256 == 0 else 128
    for t in range(cells // tile):
        cols = slice(t * tile, (t + 1) * tile)
        u_ref[:, cols] = base_ref[:, cols] + jnp.dot(
            c_ref[...], p_ref[:, cols], preferred_element_type=F32
        )
    for g in range(bands // group_rows):
        start = first_orbital(g, group_rows, width, bands, blk)
        mine = slice(g * group_rows, (g + 1) * group_rows)
        s_ref[mine, :] = lax.dot_general(
            u_ref[mine, :].astype(BF16),
            o_ref[start : start + width, :],
            NT,
            preferred_element_type=F32,
        )
    send_ref[...] = s_ref[pl.ds(pl.multiple_of((1 - c) * half, half), half), :].astype(BF16)
    keep_ref[...] = s_ref[pl.ds(pl.multiple_of(c * half, half), half), :]


def sum_body(keep_ref, *refs):
    *taken, total_ref, low_ref = refs
    total = keep_ref[...]
    for ref in taken:
        total = total + ref[...].astype(F32)
    total_ref[...] = total
    low_ref[...] = total.astype(BF16)


def add_up(keep, taken):
    outs = [struct(keep.shape, F32), struct(keep.shape, BF16)]
    return local_call(sum_body, outs, [keep, *taken])


def project_body(core, across, group_rows, width, blk, *refs):
    size = across[0]
    blocks = refs[: 2 * size]
    o_ref, u_ref, r_ref, mask_ref, updated_ref, residual_ref, w_ref = refs[2 * size :]
    bands = o_ref.shape[0]
    half = bands // 2
    c, x = position(core), position(across)
    for k, ref in enumerate(blocks):
        side, step = divmod(k, size)
        at = (c if side == 0 else 1 - c) * half
        at = at + lax.rem(x - step + size, jnp.int32(size)) * ref.shape[0]
        w_ref[pl.ds(pl.multiple_of(at, 16), ref.shape[0]), :] = ref[...]
    for g in range(bands // group_rows):
        start = first_orbital(g, group_rows, width, bands, blk)
        mine = slice(g * group_rows, (g + 1) * group_rows)
        inside = mask_ref[mine, :].astype(F32) > 0.5
        weights = jnp.where(inside, w_ref[mine, :].astype(F32), 0.0).astype(BF16)
        residual = u_ref[mine, :] - jnp.dot(
            weights, o_ref[start : start + width, :], preferred_element_type=F32
        )
        residual_ref[mine, :] = residual.astype(BF16)
        updated_ref[mine, :] = (r_ref[mine, :].astype(F32) + STEP_SIZE * residual).astype(BF16)


def shards(
    count, response, orbitals, projectors, potential, perturbing, energies, window_start, block_count
):
    bands, local_cells = response.shape
    cells = local_cells * count
    projections = projectors.shape[0]
    halo = 6 * GY * GZ
    core, across, along = levels_of(count)
    ring = (count, 1)
    ace_scale = 1.0 / math.sqrt(cells * projections)
    window_scale = 1.0 / math.sqrt(cells * bands)
    blk = bands // NBLK
    group_rows = GROUP_BLOCKS * blk
    width = (GROUP_BLOCKS + 2 * REACH) * blk
    half = bands // 2
    step = 16 * across[0]
    rows_x = (2 * half // 3 + step // 2) // step * step
    rows_z = half - rows_x
    matrix = jnp.asarray(plane_matrix())
    lines = (potential[None, :], perturbing[None, :])
    columns = tuple(a[:, None] for a in (energies, window_start, block_count))

    def to(array, level):
        return [shifted(array, count, level, k) for k in range(1, level[0])]

    def parts_to(parts, level):
        return [shifted(part, count, level, k + 1) for k, part in enumerate(parts)]

    low = shifted(response[:, local_cells - halo :], count, ring, 1)

    (sent,) = partial_intersections(response, projectors, core, [(True, 0, half)])
    sent = shifted(sent, count, core, 1)
    keep_z, keep_x = partial_intersections(
        response, projectors, core, [(False, rows_x, rows_z), (False, 0, rows_x)]
    )
    keep_z, *parts_z = split(keep_z, [sent], along, 1, rows_x)
    keep_x, *parts_x = split(keep_x, [sent], across, 0, 0)
    taken_z, taken_x = lax.optimization_barrier(
        (parts_to(parts_z, along), parts_to(parts_x, across))
    )
    keep_x, *parts_x = split(keep_x, taken_x, along, 1)
    keep_z, *parts_z = split(keep_z, taken_z, across, 0)
    taken_x, taken_z = lax.optimization_barrier(
        (parts_to(parts_x, along), parts_to(parts_z, across))
    )
    share_z = finish(keep_z, taken_z, ace_scale)
    share_x = finish(keep_x, taken_x, ace_scale)

    head, low, _ = lax.optimization_barrier((response[:, :halo], low, share_z))
    high = shifted(head, count, ring, -1)
    base, mask = local_part(
        response, low, orbitals, matrix, lines, columns, group_rows, width, blk
    )
    pieces_x, pieces_z, base = lax.optimization_barrier(
        ([share_x, *to(share_x, along)], [share_z, *to(share_z, across)], base)
    )
    block_x = place(pieces_x, along, 1)
    block_z = place(pieces_z, across, 0)
    blocks_x = [block_x, *to(block_x, across)]
    block_z = place([block_z, *to(block_z, along)], along, 1)
    blocks = [*blocks_x, block_z]
    blocks += [shifted(block, count, core, 1) for block in blocks]

    base = add_next(base, high, group_rows)
    unprojected, send, keep = local_call(
        functools.partial(apply_body, core, across, rows_x, group_rows, width, blk),
        [
            struct((bands, local_cells), F32),
            struct((half, width), BF16),
            struct((half, width), F32),
        ],
        [*blocks, projectors, base, orbitals],
        flops=2 * bands * local_cells * (projections + width),
        scratch=[pltpu.VMEM((bands, projections), BF16), pltpu.VMEM((bands, width), F32)],
    )
    keep, *parts = split(keep, to(send, core), across, 0)
    total, low = add_up(keep, parts_to(parts, across))
    weights = finish(total, to(low, along), window_scale)
    weights = [weights, *to(weights, across)]
    weights += [shifted(block, count, core, 1) for block in weights]
    out = struct((bands, local_cells), BF16)
    return local_call(
        functools.partial(project_body, core, across, group_rows, width, blk),
        (out, out),
        [*weights, orbitals, unprojected, response, mask],
        flops=2 * bands * width * local_cells,
        scratch=[pltpu.VMEM((bands, width), BF16)],
    )


def solution(mesh):
    in_specs = (
        P("pert", "band"),
        P(None, "band"),
        P(None, "band"),
        P("band"),
        P(("pert", "band")),
        P(),
        P(),
        P(),
    )
    out_specs = (P("pert", "band"), P("pert", "band"))
    body = functools.partial(shards, mesh.shape["band"])
    return jax.shard_map(body, mesh=mesh, in_specs=in_specs, out_specs=out_specs, check_vma=False)
```

```python
import functools
import math

import jax
import jax.numpy as jnp
import ml_dtypes
import numpy as np
from jax import lax
from jax.experimental import pallas as pl
from jax.experimental.pallas import tpu as pltpu
from jax.sharding import PartitionSpec as P

GY = 8
GZ = 16
NBLK = 32
REACH = 4
GROUP_BLOCKS = 8
COEFFS = (
    -5369.0 / 1800.0,
    12.0 / 7.0,
    -15.0 / 56.0,
    10.0 / 189.0,
    -1.0 / 112.0,
    2.0 / 1925.0,
    -1.0 / 16632.0,
)
KINETIC = 0.125
STEP_SIZE = 0.3
VMEM_BYTES = 40 * 1024 * 1024
BF16 = jnp.bfloat16
F32 = jnp.float32
NT = (((1,), (1,)), ((), ()))


def levels_of(count):
    chips = count // 2
    across = 2 ** (int(math.log2(chips)) // 3)
    return (2, 1), (across, 2), (chips // across, 2 * across)


def position(level):
    size, stride = level
    return lax.rem(lax.div(lax.axis_index("band"), jnp.int32(stride)), jnp.int32(size))


def shifted(array, count, level, step):
    size, stride = level
    pairs = []
    for device in range(count):
        place = device // stride % size
        pairs.append((device, device + ((place + step) % size - place) * stride))
    return lax.ppermute(array, "band", pairs)


def plane_matrix():
    plane = GY * GZ
    matrix = 3.0 * COEFFS[0] * np.eye(plane)
    cells = np.arange(plane)
    y, z = cells // GZ, cells % GZ
    for offset in range(1, 7):
        for sign in (1, -1):
            np.add.at(matrix, ((y + sign * offset) % GY * GZ + z, cells), COEFFS[offset])
            np.add.at(matrix, (y * GZ + (z + sign * offset) % GZ, cells), COEFFS[offset])
    matrix = KINETIC * matrix
    high = matrix.astype(ml_dtypes.bfloat16)
    low = (matrix - high.astype(np.float64)).astype(ml_dtypes.bfloat16)
    return np.stack([high, low])


def whole():
    return pl.BlockSpec(memory_space=pltpu.VMEM)


def params():
    return pltpu.CompilerParams(vmem_limit_bytes=VMEM_BYTES)


def cost(flops, *arrays):
    moved = sum(math.prod(a.shape) * jnp.dtype(a.dtype).itemsize for a in arrays)
    return pl.CostEstimate(flops=int(flops), bytes_accessed=int(moved), transcendentals=0)


def local_call(body, outs, args, flops=0, scratch=()):
    return pl.pallas_call(
        body,
        out_shape=outs,
        in_specs=[whole() for _ in args],
        out_specs=jax.tree.map(lambda _: whole(), outs),
        scratch_shapes=scratch,
        compiler_params=params(),
        cost_estimate=cost(flops, *args, *jax.tree.leaves(outs)),
    )(*args)


def struct(shape, dtype):
    return jax.ShapeDtypeStruct(shape, dtype)


def partial_body(core, other, r_ref, p_ref, out_ref):
    rows = out_ref.shape[0]
    c = position(core)
    row = pl.multiple_of((1 - c if other else c) * rows, rows)
    out_ref[...] = lax.dot_general(
        r_ref[pl.ds(row, rows), :], p_ref[...], NT, preferred_element_type=F32
    ).astype(out_ref.dtype)


def partial_intersections(response, projectors, core, other):
    bands, cells = response.shape
    count = projectors.shape[0]
    rows = bands // 2
    tile = min(512, count)
    out = struct((rows, count), BF16 if other else F32)
    return pl.pallas_call(
        functools.partial(partial_body, core, other),
        grid=(count // tile,),
        out_shape=out,
        in_specs=[
            pl.BlockSpec((bands, cells), lambda i: (0, 0)),
            pl.BlockSpec((tile, cells), lambda i: (i, 0)),
        ],
        out_specs=pl.BlockSpec((rows, tile), lambda i: (0, i)),
        compiler_params=params(),
        cost_estimate=cost(2 * rows * cells * count, projectors, out),
    )(response, projectors)


def split_body(received, level, along, first, *refs):
    keep_ref, taken, (own_ref, *sends) = refs[0], refs[1 : 1 + received], refs[1 + received :]
    size, _ = level
    me = position(level)
    rows, width = own_ref.shape
    for step, out in enumerate((own_ref, *sends)):
        at = lax.rem(me + step, jnp.int32(size))
        if along == 0:
            part = (pl.ds(pl.multiple_of(at * rows + first, 16), rows), slice(None))
        else:
            part = (slice(first, first + rows), pl.ds(pl.multiple_of(at * width, width), width))
        total = keep_ref[part]
        for ref in taken:
            total = total + ref[part].astype(F32)
        out[...] = total.astype(out.dtype)


def split(keep, taken, level, along, rows=None, first=0):
    size, _ = level
    shape = [rows or keep.shape[0], keep.shape[1]]
    shape[along] //= size
    outs = [struct(shape, F32)] + [struct(shape, BF16)] * (size - 1)
    return local_call(
        functools.partial(split_body, len(taken), level, along, first), outs, [keep, *taken]
    )


def finish_body(scale, keep_ref, *refs):
    *taken, out_ref = refs
    total = keep_ref[...]
    for ref in taken:
        total = total + ref[...].astype(F32)
    out_ref[...] = (total * scale).astype(out_ref.dtype)


def finish(keep, taken, scale):
    return local_call(
        functools.partial(finish_body, scale), struct(keep.shape, BF16), [keep, *taken]
    )


def place_body(level, along, *refs):
    *parts, out_ref = refs
    size, _ = level
    me = position(level)
    width = parts[0].shape[along]
    for step, ref in enumerate(parts):
        at = pl.multiple_of(lax.rem(me - step + size, jnp.int32(size)) * width, width)
        if along == 0:
            out_ref[pl.ds(at, width), :] = ref[...]
        else:
            out_ref[:, pl.ds(at, width)] = ref[...]


def place(parts, level, along):
    shape = list(parts[0].shape)
    shape[along] *= level[0]
    return local_call(functools.partial(place_body, level, along), struct(shape, BF16), parts)


def local_body(depth, sizes, *refs):
    r_ref, l_ref, h_ref, o_ref, m_ref, pot_ref, v_ref, e_ref = refs[:8]
    first_ref, many_ref, out_ref, mask_ref = refs[8:]
    plane = GY * GZ
    reach = 6

    def plane_at(j):
        if j < 0:
            ref, k = l_ref, j + reach
        elif j < depth:
            ref, k = r_ref, j
        else:
            ref, k = h_ref, j - depth
        return ref[:, k * plane : (k + 1) * plane]

    for j in range(depth):
        cols = slice(j * plane, (j + 1) * plane)
        low = plane_at(j)
        total = jnp.dot(low, m_ref[0], preferred_element_type=F32)
        total = total + jnp.dot(low, m_ref[1], preferred_element_type=F32)
        for offset in range(1, 7):
            pair = plane_at(j + offset).astype(F32) + plane_at(j - offset).astype(F32)
            total = total + (KINETIC * COEFFS[offset]) * pair
        total = total + (e_ref[...] - pot_ref[:, cols]) * low.astype(F32)
        out_ref[:, cols] = total - v_ref[:, cols] * o_ref[:, cols].astype(F32)
    group_rows, width, blk, bands = sizes
    start = jnp.clip(pl.program_id(0) * group_rows - REACH * blk, 0, bands - width)
    block = (lax.broadcasted_iota(jnp.int32, mask_ref.shape, 1) + start) // blk
    lowest = first_ref[...]
    inside = (block >= lowest) & (block < lowest + many_ref[...])
    mask_ref[...] = jnp.where(inside, 1.0, 0.0).astype(BF16)


def local_part(response, low, high, orbitals, matrix, lines, columns, group_rows, width, blk):
    bands, cells = response.shape
    depth = cells // (GY * GZ)
    outs = [struct((bands, cells), F32), struct((bands, width), BF16)]
    here = pl.BlockSpec((group_rows, cells), lambda i: (i, 0))
    side = pl.BlockSpec((group_rows, low.shape[1]), lambda i: (i, 0))
    line = pl.BlockSpec((1, cells), lambda i: (0, 0))
    column = pl.BlockSpec((group_rows, 1), lambda i: (i, 0))
    return pl.pallas_call(
        functools.partial(local_body, depth, (group_rows, width, blk, bands)),
        grid=(bands // group_rows,),
        out_shape=outs,
        in_specs=[
            here,
            side,
            side,
            here,
            pl.BlockSpec(matrix.shape, lambda i: (0, 0, 0)),
            line,
            line,
            column,
            column,
            column,
        ],
        out_specs=[here, pl.BlockSpec((group_rows, width), lambda i: (i, 0))],
        compiler_params=params(),
        cost_estimate=cost(2 * bands * cells * 300, low, high, low, low, *outs),
    )(response, low, high, orbitals, matrix, *lines, *columns)


def first_orbital(group, group_rows, width, bands, blk):
    return max(0, min(group * group_rows - REACH * blk, bands - width))


def apply_body(core, across, rows_x, group_rows, width, blk, *refs):
    size = across[0]
    blocks = refs[: 2 * (size + 1)]
    p_ref, base_ref, o_ref, u_ref, send_ref, keep_ref, c_ref, s_ref = refs[2 * (size + 1) :]
    bands, cells = u_ref.shape
    c, x = position(core), position(across)
    half = bands // 2
    share = rows_x // size
    for k, ref in enumerate(blocks):
        side, step = divmod(k, size + 1)
        at = (c if side == 0 else 1 - c) * half
        if step < size:
            at = at + lax.rem(x - step + size, jnp.int32(size)) * share
        else:
            at = at + rows_x
        c_ref[pl.ds(pl.multiple_of(at, 16), ref.shape[0]), :] = ref[...]
    tile = 256 if cells % 256 == 0 else 128
    for t in range(cells // tile):
        cols = slice(t * tile, (t + 1) * tile)
        u_ref[:, cols] = base_ref[:, cols] + jnp.dot(
            c_ref[...], p_ref[:, cols], preferred_element_type=F32
        )
    for g in range(bands // group_rows):
        start = first_orbital(g, group_rows, width, bands, blk)
        mine = slice(g * group_rows, (g + 1) * group_rows)
        s_ref[mine, :] = lax.dot_general(
            u_ref[mine, :].astype(BF16),
            o_ref[start : start + width, :],
            NT,
            preferred_element_type=F32,
        )
    send_ref[...] = s_ref[pl.ds(pl.multiple_of((1 - c) * half, half), half), :].astype(BF16)
    keep_ref[...] = s_ref[pl.ds(pl.multiple_of(c * half, half), half), :]


def sum_body(keep_ref, *refs):
    *taken, total_ref, low_ref = refs
    total = keep_ref[...]
    for ref in taken:
        total = total + ref[...].astype(F32)
    total_ref[...] = total
    low_ref[...] = total.astype(BF16)


def add_up(keep, taken):
    outs = [struct(keep.shape, F32), struct(keep.shape, BF16)]
    return local_call(sum_body, outs, [keep, *taken])


def project_body(core, across, width, blk, *refs):
    size = across[0]
    blocks = refs[: 2 * size]
    o_ref, u_ref, r_ref, mask_ref, updated_ref, residual_ref, w_ref = refs[2 * size :]
    bands = o_ref.shape[0]
    half = bands // 2
    group_rows = u_ref.shape[0]
    g = pl.program_id(0)

    @pl.when(g == 0)
    def _():
        c, x = position(core), position(across)
        for k, ref in enumerate(blocks):
            side, step = divmod(k, size)
            at = (c if side == 0 else 1 - c) * half
            at = at + lax.rem(x - step + size, jnp.int32(size)) * ref.shape[0]
            w_ref[pl.ds(pl.multiple_of(at, 16), ref.shape[0]), :] = ref[...]

    start = jnp.clip(g * group_rows - REACH * blk, 0, bands - width)
    window = o_ref[pl.ds(pl.multiple_of(start, blk), width), :]
    mine = pl.ds(pl.multiple_of(g * group_rows, group_rows), group_rows)
    inside = mask_ref[...].astype(F32) > 0.5
    weights = jnp.where(inside, w_ref[mine, :].astype(F32), 0.0).astype(BF16)
    residual = u_ref[...] - jnp.dot(weights, window, preferred_element_type=F32)
    residual_ref[...] = residual.astype(BF16)
    updated_ref[...] = (r_ref[...].astype(F32) + STEP_SIZE * residual).astype(BF16)


def project(weights, orbitals, unprojected, response, mask, core, across, group_rows, blk):
    bands, cells = response.shape
    width = mask.shape[1]
    out = struct((bands, cells), BF16)
    here = pl.BlockSpec((group_rows, cells), lambda g: (g, 0))

    def full(a):
        return pl.BlockSpec(a.shape, lambda g: (0, 0))

    return pl.pallas_call(
        functools.partial(project_body, core, across, width, blk),
        grid=(bands // group_rows,),
        out_shape=(out, out),
        in_specs=[
            *[full(a) for a in weights],
            full(orbitals),
            here,
            here,
            pl.BlockSpec((group_rows, width), lambda g: (g, 0)),
        ],
        out_specs=(here, here),
        scratch_shapes=[pltpu.VMEM((bands, width), BF16)],
        compiler_params=params(),
        cost_estimate=cost(2 * bands * width * cells, orbitals, unprojected, response, out, out),
    )(*weights, orbitals, unprojected, response, mask)


def shards(
    count, response, orbitals, projectors, potential, perturbing, energies, window_start, block_count
):
    bands, local_cells = response.shape
    cells = local_cells * count
    projections = projectors.shape[0]
    halo = 6 * GY * GZ
    core, across, along = levels_of(count)
    ring = (count, 1)
    ace_scale = 1.0 / math.sqrt(cells * projections)
    window_scale = 1.0 / math.sqrt(cells * bands)
    blk = bands // NBLK
    group_rows = GROUP_BLOCKS * blk
    width = (GROUP_BLOCKS + 2 * REACH) * blk
    half = bands // 2
    rows_x = half // 2
    rows_z = half - rows_x
    matrix = jnp.asarray(plane_matrix())
    lines = (potential[None, :], perturbing[None, :])
    columns = tuple(a[:, None] for a in (energies, window_start, block_count))

    def to(array, level):
        return [shifted(array, count, level, k) for k in range(1, level[0])]

    def parts_to(parts, level):
        return [shifted(part, count, level, k + 1) for k, part in enumerate(parts)]

    low = shifted(response[:, local_cells - halo :], count, ring, 1)
    high = shifted(response[:, :halo], count, ring, -1)

    sent = shifted(partial_intersections(response, projectors, core, True), count, core, 1)
    keep = partial_intersections(response, projectors, core, False)
    keep_z, *parts_z = split(keep, [sent], along, 1, rows_z, rows_x)
    keep_x, *parts_x = split(keep, [sent], across, 0, rows_x, 0)
    taken_z, taken_x, low, high = lax.optimization_barrier(
        (parts_to(parts_z, along), parts_to(parts_x, across), low, high)
    )
    base, mask = local_part(
        response, low, high, orbitals, matrix, lines, columns, group_rows, width, blk
    )
    keep_x, *parts_x = split(keep_x, taken_x, along, 1)
    keep_z, *parts_z = split(keep_z, taken_z, across, 0)
    taken_x, taken_z, base = lax.optimization_barrier(
        (parts_to(parts_x, along), parts_to(parts_z, across), base)
    )
    share_z = finish(keep_z, taken_z, ace_scale)
    share_x = finish(keep_x, taken_x, ace_scale)

    pieces_x, pieces_z = lax.optimization_barrier(
        ([share_x, *to(share_x, along)], [share_z, *to(share_z, across)])
    )
    block_x = place(pieces_x, along, 1)
    block_z = place(pieces_z, across, 0)
    blocks_x = [block_x, *to(block_x, across)]
    block_z = place([block_z, *to(block_z, along)], along, 1)
    blocks = [*blocks_x, block_z]
    blocks += [shifted(block, count, core, 1) for block in blocks]

    unprojected, send, keep = local_call(
        functools.partial(apply_body, core, across, rows_x, group_rows, width, blk),
        [
            struct((bands, local_cells), F32),
            struct((half, width), BF16),
            struct((half, width), F32),
        ],
        [*blocks, projectors, base, orbitals],
        flops=2 * bands * local_cells * (projections + width),
        scratch=[pltpu.VMEM((bands, projections), BF16), pltpu.VMEM((bands, width), F32)],
    )
    keep, *parts = split(keep, to(send, core), across, 0)
    total, low = add_up(keep, parts_to(parts, across))
    weights = finish(total, to(low, along), window_scale)
    weights = [weights, *to(weights, across)]
    weights += [shifted(block, count, core, 1) for block in weights]
    return project(
        weights, orbitals, unprojected, response, mask, core, across, group_rows, blk
    )


def solution(mesh):
    in_specs = (
        P("pert", "band"),
        P(None, "band"),
        P(None, "band"),
        P("band"),
        P(("pert", "band")),
        P(),
        P(),
        P(),
    )
    out_specs = (P("pert", "band"), P("pert", "band"))
    body = functools.partial(shards, mesh.shape["band"])
    return jax.shard_map(body, mesh=mesh, in_specs=in_specs, out_specs=out_specs, check_vma=False)
```

```python
import functools
import math

import jax
import jax.numpy as jnp
import ml_dtypes
import numpy as np
from jax import lax
from jax.experimental import pallas as pl
from jax.experimental.pallas import tpu as pltpu
from jax.sharding import PartitionSpec as P

GY = 8
GZ = 16
NBLK = 32
REACH = 4
GROUP_BLOCKS = 8
COEFFS = (
    -5369.0 / 1800.0,
    12.0 / 7.0,
    -15.0 / 56.0,
    10.0 / 189.0,
    -1.0 / 112.0,
    2.0 / 1925.0,
    -1.0 / 16632.0,
)
KINETIC = 0.125
STEP_SIZE = 0.3
MIB = 1024 * 1024
VMEM_BYTES = 40 * MIB
REDUCE_SHARE = 0.25
GATHER_SHARE = 0.5
BF16 = jnp.bfloat16
F32 = jnp.float32
NT = (((1,), (1,)), ((), ()))


def levels_of(count):
    chips = count // 2
    across = 2 ** (int(math.log2(chips)) // 3)
    return (2, 1), (across, 2), (chips // across, 2 * across)


def position(level):
    size, stride = level
    return lax.rem(lax.div(lax.axis_index("band"), jnp.int32(stride)), jnp.int32(size))


def shifted(array, count, level, step):
    size, stride = level
    pairs = []
    for device in range(count):
        place = device // stride % size
        pairs.append((device, device + ((place + step) % size - place) * stride))
    return lax.ppermute(array, "band", pairs)


def plane_matrix():
    plane = GY * GZ
    matrix = 3.0 * COEFFS[0] * np.eye(plane)
    cells = np.arange(plane)
    y, z = cells // GZ, cells % GZ
    for offset in range(1, 7):
        for sign in (1, -1):
            np.add.at(matrix, ((y + sign * offset) % GY * GZ + z, cells), COEFFS[offset])
            np.add.at(matrix, (y * GZ + (z + sign * offset) % GZ, cells), COEFFS[offset])
    matrix = KINETIC * matrix
    high = matrix.astype(ml_dtypes.bfloat16)
    low = (matrix - high.astype(np.float64)).astype(ml_dtypes.bfloat16)
    return np.stack([high, low])


def whole():
    return pl.BlockSpec(memory_space=pltpu.VMEM)


def params(size=VMEM_BYTES):
    return pltpu.CompilerParams(vmem_limit_bytes=size)


def cost(flops, *arrays):
    moved = sum(math.prod(a.shape) * jnp.dtype(a.dtype).itemsize for a in arrays)
    return pl.CostEstimate(flops=int(flops), bytes_accessed=int(moved), transcendentals=0)


def local_call(body, outs, args, flops=0, scratch=()):
    return pl.pallas_call(
        body,
        out_shape=outs,
        in_specs=[whole() for _ in args],
        out_specs=jax.tree.map(lambda _: whole(), outs),
        scratch_shapes=scratch,
        compiler_params=params(),
        cost_estimate=cost(flops, *args, *jax.tree.leaves(outs)),
    )(*args)


def struct(shape, dtype):
    return jax.ShapeDtypeStruct(shape, dtype)


def partial_body(core, other, r_ref, p_ref, out_ref):
    rows = out_ref.shape[0]
    c = position(core)
    row = pl.multiple_of((1 - c if other else c) * rows, rows)
    out_ref[...] = lax.dot_general(
        r_ref[pl.ds(row, rows), :], p_ref[...], NT, preferred_element_type=F32
    ).astype(out_ref.dtype)


def partial_intersections(response, projectors, core, other):
    bands, cells = response.shape
    count = projectors.shape[0]
    rows = bands // 2
    tile = min(512, count)
    out = struct((rows, count), BF16 if other else F32)
    return pl.pallas_call(
        functools.partial(partial_body, core, other),
        grid=(count // tile,),
        out_shape=out,
        in_specs=[
            pl.BlockSpec((bands, cells), lambda i: (0, 0)),
            pl.BlockSpec((tile, cells), lambda i: (i, 0)),
        ],
        out_specs=pl.BlockSpec((rows, tile), lambda i: (0, i)),
        compiler_params=params((56 if other else 40) * MIB),
        cost_estimate=cost(2 * rows * cells * count, projectors, out),
    )(response, projectors)


def rows_at(place, size):
    return pl.ds(pl.multiple_of(place * size, 16), size)


def cols_at(place, size):
    return pl.ds(pl.multiple_of(place * size, size), size)


def total_of(keep_ref, taken, part):
    total = keep_ref[part]
    for ref in taken:
        total = total + ref[part].astype(F32)
    return total


def first_x_body(level, block, keep_ref, taken_ref, *outs):
    me = position(level)
    rows = outs[0].shape[0]
    for step, out in enumerate(outs):
        at = lax.rem(me + step, jnp.int32(level[0])) * block
        part = (pl.ds(pl.multiple_of(at, 16), rows), slice(None))
        out[...] = total_of(keep_ref, [taken_ref], part).astype(out.dtype)


def first_z_body(level, block, first, keep_ref, taken_ref, *outs):
    me = position(level)
    rows = block - first
    width = outs[0].shape[1]
    for step, out in enumerate(outs):
        cols = cols_at(lax.rem(me + step, jnp.int32(level[0])), width)
        for i in range(out.shape[0] // rows):
            part = (slice(i * block + first, (i + 1) * block), cols)
            mine = slice(i * rows, (i + 1) * rows)
            out[mine, :] = total_of(keep_ref, [taken_ref], part).astype(out.dtype)


def split_body(received, level, along, *refs):
    keep_ref, taken, outs = refs[0], refs[1 : 1 + received], refs[1 + received :]
    me = position(level)
    rows, width = outs[0].shape
    for step, out in enumerate(outs):
        at = lax.rem(me + step, jnp.int32(level[0]))
        if along == 0:
            part = (rows_at(at, rows), slice(None))
        else:
            part = (slice(None), cols_at(at, width))
        out[...] = total_of(keep_ref, taken, part).astype(out.dtype)


def shares_of(shape, count):
    return [struct(shape, F32)] + [struct(shape, BF16)] * (count - 1)


def split(keep, taken, level, along):
    shape = list(keep.shape)
    shape[along] //= level[0]
    return local_call(
        functools.partial(split_body, len(taken), level, along),
        shares_of(shape, level[0]),
        [keep, *taken],
    )


def finish_body(scale, keep_ref, *refs):
    *taken, out_ref = refs
    out_ref[...] = (total_of(keep_ref, taken, ...) * scale).astype(out_ref.dtype)


def finish(keep, taken, scale):
    return local_call(
        functools.partial(finish_body, scale), struct(keep.shape, BF16), [keep, *taken]
    )


def finish_both_body(scale, received, *refs):
    outs = refs[-2:]
    cut = outs[0].shape[0]
    row = 0
    for keep_ref, *taken in (refs[: 1 + received], refs[1 + received : -2]):
        low = (total_of(keep_ref, taken, ...) * scale).astype(BF16)
        end = row + keep_ref.shape[0]
        for out, first, last in ((outs[0], 0, cut), (outs[1], cut, cut + outs[1].shape[0])):
            top, bottom = max(row, first), min(end, last)
            if top < bottom:
                out[top - first : bottom - first, :] = low[top - row : bottom - row, :]
        row = end


def place_body(level, along, *refs):
    *parts, out_ref = refs
    size, _ = level
    me = position(level)
    width = parts[0].shape[along]
    for step, ref in enumerate(parts):
        at = pl.multiple_of(lax.rem(me - step + size, jnp.int32(size)) * width, width)
        if along == 0:
            out_ref[pl.ds(at, width), :] = ref[...]
        else:
            out_ref[:, pl.ds(at, width)] = ref[...]


def place(parts, level, along):
    shape = list(parts[0].shape)
    shape[along] *= level[0]
    return local_call(functools.partial(place_body, level, along), struct(shape, BF16), parts)


def local_body(depth, sizes, *refs):
    r_ref, l_ref, h_ref, o_ref, m_ref, pot_ref, v_ref, e_ref = refs[:8]
    first_ref, many_ref, out_ref, mask_ref = refs[8:]
    plane = GY * GZ
    reach = 6

    def plane_at(j):
        if j < 0:
            ref, k = l_ref, j + reach
        elif j < depth:
            ref, k = r_ref, j
        else:
            ref, k = h_ref, j - depth
        return ref[:, k * plane : (k + 1) * plane]

    for j in range(depth):
        cols = slice(j * plane, (j + 1) * plane)
        low = plane_at(j)
        total = jnp.dot(low, m_ref[0], preferred_element_type=F32)
        total = total + jnp.dot(low, m_ref[1], preferred_element_type=F32)
        for offset in range(1, 7):
            pair = plane_at(j + offset).astype(F32) + plane_at(j - offset).astype(F32)
            total = total + (KINETIC * COEFFS[offset]) * pair
        total = total + (e_ref[...] - pot_ref[:, cols]) * low.astype(F32)
        out_ref[:, cols] = total - v_ref[:, cols] * o_ref[:, cols].astype(F32)
    group_rows, width, blk, bands = sizes
    start = jnp.clip(pl.program_id(0) * group_rows - REACH * blk, 0, bands - width)
    block = (lax.broadcasted_iota(jnp.int32, mask_ref.shape, 1) + start) // blk
    lowest = first_ref[...]
    inside = (block >= lowest) & (block < lowest + many_ref[...])
    mask_ref[...] = jnp.where(inside, 1.0, 0.0).astype(BF16)


def local_part(response, low, high, orbitals, matrix, lines, columns, group_rows, width, blk):
    bands, cells = response.shape
    depth = cells // (GY * GZ)
    outs = [struct((bands, cells), F32), struct((bands, width), BF16)]
    here = pl.BlockSpec((group_rows, cells), lambda i: (i, 0))
    side = pl.BlockSpec((group_rows, low.shape[1]), lambda i: (i, 0))
    line = pl.BlockSpec((1, cells), lambda i: (0, 0))
    column = pl.BlockSpec((group_rows, 1), lambda i: (i, 0))
    return pl.pallas_call(
        functools.partial(local_body, depth, (group_rows, width, blk, bands)),
        grid=(bands // group_rows,),
        out_shape=outs,
        in_specs=[
            here,
            side,
            side,
            here,
            pl.BlockSpec(matrix.shape, lambda i: (0, 0, 0)),
            line,
            line,
            column,
            column,
            column,
        ],
        out_specs=[here, pl.BlockSpec((group_rows, width), lambda i: (i, 0))],
        compiler_params=params(),
        cost_estimate=cost(2 * bands * cells * 300, low, high, low, low, *outs),
    )(response, low, high, orbitals, matrix, *lines, *columns)


def first_orbital(group, group_rows, width, bands, blk):
    return max(0, min(group * group_rows - REACH * blk, bands - width))


def apply_body(core, across, block, group_rows, width, blk, *refs):
    size = across[0]
    blocks = refs[: 2 * (size + 1)]
    p_ref, base_ref, o_ref, u_ref, send_ref, keep_ref, c_ref, s_ref = refs[2 * (size + 1) :]
    bands, cells = u_ref.shape
    c, x = position(core), position(across)
    half = bands // 2
    first = blocks[0].shape[0]
    for k, ref in enumerate(blocks):
        side, step = divmod(k, size + 1)
        at = (c if side == 0 else 1 - c) * half
        if step < size:
            at = at + lax.rem(x - step + size, jnp.int32(size)) * block
            c_ref[pl.ds(pl.multiple_of(at, 16), first), :] = ref[...]
        else:
            rest = block - first
            for i in range(size):
                there = pl.ds(pl.multiple_of(at + i * block + first, 16), rest)
                c_ref[there, :] = ref[i * rest : (i + 1) * rest, :]
    tile = 256 if cells % 256 == 0 else 128
    for t in range(cells // tile):
        cols = slice(t * tile, (t + 1) * tile)
        u_ref[:, cols] = base_ref[:, cols] + jnp.dot(
            c_ref[...], p_ref[:, cols], preferred_element_type=F32
        )
    for g in range(bands // group_rows):
        start = first_orbital(g, group_rows, width, bands, blk)
        mine = slice(g * group_rows, (g + 1) * group_rows)
        s_ref[mine, :] = lax.dot_general(
            u_ref[mine, :].astype(BF16),
            o_ref[start : start + width, :],
            NT,
            preferred_element_type=F32,
        )
    send_ref[...] = s_ref[pl.ds(pl.multiple_of((1 - c) * half, half), half), :].astype(BF16)
    keep_ref[...] = s_ref[pl.ds(pl.multiple_of(c * half, half), half), :]


def sum_body(keep_ref, *refs):
    *taken, total_ref, low_ref = refs
    total = keep_ref[...]
    for ref in taken:
        total = total + ref[...].astype(F32)
    total_ref[...] = total
    low_ref[...] = total.astype(BF16)


def add_up(keep, taken):
    outs = [struct(keep.shape, F32), struct(keep.shape, BF16)]
    return local_call(sum_body, outs, [keep, *taken])


def project_body(core, across, width, blk, *refs):
    size = across[0]
    blocks = refs[: 2 * size]
    o_ref, u_ref, r_ref, mask_ref, updated_ref, residual_ref, w_ref = refs[2 * size :]
    bands = o_ref.shape[0]
    half = bands // 2
    group_rows = u_ref.shape[0]
    g = pl.program_id(0)

    @pl.when(g == 0)
    def _():
        c, x = position(core), position(across)
        for k, ref in enumerate(blocks):
            side, step = divmod(k, size)
            at = (c if side == 0 else 1 - c) * half
            at = at + lax.rem(x - step + size, jnp.int32(size)) * ref.shape[0]
            w_ref[pl.ds(pl.multiple_of(at, 16), ref.shape[0]), :] = ref[...]

    start = jnp.clip(g * group_rows - REACH * blk, 0, bands - width)
    window = o_ref[pl.ds(pl.multiple_of(start, blk), width), :]
    mine = pl.ds(pl.multiple_of(g * group_rows, group_rows), group_rows)
    inside = mask_ref[...].astype(F32) > 0.5
    weights = jnp.where(inside, w_ref[mine, :].astype(F32), 0.0).astype(BF16)
    residual = u_ref[...] - jnp.dot(weights, window, preferred_element_type=F32)
    residual_ref[...] = residual.astype(BF16)
    updated_ref[...] = (r_ref[...].astype(F32) + STEP_SIZE * residual).astype(BF16)


def project(weights, orbitals, unprojected, response, mask, core, across, group_rows, blk):
    bands, cells = response.shape
    width = mask.shape[1]
    out = struct((bands, cells), BF16)
    here = pl.BlockSpec((group_rows, cells), lambda g: (g, 0))

    def full(a):
        return pl.BlockSpec(a.shape, lambda g: (0, 0))

    return pl.pallas_call(
        functools.partial(project_body, core, across, width, blk),
        grid=(bands // group_rows,),
        out_shape=(out, out),
        in_specs=[
            *[full(a) for a in weights],
            full(orbitals),
            here,
            here,
            pl.BlockSpec((group_rows, width), lambda g: (g, 0)),
        ],
        out_specs=(here, here),
        scratch_shapes=[pltpu.VMEM((bands, width), BF16)],
        compiler_params=params(),
        cost_estimate=cost(2 * bands * width * cells, orbitals, unprojected, response, out, out),
    )(*weights, orbitals, unprojected, response, mask)


def shards(
    count, response, orbitals, projectors, potential, perturbing, energies, window_start, block_count
):
    bands, local_cells = response.shape
    cells = local_cells * count
    projections = projectors.shape[0]
    halo = 6 * GY * GZ
    core, across, along = levels_of(count)
    ring = (count, 1)
    ace_scale = 1.0 / math.sqrt(cells * projections)
    window_scale = 1.0 / math.sqrt(cells * bands)
    blk = bands // NBLK
    group_rows = GROUP_BLOCKS * blk
    width = (GROUP_BLOCKS + 2 * REACH) * blk
    half = bands // 2
    block = half // across[0]
    first = max(16, round(REDUCE_SHARE * block / 16) * 16)
    gather_first = max(16, round(GATHER_SHARE * block / 16) * 16)
    matrix = jnp.asarray(plane_matrix())
    lines = (potential[None, :], perturbing[None, :])
    columns = tuple(a[:, None] for a in (energies, window_start, block_count))

    def to(array, level):
        return [shifted(array, count, level, k) for k in range(1, level[0])]

    def parts_to(parts, level):
        return [shifted(part, count, level, k + 1) for k, part in enumerate(parts)]

    low = shifted(response[:, local_cells - halo :], count, ring, 1)
    high = shifted(response[:, :halo], count, ring, -1)

    sent = shifted(partial_intersections(response, projectors, core, True), count, core, 1)
    keep = partial_intersections(response, projectors, core, False)
    keep_z, *parts_z = local_call(
        functools.partial(first_z_body, along, block, first),
        shares_of((half - across[0] * first, projections // along[0]), along[0]),
        [keep, sent],
    )
    keep_x, *parts_x = local_call(
        functools.partial(first_x_body, across, block),
        shares_of((first, projections), across[0]),
        [keep, sent],
    )
    taken_z, taken_x, low, high = lax.optimization_barrier(
        (parts_to(parts_z, along), parts_to(parts_x, across), low, high)
    )
    keep_x, *parts_x = split(keep_x, taken_x, along, 1)
    keep_z, *parts_z = split(keep_z, taken_z, across, 0)
    taken_x, taken_z = lax.optimization_barrier(
        (parts_to(parts_x, along), parts_to(parts_z, across))
    )
    share_x, share_z = local_call(
        functools.partial(finish_both_body, ace_scale, len(taken_x)),
        [
            struct((gather_first, projections // along[0]), BF16),
            struct((block - gather_first, projections // along[0]), BF16),
        ],
        [keep_x, *taken_x, keep_z, *taken_z],
    )

    pieces_x, pieces_z, low, high = lax.optimization_barrier(
        ([share_x, *to(share_x, along)], [share_z, *to(share_z, across)], low, high)
    )
    base, mask = local_part(
        response, low, high, orbitals, matrix, lines, columns, group_rows, width, blk
    )
    block_x = place(pieces_x, along, 1)
    block_z = place(pieces_z, across, 0)
    blocks_x = [block_x, *to(block_x, across)]
    pieces_z, base = lax.optimization_barrier(([block_z, *to(block_z, along)], base))
    blocks = [*blocks_x, place(pieces_z, along, 1)]
    blocks += [shifted(part, count, core, 1) for part in blocks]

    unprojected, send, keep = local_call(
        functools.partial(apply_body, core, across, block, group_rows, width, blk),
        [
            struct((bands, local_cells), F32),
            struct((half, width), BF16),
            struct((half, width), F32),
        ],
        [*blocks, projectors, base, orbitals],
        flops=2 * bands * local_cells * (projections + width),
        scratch=[pltpu.VMEM((bands, projections), BF16), pltpu.VMEM((bands, width), F32)],
    )
    keep, *parts = split(keep, to(send, core), across, 0)
    total, low = add_up(keep, parts_to(parts, across))
    weights = finish(total, to(low, along), window_scale)
    weights = [weights, *to(weights, across)]
    weights += [shifted(part, count, core, 1) for part in weights]
    return project(
        weights, orbitals, unprojected, response, mask, core, across, group_rows, blk
    )


def solution(mesh):
    in_specs = (
        P("pert", "band"),
        P(None, "band"),
        P(None, "band"),
        P("band"),
        P(("pert", "band")),
        P(),
        P(),
        P(),
    )
    out_specs = (P("pert", "band"), P("pert", "band"))
    body = functools.partial(shards, mesh.shape["band"])
    return jax.shard_map(body, mesh=mesh, in_specs=in_specs, out_specs=out_specs, check_vma=False)
```

```python
import functools
import math

import jax
import jax.numpy as jnp
import ml_dtypes
import numpy as np
from jax import lax
from jax.experimental import pallas as pl
from jax.experimental.pallas import tpu as pltpu
from jax.sharding import PartitionSpec as P

GY = 8
GZ = 16
NBLK = 32
REACH = 4
GROUP_BLOCKS = 8
COEFFS = (
    -5369.0 / 1800.0,
    12.0 / 7.0,
    -15.0 / 56.0,
    10.0 / 189.0,
    -1.0 / 112.0,
    2.0 / 1925.0,
    -1.0 / 16632.0,
)
KINETIC = 0.125
STEP_SIZE = 0.3
MIB = 1024 * 1024
VMEM_BYTES = 40 * MIB
REDUCE_SHARE = 0.375
GATHER_SHARE = 0.5
BF16 = jnp.bfloat16
F32 = jnp.float32
NT = (((1,), (1,)), ((), ()))


def levels_of(count):
    chips = count // 2
    across = 2 ** (int(math.log2(chips)) // 3)
    return (2, 1), (across, 2), (chips // across, 2 * across)


def position(level):
    size, stride = level
    return lax.rem(lax.div(lax.axis_index("band"), jnp.int32(stride)), jnp.int32(size))


def shifted(array, count, level, step):
    size, stride = level
    pairs = []
    for device in range(count):
        place = device // stride % size
        pairs.append((device, device + ((place + step) % size - place) * stride))
    return lax.ppermute(array, "band", pairs)


def plane_matrix():
    plane = GY * GZ
    matrix = 3.0 * COEFFS[0] * np.eye(plane)
    cells = np.arange(plane)
    y, z = cells // GZ, cells % GZ
    for offset in range(1, 7):
        for sign in (1, -1):
            np.add.at(matrix, ((y + sign * offset) % GY * GZ + z, cells), COEFFS[offset])
            np.add.at(matrix, (y * GZ + (z + sign * offset) % GZ, cells), COEFFS[offset])
    matrix = KINETIC * matrix
    high = matrix.astype(ml_dtypes.bfloat16)
    low = (matrix - high.astype(np.float64)).astype(ml_dtypes.bfloat16)
    return np.stack([high, low])


def whole():
    return pl.BlockSpec(memory_space=pltpu.VMEM)


def params(size=VMEM_BYTES):
    return pltpu.CompilerParams(vmem_limit_bytes=size)


def cost(flops, *arrays):
    moved = sum(math.prod(a.shape) * jnp.dtype(a.dtype).itemsize for a in arrays)
    return pl.CostEstimate(flops=int(flops), bytes_accessed=int(moved), transcendentals=0)


def local_call(body, outs, args, flops=0, scratch=()):
    return pl.pallas_call(
        body,
        out_shape=outs,
        in_specs=[whole() for _ in args],
        out_specs=jax.tree.map(lambda _: whole(), outs),
        scratch_shapes=scratch,
        compiler_params=params(),
        cost_estimate=cost(flops, *args, *jax.tree.leaves(outs)),
    )(*args)


def struct(shape, dtype):
    return jax.ShapeDtypeStruct(shape, dtype)


def partial_body(core, other, block, r_ref, p_ref, x_ref, z_ref):
    rows = x_ref.shape[0] + z_ref.shape[0]
    size = rows // block
    first, rest = x_ref.shape[0] // size, z_ref.shape[0] // size
    c = position(core)
    row = pl.multiple_of((1 - c if other else c) * rows, rows)
    part = lax.dot_general(
        r_ref[pl.ds(row, rows), :], p_ref[...], NT, preferred_element_type=F32
    ).astype(x_ref.dtype)
    for i in range(size):
        x_ref[i * first : (i + 1) * first, :] = part[i * block : i * block + first, :]
        z_ref[i * rest : (i + 1) * rest, :] = part[i * block + first : (i + 1) * block, :]


def partial_intersections(response, projectors, core, other, block, first):
    bands, cells = response.shape
    count = projectors.shape[0]
    rows = bands // 2
    tile = min(512, count)
    rows_x = rows // block * first
    outs = [struct((n, count), BF16 if other else F32) for n in (rows_x, rows - rows_x)]
    return pl.pallas_call(
        functools.partial(partial_body, core, other, block),
        grid=(count // tile,),
        out_shape=outs,
        in_specs=[
            pl.BlockSpec((bands, cells), lambda i: (0, 0)),
            pl.BlockSpec((tile, cells), lambda i: (i, 0)),
        ],
        out_specs=[pl.BlockSpec((out.shape[0], tile), lambda i: (0, i)) for out in outs],
        compiler_params=params(),
        cost_estimate=cost(2 * rows * cells * count, projectors, *outs),
    )(response, projectors)


def rows_at(place, size):
    return pl.ds(pl.multiple_of(place * size, 16), size)


def cols_at(place, size):
    return pl.ds(pl.multiple_of(place * size, size), size)


def total_of(keep_ref, taken, part):
    total = keep_ref[part]
    for ref in taken:
        total = total + ref[part].astype(F32)
    return total


def split_body(received, level, along, *refs):
    keep_ref, taken, outs = refs[0], refs[1 : 1 + received], refs[1 + received :]
    me = position(level)
    rows, width = outs[0].shape
    for step, out in enumerate(outs):
        at = lax.rem(me + step, jnp.int32(level[0]))
        if along == 0:
            part = (rows_at(at, rows), slice(None))
        else:
            part = (slice(None), cols_at(at, width))
        out[...] = total_of(keep_ref, taken, part).astype(out.dtype)


def shares_of(shape, count):
    return [struct(shape, F32)] + [struct(shape, BF16)] * (count - 1)


def split(keep, taken, level, along):
    shape = list(keep.shape)
    shape[along] //= level[0]
    return local_call(
        functools.partial(split_body, len(taken), level, along),
        shares_of(shape, level[0]),
        [keep, *taken],
    )


def finish_body(scale, keep_ref, *refs):
    *taken, out_ref = refs
    out_ref[...] = (total_of(keep_ref, taken, ...) * scale).astype(out_ref.dtype)


def finish(keep, taken, scale):
    return local_call(
        functools.partial(finish_body, scale), struct(keep.shape, BF16), [keep, *taken]
    )


def finish_both_body(scale, received, *refs):
    outs = refs[-2:]
    cut = outs[0].shape[0]
    row = 0
    for keep_ref, *taken in (refs[: 1 + received], refs[1 + received : -2]):
        low = (total_of(keep_ref, taken, ...) * scale).astype(BF16)
        end = row + keep_ref.shape[0]
        for out, first, last in ((outs[0], 0, cut), (outs[1], cut, cut + outs[1].shape[0])):
            top, bottom = max(row, first), min(end, last)
            if top < bottom:
                out[top - first : bottom - first, :] = low[top - row : bottom - row, :]
        row = end


def place_body(level, along, *refs):
    *parts, out_ref = refs
    size, _ = level
    me = position(level)
    width = parts[0].shape[along]
    for step, ref in enumerate(parts):
        at = pl.multiple_of(lax.rem(me - step + size, jnp.int32(size)) * width, width)
        if along == 0:
            out_ref[pl.ds(at, width), :] = ref[...]
        else:
            out_ref[:, pl.ds(at, width)] = ref[...]


def place(parts, level, along):
    shape = list(parts[0].shape)
    shape[along] *= level[0]
    return local_call(functools.partial(place_body, level, along), struct(shape, BF16), parts)


def local_body(depth, sizes, *refs):
    r_ref, l_ref, h_ref, o_ref, m_ref, pot_ref, v_ref, e_ref = refs[:8]
    first_ref, many_ref, out_ref, mask_ref = refs[8:]
    plane = GY * GZ
    reach = 6

    def plane_at(j):
        if j < 0:
            ref, k = l_ref, j + reach
        elif j < depth:
            ref, k = r_ref, j
        else:
            ref, k = h_ref, j - depth
        return ref[:, k * plane : (k + 1) * plane]

    for j in range(depth):
        cols = slice(j * plane, (j + 1) * plane)
        low = plane_at(j)
        total = jnp.dot(low, m_ref[0], preferred_element_type=F32)
        total = total + jnp.dot(low, m_ref[1], preferred_element_type=F32)
        for offset in range(1, 7):
            pair = plane_at(j + offset).astype(F32) + plane_at(j - offset).astype(F32)
            total = total + (KINETIC * COEFFS[offset]) * pair
        total = total + (e_ref[...] - pot_ref[:, cols]) * low.astype(F32)
        out_ref[:, cols] = total - v_ref[:, cols] * o_ref[:, cols].astype(F32)
    group_rows, width, blk, bands = sizes
    start = jnp.clip(pl.program_id(0) * group_rows - REACH * blk, 0, bands - width)
    block = (lax.broadcasted_iota(jnp.int32, mask_ref.shape, 1) + start) // blk
    lowest = first_ref[...]
    inside = (block >= lowest) & (block < lowest + many_ref[...])
    mask_ref[...] = jnp.where(inside, 1.0, 0.0).astype(BF16)


def local_part(response, low, high, orbitals, matrix, lines, columns, group_rows, width, blk):
    bands, cells = response.shape
    depth = cells // (GY * GZ)
    outs = [struct((bands, cells), F32), struct((bands, width), BF16)]
    here = pl.BlockSpec((group_rows, cells), lambda i: (i, 0))
    side = pl.BlockSpec((group_rows, low.shape[1]), lambda i: (i, 0))
    line = pl.BlockSpec((1, cells), lambda i: (0, 0))
    column = pl.BlockSpec((group_rows, 1), lambda i: (i, 0))
    return pl.pallas_call(
        functools.partial(local_body, depth, (group_rows, width, blk, bands)),
        grid=(bands // group_rows,),
        out_shape=outs,
        in_specs=[
            here,
            side,
            side,
            here,
            pl.BlockSpec(matrix.shape, lambda i: (0, 0, 0)),
            line,
            line,
            column,
            column,
            column,
        ],
        out_specs=[here, pl.BlockSpec((group_rows, width), lambda i: (i, 0))],
        compiler_params=params(),
        cost_estimate=cost(2 * bands * cells * 300, low, high, low, low, *outs),
    )(response, low, high, orbitals, matrix, *lines, *columns)


def first_orbital(group, group_rows, width, bands, blk):
    return max(0, min(group * group_rows - REACH * blk, bands - width))


def apply_body(core, across, block, group_rows, width, blk, *refs):
    size = across[0]
    blocks = refs[: 2 * (size + 1)]
    p_ref, base_ref, o_ref, u_ref, send_ref, keep_ref, c_ref, s_ref = refs[2 * (size + 1) :]
    bands, cells = u_ref.shape
    c, x = position(core), position(across)
    half = bands // 2
    first = blocks[0].shape[0]
    for k, ref in enumerate(blocks):
        side, step = divmod(k, size + 1)
        at = (c if side == 0 else 1 - c) * half
        if step < size:
            at = at + lax.rem(x - step + size, jnp.int32(size)) * block
            c_ref[pl.ds(pl.multiple_of(at, 16), first), :] = ref[...]
        else:
            rest = block - first
            for i in range(size):
                there = pl.ds(pl.multiple_of(at + i * block + first, 16), rest)
                c_ref[there, :] = ref[i * rest : (i + 1) * rest, :]
    tile = 256 if cells % 256 == 0 else 128
    for t in range(cells // tile):
        cols = slice(t * tile, (t + 1) * tile)
        u_ref[:, cols] = base_ref[:, cols] + jnp.dot(
            c_ref[...], p_ref[:, cols], preferred_element_type=F32
        )
    for g in range(bands // group_rows):
        start = first_orbital(g, group_rows, width, bands, blk)
        mine = slice(g * group_rows, (g + 1) * group_rows)
        s_ref[mine, :] = lax.dot_general(
            u_ref[mine, :].astype(BF16),
            o_ref[start : start + width, :],
            NT,
            preferred_element_type=F32,
        )
    send_ref[...] = s_ref[pl.ds(pl.multiple_of((1 - c) * half, half), half), :].astype(BF16)
    keep_ref[...] = s_ref[pl.ds(pl.multiple_of(c * half, half), half), :]


def sum_body(keep_ref, *refs):
    *taken, total_ref, low_ref = refs
    total = keep_ref[...]
    for ref in taken:
        total = total + ref[...].astype(F32)
    total_ref[...] = total
    low_ref[...] = total.astype(BF16)


def add_up(keep, taken):
    outs = [struct(keep.shape, F32), struct(keep.shape, BF16)]
    return local_call(sum_body, outs, [keep, *taken])


def project_body(core, across, width, blk, *refs):
    size = across[0]
    blocks = refs[: 2 * size]
    o_ref, u_ref, r_ref, mask_ref, updated_ref, residual_ref, w_ref = refs[2 * size :]
    bands = o_ref.shape[0]
    half = bands // 2
    group_rows = u_ref.shape[0]
    g = pl.program_id(0)

    @pl.when(g == 0)
    def _():
        c, x = position(core), position(across)
        for k, ref in enumerate(blocks):
            side, step = divmod(k, size)
            at = (c if side == 0 else 1 - c) * half
            at = at + lax.rem(x - step + size, jnp.int32(size)) * ref.shape[0]
            w_ref[pl.ds(pl.multiple_of(at, 16), ref.shape[0]), :] = ref[...]

    start = jnp.clip(g * group_rows - REACH * blk, 0, bands - width)
    window = o_ref[pl.ds(pl.multiple_of(start, blk), width), :]
    mine = pl.ds(pl.multiple_of(g * group_rows, group_rows), group_rows)
    inside = mask_ref[...].astype(F32) > 0.5
    weights = jnp.where(inside, w_ref[mine, :].astype(F32), 0.0).astype(BF16)
    residual = u_ref[...] - jnp.dot(weights, window, preferred_element_type=F32)
    residual_ref[...] = residual.astype(BF16)
    updated_ref[...] = (r_ref[...].astype(F32) + STEP_SIZE * residual).astype(BF16)


def project(weights, orbitals, unprojected, response, mask, core, across, group_rows, blk):
    bands, cells = response.shape
    width = mask.shape[1]
    out = struct((bands, cells), BF16)
    here = pl.BlockSpec((group_rows, cells), lambda g: (g, 0))

    def full(a):
        return pl.BlockSpec(a.shape, lambda g: (0, 0))

    return pl.pallas_call(
        functools.partial(project_body, core, across, width, blk),
        grid=(bands // group_rows,),
        out_shape=(out, out),
        in_specs=[
            *[full(a) for a in weights],
            full(orbitals),
            here,
            here,
            pl.BlockSpec((group_rows, width), lambda g: (g, 0)),
        ],
        out_specs=(here, here),
        scratch_shapes=[pltpu.VMEM((bands, width), BF16)],
        compiler_params=params(),
        cost_estimate=cost(2 * bands * width * cells, orbitals, unprojected, response, out, out),
    )(*weights, orbitals, unprojected, response, mask)


def shards(
    count, response, orbitals, projectors, potential, perturbing, energies, window_start, block_count
):
    bands, local_cells = response.shape
    cells = local_cells * count
    projections = projectors.shape[0]
    halo = 6 * GY * GZ
    core, across, along = levels_of(count)
    ring = (count, 1)
    ace_scale = 1.0 / math.sqrt(cells * projections)
    window_scale = 1.0 / math.sqrt(cells * bands)
    blk = bands // NBLK
    group_rows = GROUP_BLOCKS * blk
    width = (GROUP_BLOCKS + 2 * REACH) * blk
    half = bands // 2
    block = half // across[0]
    first = max(16, round(REDUCE_SHARE * block / 16) * 16)
    gather_first = max(16, round(GATHER_SHARE * block / 16) * 16)
    matrix = jnp.asarray(plane_matrix())
    lines = (potential[None, :], perturbing[None, :])
    columns = tuple(a[:, None] for a in (energies, window_start, block_count))

    def to(array, level):
        return [shifted(array, count, level, k) for k in range(1, level[0])]

    def parts_to(parts, level):
        return [shifted(part, count, level, k + 1) for k, part in enumerate(parts)]

    low = shifted(response[:, local_cells - halo :], count, ring, 1)
    high = shifted(response[:, :halo], count, ring, -1)

    sent_x, sent_z = partial_intersections(response, projectors, core, True, block, first)
    sent_z = shifted(sent_z, count, core, 1)
    sent_x = shifted(sent_x, count, core, 1)
    keep_x, keep_z = partial_intersections(response, projectors, core, False, block, first)
    keep_z, *parts_z = split(keep_z, [sent_z], along, 1)
    keep_x, *parts_x = split(keep_x, [sent_x], across, 0)
    taken_z, taken_x, low, high = lax.optimization_barrier(
        (parts_to(parts_z, along), parts_to(parts_x, across), low, high)
    )
    keep_x, *parts_x = split(keep_x, taken_x, along, 1)
    keep_z, *parts_z = split(keep_z, taken_z, across, 0)
    taken_x, taken_z = lax.optimization_barrier(
        (parts_to(parts_x, along), parts_to(parts_z, across))
    )
    share_x, share_z = local_call(
        functools.partial(finish_both_body, ace_scale, len(taken_x)),
        [
            struct((gather_first, projections // along[0]), BF16),
            struct((block - gather_first, projections // along[0]), BF16),
        ],
        [keep_x, *taken_x, keep_z, *taken_z],
    )

    pieces_x, pieces_z, low, high = lax.optimization_barrier(
        ([share_x, *to(share_x, along)], [share_z, *to(share_z, across)], low, high)
    )
    base, mask = local_part(
        response, low, high, orbitals, matrix, lines, columns, group_rows, width, blk
    )
    block_x = place(pieces_x, along, 1)
    block_z = place(pieces_z, across, 0)
    blocks_x = [block_x, *to(block_x, across)]
    pieces_z, base = lax.optimization_barrier(([block_z, *to(block_z, along)], base))
    blocks = [*blocks_x, place(pieces_z, along, 1)]
    blocks += [shifted(part, count, core, 1) for part in blocks]

    unprojected, send, keep = local_call(
        functools.partial(apply_body, core, across, block, group_rows, width, blk),
        [
            struct((bands, local_cells), F32),
            struct((half, width), BF16),
            struct((half, width), F32),
        ],
        [*blocks, projectors, base, orbitals],
        flops=2 * bands * local_cells * (projections + width),
        scratch=[pltpu.VMEM((bands, projections), BF16), pltpu.VMEM((bands, width), F32)],
    )
    keep, *parts = split(keep, to(send, core), across, 0)
    total, low = add_up(keep, parts_to(parts, across))
    weights = finish(total, to(low, along), window_scale)
    weights = [weights, *to(weights, across)]
    weights += [shifted(part, count, core, 1) for part in weights]
    return project(
        weights, orbitals, unprojected, response, mask, core, across, group_rows, blk
    )


def solution(mesh):
    in_specs = (
        P("pert", "band"),
        P(None, "band"),
        P(None, "band"),
        P("band"),
        P(("pert", "band")),
        P(),
        P(),
        P(),
    )
    out_specs = (P("pert", "band"), P("pert", "band"))
    body = functools.partial(shards, mesh.shape["band"])
    return jax.shard_map(body, mesh=mesh, in_specs=in_specs, out_specs=out_specs, check_vma=False)
```

```python
import functools
import math

import jax
import jax.numpy as jnp
import ml_dtypes
import numpy as np
from jax import lax
from jax.experimental import pallas as pl
from jax.experimental.pallas import tpu as pltpu
from jax.sharding import PartitionSpec as P

GY = 8
GZ = 16
NBLK = 32
REACH = 4
GROUP_BLOCKS = 8
COEFFS = (
    -5369.0 / 1800.0,
    12.0 / 7.0,
    -15.0 / 56.0,
    10.0 / 189.0,
    -1.0 / 112.0,
    2.0 / 1925.0,
    -1.0 / 16632.0,
)
KINETIC = 0.125
STEP_SIZE = 0.3
MIB = 1024 * 1024
VMEM_BYTES = 40 * MIB
REDUCE_SHARE = 0.5
GATHER_SHARE = 0.5
BF16 = jnp.bfloat16
F32 = jnp.float32
NT = (((1,), (1,)), ((), ()))


def levels_of(count):
    chips = count // 2
    across = 2 ** (int(math.log2(chips)) // 3)
    return (2, 1), (across, 2), (chips // across, 2 * across)


def position(level):
    size, stride = level
    return lax.rem(lax.div(lax.axis_index("band"), jnp.int32(stride)), jnp.int32(size))


def neighbour(array, count, step):
    return lax.ppermute(array, "band", [(i, (i + step) % count) for i in range(count)])


def swapped(array, count, level, step):
    size, stride = level
    pairs = []
    for device in range(count):
        place = device // stride % size
        pairs.append((device, device + ((place ^ step) - place) * stride))
    return lax.ppermute(array, "band", pairs)


def plane_matrix():
    plane = GY * GZ
    matrix = 3.0 * COEFFS[0] * np.eye(plane)
    cells = np.arange(plane)
    y, z = cells // GZ, cells % GZ
    for offset in range(1, 7):
        for sign in (1, -1):
            np.add.at(matrix, ((y + sign * offset) % GY * GZ + z, cells), COEFFS[offset])
            np.add.at(matrix, (y * GZ + (z + sign * offset) % GZ, cells), COEFFS[offset])
    matrix = KINETIC * matrix
    high = matrix.astype(ml_dtypes.bfloat16)
    low = (matrix - high.astype(np.float64)).astype(ml_dtypes.bfloat16)
    return np.stack([high, low])


def whole():
    return pl.BlockSpec(memory_space=pltpu.VMEM)


def params(size=VMEM_BYTES):
    return pltpu.CompilerParams(vmem_limit_bytes=size)


def cost(flops, *arrays):
    moved = sum(math.prod(a.shape) * jnp.dtype(a.dtype).itemsize for a in arrays)
    return pl.CostEstimate(flops=int(flops), bytes_accessed=int(moved), transcendentals=0)


def local_call(body, outs, args, flops=0, scratch=()):
    return pl.pallas_call(
        body,
        out_shape=outs,
        in_specs=[whole() for _ in args],
        out_specs=jax.tree.map(lambda _: whole(), outs),
        scratch_shapes=scratch,
        compiler_params=params(),
        cost_estimate=cost(flops, *args, *jax.tree.leaves(outs)),
    )(*args)


def struct(shape, dtype):
    return jax.ShapeDtypeStruct(shape, dtype)


def partial_body(core, other, block, r_ref, p_ref, x_ref, z_ref):
    rows = x_ref.shape[0] + z_ref.shape[0]
    size = rows // block
    first, rest = x_ref.shape[0] // size, z_ref.shape[0] // size
    c = position(core)
    row = pl.multiple_of((1 - c if other else c) * rows, rows)
    part = lax.dot_general(
        r_ref[pl.ds(row, rows), :], p_ref[...], NT, preferred_element_type=F32
    ).astype(x_ref.dtype)
    for i in range(size):
        x_ref[i * first : (i + 1) * first, :] = part[i * block : i * block + first, :]
        z_ref[i * rest : (i + 1) * rest, :] = part[i * block + first : (i + 1) * block, :]


def partial_intersections(response, projectors, core, other, block, first):
    bands, cells = response.shape
    count = projectors.shape[0]
    rows = bands // 2
    tile = min(512, count)
    rows_x = rows // block * first
    outs = [struct((n, count), BF16 if other else F32) for n in (rows_x, rows - rows_x)]
    return pl.pallas_call(
        functools.partial(partial_body, core, other, block),
        grid=(count // tile,),
        out_shape=outs,
        in_specs=[
            pl.BlockSpec((bands, cells), lambda i: (0, 0)),
            pl.BlockSpec((tile, cells), lambda i: (i, 0)),
        ],
        out_specs=[pl.BlockSpec((out.shape[0], tile), lambda i: (0, i)) for out in outs],
        compiler_params=params(),
        cost_estimate=cost(2 * rows * cells * count, projectors, *outs),
    )(response, projectors)


def rows_at(place, size):
    return pl.ds(pl.multiple_of(place * size, 16), size)


def cols_at(place, size):
    return pl.ds(pl.multiple_of(place * size, size), size)


def total_of(keep_ref, taken, part):
    total = keep_ref[part]
    for ref in taken:
        total = total + ref[part].astype(F32)
    return total


def split_body(received, level, along, *refs):
    keep_ref, taken, outs = refs[0], refs[1 : 1 + received], refs[1 + received :]
    me = position(level)
    rows, width = outs[0].shape
    for step, out in enumerate(outs):
        at = me ^ step
        if along == 0:
            part = (rows_at(at, rows), slice(None))
        else:
            part = (slice(None), cols_at(at, width))
        out[...] = total_of(keep_ref, taken, part).astype(out.dtype)


def shares_of(shape, count):
    return [struct(shape, F32)] + [struct(shape, BF16)] * (count - 1)


def split(keep, taken, level, along):
    shape = list(keep.shape)
    shape[along] //= level[0]
    return local_call(
        functools.partial(split_body, len(taken), level, along),
        shares_of(shape, level[0]),
        [keep, *taken],
    )


def finish_body(scale, keep_ref, *refs):
    *taken, out_ref = refs
    out_ref[...] = (total_of(keep_ref, taken, ...) * scale).astype(out_ref.dtype)


def finish(keep, taken, scale):
    return local_call(
        functools.partial(finish_body, scale), struct(keep.shape, BF16), [keep, *taken]
    )


def finish_both_body(scale, received, *refs):
    outs = refs[-2:]
    cut = outs[0].shape[0]
    row = 0
    for keep_ref, *taken in (refs[: 1 + received], refs[1 + received : -2]):
        low = (total_of(keep_ref, taken, ...) * scale).astype(BF16)
        end = row + keep_ref.shape[0]
        for out, first, last in ((outs[0], 0, cut), (outs[1], cut, cut + outs[1].shape[0])):
            top, bottom = max(row, first), min(end, last)
            if top < bottom:
                out[top - first : bottom - first, :] = low[top - row : bottom - row, :]
        row = end


def place_body(level, along, *refs):
    *parts, out_ref = refs
    me = position(level)
    width = parts[0].shape[along]
    for step, ref in enumerate(parts):
        at = pl.multiple_of((me ^ step) * width, width)
        if along == 0:
            out_ref[pl.ds(at, width), :] = ref[...]
        else:
            out_ref[:, pl.ds(at, width)] = ref[...]


def place(parts, level, along):
    shape = list(parts[0].shape)
    shape[along] *= level[0]
    return local_call(functools.partial(place_body, level, along), struct(shape, BF16), parts)


def local_body(depth, sizes, *refs):
    r_ref, l_ref, h_ref, o_ref, m_ref, pot_ref, v_ref, e_ref = refs[:8]
    first_ref, many_ref, out_ref, mask_ref = refs[8:]
    plane = GY * GZ
    reach = 6

    def plane_at(j):
        if j < 0:
            ref, k = l_ref, j + reach
        elif j < depth:
            ref, k = r_ref, j
        else:
            ref, k = h_ref, j - depth
        return ref[:, k * plane : (k + 1) * plane]

    for j in range(depth):
        cols = slice(j * plane, (j + 1) * plane)
        low = plane_at(j)
        total = jnp.dot(low, m_ref[0], preferred_element_type=F32)
        total = total + jnp.dot(low, m_ref[1], preferred_element_type=F32)
        for offset in range(1, 7):
            pair = plane_at(j + offset).astype(F32) + plane_at(j - offset).astype(F32)
            total = total + (KINETIC * COEFFS[offset]) * pair
        total = total + (e_ref[...] - pot_ref[:, cols]) * low.astype(F32)
        out_ref[:, cols] = total - v_ref[:, cols] * o_ref[:, cols].astype(F32)
    group_rows, blk = sizes
    block = lax.broadcasted_iota(jnp.int32, mask_ref.shape, 1) // blk
    block = block + (pl.program_id(0) * (group_rows // blk) - REACH)
    lowest = first_ref[...]
    inside = (block >= lowest) & (block < lowest + many_ref[...])
    mask_ref[...] = jnp.where(inside, 1.0, 0.0).astype(BF16)


def local_part(response, low, high, orbitals, matrix, lines, columns, group_rows, width, blk):
    bands, cells = response.shape
    depth = cells // (GY * GZ)
    outs = [struct((bands, cells), F32), struct((bands, width), BF16)]
    here = pl.BlockSpec((group_rows, cells), lambda i: (i, 0))
    side = pl.BlockSpec((group_rows, low.shape[1]), lambda i: (i, 0))
    line = pl.BlockSpec((1, cells), lambda i: (0, 0))
    column = pl.BlockSpec((group_rows, 1), lambda i: (i, 0))
    return pl.pallas_call(
        functools.partial(local_body, depth, (group_rows, blk)),
        grid=(bands // group_rows,),
        out_shape=outs,
        in_specs=[
            here,
            side,
            side,
            here,
            pl.BlockSpec(matrix.shape, lambda i: (0, 0, 0)),
            line,
            line,
            column,
            column,
            column,
        ],
        out_specs=[here, pl.BlockSpec((group_rows, width), lambda i: (i, 0))],
        compiler_params=params(),
        cost_estimate=cost(2 * bands * cells * 300, low, high, low, low, *outs),
    )(response, low, high, orbitals, matrix, *lines, *columns)


def pad_orbitals(o_ref, pad_ref, blk):
    bands, cells = o_ref.shape
    edge = REACH * blk
    pad_ref[:edge, :] = jnp.zeros((edge, cells), pad_ref.dtype)
    pad_ref[edge : edge + bands, :] = o_ref[...]
    pad_ref[edge + bands :, :] = jnp.zeros((edge, cells), pad_ref.dtype)


def subgroup(shape, blk):
    return lax.broadcasted_iota(jnp.int32, shape, 1) // (2 * blk)


def packed(sums, blk):
    rows = sums.shape[0]
    sub = 2 * blk
    near, far = sums[:, :rows], sums[:, rows:]
    column = subgroup((rows, rows), blk)
    row = lax.broadcasted_iota(jnp.int32, (rows, rows), 0) // sub
    main = jnp.where(column >= row, near, far)
    rest = far[:sub, :]
    for k in range(1, rows // sub):
        rest = jnp.where(column[:sub, :] == k, far[k * sub : (k + 1) * sub, :], rest)
    return main, rest


def unpacked(main, rest, blk):
    rows = main.shape[0]
    sub = 2 * blk
    column = subgroup((rows, rows), blk)
    row = lax.broadcasted_iota(jnp.int32, (rows, rows), 0) // sub
    near = jnp.where(column >= row, main, 0.0)
    last = jnp.where(column == row, jnp.concatenate([rest] * (rows // sub), axis=0), 0.0)
    return near, jnp.where(column < row, main, last)


def apply_body(core, across, block, group_rows, blk, other, *refs):
    size = across[0]
    blocks = refs[: size + 1]
    p_ref, base_ref, o_ref, u_ref, s_ref, c_ref, pad_ref = refs[size + 1 :]
    rows, cells = u_ref.shape
    c, x = position(core), position(across)
    side = 1 - c if other else c
    first = blocks[0].shape[0]
    for step, ref in enumerate(blocks[:size]):
        at = (x ^ step) * block
        c_ref[pl.ds(pl.multiple_of(at, 16), first), :] = ref[...]
    rest = block - first
    for i in range(size):
        there = slice(i * block + first, (i + 1) * block)
        c_ref[there, :] = blocks[size][i * rest : (i + 1) * rest, :]
    mine = pl.ds(pl.multiple_of(side * rows, rows), rows)
    tile = 256 if cells % 256 == 0 else 128
    for t in range(cells // tile):
        cols = slice(t * tile, (t + 1) * tile)
        u_ref[:, cols] = base_ref[mine, cols] + jnp.dot(
            c_ref[...], p_ref[:, cols], preferred_element_type=F32
        )
    pad_orbitals(o_ref, pad_ref, blk)
    height = group_rows + 2 * blk
    for g in range(rows // group_rows):
        start = pl.multiple_of(side * rows + g * group_rows, group_rows)
        sums = lax.dot_general(
            u_ref[g * group_rows : (g + 1) * group_rows, :].astype(BF16),
            pad_ref[pl.ds(start, 2 * group_rows), :],
            NT,
            preferred_element_type=F32,
        )
        main, rest_sums = packed(sums, blk)
        s_ref[g * height : g * height + group_rows, :] = main.astype(s_ref.dtype)
        s_ref[g * height + group_rows : (g + 1) * height, :] = rest_sums.astype(s_ref.dtype)


def apply(blocks, projectors, base, orbitals, core, across, block, group_rows, blk, other):
    bands, cells = base.shape
    rows = bands // 2
    count = projectors.shape[0]
    height = rows // group_rows * (group_rows + 2 * blk)
    return local_call(
        functools.partial(apply_body, core, across, block, group_rows, blk, other),
        [struct((rows, cells), F32), struct((height, group_rows), BF16 if other else F32)],
        [*blocks, projectors, base, orbitals],
        flops=2 * rows * cells * (count + 2 * group_rows),
        scratch=[
            pltpu.VMEM((rows, count), BF16),
            pltpu.VMEM((bands + 2 * REACH * blk, cells), BF16),
        ],
    )


def sum_body(keep_ref, *refs):
    *taken, total_ref, low_ref = refs
    total = total_of(keep_ref, taken, ...)
    total_ref[...] = total
    low_ref[...] = total.astype(BF16)


def add_up(keep, taken):
    outs = [struct(keep.shape, F32), struct(keep.shape, BF16)]
    return local_call(sum_body, outs, [keep, *taken])


def project_body(core, blk, *refs):
    w_own, w_other, u_own, u_other, o_ref, r_ref, mask_ref = refs[:7]
    updated_ref, residual_ref, pad_ref, w_ref, u_ref = refs[7:]
    rows = u_ref.shape[0]
    height = w_ref.shape[0]
    per = u_own.shape[0] // rows
    g = pl.program_id(0)
    own = lax.div(g, jnp.int32(per)) == position(core)
    local = lax.rem(g, jnp.int32(per))
    w_rows = pl.ds(pl.multiple_of(local * height, 16), height)
    u_rows = pl.ds(pl.multiple_of(local * rows, rows), rows)

    @pl.when(g == 0)
    def _():
        pad_orbitals(o_ref, pad_ref, blk)

    @pl.when(own)
    def _():
        w_ref[...] = w_own[w_rows, :]
        u_ref[...] = u_own[u_rows, :]

    @pl.when(jnp.logical_not(own))
    def _():
        w_ref[...] = w_other[w_rows, :]
        u_ref[...] = u_other[u_rows, :]

    main, rest = w_ref[:rows, :].astype(F32), w_ref[rows:, :].astype(F32)
    start = pl.multiple_of(g * rows, rows)
    residual = u_ref[...]
    for k, part in enumerate(unpacked(main, rest, blk)):
        inside = mask_ref[:, k * rows : (k + 1) * rows].astype(F32) > 0.5
        weights = jnp.where(inside, part, 0.0).astype(BF16)
        window = pad_ref[pl.ds(pl.multiple_of(start + k * rows, rows), rows), :]
        residual = residual - jnp.dot(weights, window, preferred_element_type=F32)
    residual_ref[...] = residual.astype(BF16)
    updated_ref[...] = (r_ref[...].astype(F32) + STEP_SIZE * residual).astype(BF16)


def project(weights, unprojected, orbitals, response, mask, core, group_rows, blk):
    bands, cells = response.shape
    out = struct((bands, cells), BF16)
    here = pl.BlockSpec((group_rows, cells), lambda g: (g, 0))

    def full(a):
        return pl.BlockSpec(a.shape, lambda g: (0, 0))

    return pl.pallas_call(
        functools.partial(project_body, core, blk),
        grid=(bands // group_rows,),
        out_shape=(out, out),
        in_specs=[
            *[full(a) for a in (*weights, *unprojected, orbitals)],
            here,
            pl.BlockSpec((group_rows, mask.shape[1]), lambda g: (g, 0)),
        ],
        out_specs=(here, here),
        scratch_shapes=[
            pltpu.VMEM((bands + 2 * REACH * blk, cells), BF16),
            pltpu.VMEM((group_rows + 2 * blk, group_rows), BF16),
            pltpu.VMEM((group_rows, cells), F32),
        ],
        compiler_params=params(),
        cost_estimate=cost(
            4 * bands * group_rows * cells, orbitals, *unprojected, response, out, out
        ),
    )(*weights, *unprojected, orbitals, response, mask)


def shards(
    count, response, orbitals, projectors, potential, perturbing, energies, window_start, block_count
):
    bands, local_cells = response.shape
    cells = local_cells * count
    projections = projectors.shape[0]
    halo = 6 * GY * GZ
    core, across, along = levels_of(count)
    ace_scale = 1.0 / math.sqrt(cells * projections)
    window_scale = 1.0 / math.sqrt(cells * bands)
    blk = bands // NBLK
    group_rows = GROUP_BLOCKS * blk
    width = 2 * group_rows
    half = bands // 2
    block = half // across[0]
    first = max(16, round(REDUCE_SHARE * block / 16) * 16)
    gather_first = max(16, round(GATHER_SHARE * block / 16) * 16)
    matrix = jnp.asarray(plane_matrix())
    lines = (potential[None, :], perturbing[None, :])
    columns = tuple(a[:, None] for a in (energies, window_start, block_count))

    def to(array, level):
        return [swapped(array, count, level, k) for k in range(1, level[0])]

    def parts_to(parts, level):
        return [swapped(part, count, level, k + 1) for k, part in enumerate(parts)]

    low = neighbour(response[:, local_cells - halo :], count, 1)

    sent_x, sent_z = partial_intersections(response, projectors, core, True, block, first)
    sent_z = swapped(sent_z, count, core, 1)
    sent_x = swapped(sent_x, count, core, 1)
    keep_x, keep_z = partial_intersections(response, projectors, core, False, block, first)
    keep_z, *parts_z = split(keep_z, [sent_z], along, 1)
    keep_x, *parts_x = split(keep_x, [sent_x], across, 0)
    taken_z, taken_x, low, head = lax.optimization_barrier(
        (parts_to(parts_z, along), parts_to(parts_x, across), low, response[:, :halo])
    )
    high = neighbour(head, count, -1)
    keep_x, *parts_x = split(keep_x, taken_x, along, 1)
    keep_z, *parts_z = split(keep_z, taken_z, across, 0)
    taken_x, taken_z = lax.optimization_barrier(
        (parts_to(parts_x, along), parts_to(parts_z, across))
    )
    share_x, share_z = local_call(
        functools.partial(finish_both_body, ace_scale, len(taken_x)),
        [
            struct((gather_first, projections // along[0]), BF16),
            struct((block - gather_first, projections // along[0]), BF16),
        ],
        [keep_x, *taken_x, keep_z, *taken_z],
    )

    pieces_x, pieces_z, low, high = lax.optimization_barrier(
        ([share_x, *to(share_x, along)], [share_z, *to(share_z, across)], low, high)
    )
    base, mask = local_part(
        response, low, high, orbitals, matrix, lines, columns, group_rows, width, blk
    )
    block_x = place(pieces_x, along, 1)
    block_z = place(pieces_z, across, 0)
    blocks_x = [block_x, *to(block_x, across)]
    pieces_z, base = lax.optimization_barrier(([block_z, *to(block_z, along)], base))
    blocks = [*blocks_x, place(pieces_z, along, 1)]
    others = [swapped(part, count, core, 1) for part in blocks]
    sizes = (core, across, block, group_rows, blk)
    wide, keep = apply(blocks, projectors, base, orbitals, *sizes, False)
    others, keep = lax.optimization_barrier((others, keep))
    other_wide, part = apply(others, projectors, base, orbitals, *sizes, True)
    unprojected = (wide, other_wide)
    total, part = add_up(keep, to(part, core))
    total, part = add_up(total, to(part, across))
    own = finish(total, to(part, along), window_scale)
    weights = (own, *to(own, core))
    return project(weights, unprojected, orbitals, response, mask, core, group_rows, blk)


def solution(mesh):
    in_specs = (
        P("pert", "band"),
        P(None, "band"),
        P(None, "band"),
        P("band"),
        P(("pert", "band")),
        P(),
        P(),
        P(),
    )
    out_specs = (P("pert", "band"), P("pert", "band"))
    body = functools.partial(shards, mesh.shape["band"])
    return jax.shard_map(body, mesh=mesh, in_specs=in_specs, out_specs=out_specs, check_vma=False)
```

```python
import functools
import math

import jax
import jax.numpy as jnp
import ml_dtypes
import numpy as np
from jax import lax
from jax.experimental import pallas as pl
from jax.experimental.pallas import tpu as pltpu
from jax.sharding import PartitionSpec as P

GY = 8
GZ = 16
NBLK = 32
REACH = 4
GROUP_BLOCKS = 8
COEFFS = (
    -5369.0 / 1800.0,
    12.0 / 7.0,
    -15.0 / 56.0,
    10.0 / 189.0,
    -1.0 / 112.0,
    2.0 / 1925.0,
    -1.0 / 16632.0,
)
KINETIC = 0.125
STEP_SIZE = 0.3
MIB = 1024 * 1024
VMEM_BYTES = 24 * MIB
REDUCE_SHARE = 0.5
GATHER_SHARE = 0.5
BF16 = jnp.bfloat16
F32 = jnp.float32
NT = (((1,), (1,)), ((), ()))


def levels_of(count):
    chips = count // 2
    across = 2 ** (int(math.log2(chips)) // 3)
    return (2, 1), (across, 2), (chips // across, 2 * across)


def position(level):
    size, stride = level
    return lax.rem(lax.div(lax.axis_index("band"), jnp.int32(stride)), jnp.int32(size))


def neighbour(array, count, step):
    return lax.ppermute(array, "band", [(i, (i + step) % count) for i in range(count)])


def swapped(array, count, level, step):
    size, stride = level
    pairs = []
    for device in range(count):
        place = device // stride % size
        pairs.append((device, device + ((place ^ step) - place) * stride))
    return lax.ppermute(array, "band", pairs)


def plane_matrix():
    plane = GY * GZ
    matrix = 3.0 * COEFFS[0] * np.eye(plane)
    cells = np.arange(plane)
    y, z = cells // GZ, cells % GZ
    for offset in range(1, 7):
        for sign in (1, -1):
            np.add.at(matrix, ((y + sign * offset) % GY * GZ + z, cells), COEFFS[offset])
            np.add.at(matrix, (y * GZ + (z + sign * offset) % GZ, cells), COEFFS[offset])
    matrix = KINETIC * matrix
    high = matrix.astype(ml_dtypes.bfloat16)
    low = (matrix - high.astype(np.float64)).astype(ml_dtypes.bfloat16)
    return np.stack([high, low])


def whole():
    return pl.BlockSpec(memory_space=pltpu.VMEM)


def params(size=VMEM_BYTES):
    return pltpu.CompilerParams(vmem_limit_bytes=size)


def cost(flops, *arrays):
    moved = sum(math.prod(a.shape) * jnp.dtype(a.dtype).itemsize for a in arrays)
    return pl.CostEstimate(flops=int(flops), bytes_accessed=int(moved), transcendentals=0)


def local_call(body, outs, args, flops=0, scratch=()):
    return pl.pallas_call(
        body,
        out_shape=outs,
        in_specs=[whole() for _ in args],
        out_specs=jax.tree.map(lambda _: whole(), outs),
        scratch_shapes=scratch,
        compiler_params=params(),
        cost_estimate=cost(flops, *args, *jax.tree.leaves(outs)),
    )(*args)


def struct(shape, dtype):
    return jax.ShapeDtypeStruct(shape, dtype)


def cut(part, block, x_ref, z_ref, cols):
    size = part.shape[0] // block
    first, rest = x_ref.shape[0] // size, z_ref.shape[0] // size
    part = part.astype(x_ref.dtype)
    for i in range(size):
        x_ref[i * first : (i + 1) * first, cols] = part[i * block : i * block + first, :]
        z_ref[i * rest : (i + 1) * rest, cols] = part[i * block + first : (i + 1) * block, :]


def first_body(core, block, tile, r_ref, p_ref, *refs):
    sent_x, sent_z, keep_x, keep_z, r_held, p_held, r_sem, p_sem = refs
    rows = r_held.shape[0] // 2
    r_copy = pltpu.make_async_copy(r_ref, r_held, r_sem)
    r_copy.start()
    copies = []
    for t in range(p_held.shape[0] // tile):
        part = pl.ds(t * tile, tile)
        copies.append(pltpu.make_async_copy(p_ref.at[part, :], p_held.at[part, :], p_sem.at[t]))
        copies[-1].start()
    c = position(core)
    r_copy.wait()
    for t, copy in enumerate(copies):
        copy.wait()
        cols = slice(t * tile, (t + 1) * tile)
        for side, x_ref, z_ref in ((1 - c, sent_x, sent_z), (c, keep_x, keep_z)):
            part = lax.dot_general(
                r_held[pl.ds(pl.multiple_of(side * rows, rows), rows), :],
                p_held[cols, :],
                NT,
                preferred_element_type=F32,
            )
            cut(part, block, x_ref, z_ref, cols)


def first_sums(response, projectors, core, block, first):
    bands, cells = response.shape
    count = projectors.shape[0]
    rows = bands // 2
    tile = min(512, count)
    rows_x = rows // block * first
    outs = [struct((n, count), t) for t in (BF16, F32) for n in (rows_x, rows - rows_x)]
    return pl.pallas_call(
        functools.partial(first_body, core, block, tile),
        out_shape=outs,
        in_specs=[pl.BlockSpec(memory_space=pltpu.HBM)] * 2,
        out_specs=[whole() for _ in outs],
        scratch_shapes=[
            pltpu.VMEM((bands, cells), response.dtype),
            pltpu.VMEM((count, cells), projectors.dtype),
            pltpu.SemaphoreType.DMA,
            pltpu.SemaphoreType.DMA((count // tile,)),
        ],
        compiler_params=params(),
        cost_estimate=cost(2 * bands * cells * count, projectors, *outs),
    )(
        pltpu.with_memory_space_constraint(response, pltpu.HBM),
        pltpu.with_memory_space_constraint(projectors, pltpu.HBM),
    )


def rows_at(place, size):
    return pl.ds(pl.multiple_of(place * size, 16), size)


def cols_at(place, size):
    return pl.ds(pl.multiple_of(place * size, size), size)


def total_of(keep_ref, taken, part):
    total = keep_ref[part]
    for ref in taken:
        total = total + ref[part].astype(F32)
    return total


def split_body(received, level, along, *refs):
    keep_ref, taken, outs = refs[0], refs[1 : 1 + received], refs[1 + received :]
    me = position(level)
    rows, width = outs[0].shape
    for step, out in enumerate(outs):
        at = me ^ step
        if along == 0:
            part = (rows_at(at, rows), slice(None))
        else:
            part = (slice(None), cols_at(at, width))
        out[...] = total_of(keep_ref, taken, part).astype(out.dtype)


def shares_of(shape, count):
    return [struct(shape, F32)] + [struct(shape, BF16)] * (count - 1)


def split(keep, taken, level, along):
    shape = list(keep.shape)
    shape[along] //= level[0]
    return local_call(
        functools.partial(split_body, len(taken), level, along),
        shares_of(shape, level[0]),
        [keep, *taken],
    )


def finish_body(scale, keep_ref, *refs):
    *taken, out_ref = refs
    out_ref[...] = (total_of(keep_ref, taken, ...) * scale).astype(out_ref.dtype)


def finish(keep, taken, scale):
    return local_call(
        functools.partial(finish_body, scale), struct(keep.shape, BF16), [keep, *taken]
    )


def finish_both_body(scale, received, *refs):
    outs = refs[-2:]
    cut = outs[0].shape[0]
    row = 0
    for keep_ref, *taken in (refs[: 1 + received], refs[1 + received : -2]):
        low = (total_of(keep_ref, taken, ...) * scale).astype(BF16)
        end = row + keep_ref.shape[0]
        for out, first, last in ((outs[0], 0, cut), (outs[1], cut, cut + outs[1].shape[0])):
            top, bottom = max(row, first), min(end, last)
            if top < bottom:
                out[top - first : bottom - first, :] = low[top - row : bottom - row, :]
        row = end


def place_body(level, along, *refs):
    *parts, out_ref = refs
    me = position(level)
    width = parts[0].shape[along]
    for step, ref in enumerate(parts):
        at = pl.multiple_of((me ^ step) * width, width)
        if along == 0:
            out_ref[pl.ds(at, width), :] = ref[...]
        else:
            out_ref[:, pl.ds(at, width)] = ref[...]


def place(parts, level, along):
    shape = list(parts[0].shape)
    shape[along] *= level[0]
    return local_call(functools.partial(place_body, level, along), struct(shape, BF16), parts)


def turned(row, width):
    return jnp.transpose(jnp.broadcast_to(row, (width, row.shape[1])))


def local_body(depth, sizes, *refs):
    r_ref, l_ref, h_ref, o_ref, m_ref, pot_ref, v_ref, e_ref = refs[:8]
    first_ref, many_ref, out_ref, mask_ref = refs[8:]
    plane = GY * GZ
    reach = 6

    def plane_at(j):
        if j < 0:
            ref, k = l_ref, j + reach
        elif j < depth:
            ref, k = r_ref, j
        else:
            ref, k = h_ref, j - depth
        return ref[:, k * plane : (k + 1) * plane]

    group_rows, blk = sizes
    energy = turned(e_ref[...], plane)
    for j in range(depth):
        cols = slice(j * plane, (j + 1) * plane)
        low = plane_at(j)
        total = jnp.dot(low, m_ref[0], preferred_element_type=F32)
        total = total + jnp.dot(low, m_ref[1], preferred_element_type=F32)
        for offset in range(1, 7):
            pair = plane_at(j + offset).astype(F32) + plane_at(j - offset).astype(F32)
            total = total + (KINETIC * COEFFS[offset]) * pair
        total = total + (energy - pot_ref[:, cols]) * low.astype(F32)
        out_ref[:, cols] = total - v_ref[:, cols] * o_ref[:, cols].astype(F32)
    width = mask_ref.shape[1]
    block = lax.broadcasted_iota(jnp.int32, mask_ref.shape, 1) // blk
    block = (block + (pl.program_id(0) * (group_rows // blk) - REACH)).astype(F32)
    lowest = turned(first_ref[...].astype(F32), width)
    inside = (block >= lowest) & (block < lowest + turned(many_ref[...].astype(F32), width))
    mask_ref[...] = jnp.where(inside, 1.0, 0.0).astype(BF16)


def local_part(response, low, high, orbitals, matrix, lines, bounds, group_rows, width, blk):
    bands, cells = response.shape
    depth = cells // (GY * GZ)
    outs = [struct((bands, cells), F32), struct((bands, width), BF16)]
    here = pl.BlockSpec((group_rows, cells), lambda i: (i, 0))
    side = pl.BlockSpec((group_rows, low.shape[1]), lambda i: (i, 0))
    line = pl.BlockSpec((1, cells), lambda i: (0, 0))
    band = pl.BlockSpec((1, group_rows), lambda i: (0, i))
    return pl.pallas_call(
        functools.partial(local_body, depth, (group_rows, blk)),
        grid=(bands // group_rows,),
        out_shape=outs,
        in_specs=[
            here,
            side,
            side,
            here,
            pl.BlockSpec(matrix.shape, lambda i: (0, 0, 0)),
            line,
            line,
            band,
            band,
            band,
        ],
        out_specs=[here, pl.BlockSpec((group_rows, width), lambda i: (i, 0))],
        compiler_params=params(),
        cost_estimate=cost(2 * bands * cells * 300, low, high, low, low, *outs),
    )(response, low, high, orbitals, matrix, *lines, *bounds)


def pad_orbitals(o_ref, pad_ref, blk):
    bands, cells = o_ref.shape
    edge = REACH * blk
    pad_ref[:edge, :] = jnp.zeros((edge, cells), pad_ref.dtype)
    pad_ref[edge : edge + bands, :] = o_ref[...]
    pad_ref[edge + bands :, :] = jnp.zeros((edge, cells), pad_ref.dtype)


def subgroup(shape, blk):
    return lax.broadcasted_iota(jnp.int32, shape, 1) // (2 * blk)


def packed(sums, blk):
    rows = sums.shape[0]
    sub = 2 * blk
    near, far = sums[:, :rows], sums[:, rows:]
    column = subgroup((rows, rows), blk)
    row = lax.broadcasted_iota(jnp.int32, (rows, rows), 0) // sub
    main = jnp.where(column >= row, near, far)
    rest = far[:sub, :]
    for k in range(1, rows // sub):
        rest = jnp.where(column[:sub, :] == k, far[k * sub : (k + 1) * sub, :], rest)
    return main, rest


def unpacked(main, rest, blk):
    rows = main.shape[0]
    sub = 2 * blk
    column = subgroup((rows, rows), blk)
    row = lax.broadcasted_iota(jnp.int32, (rows, rows), 0) // sub
    near = jnp.where(column >= row, main, 0.0)
    last = jnp.where(column == row, jnp.concatenate([rest] * (rows // sub), axis=0), 0.0)
    return near, jnp.where(column < row, main, last)


def apply_body(core, across, block, group_rows, blk, other, *refs):
    size = across[0]
    blocks = refs[: size + 1]
    p_ref, base_ref, o_ref, u_ref, s_ref, c_ref, pad_ref = refs[size + 1 :]
    rows, cells = u_ref.shape
    c, x = position(core), position(across)
    side = 1 - c if other else c
    first = blocks[0].shape[0]
    for step, ref in enumerate(blocks[:size]):
        at = (x ^ step) * block
        c_ref[pl.ds(pl.multiple_of(at, 16), first), :] = ref[...]
    rest = block - first
    for i in range(size):
        there = slice(i * block + first, (i + 1) * block)
        c_ref[there, :] = blocks[size][i * rest : (i + 1) * rest, :]
    mine = pl.ds(pl.multiple_of(side * rows, rows), rows)
    tile = 256 if cells % 256 == 0 else 128
    for t in range(cells // tile):
        cols = slice(t * tile, (t + 1) * tile)
        u_ref[:, cols] = base_ref[mine, cols] + jnp.dot(
            c_ref[...], p_ref[:, cols], preferred_element_type=F32
        )
    pad_orbitals(o_ref, pad_ref, blk)
    height = group_rows + 2 * blk
    for g in range(rows // group_rows):
        start = pl.multiple_of(side * rows + g * group_rows, group_rows)
        sums = lax.dot_general(
            u_ref[g * group_rows : (g + 1) * group_rows, :].astype(BF16),
            pad_ref[pl.ds(start, 2 * group_rows), :],
            NT,
            preferred_element_type=F32,
        )
        main, rest_sums = packed(sums, blk)
        s_ref[g * height : g * height + group_rows, :] = main.astype(s_ref.dtype)
        s_ref[g * height + group_rows : (g + 1) * height, :] = rest_sums.astype(s_ref.dtype)


def apply(blocks, projectors, base, orbitals, core, across, block, group_rows, blk, other):
    bands, cells = base.shape
    rows = bands // 2
    count = projectors.shape[0]
    height = rows // group_rows * (group_rows + 2 * blk)
    return local_call(
        functools.partial(apply_body, core, across, block, group_rows, blk, other),
        [struct((rows, cells), F32), struct((height, group_rows), BF16 if other else F32)],
        [*blocks, projectors, base, orbitals],
        flops=2 * rows * cells * (count + 2 * group_rows),
        scratch=[
            pltpu.VMEM((rows, count), BF16),
            pltpu.VMEM((bands + 2 * REACH * blk, cells), BF16),
        ],
    )


def sum_body(keep_ref, *refs):
    *taken, total_ref, low_ref = refs
    total = total_of(keep_ref, taken, ...)
    total_ref[...] = total
    low_ref[...] = total.astype(BF16)


def add_up(keep, taken):
    outs = [struct(keep.shape, F32), struct(keep.shape, BF16)]
    return local_call(sum_body, outs, [keep, *taken])


def project_body(core, blk, *refs):
    w_own, w_other, u_own, u_other, o_ref, r_ref, mask_ref = refs[:7]
    updated_ref, residual_ref, pad_ref, w_ref, u_ref = refs[7:]
    rows = u_ref.shape[0]
    height = w_ref.shape[0]
    per = u_own.shape[0] // rows
    g = pl.program_id(0)
    own = lax.div(g, jnp.int32(per)) == position(core)
    local = lax.rem(g, jnp.int32(per))
    w_rows = pl.ds(pl.multiple_of(local * height, 16), height)
    u_rows = pl.ds(pl.multiple_of(local * rows, rows), rows)

    @pl.when(g == 0)
    def _():
        pad_orbitals(o_ref, pad_ref, blk)

    @pl.when(own)
    def _():
        w_ref[...] = w_own[w_rows, :]
        u_ref[...] = u_own[u_rows, :]

    @pl.when(jnp.logical_not(own))
    def _():
        w_ref[...] = w_other[w_rows, :]
        u_ref[...] = u_other[u_rows, :]

    main, rest = w_ref[:rows, :].astype(F32), w_ref[rows:, :].astype(F32)
    start = pl.multiple_of(g * rows, rows)
    residual = u_ref[...]
    for k, part in enumerate(unpacked(main, rest, blk)):
        inside = mask_ref[:, k * rows : (k + 1) * rows].astype(F32) > 0.5
        weights = jnp.where(inside, part, 0.0).astype(BF16)
        window = pad_ref[pl.ds(pl.multiple_of(start + k * rows, rows), rows), :]
        residual = residual - jnp.dot(weights, window, preferred_element_type=F32)
    residual_ref[...] = residual.astype(BF16)
    updated_ref[...] = (r_ref[...].astype(F32) + STEP_SIZE * residual).astype(BF16)


def project(weights, unprojected, orbitals, response, mask, core, group_rows, blk):
    bands, cells = response.shape
    out = struct((bands, cells), BF16)
    here = pl.BlockSpec((group_rows, cells), lambda g: (g, 0))

    def full(a):
        return pl.BlockSpec(a.shape, lambda g: (0, 0))

    return pl.pallas_call(
        functools.partial(project_body, core, blk),
        grid=(bands // group_rows,),
        out_shape=(out, out),
        in_specs=[
            *[full(a) for a in (*weights, *unprojected, orbitals)],
            here,
            pl.BlockSpec((group_rows, mask.shape[1]), lambda g: (g, 0)),
        ],
        out_specs=(here, here),
        scratch_shapes=[
            pltpu.VMEM((bands + 2 * REACH * blk, cells), BF16),
            pltpu.VMEM((group_rows + 2 * blk, group_rows), BF16),
            pltpu.VMEM((group_rows, cells), F32),
        ],
        compiler_params=params(),
        cost_estimate=cost(
            4 * bands * group_rows * cells, orbitals, *unprojected, response, out, out
        ),
    )(*weights, *unprojected, orbitals, response, mask)


def shards(
    count, response, orbitals, projectors, potential, perturbing, energies, window_start, block_count
):
    bands, local_cells = response.shape
    cells = local_cells * count
    projections = projectors.shape[0]
    halo = 6 * GY * GZ
    core, across, along = levels_of(count)
    ace_scale = 1.0 / math.sqrt(cells * projections)
    window_scale = 1.0 / math.sqrt(cells * bands)
    blk = bands // NBLK
    group_rows = GROUP_BLOCKS * blk
    width = 2 * group_rows
    half = bands // 2
    block = half // across[0]
    first = max(16, round(REDUCE_SHARE * block / 16) * 16)
    gather_first = max(16, round(GATHER_SHARE * block / 16) * 16)
    matrix = jnp.asarray(plane_matrix())
    lines = (potential[None, :], perturbing[None, :])
    bounds = tuple(a[None, :] for a in (energies, window_start, block_count))

    def to(array, level):
        return [swapped(array, count, level, k) for k in range(1, level[0])]

    def parts_to(parts, level):
        return [swapped(part, count, level, k + 1) for k, part in enumerate(parts)]

    low = neighbour(response[:, local_cells - halo :], count, 1)

    sent_x, sent_z, keep_x, keep_z = first_sums(response, projectors, core, block, first)
    sent_z = swapped(sent_z, count, core, 1)
    sent_x = swapped(sent_x, count, core, 1)
    low, head = lax.optimization_barrier((low, response[:, :halo]))
    high = neighbour(head, count, -1)
    keep_z, *parts_z = split(keep_z, [sent_z], along, 1)
    keep_x, *parts_x = split(keep_x, [sent_x], across, 0)
    parts_x, low = lax.optimization_barrier((parts_x, low))
    taken_z, taken_x, low, high = lax.optimization_barrier(
        (parts_to(parts_z, along), parts_to(parts_x, across), low, high)
    )
    keep_x, *parts_x = split(keep_x, taken_x, along, 1)
    low, head, _ = lax.optimization_barrier((low, response[:, :halo], keep_x))
    high = neighbour(head, count, -1)
    keep_z, *parts_z = split(keep_z, taken_z, across, 0)
    taken_x, taken_z = lax.optimization_barrier(
        (parts_to(parts_x, along), parts_to(parts_z, across))
    )
    share_x, share_z = local_call(
        functools.partial(finish_both_body, ace_scale, len(taken_x)),
        [
            struct((gather_first, projections // along[0]), BF16),
            struct((block - gather_first, projections // along[0]), BF16),
        ],
        [keep_x, *taken_x, keep_z, *taken_z],
    )

    pieces_x, pieces_z, bounds = lax.optimization_barrier(
        ([share_x, *to(share_x, along)], [share_z, *to(share_z, across)], bounds)
    )
    base, mask = local_part(
        response, low, high, orbitals, matrix, lines, bounds, group_rows, width, blk
    )
    block_x = place(pieces_x, along, 1)
    block_z = place(pieces_z, across, 0)
    blocks_x = [block_x, *to(block_x, across)]
    pieces_z, base = lax.optimization_barrier(([block_z, *to(block_z, along)], base))
    blocks = [*blocks_x, place(pieces_z, along, 1)]
    others = [swapped(part, count, core, 1) for part in blocks]
    sizes = (core, across, block, group_rows, blk)
    wide, keep = apply(blocks, projectors, base, orbitals, *sizes, False)
    others, keep = lax.optimization_barrier((others, keep))
    other_wide, part = apply(others, projectors, base, orbitals, *sizes, True)
    unprojected = (wide, other_wide)
    total, part = add_up(keep, to(part, core))
    total, part = add_up(total, to(part, across))
    own = finish(total, to(part, along), window_scale)
    weights = (own, *to(own, core))
    return project(weights, unprojected, orbitals, response, mask, core, group_rows, blk)


def solution(mesh):
    in_specs = (
        P("pert", "band"),
        P(None, "band"),
        P(None, "band"),
        P("band"),
        P(("pert", "band")),
        P(),
        P(),
        P(),
    )
    out_specs = (P("pert", "band"), P("pert", "band"))
    body = functools.partial(shards, mesh.shape["band"])
    return jax.shard_map(body, mesh=mesh, in_specs=in_specs, out_specs=out_specs, check_vma=False)
```

```python
import functools
import math

import jax
import jax.numpy as jnp
import ml_dtypes
import numpy as np
from jax import lax
from jax.experimental import pallas as pl
from jax.experimental.pallas import tpu as pltpu
from jax.sharding import PartitionSpec as P

GY = 8
GZ = 16
NBLK = 32
REACH = 4
GROUP_BLOCKS = 8
COEFFS = (
    -5369.0 / 1800.0,
    12.0 / 7.0,
    -15.0 / 56.0,
    10.0 / 189.0,
    -1.0 / 112.0,
    2.0 / 1925.0,
    -1.0 / 16632.0,
)
KINETIC = 0.125
STEP_SIZE = 0.3
MIB = 1024 * 1024
VMEM_BYTES = 24 * MIB
REDUCE_SHARE = 0.5
GATHER_SHARE = 0.5
BF16 = jnp.bfloat16
F32 = jnp.float32
NT = (((1,), (1,)), ((), ()))


def levels_of(count):
    chips = count // 2
    across = 2 ** (int(math.log2(chips)) // 3)
    return (2, 1), (across, 2), (chips // across, 2 * across)


def position(level):
    size, stride = level
    return lax.rem(lax.div(lax.axis_index("band"), jnp.int32(stride)), jnp.int32(size))


def neighbour(array, count, step):
    return lax.ppermute(array, "band", [(i, (i + step) % count) for i in range(count)])


def swapped(array, count, level, step):
    size, stride = level
    pairs = []
    for device in range(count):
        place = device // stride % size
        pairs.append((device, device + ((place ^ step) - place) * stride))
    return lax.ppermute(array, "band", pairs)


def plane_matrix():
    plane = GY * GZ
    matrix = 3.0 * COEFFS[0] * np.eye(plane)
    cells = np.arange(plane)
    y, z = cells // GZ, cells % GZ
    for offset in range(1, 7):
        for sign in (1, -1):
            np.add.at(matrix, ((y + sign * offset) % GY * GZ + z, cells), COEFFS[offset])
            np.add.at(matrix, (y * GZ + (z + sign * offset) % GZ, cells), COEFFS[offset])
    matrix = KINETIC * matrix
    high = matrix.astype(ml_dtypes.bfloat16)
    low = (matrix - high.astype(np.float64)).astype(ml_dtypes.bfloat16)
    return np.stack([high, low])


def whole():
    return pl.BlockSpec(memory_space=pltpu.VMEM)


def params(size=VMEM_BYTES):
    return pltpu.CompilerParams(vmem_limit_bytes=size)


def cost(flops, *arrays):
    moved = sum(math.prod(a.shape) * jnp.dtype(a.dtype).itemsize for a in arrays)
    return pl.CostEstimate(flops=int(flops), bytes_accessed=int(moved), transcendentals=0)


def local_call(body, outs, args, flops=0, scratch=()):
    return pl.pallas_call(
        body,
        out_shape=outs,
        in_specs=[whole() for _ in args],
        out_specs=jax.tree.map(lambda _: whole(), outs),
        scratch_shapes=scratch,
        compiler_params=params(),
        cost_estimate=cost(flops, *args, *jax.tree.leaves(outs)),
    )(*args)


def struct(shape, dtype):
    return jax.ShapeDtypeStruct(shape, dtype)


def cut(part, block, x_ref, z_ref, cols):
    size = part.shape[0] // block
    first, rest = x_ref.shape[0] // size, z_ref.shape[0] // size
    part = part.astype(x_ref.dtype)
    for i in range(size):
        x_ref[i * first : (i + 1) * first, cols] = part[i * block : i * block + first, :]
        z_ref[i * rest : (i + 1) * rest, cols] = part[i * block + first : (i + 1) * block, :]


def first_body(core, block, tile, r_ref, p_ref, *refs):
    sent_x, sent_z, keep_x, keep_z, r_held, p_held, r_sem, p_sem = refs
    rows = r_held.shape[0] // 2
    r_copy = pltpu.make_async_copy(r_ref, r_held, r_sem)
    r_copy.start()
    copies = []
    for t in range(p_held.shape[0] // tile):
        part = pl.ds(t * tile, tile)
        copies.append(pltpu.make_async_copy(p_ref.at[part, :], p_held.at[part, :], p_sem.at[t]))
        copies[-1].start()
    c = position(core)
    r_copy.wait()
    for t, copy in enumerate(copies):
        copy.wait()
        cols = slice(t * tile, (t + 1) * tile)
        for side, x_ref, z_ref in ((1 - c, sent_x, sent_z), (c, keep_x, keep_z)):
            part = lax.dot_general(
                r_held[pl.ds(pl.multiple_of(side * rows, rows), rows), :],
                p_held[cols, :],
                NT,
                preferred_element_type=F32,
            )
            cut(part, block, x_ref, z_ref, cols)


def first_sums(response, projectors, core, block, first):
    bands, cells = response.shape
    count = projectors.shape[0]
    rows = bands // 2
    tile = min(512, count)
    rows_x = rows // block * first
    outs = [struct((n, count), t) for t in (BF16, F32) for n in (rows_x, rows - rows_x)]
    return pl.pallas_call(
        functools.partial(first_body, core, block, tile),
        out_shape=outs,
        in_specs=[pl.BlockSpec(memory_space=pltpu.HBM)] * 2,
        out_specs=[whole() for _ in outs],
        scratch_shapes=[
            pltpu.VMEM((bands, cells), response.dtype),
            pltpu.VMEM((count, cells), projectors.dtype),
            pltpu.SemaphoreType.DMA,
            pltpu.SemaphoreType.DMA((count // tile,)),
        ],
        compiler_params=params(),
        cost_estimate=cost(2 * bands * cells * count, projectors, *outs),
    )(
        pltpu.with_memory_space_constraint(response, pltpu.HBM),
        pltpu.with_memory_space_constraint(projectors, pltpu.HBM),
    )


def rows_at(place, size):
    return pl.ds(pl.multiple_of(place * size, 16), size)


def cols_at(place, size):
    return pl.ds(pl.multiple_of(place * size, size), size)


def total_of(keep_ref, taken, part):
    total = keep_ref[part]
    for ref in taken:
        total = total + ref[part].astype(F32)
    return total


def split_body(received, level, along, *refs):
    keep_ref, taken, outs = refs[0], refs[1 : 1 + received], refs[1 + received :]
    me = position(level)
    rows, width = outs[0].shape
    for step, out in enumerate(outs):
        at = me ^ step
        if along == 0:
            part = (rows_at(at, rows), slice(None))
        else:
            part = (slice(None), cols_at(at, width))
        out[...] = total_of(keep_ref, taken, part).astype(out.dtype)


def shares_of(shape, count):
    return [struct(shape, F32)] + [struct(shape, BF16)] * (count - 1)


def split(keep, taken, level, along):
    shape = list(keep.shape)
    shape[along] //= level[0]
    return local_call(
        functools.partial(split_body, len(taken), level, along),
        shares_of(shape, level[0]),
        [keep, *taken],
    )


def finish_body(scale, keep_ref, *refs):
    *taken, out_ref = refs
    out_ref[...] = (total_of(keep_ref, taken, ...) * scale).astype(out_ref.dtype)


def finish(keep, taken, scale):
    return local_call(
        functools.partial(finish_body, scale), struct(keep.shape, BF16), [keep, *taken]
    )


def finish_both_body(scale, received, *refs):
    outs = refs[-2:]
    cut = outs[0].shape[0]
    row = 0
    for keep_ref, *taken in (refs[: 1 + received], refs[1 + received : -2]):
        low = (total_of(keep_ref, taken, ...) * scale).astype(BF16)
        end = row + keep_ref.shape[0]
        for out, first, last in ((outs[0], 0, cut), (outs[1], cut, cut + outs[1].shape[0])):
            top, bottom = max(row, first), min(end, last)
            if top < bottom:
                out[top - first : bottom - first, :] = low[top - row : bottom - row, :]
        row = end


def place_body(level, along, *refs):
    *parts, out_ref = refs
    me = position(level)
    width = parts[0].shape[along]
    for step, ref in enumerate(parts):
        at = pl.multiple_of((me ^ step) * width, width)
        if along == 0:
            out_ref[pl.ds(at, width), :] = ref[...]
        else:
            out_ref[:, pl.ds(at, width)] = ref[...]


def place(parts, level, along):
    shape = list(parts[0].shape)
    shape[along] *= level[0]
    return local_call(functools.partial(place_body, level, along), struct(shape, BF16), parts)


def turned(row, width):
    return jnp.transpose(jnp.broadcast_to(row, (width, row.shape[1])))


def local_body(depth, sizes, *refs):
    r_ref, l_ref, h_ref, o_ref, m_ref, pot_ref, v_ref, e_ref = refs[:8]
    first_ref, many_ref, out_ref, mask_ref = refs[8:]
    plane = GY * GZ
    reach = 6

    def plane_at(j):
        if j < 0:
            ref, k = l_ref, j + reach
        elif j < depth:
            ref, k = r_ref, j
        else:
            ref, k = h_ref, j - depth
        return ref[:, k * plane : (k + 1) * plane]

    group_rows, blk = sizes
    energy = turned(e_ref[...], plane)
    for j in range(depth):
        cols = slice(j * plane, (j + 1) * plane)
        low = plane_at(j)
        total = jnp.dot(low, m_ref[0], preferred_element_type=F32)
        total = total + jnp.dot(low, m_ref[1], preferred_element_type=F32)
        for offset in range(1, 7):
            pair = plane_at(j + offset).astype(F32) + plane_at(j - offset).astype(F32)
            total = total + (KINETIC * COEFFS[offset]) * pair
        total = total + (energy - pot_ref[:, cols]) * low.astype(F32)
        out_ref[:, cols] = total - v_ref[:, cols] * o_ref[:, cols].astype(F32)
    width = mask_ref.shape[1]
    block = lax.broadcasted_iota(jnp.int32, mask_ref.shape, 1) // blk
    block = (block + (pl.program_id(0) * (group_rows // blk) - REACH)).astype(F32)
    lowest = turned(first_ref[...].astype(F32), width)
    inside = (block >= lowest) & (block < lowest + turned(many_ref[...].astype(F32), width))
    mask_ref[...] = jnp.where(inside, 1.0, 0.0).astype(BF16)


def local_part(response, low, high, orbitals, matrix, lines, bounds, group_rows, width, blk):
    bands, cells = response.shape
    depth = cells // (GY * GZ)
    outs = [struct((bands, cells), F32), struct((bands, width), BF16)]
    here = pl.BlockSpec((group_rows, cells), lambda i: (i, 0))
    side = pl.BlockSpec((group_rows, low.shape[1]), lambda i: (i, 0))
    line = pl.BlockSpec((1, cells), lambda i: (0, 0))
    band = pl.BlockSpec((1, group_rows), lambda i: (0, i))
    return pl.pallas_call(
        functools.partial(local_body, depth, (group_rows, blk)),
        grid=(bands // group_rows,),
        out_shape=outs,
        in_specs=[
            here,
            side,
            side,
            here,
            pl.BlockSpec(matrix.shape, lambda i: (0, 0, 0)),
            line,
            line,
            band,
            band,
            band,
        ],
        out_specs=[here, pl.BlockSpec((group_rows, width), lambda i: (i, 0))],
        compiler_params=params(),
        cost_estimate=cost(2 * bands * cells * 300, low, high, low, low, *outs),
    )(response, low, high, orbitals, matrix, *lines, *bounds)


def pad_orbitals(o_ref, pad_ref, blk):
    bands, cells = o_ref.shape
    edge = REACH * blk
    pad_ref[:edge, :] = jnp.zeros((edge, cells), pad_ref.dtype)
    pad_ref[edge : edge + bands, :] = o_ref[...]
    pad_ref[edge + bands :, :] = jnp.zeros((edge, cells), pad_ref.dtype)


def subgroup(shape, blk):
    return lax.broadcasted_iota(jnp.int32, shape, 1) // (2 * blk)


def packed(sums, blk):
    rows = sums.shape[0]
    sub = 2 * blk
    near, far = sums[:, :rows], sums[:, rows:]
    column = subgroup((rows, rows), blk)
    row = lax.broadcasted_iota(jnp.int32, (rows, rows), 0) // sub
    main = jnp.where(column >= row, near, far)
    rest = far[:sub, :]
    for k in range(1, rows // sub):
        rest = jnp.where(column[:sub, :] == k, far[k * sub : (k + 1) * sub, :], rest)
    return main, rest


def unpacked(main, rest, blk):
    rows = main.shape[0]
    sub = 2 * blk
    column = subgroup((rows, rows), blk)
    row = lax.broadcasted_iota(jnp.int32, (rows, rows), 0) // sub
    near = jnp.where(column >= row, main, 0.0)
    last = jnp.where(column == row, jnp.concatenate([rest] * (rows // sub), axis=0), 0.0)
    return near, jnp.where(column < row, main, last)


def apply_body(core, across, block, group_rows, blk, other, *refs):
    size = across[0]
    blocks = refs[: size + 1]
    p_ref, base_ref, o_ref, u_ref, s_ref, c_ref, pad_ref = refs[size + 1 :]
    rows, cells = u_ref.shape
    c, x = position(core), position(across)
    side = 1 - c if other else c
    first = blocks[0].shape[0]
    for step, ref in enumerate(blocks[:size]):
        at = (x ^ step) * block
        c_ref[pl.ds(pl.multiple_of(at, 16), first), :] = ref[...]
    rest = block - first
    for i in range(size):
        there = slice(i * block + first, (i + 1) * block)
        c_ref[there, :] = blocks[size][i * rest : (i + 1) * rest, :]
    mine = pl.ds(pl.multiple_of(side * rows, rows), rows)
    tile = 256 if cells % 256 == 0 else 128
    for t in range(cells // tile):
        cols = slice(t * tile, (t + 1) * tile)
        u_ref[:, cols] = base_ref[mine, cols] + jnp.dot(
            c_ref[...], p_ref[:, cols], preferred_element_type=F32
        )
    pad_orbitals(o_ref, pad_ref, blk)
    height = group_rows + 2 * blk
    for g in range(rows // group_rows):
        start = pl.multiple_of(side * rows + g * group_rows, group_rows)
        sums = lax.dot_general(
            u_ref[g * group_rows : (g + 1) * group_rows, :].astype(BF16),
            pad_ref[pl.ds(start, 2 * group_rows), :],
            NT,
            preferred_element_type=F32,
        )
        main, rest_sums = packed(sums, blk)
        s_ref[g * height : g * height + group_rows, :] = main.astype(s_ref.dtype)
        s_ref[g * height + group_rows : (g + 1) * height, :] = rest_sums.astype(s_ref.dtype)


def apply(blocks, projectors, base, orbitals, core, across, block, group_rows, blk, other):
    bands, cells = base.shape
    rows = bands // 2
    count = projectors.shape[0]
    height = rows // group_rows * (group_rows + 2 * blk)
    return local_call(
        functools.partial(apply_body, core, across, block, group_rows, blk, other),
        [struct((rows, cells), F32), struct((height, group_rows), BF16 if other else F32)],
        [*blocks, projectors, base, orbitals],
        flops=2 * rows * cells * (count + 2 * group_rows),
        scratch=[
            pltpu.VMEM((rows, count), BF16),
            pltpu.VMEM((bands + 2 * REACH * blk, cells), BF16),
        ],
    )


def sum_body(keep_ref, *refs):
    *taken, total_ref, low_ref = refs
    total = total_of(keep_ref, taken, ...)
    total_ref[...] = total
    low_ref[...] = total.astype(BF16)


def add_up(keep, taken):
    outs = [struct(keep.shape, F32), struct(keep.shape, BF16)]
    return local_call(sum_body, outs, [keep, *taken])


def project_body(core, blk, *refs):
    w_own, w_other, u_own, u_other, o_ref, r_ref, mask_ref = refs[:7]
    updated_ref, residual_ref, pad_ref, w_ref, u_ref = refs[7:]
    rows = u_ref.shape[0]
    height = w_ref.shape[0]
    per = u_own.shape[0] // rows
    g = pl.program_id(0)
    own = lax.div(g, jnp.int32(per)) == position(core)
    local = lax.rem(g, jnp.int32(per))
    w_rows = pl.ds(pl.multiple_of(local * height, 16), height)
    u_rows = pl.ds(pl.multiple_of(local * rows, rows), rows)

    @pl.when(g == 0)
    def _():
        pad_orbitals(o_ref, pad_ref, blk)

    @pl.when(own)
    def _():
        w_ref[...] = w_own[w_rows, :]
        u_ref[...] = u_own[u_rows, :]

    @pl.when(jnp.logical_not(own))
    def _():
        w_ref[...] = w_other[w_rows, :]
        u_ref[...] = u_other[u_rows, :]

    main, rest = w_ref[:rows, :].astype(F32), w_ref[rows:, :].astype(F32)
    start = pl.multiple_of(g * rows, rows)
    residual = u_ref[...]
    for k, part in enumerate(unpacked(main, rest, blk)):
        inside = mask_ref[:, k * rows : (k + 1) * rows].astype(F32) > 0.5
        weights = jnp.where(inside, part, 0.0).astype(BF16)
        window = pad_ref[pl.ds(pl.multiple_of(start + k * rows, rows), rows), :]
        residual = residual - jnp.dot(weights, window, preferred_element_type=F32)
    residual_ref[...] = residual.astype(BF16)
    updated_ref[...] = (r_ref[...].astype(F32) + STEP_SIZE * residual).astype(BF16)


def project(weights, unprojected, orbitals, response, mask, core, group_rows, blk):
    bands, cells = response.shape
    out = struct((bands, cells), BF16)
    here = pl.BlockSpec((group_rows, cells), lambda g: (g, 0))

    def full(a):
        return pl.BlockSpec(a.shape, lambda g: (0, 0))

    return pl.pallas_call(
        functools.partial(project_body, core, blk),
        grid=(bands // group_rows,),
        out_shape=(out, out),
        in_specs=[
            *[full(a) for a in (*weights, *unprojected, orbitals)],
            here,
            pl.BlockSpec((group_rows, mask.shape[1]), lambda g: (g, 0)),
        ],
        out_specs=(here, here),
        scratch_shapes=[
            pltpu.VMEM((bands + 2 * REACH * blk, cells), BF16),
            pltpu.VMEM((group_rows + 2 * blk, group_rows), BF16),
            pltpu.VMEM((group_rows, cells), F32),
        ],
        compiler_params=params(),
        cost_estimate=cost(
            4 * bands * group_rows * cells, orbitals, *unprojected, response, out, out
        ),
    )(*weights, *unprojected, orbitals, response, mask)


def shards(
    count, response, orbitals, projectors, potential, perturbing, energies, window_start, block_count
):
    bands, local_cells = response.shape
    cells = local_cells * count
    projections = projectors.shape[0]
    halo = 6 * GY * GZ
    core, across, along = levels_of(count)
    ace_scale = 1.0 / math.sqrt(cells * projections)
    window_scale = 1.0 / math.sqrt(cells * bands)
    blk = bands // NBLK
    group_rows = GROUP_BLOCKS * blk
    width = 2 * group_rows
    half = bands // 2
    block = half // across[0]
    first = max(16, round(REDUCE_SHARE * block / 16) * 16)
    gather_first = max(16, round(GATHER_SHARE * block / 16) * 16)
    matrix = jnp.asarray(plane_matrix())
    lines = (potential[None, :], perturbing[None, :])
    bounds = tuple(a[None, :] for a in (energies, window_start, block_count))

    def to(array, level):
        return [swapped(array, count, level, k) for k in range(1, level[0])]

    def parts_to(parts, level):
        return [swapped(part, count, level, k + 1) for k, part in enumerate(parts)]

    low = neighbour(response[:, local_cells - halo :], count, 1)
    high = neighbour(response[:, :halo], count, -1)

    sent_x, sent_z, keep_x, keep_z = first_sums(response, projectors, core, block, first)
    sent_z = swapped(sent_z, count, core, 1)
    sent_x = swapped(sent_x, count, core, 1)
    keep_z, *parts_z = split(keep_z, [sent_z], along, 1)
    keep_x, *parts_x = split(keep_x, [sent_x], across, 0)
    parts_z[-1], low = lax.optimization_barrier((parts_z[-1], low))
    taken_z, taken_x, low, high = lax.optimization_barrier(
        (parts_to(parts_z, along), parts_to(parts_x, across), low, high)
    )
    keep_x, *parts_x = split(keep_x, taken_x, along, 1)
    keep_z, *parts_z = split(keep_z, taken_z, across, 0)
    taken_x, taken_z = lax.optimization_barrier(
        (parts_to(parts_x, along), parts_to(parts_z, across))
    )
    share_x, share_z = local_call(
        functools.partial(finish_both_body, ace_scale, len(taken_x)),
        [
            struct((gather_first, projections // along[0]), BF16),
            struct((block - gather_first, projections // along[0]), BF16),
        ],
        [keep_x, *taken_x, keep_z, *taken_z],
    )

    pieces_x, pieces_z, bounds = lax.optimization_barrier(
        ([share_x, *to(share_x, along)], [share_z, *to(share_z, across)], bounds)
    )
    base, mask = local_part(
        response, low, high, orbitals, matrix, lines, bounds, group_rows, width, blk
    )
    block_x = place(pieces_x, along, 1)
    block_z = place(pieces_z, across, 0)
    blocks_x = [block_x, *to(block_x, across)]
    pieces_z, base = lax.optimization_barrier(([block_z, *to(block_z, along)], base))
    blocks = [*blocks_x, place(pieces_z, along, 1)]
    others = [swapped(part, count, core, 1) for part in blocks]
    sizes = (core, across, block, group_rows, blk)
    wide, keep = apply(blocks, projectors, base, orbitals, *sizes, False)
    others, keep = lax.optimization_barrier((others, keep))
    other_wide, part = apply(others, projectors, base, orbitals, *sizes, True)
    unprojected = (wide, other_wide)
    total, part = add_up(keep, to(part, core))
    total, part = add_up(total, to(part, across))
    own = finish(total, to(part, along), window_scale)
    weights = (own, *to(own, core))
    return project(weights, unprojected, orbitals, response, mask, core, group_rows, blk)


def solution(mesh):
    in_specs = (
        P("pert", "band"),
        P(None, "band"),
        P(None, "band"),
        P("band"),
        P(("pert", "band")),
        P(),
        P(),
        P(),
    )
    out_specs = (P("pert", "band"), P("pert", "band"))
    body = functools.partial(shards, mesh.shape["band"])
    return jax.shard_map(body, mesh=mesh, in_specs=in_specs, out_specs=out_specs, check_vma=False)
```

```python
import functools
import math

import jax
import jax.numpy as jnp
import ml_dtypes
import numpy as np
from jax import lax
from jax.experimental import pallas as pl
from jax.experimental.pallas import tpu as pltpu
from jax.sharding import PartitionSpec as P

GY = 8
GZ = 16
NBLK = 32
REACH = 4
GROUP_BLOCKS = 8
COEFFS = (
    -5369.0 / 1800.0,
    12.0 / 7.0,
    -15.0 / 56.0,
    10.0 / 189.0,
    -1.0 / 112.0,
    2.0 / 1925.0,
    -1.0 / 16632.0,
)
KINETIC = 0.125
STEP_SIZE = 0.3
MIB = 1024 * 1024
VMEM_BYTES = 24 * MIB
FIRST_SHARE = 0.5
BF16 = jnp.bfloat16
F32 = jnp.float32
NT = (((1,), (1,)), ((), ()))


def levels_of(count):
    chips = count // 2
    across = 2 ** (int(math.log2(chips)) // 3)
    return (2, 1), (across, 2), (chips // across, 2 * across)


def position(level):
    size, stride = level
    return lax.rem(lax.div(lax.axis_index("band"), jnp.int32(stride)), jnp.int32(size))


def neighbour(array, count, step):
    return lax.ppermute(array, "band", [(i, (i + step) % count) for i in range(count)])


def swapped(array, count, level, step):
    size, stride = level
    pairs = []
    for device in range(count):
        place = device // stride % size
        pairs.append((device, device + ((place ^ step) - place) * stride))
    return lax.ppermute(array, "band", pairs)


def plane_matrix():
    plane = GY * GZ
    matrix = 3.0 * COEFFS[0] * np.eye(plane)
    cells = np.arange(plane)
    y, z = cells // GZ, cells % GZ
    for offset in range(1, 7):
        for sign in (1, -1):
            np.add.at(matrix, ((y + sign * offset) % GY * GZ + z, cells), COEFFS[offset])
            np.add.at(matrix, (y * GZ + (z + sign * offset) % GZ, cells), COEFFS[offset])
    matrix = KINETIC * matrix
    high = matrix.astype(ml_dtypes.bfloat16)
    low = (matrix - high.astype(np.float64)).astype(ml_dtypes.bfloat16)
    return np.stack([high, low])


def whole():
    return pl.BlockSpec(memory_space=pltpu.VMEM)


def params(size=VMEM_BYTES):
    return pltpu.CompilerParams(vmem_limit_bytes=size)


def cost(flops, *arrays):
    moved = sum(math.prod(a.shape) * jnp.dtype(a.dtype).itemsize for a in arrays)
    return pl.CostEstimate(flops=int(flops), bytes_accessed=int(moved), transcendentals=0)


def local_call(body, outs, args, flops=0, scratch=()):
    return pl.pallas_call(
        body,
        out_shape=outs,
        in_specs=[whole() for _ in args],
        out_specs=jax.tree.map(lambda _: whole(), outs),
        scratch_shapes=scratch,
        compiler_params=params(),
        cost_estimate=cost(flops, *args, *jax.tree.leaves(outs)),
    )(*args)


def struct(shape, dtype):
    return jax.ShapeDtypeStruct(shape, dtype)


def cut(part, block, x_ref, z_ref, cols):
    size = part.shape[0] // block
    first, rest = x_ref.shape[0] // size, z_ref.shape[0] // size
    part = part.astype(x_ref.dtype)
    for i in range(size):
        x_ref[i * first : (i + 1) * first, cols] = part[i * block : i * block + first, :]
        z_ref[i * rest : (i + 1) * rest, cols] = part[i * block + first : (i + 1) * block, :]


def first_body(core, block, tile, r_ref, p_ref, *refs):
    sent_x, sent_z, keep_x, keep_z, r_held, p_held, r_sem, p_sem = refs
    rows = r_held.shape[0] // 2
    r_copy = pltpu.make_async_copy(r_ref, r_held, r_sem)
    r_copy.start()
    copies = []
    for t in range(p_held.shape[0] // tile):
        part = pl.ds(t * tile, tile)
        copies.append(pltpu.make_async_copy(p_ref.at[part, :], p_held.at[part, :], p_sem.at[t]))
        copies[-1].start()
    c = position(core)
    r_copy.wait()
    for t, copy in enumerate(copies):
        copy.wait()
        cols = slice(t * tile, (t + 1) * tile)
        for side, x_ref, z_ref in ((1 - c, sent_x, sent_z), (c, keep_x, keep_z)):
            part = lax.dot_general(
                r_held[pl.ds(pl.multiple_of(side * rows, rows), rows), :],
                p_held[cols, :],
                NT,
                preferred_element_type=F32,
            )
            cut(part, block, x_ref, z_ref, cols)


def first_sums(response, projectors, core, block, first):
    bands, cells = response.shape
    count = projectors.shape[0]
    rows = bands // 2
    tile = min(512, count)
    rows_x = rows // block * first
    outs = [struct((n, count), t) for t in (BF16, F32) for n in (rows_x, rows - rows_x)]
    return pl.pallas_call(
        functools.partial(first_body, core, block, tile),
        out_shape=outs,
        in_specs=[pl.BlockSpec(memory_space=pltpu.HBM)] * 2,
        out_specs=[whole() for _ in outs],
        scratch_shapes=[
            pltpu.VMEM((bands, cells), response.dtype),
            pltpu.VMEM((count, cells), projectors.dtype),
            pltpu.SemaphoreType.DMA,
            pltpu.SemaphoreType.DMA((count // tile,)),
        ],
        compiler_params=params(),
        cost_estimate=cost(2 * bands * cells * count, projectors, *outs),
    )(
        pltpu.with_memory_space_constraint(response, pltpu.HBM),
        pltpu.with_memory_space_constraint(projectors, pltpu.HBM),
    )


def rows_at(place, size):
    return pl.ds(pl.multiple_of(place * size, 16), size)


def cols_at(place, size):
    return pl.ds(pl.multiple_of(place * size, size), size)


def total_of(keep_ref, taken, part):
    total = keep_ref[part]
    for ref in taken:
        total = total + ref[part].astype(F32)
    return total


def split_body(received, level, along, *refs):
    keep_ref, taken, outs = refs[0], refs[1 : 1 + received], refs[1 + received :]
    me = position(level)
    rows, width = outs[0].shape
    for step, out in enumerate(outs):
        at = me ^ step
        if along == 0:
            part = (rows_at(at, rows), slice(None))
        else:
            part = (slice(None), cols_at(at, width))
        out[...] = total_of(keep_ref, taken, part).astype(out.dtype)


def shares_of(shape, count):
    return [struct(shape, F32)] + [struct(shape, BF16)] * (count - 1)


def split(keep, taken, level, along):
    shape = list(keep.shape)
    shape[along] //= level[0]
    return local_call(
        functools.partial(split_body, len(taken), level, along),
        shares_of(shape, level[0]),
        [keep, *taken],
    )


def finish_body(scale, keep_ref, *refs):
    *taken, out_ref = refs
    out_ref[...] = (total_of(keep_ref, taken, ...) * scale).astype(out_ref.dtype)


def finish(keep, taken, scale):
    return local_call(
        functools.partial(finish_body, scale), struct(keep.shape, BF16), [keep, *taken]
    )


def place_body(level, along, *refs):
    *parts, out_ref = refs
    me = position(level)
    width = parts[0].shape[along]
    for step, ref in enumerate(parts):
        at = pl.multiple_of((me ^ step) * width, width)
        if along == 0:
            out_ref[pl.ds(at, width), :] = ref[...]
        else:
            out_ref[:, pl.ds(at, width)] = ref[...]


def place(parts, level, along):
    shape = list(parts[0].shape)
    shape[along] *= level[0]
    return local_call(functools.partial(place_body, level, along), struct(shape, BF16), parts)


def turned(row, width):
    return jnp.transpose(jnp.broadcast_to(row, (width, row.shape[1])))


def local_body(depth, sizes, *refs):
    r_ref, l_ref, h_ref, o_ref, m_ref, pot_ref, v_ref, e_ref = refs[:8]
    first_ref, many_ref, out_ref, mask_ref = refs[8:]
    plane = GY * GZ
    reach = 6

    def plane_at(j):
        if j < 0:
            ref, k = l_ref, j + reach
        elif j < depth:
            ref, k = r_ref, j
        else:
            ref, k = h_ref, j - depth
        return ref[:, k * plane : (k + 1) * plane]

    group_rows, blk = sizes
    energy = turned(e_ref[...], plane)
    for j in range(depth):
        cols = slice(j * plane, (j + 1) * plane)
        low = plane_at(j)
        total = jnp.dot(low, m_ref[0], preferred_element_type=F32)
        total = total + jnp.dot(low, m_ref[1], preferred_element_type=F32)
        for offset in range(1, 7):
            pair = plane_at(j + offset).astype(F32) + plane_at(j - offset).astype(F32)
            total = total + (KINETIC * COEFFS[offset]) * pair
        total = total + (energy - pot_ref[:, cols]) * low.astype(F32)
        out_ref[:, cols] = total - v_ref[:, cols] * o_ref[:, cols].astype(F32)
    width = mask_ref.shape[1]
    block = lax.broadcasted_iota(jnp.int32, mask_ref.shape, 1) // blk
    block = (block + (pl.program_id(0) * (group_rows // blk) - REACH)).astype(F32)
    lowest = turned(first_ref[...].astype(F32), width)
    inside = (block >= lowest) & (block < lowest + turned(many_ref[...].astype(F32), width))
    mask_ref[...] = jnp.where(inside, 1.0, 0.0).astype(BF16)


def local_part(response, low, high, orbitals, matrix, lines, bounds, group_rows, width, blk):
    bands, cells = response.shape
    depth = cells // (GY * GZ)
    outs = [struct((bands, cells), F32), struct((bands, width), BF16)]
    here = pl.BlockSpec((group_rows, cells), lambda i: (i, 0))
    side = pl.BlockSpec((group_rows, low.shape[1]), lambda i: (i, 0))
    line = pl.BlockSpec((1, cells), lambda i: (0, 0))
    band = pl.BlockSpec((1, group_rows), lambda i: (0, i))
    return pl.pallas_call(
        functools.partial(local_body, depth, (group_rows, blk)),
        grid=(bands // group_rows,),
        out_shape=outs,
        in_specs=[
            here,
            side,
            side,
            here,
            pl.BlockSpec(matrix.shape, lambda i: (0, 0, 0)),
            line,
            line,
            band,
            band,
            band,
        ],
        out_specs=[here, pl.BlockSpec((group_rows, width), lambda i: (i, 0))],
        compiler_params=params(),
        cost_estimate=cost(2 * bands * cells * 300, low, high, low, low, *outs),
    )(response, low, high, orbitals, matrix, *lines, *bounds)


def pad_orbitals(o_ref, pad_ref, blk):
    bands, cells = o_ref.shape
    edge = REACH * blk
    pad_ref[:edge, :] = jnp.zeros((edge, cells), pad_ref.dtype)
    pad_ref[edge : edge + bands, :] = o_ref[...]
    pad_ref[edge + bands :, :] = jnp.zeros((edge, cells), pad_ref.dtype)


def subgroup(shape, blk):
    return lax.broadcasted_iota(jnp.int32, shape, 1) // (2 * blk)


def packed(sums, blk):
    rows = sums.shape[0]
    sub = 2 * blk
    near, far = sums[:, :rows], sums[:, rows:]
    column = subgroup((rows, rows), blk)
    row = lax.broadcasted_iota(jnp.int32, (rows, rows), 0) // sub
    main = jnp.where(column >= row, near, far)
    rest = far[:sub, :]
    for k in range(1, rows // sub):
        rest = jnp.where(column[:sub, :] == k, far[k * sub : (k + 1) * sub, :], rest)
    return main, rest


def unpacked(main, rest, blk):
    rows = main.shape[0]
    sub = 2 * blk
    column = subgroup((rows, rows), blk)
    row = lax.broadcasted_iota(jnp.int32, (rows, rows), 0) // sub
    near = jnp.where(column >= row, main, 0.0)
    last = jnp.where(column == row, jnp.concatenate([rest] * (rows // sub), axis=0), 0.0)
    return near, jnp.where(column < row, main, last)


def apply_body(core, across, block, group_rows, blk, other, *refs):
    size = across[0]
    blocks = refs[: size + 1]
    p_ref, base_ref, o_ref, u_ref, s_ref, c_ref, pad_ref = refs[size + 1 :]
    rows, cells = u_ref.shape
    c, x = position(core), position(across)
    side = 1 - c if other else c
    first = blocks[0].shape[0]
    for step, ref in enumerate(blocks[:size]):
        at = (x ^ step) * block
        c_ref[pl.ds(pl.multiple_of(at, 16), first), :] = ref[...]
    rest = block - first
    for i in range(size):
        there = slice(i * block + first, (i + 1) * block)
        c_ref[there, :] = blocks[size][i * rest : (i + 1) * rest, :]
    mine = pl.ds(pl.multiple_of(side * rows, rows), rows)
    tile = 256 if cells % 256 == 0 else 128
    for t in range(cells // tile):
        cols = slice(t * tile, (t + 1) * tile)
        u_ref[:, cols] = base_ref[mine, cols] + jnp.dot(
            c_ref[...], p_ref[:, cols], preferred_element_type=F32
        )
    pad_orbitals(o_ref, pad_ref, blk)
    height = group_rows + 2 * blk
    for g in range(rows // group_rows):
        start = pl.multiple_of(side * rows + g * group_rows, group_rows)
        sums = lax.dot_general(
            u_ref[g * group_rows : (g + 1) * group_rows, :].astype(BF16),
            pad_ref[pl.ds(start, 2 * group_rows), :],
            NT,
            preferred_element_type=F32,
        )
        main, rest_sums = packed(sums, blk)
        s_ref[g * height : g * height + group_rows, :] = main.astype(s_ref.dtype)
        s_ref[g * height + group_rows : (g + 1) * height, :] = rest_sums.astype(s_ref.dtype)


def apply(blocks, projectors, base, orbitals, core, across, block, group_rows, blk, other):
    bands, cells = base.shape
    rows = bands // 2
    count = projectors.shape[0]
    height = rows // group_rows * (group_rows + 2 * blk)
    return local_call(
        functools.partial(apply_body, core, across, block, group_rows, blk, other),
        [struct((rows, cells), F32), struct((height, group_rows), BF16 if other else F32)],
        [*blocks, projectors, base, orbitals],
        flops=2 * rows * cells * (count + 2 * group_rows),
        scratch=[
            pltpu.VMEM((rows, count), BF16),
            pltpu.VMEM((bands + 2 * REACH * blk, cells), BF16),
        ],
    )


def sum_body(keep_ref, *refs):
    *taken, total_ref, low_ref = refs
    total = total_of(keep_ref, taken, ...)
    total_ref[...] = total
    low_ref[...] = total.astype(BF16)


def add_up(keep, taken):
    outs = [struct(keep.shape, F32), struct(keep.shape, BF16)]
    return local_call(sum_body, outs, [keep, *taken])


def project_body(core, blk, *refs):
    w_own, w_other, u_own, u_other, o_ref, r_ref, mask_ref = refs[:7]
    updated_ref, residual_ref, pad_ref, w_ref, u_ref = refs[7:]
    rows = u_ref.shape[0]
    height = w_ref.shape[0]
    per = u_own.shape[0] // rows
    g = pl.program_id(0)
    own = lax.div(g, jnp.int32(per)) == position(core)
    local = lax.rem(g, jnp.int32(per))
    w_rows = pl.ds(pl.multiple_of(local * height, 16), height)
    u_rows = pl.ds(pl.multiple_of(local * rows, rows), rows)

    @pl.when(g == 0)
    def _():
        pad_orbitals(o_ref, pad_ref, blk)

    @pl.when(own)
    def _():
        w_ref[...] = w_own[w_rows, :]
        u_ref[...] = u_own[u_rows, :]

    @pl.when(jnp.logical_not(own))
    def _():
        w_ref[...] = w_other[w_rows, :]
        u_ref[...] = u_other[u_rows, :]

    main, rest = w_ref[:rows, :].astype(F32), w_ref[rows:, :].astype(F32)
    start = pl.multiple_of(g * rows, rows)
    residual = u_ref[...]
    for k, part in enumerate(unpacked(main, rest, blk)):
        inside = mask_ref[:, k * rows : (k + 1) * rows].astype(F32) > 0.5
        weights = jnp.where(inside, part, 0.0).astype(BF16)
        window = pad_ref[pl.ds(pl.multiple_of(start + k * rows, rows), rows), :]
        residual = residual - jnp.dot(weights, window, preferred_element_type=F32)
    residual_ref[...] = residual.astype(BF16)
    updated_ref[...] = (r_ref[...].astype(F32) + STEP_SIZE * residual).astype(BF16)


def project(weights, unprojected, orbitals, response, mask, core, group_rows, blk):
    bands, cells = response.shape
    out = struct((bands, cells), BF16)
    here = pl.BlockSpec((group_rows, cells), lambda g: (g, 0))

    def full(a):
        return pl.BlockSpec(a.shape, lambda g: (0, 0))

    return pl.pallas_call(
        functools.partial(project_body, core, blk),
        grid=(bands // group_rows,),
        out_shape=(out, out),
        in_specs=[
            *[full(a) for a in (*weights, *unprojected, orbitals)],
            here,
            pl.BlockSpec((group_rows, mask.shape[1]), lambda g: (g, 0)),
        ],
        out_specs=(here, here),
        scratch_shapes=[
            pltpu.VMEM((bands + 2 * REACH * blk, cells), BF16),
            pltpu.VMEM((group_rows + 2 * blk, group_rows), BF16),
            pltpu.VMEM((group_rows, cells), F32),
        ],
        compiler_params=params(),
        cost_estimate=cost(
            4 * bands * group_rows * cells, orbitals, *unprojected, response, out, out
        ),
    )(*weights, *unprojected, orbitals, response, mask)


def shards(
    count, response, orbitals, projectors, potential, perturbing, energies, window_start, block_count
):
    bands, local_cells = response.shape
    cells = local_cells * count
    projections = projectors.shape[0]
    halo = 6 * GY * GZ
    core, across, along = levels_of(count)
    ace_scale = 1.0 / math.sqrt(cells * projections)
    window_scale = 1.0 / math.sqrt(cells * bands)
    blk = bands // NBLK
    group_rows = GROUP_BLOCKS * blk
    width = 2 * group_rows
    half = bands // 2
    block = half // across[0]
    first = max(16, round(FIRST_SHARE * block / 16) * 16)
    matrix = jnp.asarray(plane_matrix())
    lines = (potential[None, :], perturbing[None, :])
    bounds = tuple(a[None, :] for a in (energies, window_start, block_count))

    def to(array, level):
        return [swapped(array, count, level, k) for k in range(1, level[0])]

    def parts_to(parts, level):
        return [swapped(part, count, level, k + 1) for k, part in enumerate(parts)]

    low = neighbour(response[:, local_cells - halo :], count, 1)
    high = neighbour(response[:, :halo], count, -1)

    sent_x, sent_z, keep_x, keep_z = first_sums(response, projectors, core, block, first)
    sent_z = swapped(sent_z, count, core, 1)
    sent_x = swapped(sent_x, count, core, 1)
    keep_z, *parts_z = split(keep_z, [sent_z], along, 1)
    keep_x, *parts_x = split(keep_x, [sent_x], across, 0)
    parts_z[-1], low = lax.optimization_barrier((parts_z[-1], low))
    taken_z, taken_x, low, high = lax.optimization_barrier(
        (parts_to(parts_z, along), parts_to(parts_x, across), low, high)
    )
    keep_x, *parts_x = split(keep_x, taken_x, along, 1)
    keep_z, *parts_z = split(keep_z, taken_z, across, 0)
    share_z = finish(keep_z, parts_to(parts_z, across), ace_scale)
    share_x = finish(keep_x, parts_to(parts_x, along), ace_scale)

    block_z = place([share_z, *to(share_z, across)], across, 0)
    pieces_x, bounds = lax.optimization_barrier(([share_x, *to(share_x, along)], bounds))
    base, mask = local_part(
        response, low, high, orbitals, matrix, lines, bounds, group_rows, width, blk
    )
    block_x = place(pieces_x, along, 1)
    blocks_x = [block_x, *to(block_x, across)]
    pieces_z, base = lax.optimization_barrier(([block_z, *to(block_z, along)], base))
    blocks = [*blocks_x, place(pieces_z, along, 1)]
    others = [swapped(part, count, core, 1) for part in blocks]
    sizes = (core, across, block, group_rows, blk)
    wide, keep = apply(blocks, projectors, base, orbitals, *sizes, False)
    others, keep = lax.optimization_barrier((others, keep))
    other_wide, part = apply(others, projectors, base, orbitals, *sizes, True)
    unprojected = (wide, other_wide)
    total, part = add_up(keep, to(part, core))
    total, part = add_up(total, to(part, across))
    own = finish(total, to(part, along), window_scale)
    weights = (own, *to(own, core))
    return project(weights, unprojected, orbitals, response, mask, core, group_rows, blk)


def solution(mesh):
    in_specs = (
        P("pert", "band"),
        P(None, "band"),
        P(None, "band"),
        P("band"),
        P(("pert", "band")),
        P(),
        P(),
        P(),
    )
    out_specs = (P("pert", "band"), P("pert", "band"))
    body = functools.partial(shards, mesh.shape["band"])
    return jax.shard_map(body, mesh=mesh, in_specs=in_specs, out_specs=out_specs, check_vma=False)
```

```python
import functools
import math

import jax
import jax.numpy as jnp
import ml_dtypes
import numpy as np
from jax import lax
from jax.experimental import pallas as pl
from jax.experimental.pallas import tpu as pltpu
from jax.sharding import PartitionSpec as P

GY = 8
GZ = 16
NBLK = 32
REACH = 4
GROUP_BLOCKS = 8
COEFFS = (
    -5369.0 / 1800.0,
    12.0 / 7.0,
    -15.0 / 56.0,
    10.0 / 189.0,
    -1.0 / 112.0,
    2.0 / 1925.0,
    -1.0 / 16632.0,
)
KINETIC = 0.125
STEP_SIZE = 0.3
MIB = 1024 * 1024
VMEM_BYTES = 24 * MIB
REDUCE_SHARE = 0.625
GATHER_SHARE = 0.5
BF16 = jnp.bfloat16
F32 = jnp.float32
NT = (((1,), (1,)), ((), ()))


def levels_of(count):
    chips = count // 2
    across = 2 ** (int(math.log2(chips)) // 3)
    return (2, 1), (across, 2), (chips // across, 2 * across)


def position(level):
    size, stride = level
    return lax.rem(lax.div(lax.axis_index("band"), jnp.int32(stride)), jnp.int32(size))


def neighbour(array, count, step):
    return lax.ppermute(array, "band", [(i, (i + step) % count) for i in range(count)])


def swapped(array, count, level, step):
    size, stride = level
    pairs = []
    for device in range(count):
        place = device // stride % size
        pairs.append((device, device + ((place ^ step) - place) * stride))
    return lax.ppermute(array, "band", pairs)


def plane_matrix():
    plane = GY * GZ
    matrix = 3.0 * COEFFS[0] * np.eye(plane)
    cells = np.arange(plane)
    y, z = cells // GZ, cells % GZ
    for offset in range(1, 7):
        for sign in (1, -1):
            np.add.at(matrix, ((y + sign * offset) % GY * GZ + z, cells), COEFFS[offset])
            np.add.at(matrix, (y * GZ + (z + sign * offset) % GZ, cells), COEFFS[offset])
    matrix = KINETIC * matrix
    high = matrix.astype(ml_dtypes.bfloat16)
    low = (matrix - high.astype(np.float64)).astype(ml_dtypes.bfloat16)
    return np.stack([high, low])


def whole():
    return pl.BlockSpec(memory_space=pltpu.VMEM)


def params(size=VMEM_BYTES):
    return pltpu.CompilerParams(vmem_limit_bytes=size)


def cost(flops, *arrays):
    moved = sum(math.prod(a.shape) * jnp.dtype(a.dtype).itemsize for a in arrays)
    return pl.CostEstimate(flops=int(flops), bytes_accessed=int(moved), transcendentals=0)


def local_call(body, outs, args, flops=0, scratch=()):
    return pl.pallas_call(
        body,
        out_shape=outs,
        in_specs=[whole() for _ in args],
        out_specs=jax.tree.map(lambda _: whole(), outs),
        scratch_shapes=scratch,
        compiler_params=params(),
        cost_estimate=cost(flops, *args, *jax.tree.leaves(outs)),
    )(*args)


def struct(shape, dtype):
    return jax.ShapeDtypeStruct(shape, dtype)


def cut(part, block, x_ref, z_ref, cols):
    size = part.shape[0] // block
    first, rest = x_ref.shape[0] // size, z_ref.shape[0] // size
    part = part.astype(x_ref.dtype)
    for i in range(size):
        x_ref[i * first : (i + 1) * first, cols] = part[i * block : i * block + first, :]
        z_ref[i * rest : (i + 1) * rest, cols] = part[i * block + first : (i + 1) * block, :]


def first_body(core, block, tile, r_ref, p_ref, *refs):
    sent_x, sent_z, keep_x, keep_z, r_held, p_held, r_sem, p_sem = refs
    rows = r_held.shape[0] // 2
    r_copy = pltpu.make_async_copy(r_ref, r_held, r_sem)
    r_copy.start()
    copies = []
    for t in range(p_held.shape[0] // tile):
        part = pl.ds(t * tile, tile)
        copies.append(pltpu.make_async_copy(p_ref.at[part, :], p_held.at[part, :], p_sem.at[t]))
        copies[-1].start()
    c = position(core)
    r_copy.wait()
    for t, copy in enumerate(copies):
        copy.wait()
        cols = slice(t * tile, (t + 1) * tile)
        for side, x_ref, z_ref in ((1 - c, sent_x, sent_z), (c, keep_x, keep_z)):
            part = lax.dot_general(
                r_held[pl.ds(pl.multiple_of(side * rows, rows), rows), :],
                p_held[cols, :],
                NT,
                preferred_element_type=F32,
            )
            cut(part, block, x_ref, z_ref, cols)


def first_sums(response, projectors, core, block, first):
    bands, cells = response.shape
    count = projectors.shape[0]
    rows = bands // 2
    tile = min(512, count)
    rows_x = rows // block * first
    outs = [struct((n, count), t) for t in (BF16, F32) for n in (rows_x, rows - rows_x)]
    return pl.pallas_call(
        functools.partial(first_body, core, block, tile),
        out_shape=outs,
        in_specs=[pl.BlockSpec(memory_space=pltpu.HBM)] * 2,
        out_specs=[whole() for _ in outs],
        scratch_shapes=[
            pltpu.VMEM((bands, cells), response.dtype),
            pltpu.VMEM((count, cells), projectors.dtype),
            pltpu.SemaphoreType.DMA,
            pltpu.SemaphoreType.DMA((count // tile,)),
        ],
        compiler_params=params(),
        cost_estimate=cost(2 * bands * cells * count, projectors, *outs),
    )(
        pltpu.with_memory_space_constraint(response, pltpu.HBM),
        pltpu.with_memory_space_constraint(projectors, pltpu.HBM),
    )


def rows_at(place, size):
    return pl.ds(pl.multiple_of(place * size, 16), size)


def cols_at(place, size):
    return pl.ds(pl.multiple_of(place * size, size), size)


def total_of(keep_ref, taken, part):
    total = keep_ref[part]
    for ref in taken:
        total = total + ref[part].astype(F32)
    return total


def split_body(received, level, along, *refs):
    keep_ref, taken, outs = refs[0], refs[1 : 1 + received], refs[1 + received :]
    me = position(level)
    rows, width = outs[0].shape
    for step, out in enumerate(outs):
        at = me ^ step
        if along == 0:
            part = (rows_at(at, rows), slice(None))
        else:
            part = (slice(None), cols_at(at, width))
        out[...] = total_of(keep_ref, taken, part).astype(out.dtype)


def shares_of(shape, count):
    return [struct(shape, F32)] + [struct(shape, BF16)] * (count - 1)


def split(keep, taken, level, along):
    shape = list(keep.shape)
    shape[along] //= level[0]
    return local_call(
        functools.partial(split_body, len(taken), level, along),
        shares_of(shape, level[0]),
        [keep, *taken],
    )


def finish_body(scale, keep_ref, *refs):
    *taken, out_ref = refs
    out_ref[...] = (total_of(keep_ref, taken, ...) * scale).astype(out_ref.dtype)


def finish(keep, taken, scale):
    return local_call(
        functools.partial(finish_body, scale), struct(keep.shape, BF16), [keep, *taken]
    )


def finish_both_body(scale, received, *refs):
    outs = refs[-2:]
    cut = outs[0].shape[0]
    row = 0
    for keep_ref, *taken in (refs[: 1 + received], refs[1 + received : -2]):
        low = (total_of(keep_ref, taken, ...) * scale).astype(BF16)
        end = row + keep_ref.shape[0]
        for out, first, last in ((outs[0], 0, cut), (outs[1], cut, cut + outs[1].shape[0])):
            top, bottom = max(row, first), min(end, last)
            if top < bottom:
                out[top - first : bottom - first, :] = low[top - row : bottom - row, :]
        row = end


def place_body(level, along, *refs):
    *parts, out_ref = refs
    me = position(level)
    width = parts[0].shape[along]
    for step, ref in enumerate(parts):
        at = pl.multiple_of((me ^ step) * width, width)
        if along == 0:
            out_ref[pl.ds(at, width), :] = ref[...]
        else:
            out_ref[:, pl.ds(at, width)] = ref[...]


def place(parts, level, along):
    shape = list(parts[0].shape)
    shape[along] *= level[0]
    return local_call(functools.partial(place_body, level, along), struct(shape, BF16), parts)


def turned(row, width):
    return jnp.transpose(jnp.broadcast_to(row, (width, row.shape[1])))


def local_body(depth, sizes, *refs):
    r_ref, l_ref, h_ref, o_ref, m_ref, pot_ref, v_ref, e_ref = refs[:8]
    first_ref, many_ref, out_ref, mask_ref = refs[8:]
    plane = GY * GZ
    reach = 6

    def plane_at(j):
        if j < 0:
            ref, k = l_ref, j + reach
        elif j < depth:
            ref, k = r_ref, j
        else:
            ref, k = h_ref, j - depth
        return ref[:, k * plane : (k + 1) * plane]

    group_rows, blk = sizes
    energy = turned(e_ref[...], plane)
    for j in range(depth):
        cols = slice(j * plane, (j + 1) * plane)
        low = plane_at(j)
        total = jnp.dot(low, m_ref[0], preferred_element_type=F32)
        total = total + jnp.dot(low, m_ref[1], preferred_element_type=F32)
        for offset in range(1, 7):
            pair = plane_at(j + offset).astype(F32) + plane_at(j - offset).astype(F32)
            total = total + (KINETIC * COEFFS[offset]) * pair
        total = total + (energy - pot_ref[:, cols]) * low.astype(F32)
        out_ref[:, cols] = total - v_ref[:, cols] * o_ref[:, cols].astype(F32)
    width = mask_ref.shape[1]
    block = lax.broadcasted_iota(jnp.int32, mask_ref.shape, 1) // blk
    block = (block + (pl.program_id(0) * (group_rows // blk) - REACH)).astype(F32)
    lowest = turned(first_ref[...].astype(F32), width)
    inside = (block >= lowest) & (block < lowest + turned(many_ref[...].astype(F32), width))
    mask_ref[...] = jnp.where(inside, 1.0, 0.0).astype(BF16)


def local_part(response, low, high, orbitals, matrix, lines, bounds, group_rows, width, blk):
    bands, cells = response.shape
    depth = cells // (GY * GZ)
    outs = [struct((bands, cells), F32), struct((bands, width), BF16)]
    here = pl.BlockSpec((group_rows, cells), lambda i: (i, 0))
    side = pl.BlockSpec((group_rows, low.shape[1]), lambda i: (i, 0))
    line = pl.BlockSpec((1, cells), lambda i: (0, 0))
    band = pl.BlockSpec((1, group_rows), lambda i: (0, i))
    return pl.pallas_call(
        functools.partial(local_body, depth, (group_rows, blk)),
        grid=(bands // group_rows,),
        out_shape=outs,
        in_specs=[
            here,
            side,
            side,
            here,
            pl.BlockSpec(matrix.shape, lambda i: (0, 0, 0)),
            line,
            line,
            band,
            band,
            band,
        ],
        out_specs=[here, pl.BlockSpec((group_rows, width), lambda i: (i, 0))],
        compiler_params=params(),
        cost_estimate=cost(2 * bands * cells * 300, low, high, low, low, *outs),
    )(response, low, high, orbitals, matrix, *lines, *bounds)


def pad_body(edge, o_ref, pad_ref):
    bands, cells = o_ref.shape
    pad_ref[:edge, :] = jnp.zeros((edge, cells), pad_ref.dtype)
    pad_ref[edge : edge + bands, :] = o_ref[...]
    pad_ref[edge + bands :, :] = jnp.zeros((edge, cells), pad_ref.dtype)


def pad_orbitals(orbitals, blk):
    bands, cells = orbitals.shape
    edge = REACH * blk
    return local_call(
        functools.partial(pad_body, edge),
        struct((bands + 2 * edge, cells), orbitals.dtype),
        [orbitals],
    )


def subgroup(shape, blk):
    return lax.broadcasted_iota(jnp.int32, shape, 1) // (2 * blk)


def packed(sums, blk):
    rows = sums.shape[0]
    sub = 2 * blk
    near, far = sums[:, :rows], sums[:, rows:]
    column = subgroup((rows, rows), blk)
    row = lax.broadcasted_iota(jnp.int32, (rows, rows), 0) // sub
    main = jnp.where(column >= row, near, far)
    rest = far[:sub, :]
    for k in range(1, rows // sub):
        rest = jnp.where(column[:sub, :] == k, far[k * sub : (k + 1) * sub, :], rest)
    return main, rest


def unpacked(main, rest, blk):
    rows = main.shape[0]
    sub = 2 * blk
    column = subgroup((rows, rows), blk)
    row = lax.broadcasted_iota(jnp.int32, (rows, rows), 0) // sub
    near = jnp.where(column >= row, main, 0.0)
    last = jnp.where(column == row, jnp.concatenate([rest] * (rows // sub), axis=0), 0.0)
    return near, jnp.where(column < row, main, last)


def apply_body(core, across, block, group_rows, blk, other, *refs):
    size = across[0]
    blocks = refs[: size + 1]
    p_ref, base_ref, pad_ref, u_ref, s_ref, c_ref = refs[size + 1 :]
    rows, cells = u_ref.shape
    c, x = position(core), position(across)
    side = 1 - c if other else c
    first = blocks[0].shape[0]
    for step, ref in enumerate(blocks[:size]):
        at = (x ^ step) * block
        c_ref[pl.ds(pl.multiple_of(at, 16), first), :] = ref[...]
    rest = block - first
    for i in range(size):
        there = slice(i * block + first, (i + 1) * block)
        c_ref[there, :] = blocks[size][i * rest : (i + 1) * rest, :]
    mine = pl.ds(pl.multiple_of(side * rows, rows), rows)
    tile = 256 if cells % 256 == 0 else 128
    for t in range(cells // tile):
        cols = slice(t * tile, (t + 1) * tile)
        u_ref[:, cols] = base_ref[mine, cols] + jnp.dot(
            c_ref[...], p_ref[:, cols], preferred_element_type=F32
        )
    height = group_rows + 2 * blk
    for g in range(rows // group_rows):
        start = pl.multiple_of(side * rows + g * group_rows, group_rows)
        sums = lax.dot_general(
            u_ref[g * group_rows : (g + 1) * group_rows, :].astype(BF16),
            pad_ref[pl.ds(start, 2 * group_rows), :],
            NT,
            preferred_element_type=F32,
        )
        main, rest_sums = packed(sums, blk)
        s_ref[g * height : g * height + group_rows, :] = main.astype(s_ref.dtype)
        s_ref[g * height + group_rows : (g + 1) * height, :] = rest_sums.astype(s_ref.dtype)


def apply(blocks, projectors, base, padded, core, across, block, group_rows, blk, other):
    bands, cells = base.shape
    rows = bands // 2
    count = projectors.shape[0]
    height = rows // group_rows * (group_rows + 2 * blk)
    return local_call(
        functools.partial(apply_body, core, across, block, group_rows, blk, other),
        [struct((rows, cells), F32), struct((height, group_rows), BF16 if other else F32)],
        [*blocks, projectors, base, padded],
        flops=2 * rows * cells * (count + 2 * group_rows),
        scratch=[pltpu.VMEM((rows, count), BF16)],
    )


def sum_body(keep_ref, *refs):
    *taken, total_ref, low_ref = refs
    total = total_of(keep_ref, taken, ...)
    total_ref[...] = total
    low_ref[...] = total.astype(BF16)


def add_up(keep, taken):
    outs = [struct(keep.shape, F32), struct(keep.shape, BF16)]
    return local_call(sum_body, outs, [keep, *taken])


def project_body(core, blk, *refs):
    w_own, w_other, u_own, u_other, pad_ref, r_ref, mask_ref = refs[:7]
    updated_ref, residual_ref, w_ref, u_ref = refs[7:]
    rows = u_ref.shape[0]
    height = w_ref.shape[0]
    per = u_own.shape[0] // rows
    g = pl.program_id(0)
    own = lax.div(g, jnp.int32(per)) == position(core)
    local = lax.rem(g, jnp.int32(per))
    w_rows = pl.ds(pl.multiple_of(local * height, 16), height)
    u_rows = pl.ds(pl.multiple_of(local * rows, rows), rows)

    @pl.when(own)
    def _():
        w_ref[...] = w_own[w_rows, :]
        u_ref[...] = u_own[u_rows, :]

    @pl.when(jnp.logical_not(own))
    def _():
        w_ref[...] = w_other[w_rows, :]
        u_ref[...] = u_other[u_rows, :]

    main, rest = w_ref[:rows, :].astype(F32), w_ref[rows:, :].astype(F32)
    start = pl.multiple_of(g * rows, rows)
    residual = u_ref[...]
    for k, part in enumerate(unpacked(main, rest, blk)):
        inside = mask_ref[:, k * rows : (k + 1) * rows].astype(F32) > 0.5
        weights = jnp.where(inside, part, 0.0).astype(BF16)
        window = pad_ref[pl.ds(pl.multiple_of(start + k * rows, rows), rows), :]
        residual = residual - jnp.dot(weights, window, preferred_element_type=F32)
    residual_ref[...] = residual.astype(BF16)
    updated_ref[...] = (r_ref[...].astype(F32) + STEP_SIZE * residual).astype(BF16)


def project(weights, unprojected, padded, response, mask, core, group_rows, blk):
    bands, cells = response.shape
    out = struct((bands, cells), BF16)
    here = pl.BlockSpec((group_rows, cells), lambda g: (g, 0))

    def full(a):
        return pl.BlockSpec(a.shape, lambda g: (0, 0))

    return pl.pallas_call(
        functools.partial(project_body, core, blk),
        grid=(bands // group_rows,),
        out_shape=(out, out),
        in_specs=[
            *[full(a) for a in (*weights, *unprojected, padded)],
            here,
            pl.BlockSpec((group_rows, mask.shape[1]), lambda g: (g, 0)),
        ],
        out_specs=(here, here),
        scratch_shapes=[
            pltpu.VMEM((group_rows + 2 * blk, group_rows), BF16),
            pltpu.VMEM((group_rows, cells), F32),
        ],
        compiler_params=params(),
        cost_estimate=cost(
            4 * bands * group_rows * cells, padded, *unprojected, response, out, out
        ),
    )(*weights, *unprojected, padded, response, mask)


def shards(
    count, response, orbitals, projectors, potential, perturbing, energies, window_start, block_count
):
    bands, local_cells = response.shape
    cells = local_cells * count
    projections = projectors.shape[0]
    halo = 6 * GY * GZ
    core, across, along = levels_of(count)
    ace_scale = 1.0 / math.sqrt(cells * projections)
    window_scale = 1.0 / math.sqrt(cells * bands)
    blk = bands // NBLK
    group_rows = GROUP_BLOCKS * blk
    width = 2 * group_rows
    half = bands // 2
    block = half // across[0]
    first = max(16, round(REDUCE_SHARE * block / 16) * 16)
    gather_first = max(16, round(GATHER_SHARE * block / 16) * 16)
    matrix = jnp.asarray(plane_matrix())
    lines = (potential[None, :], perturbing[None, :])
    bounds = tuple(a[None, :] for a in (energies, window_start, block_count))

    def to(array, level):
        return [swapped(array, count, level, k) for k in range(1, level[0])]

    def parts_to(parts, level):
        return [swapped(part, count, level, k + 1) for k, part in enumerate(parts)]

    low = neighbour(response[:, local_cells - halo :], count, 1)

    sent_x, sent_z, keep_x, keep_z = first_sums(response, projectors, core, block, first)
    sent_z = swapped(sent_z, count, core, 1)
    sent_x = swapped(sent_x, count, core, 1)
    head, sent_z = lax.optimization_barrier((response[:, :halo], sent_z))
    high = neighbour(head, count, -1)
    keep_z, *parts_z = split(keep_z, [sent_z], along, 1)
    keep_x, *parts_x = split(keep_x, [sent_x], across, 0)
    parts_z[-1], low = lax.optimization_barrier((parts_z[-1], low))
    taken_z, taken_x, low, high = lax.optimization_barrier(
        (parts_to(parts_z, along), parts_to(parts_x, across), low, high)
    )
    keep_x, *parts_x = split(keep_x, taken_x, along, 1)
    keep_z, *parts_z = split(keep_z, taken_z, across, 0)
    taken_x, taken_z = lax.optimization_barrier(
        (parts_to(parts_x, along), parts_to(parts_z, across))
    )
    share_x, share_z = local_call(
        functools.partial(finish_both_body, ace_scale, len(taken_x)),
        [
            struct((gather_first, projections // along[0]), BF16),
            struct((block - gather_first, projections // along[0]), BF16),
        ],
        [keep_x, *taken_x, keep_z, *taken_z],
    )

    pieces_x, pieces_z, bounds = lax.optimization_barrier(
        ([share_x, *to(share_x, along)], [share_z, *to(share_z, across)], bounds)
    )
    base, mask = local_part(
        response, low, high, orbitals, matrix, lines, bounds, group_rows, width, blk
    )
    block_x = place(pieces_x, along, 1)
    block_z = place(pieces_z, across, 0)
    blocks_x = [block_x, *to(block_x, across)]
    pieces_z, base, padded = lax.optimization_barrier(
        ([block_z, *to(block_z, along)], base, pad_orbitals(orbitals, blk))
    )
    blocks = [*blocks_x, place(pieces_z, along, 1)]
    others = [swapped(part, count, core, 1) for part in blocks]
    sizes = (core, across, block, group_rows, blk)
    wide, keep = apply(blocks, projectors, base, padded, *sizes, False)
    others, keep = lax.optimization_barrier((others, keep))
    other_wide, part = apply(others, projectors, base, padded, *sizes, True)
    unprojected = (wide, other_wide)
    total, part = add_up(keep, to(part, core))
    total, part = add_up(total, to(part, across))
    own = finish(total, to(part, along), window_scale)
    weights = (own, *to(own, core))
    return project(weights, unprojected, padded, response, mask, core, group_rows, blk)


def solution(mesh):
    in_specs = (
        P("pert", "band"),
        P(None, "band"),
        P(None, "band"),
        P("band"),
        P(("pert", "band")),
        P(),
        P(),
        P(),
    )
    out_specs = (P("pert", "band"), P("pert", "band"))
    body = functools.partial(shards, mesh.shape["band"])
    return jax.shard_map(body, mesh=mesh, in_specs=in_specs, out_specs=out_specs, check_vma=False)
```

```python
import functools
import math

import jax
import jax.numpy as jnp
import ml_dtypes
import numpy as np
from jax import lax
from jax.experimental import pallas as pl
from jax.experimental.pallas import tpu as pltpu
from jax.sharding import PartitionSpec as P

GY = 8
GZ = 16
NBLK = 32
REACH = 4
GROUP_BLOCKS = 8
COEFFS = (
    -5369.0 / 1800.0,
    12.0 / 7.0,
    -15.0 / 56.0,
    10.0 / 189.0,
    -1.0 / 112.0,
    2.0 / 1925.0,
    -1.0 / 16632.0,
)
KINETIC = 0.125
STEP_SIZE = 0.3
MIB = 1024 * 1024
VMEM_BYTES = 24 * MIB
REDUCE_SHARE = 0.5
GATHER_SHARE = 0.5
BF16 = jnp.bfloat16
F32 = jnp.float32
NT = (((1,), (1,)), ((), ()))


def levels_of(count):
    chips = count // 2
    across = 2 ** (int(math.log2(chips)) // 3)
    return (2, 1), (across, 2), (chips // across, 2 * across)


def position(level):
    size, stride = level
    return lax.rem(lax.div(lax.axis_index("band"), jnp.int32(stride)), jnp.int32(size))


def neighbour(array, count, step):
    return lax.ppermute(array, "band", [(i, (i + step) % count) for i in range(count)])


def swapped(array, count, level, step):
    size, stride = level
    pairs = []
    for device in range(count):
        place = device // stride % size
        pairs.append((device, device + ((place ^ step) - place) * stride))
    return lax.ppermute(array, "band", pairs)


def plane_matrix():
    plane = GY * GZ
    matrix = 3.0 * COEFFS[0] * np.eye(plane)
    cells = np.arange(plane)
    y, z = cells // GZ, cells % GZ
    for offset in range(1, 7):
        for sign in (1, -1):
            np.add.at(matrix, ((y + sign * offset) % GY * GZ + z, cells), COEFFS[offset])
            np.add.at(matrix, (y * GZ + (z + sign * offset) % GZ, cells), COEFFS[offset])
    matrix = KINETIC * matrix
    high = matrix.astype(ml_dtypes.bfloat16)
    low = (matrix - high.astype(np.float64)).astype(ml_dtypes.bfloat16)
    return np.stack([high, low])


def whole():
    return pl.BlockSpec(memory_space=pltpu.VMEM)


def params(size=VMEM_BYTES):
    return pltpu.CompilerParams(vmem_limit_bytes=size)


def cost(flops, *arrays):
    moved = sum(math.prod(a.shape) * jnp.dtype(a.dtype).itemsize for a in arrays)
    return pl.CostEstimate(flops=int(flops), bytes_accessed=int(moved), transcendentals=0)


def local_call(body, outs, args, flops=0, scratch=()):
    return pl.pallas_call(
        body,
        out_shape=outs,
        in_specs=[whole() for _ in args],
        out_specs=jax.tree.map(lambda _: whole(), outs),
        scratch_shapes=scratch,
        compiler_params=params(),
        cost_estimate=cost(flops, *args, *jax.tree.leaves(outs)),
    )(*args)


def struct(shape, dtype):
    return jax.ShapeDtypeStruct(shape, dtype)


def cut(part, block, x_ref, z_ref, cols):
    size = part.shape[0] // block
    first, rest = x_ref.shape[0] // size, z_ref.shape[0] // size
    part = part.astype(x_ref.dtype)
    for i in range(size):
        x_ref[i * first : (i + 1) * first, cols] = part[i * block : i * block + first, :]
        z_ref[i * rest : (i + 1) * rest, cols] = part[i * block + first : (i + 1) * block, :]


def first_body(core, block, tile, r_ref, p_ref, *refs):
    sent_x, sent_z, keep_x, keep_z, r_held, p_held, r_sem, p_sem = refs
    rows = r_held.shape[0] // 2
    r_copy = pltpu.make_async_copy(r_ref, r_held, r_sem)
    r_copy.start()
    copies = []
    for t in range(p_held.shape[0] // tile):
        part = pl.ds(t * tile, tile)
        copies.append(pltpu.make_async_copy(p_ref.at[part, :], p_held.at[part, :], p_sem.at[t]))
        copies[-1].start()
    c = position(core)
    r_copy.wait()
    for t, copy in enumerate(copies):
        copy.wait()
        cols = slice(t * tile, (t + 1) * tile)
        for side, x_ref, z_ref in ((1 - c, sent_x, sent_z), (c, keep_x, keep_z)):
            part = lax.dot_general(
                r_held[pl.ds(pl.multiple_of(side * rows, rows), rows), :],
                p_held[cols, :],
                NT,
                preferred_element_type=F32,
            )
            cut(part, block, x_ref, z_ref, cols)


def first_sums(response, projectors, core, block, first):
    bands, cells = response.shape
    count = projectors.shape[0]
    rows = bands // 2
    tile = min(512, count)
    rows_x = rows // block * first
    outs = [struct((n, count), t) for t in (BF16, F32) for n in (rows_x, rows - rows_x)]
    return pl.pallas_call(
        functools.partial(first_body, core, block, tile),
        out_shape=outs,
        in_specs=[pl.BlockSpec(memory_space=pltpu.HBM)] * 2,
        out_specs=[whole() for _ in outs],
        scratch_shapes=[
            pltpu.VMEM((bands, cells), response.dtype),
            pltpu.VMEM((count, cells), projectors.dtype),
            pltpu.SemaphoreType.DMA,
            pltpu.SemaphoreType.DMA((count // tile,)),
        ],
        compiler_params=params(),
        cost_estimate=cost(2 * bands * cells * count, projectors, *outs),
    )(
        pltpu.with_memory_space_constraint(response, pltpu.HBM),
        pltpu.with_memory_space_constraint(projectors, pltpu.HBM),
    )


def rows_at(place, size):
    return pl.ds(pl.multiple_of(place * size, 16), size)


def cols_at(place, size):
    return pl.ds(pl.multiple_of(place * size, size), size)


def total_of(keep_ref, taken, part):
    total = keep_ref[part]
    for ref in taken:
        total = total + ref[part].astype(F32)
    return total


def split_body(received, level, along, *refs):
    keep_ref, taken, outs = refs[0], refs[1 : 1 + received], refs[1 + received :]
    me = position(level)
    rows, width = outs[0].shape
    for step, out in enumerate(outs):
        at = me ^ step
        if along == 0:
            part = (rows_at(at, rows), slice(None))
        else:
            part = (slice(None), cols_at(at, width))
        out[...] = total_of(keep_ref, taken, part).astype(out.dtype)


def shares_of(shape, count):
    return [struct(shape, F32)] + [struct(shape, BF16)] * (count - 1)


def split(keep, taken, level, along):
    shape = list(keep.shape)
    shape[along] //= level[0]
    return local_call(
        functools.partial(split_body, len(taken), level, along),
        shares_of(shape, level[0]),
        [keep, *taken],
    )


def finish_body(scale, keep_ref, *refs):
    *taken, out_ref = refs
    out_ref[...] = (total_of(keep_ref, taken, ...) * scale).astype(out_ref.dtype)


def finish(keep, taken, scale):
    return local_call(
        functools.partial(finish_body, scale), struct(keep.shape, BF16), [keep, *taken]
    )


def finish_both_body(scale, received, *refs):
    outs = refs[-2:]
    cut = outs[0].shape[0]
    row = 0
    for keep_ref, *taken in (refs[: 1 + received], refs[1 + received : -2]):
        low = (total_of(keep_ref, taken, ...) * scale).astype(BF16)
        end = row + keep_ref.shape[0]
        for out, first, last in ((outs[0], 0, cut), (outs[1], cut, cut + outs[1].shape[0])):
            top, bottom = max(row, first), min(end, last)
            if top < bottom:
                out[top - first : bottom - first, :] = low[top - row : bottom - row, :]
        row = end


def place_body(level, along, *refs):
    *parts, out_ref = refs
    me = position(level)
    width = parts[0].shape[along]
    for step, ref in enumerate(parts):
        at = pl.multiple_of((me ^ step) * width, width)
        if along == 0:
            out_ref[pl.ds(at, width), :] = ref[...]
        else:
            out_ref[:, pl.ds(at, width)] = ref[...]


def place(parts, level, along):
    shape = list(parts[0].shape)
    shape[along] *= level[0]
    return local_call(functools.partial(place_body, level, along), struct(shape, BF16), parts)


def turned(row, width):
    return jnp.transpose(jnp.broadcast_to(row, (width, row.shape[1])))


def local_body(depth, sizes, *refs):
    r_ref, l_ref, h_ref, o_ref, m_ref, pot_ref, v_ref, e_ref = refs[:8]
    first_ref, many_ref, out_ref, mask_ref = refs[8:]
    plane = GY * GZ
    reach = 6

    def plane_at(j):
        if j < 0:
            ref, k = l_ref, j + reach
        elif j < depth:
            ref, k = r_ref, j
        else:
            ref, k = h_ref, j - depth
        return ref[:, k * plane : (k + 1) * plane]

    group_rows, blk = sizes
    energy = turned(e_ref[...], plane)
    for j in range(depth):
        cols = slice(j * plane, (j + 1) * plane)
        low = plane_at(j)
        total = jnp.dot(low, m_ref[0], preferred_element_type=F32)
        total = total + jnp.dot(low, m_ref[1], preferred_element_type=F32)
        for offset in range(1, 7):
            pair = plane_at(j + offset).astype(F32) + plane_at(j - offset).astype(F32)
            total = total + (KINETIC * COEFFS[offset]) * pair
        total = total + (energy - pot_ref[:, cols]) * low.astype(F32)
        out_ref[:, cols] = total - v_ref[:, cols] * o_ref[:, cols].astype(F32)
    width = mask_ref.shape[1]
    block = lax.broadcasted_iota(jnp.int32, mask_ref.shape, 1) // blk
    block = (block + (pl.program_id(0) * (group_rows // blk) - REACH)).astype(F32)
    lowest = turned(first_ref[...].astype(F32), width)
    inside = (block >= lowest) & (block < lowest + turned(many_ref[...].astype(F32), width))
    mask_ref[...] = jnp.where(inside, 1.0, 0.0).astype(BF16)


def local_part(response, low, high, orbitals, matrix, lines, bounds, group_rows, width, blk):
    bands, cells = response.shape
    depth = cells // (GY * GZ)
    outs = [struct((bands, cells), F32), struct((bands, width), BF16)]
    here = pl.BlockSpec((group_rows, cells), lambda i: (i, 0))
    side = pl.BlockSpec((group_rows, low.shape[1]), lambda i: (i, 0))
    line = pl.BlockSpec((1, cells), lambda i: (0, 0))
    band = pl.BlockSpec((1, group_rows), lambda i: (0, i))
    return pl.pallas_call(
        functools.partial(local_body, depth, (group_rows, blk)),
        grid=(bands // group_rows,),
        out_shape=outs,
        in_specs=[
            here,
            side,
            side,
            here,
            pl.BlockSpec(matrix.shape, lambda i: (0, 0, 0)),
            line,
            line,
            band,
            band,
            band,
        ],
        out_specs=[here, pl.BlockSpec((group_rows, width), lambda i: (i, 0))],
        compiler_params=params(),
        cost_estimate=cost(2 * bands * cells * 300, low, high, low, low, *outs),
    )(response, low, high, orbitals, matrix, *lines, *bounds)


def pad_body(edge, o_ref, pad_ref):
    bands, cells = o_ref.shape
    pad_ref[:edge, :] = jnp.zeros((edge, cells), pad_ref.dtype)
    pad_ref[edge : edge + bands, :] = o_ref[...]
    pad_ref[edge + bands :, :] = jnp.zeros((edge, cells), pad_ref.dtype)


def pad_orbitals(orbitals, blk):
    bands, cells = orbitals.shape
    edge = REACH * blk
    return local_call(
        functools.partial(pad_body, edge),
        struct((bands + 2 * edge, cells), orbitals.dtype),
        [orbitals],
    )


def subgroup(shape, blk):
    return lax.broadcasted_iota(jnp.int32, shape, 1) // (2 * blk)


def packed(sums, blk):
    rows = sums.shape[0]
    sub = 2 * blk
    near, far = sums[:, :rows], sums[:, rows:]
    column = subgroup((rows, rows), blk)
    row = lax.broadcasted_iota(jnp.int32, (rows, rows), 0) // sub
    main = jnp.where(column >= row, near, far)
    rest = far[:sub, :]
    for k in range(1, rows // sub):
        rest = jnp.where(column[:sub, :] == k, far[k * sub : (k + 1) * sub, :], rest)
    return main, rest


def unpacked(main, rest, blk):
    rows = main.shape[0]
    sub = 2 * blk
    column = subgroup((rows, rows), blk)
    row = lax.broadcasted_iota(jnp.int32, (rows, rows), 0) // sub
    near = jnp.where(column >= row, main, 0.0)
    last = jnp.where(column == row, jnp.concatenate([rest] * (rows // sub), axis=0), 0.0)
    return near, jnp.where(column < row, main, last)


def apply_body(core, across, block, group_rows, blk, other, *refs):
    size = across[0]
    blocks = refs[: size + 1]
    p_ref, base_ref, pad_ref, u_ref, s_ref, c_ref = refs[size + 1 :]
    rows, cells = u_ref.shape
    c, x = position(core), position(across)
    side = 1 - c if other else c
    first = blocks[0].shape[0]
    for step, ref in enumerate(blocks[:size]):
        at = (x ^ step) * block
        c_ref[pl.ds(pl.multiple_of(at, 16), first), :] = ref[...]
    rest = block - first
    for i in range(size):
        there = slice(i * block + first, (i + 1) * block)
        c_ref[there, :] = blocks[size][i * rest : (i + 1) * rest, :]
    mine = pl.ds(pl.multiple_of(side * rows, rows), rows)
    tile = 256 if cells % 256 == 0 else 128
    for t in range(cells // tile):
        cols = slice(t * tile, (t + 1) * tile)
        u_ref[:, cols] = base_ref[mine, cols] + jnp.dot(
            c_ref[...], p_ref[:, cols], preferred_element_type=F32
        )
    height = group_rows + 2 * blk
    for g in range(rows // group_rows):
        start = pl.multiple_of(side * rows + g * group_rows, group_rows)
        sums = lax.dot_general(
            u_ref[g * group_rows : (g + 1) * group_rows, :].astype(BF16),
            pad_ref[pl.ds(start, 2 * group_rows), :],
            NT,
            preferred_element_type=F32,
        )
        main, rest_sums = packed(sums, blk)
        s_ref[g * height : g * height + group_rows, :] = main.astype(s_ref.dtype)
        s_ref[g * height + group_rows : (g + 1) * height, :] = rest_sums.astype(s_ref.dtype)


def apply(blocks, projectors, base, padded, core, across, block, group_rows, blk, other):
    bands, cells = base.shape
    rows = bands // 2
    count = projectors.shape[0]
    height = rows // group_rows * (group_rows + 2 * blk)
    return local_call(
        functools.partial(apply_body, core, across, block, group_rows, blk, other),
        [struct((rows, cells), F32), struct((height, group_rows), BF16 if other else F32)],
        [*blocks, projectors, base, padded],
        flops=2 * rows * cells * (count + 2 * group_rows),
        scratch=[pltpu.VMEM((rows, count), BF16)],
    )


def sum_body(keep_ref, *refs):
    *taken, total_ref, low_ref = refs
    total = total_of(keep_ref, taken, ...)
    total_ref[...] = total
    low_ref[...] = total.astype(BF16)


def add_up(keep, taken):
    outs = [struct(keep.shape, F32), struct(keep.shape, BF16)]
    return local_call(sum_body, outs, [keep, *taken])


def project_body(core, blk, *refs):
    w_own, w_other, u_own, u_other, pad_ref, r_ref, mask_ref = refs[:7]
    updated_ref, residual_ref, w_ref, u_ref = refs[7:]
    rows = u_ref.shape[0]
    height = w_ref.shape[0]
    per = u_own.shape[0] // rows
    g = pl.program_id(0)
    own = lax.div(g, jnp.int32(per)) == position(core)
    local = lax.rem(g, jnp.int32(per))
    w_rows = pl.ds(pl.multiple_of(local * height, 16), height)
    u_rows = pl.ds(pl.multiple_of(local * rows, rows), rows)

    @pl.when(own)
    def _():
        w_ref[...] = w_own[w_rows, :]
        u_ref[...] = u_own[u_rows, :]

    @pl.when(jnp.logical_not(own))
    def _():
        w_ref[...] = w_other[w_rows, :]
        u_ref[...] = u_other[u_rows, :]

    main, rest = w_ref[:rows, :].astype(F32), w_ref[rows:, :].astype(F32)
    start = pl.multiple_of(g * rows, rows)
    residual = u_ref[...]
    for k, part in enumerate(unpacked(main, rest, blk)):
        inside = mask_ref[:, k * rows : (k + 1) * rows].astype(F32) > 0.5
        weights = jnp.where(inside, part, 0.0).astype(BF16)
        window = pad_ref[pl.ds(pl.multiple_of(start + k * rows, rows), rows), :]
        residual = residual - jnp.dot(weights, window, preferred_element_type=F32)
    residual_ref[...] = residual.astype(BF16)
    updated_ref[...] = (r_ref[...].astype(F32) + STEP_SIZE * residual).astype(BF16)


def project(weights, unprojected, padded, response, mask, core, group_rows, blk):
    bands, cells = response.shape
    out = struct((bands, cells), BF16)
    here = pl.BlockSpec((group_rows, cells), lambda g: (g, 0))

    def full(a):
        return pl.BlockSpec(a.shape, lambda g: (0, 0))

    return pl.pallas_call(
        functools.partial(project_body, core, blk),
        grid=(bands // group_rows,),
        out_shape=(out, out),
        in_specs=[
            *[full(a) for a in (*weights, *unprojected, padded)],
            here,
            pl.BlockSpec((group_rows, mask.shape[1]), lambda g: (g, 0)),
        ],
        out_specs=(here, here),
        scratch_shapes=[
            pltpu.VMEM((group_rows + 2 * blk, group_rows), BF16),
            pltpu.VMEM((group_rows, cells), F32),
        ],
        compiler_params=params(),
        cost_estimate=cost(
            4 * bands * group_rows * cells, padded, *unprojected, response, out, out
        ),
    )(*weights, *unprojected, padded, response, mask)


def shards(
    count, response, orbitals, projectors, potential, perturbing, energies, window_start, block_count
):
    bands, local_cells = response.shape
    cells = local_cells * count
    projections = projectors.shape[0]
    halo = 6 * GY * GZ
    core, across, along = levels_of(count)
    ace_scale = 1.0 / math.sqrt(cells * projections)
    window_scale = 1.0 / math.sqrt(cells * bands)
    blk = bands // NBLK
    group_rows = GROUP_BLOCKS * blk
    width = 2 * group_rows
    half = bands // 2
    block = half // across[0]
    first = max(16, round(REDUCE_SHARE * block / 16) * 16)
    gather_first = max(16, round(GATHER_SHARE * block / 16) * 16)
    matrix = jnp.asarray(plane_matrix())
    lines = (potential[None, :], perturbing[None, :])
    bounds = tuple(a[None, :] for a in (energies, window_start, block_count))

    def to(array, level):
        return [swapped(array, count, level, k) for k in range(1, level[0])]

    def parts_to(parts, level):
        return [swapped(part, count, level, k + 1) for k, part in enumerate(parts)]

    low = neighbour(response[:, local_cells - halo :], count, 1)
    high = neighbour(response[:, :halo], count, -1)

    sent_x, sent_z, keep_x, keep_z = first_sums(response, projectors, core, block, first)
    sent_z = swapped(sent_z, count, core, 1)
    sent_x = swapped(sent_x, count, core, 1)
    keep_z, *parts_z = split(keep_z, [sent_z], along, 1)
    sent_x, parts_z[0] = lax.optimization_barrier((sent_x, parts_z[0]))
    keep_x, *parts_x = split(keep_x, [sent_x], across, 0)
    parts_z[-1], low = lax.optimization_barrier((parts_z[-1], low))
    taken_z, taken_x, low, high = lax.optimization_barrier(
        (parts_to(parts_z, along), parts_to(parts_x, across), low, high)
    )
    keep_x, *parts_x = split(keep_x, taken_x, along, 1)
    keep_z, *parts_z = split(keep_z, taken_z, across, 0)
    taken_x, taken_z = lax.optimization_barrier(
        (parts_to(parts_x, along), parts_to(parts_z, across))
    )
    share_x, share_z = local_call(
        functools.partial(finish_both_body, ace_scale, len(taken_x)),
        [
            struct((gather_first, projections // along[0]), BF16),
            struct((block - gather_first, projections // along[0]), BF16),
        ],
        [keep_x, *taken_x, keep_z, *taken_z],
    )

    pieces_x, pieces_z, bounds = lax.optimization_barrier(
        ([share_x, *to(share_x, along)], [share_z, *to(share_z, across)], bounds)
    )
    base, mask = local_part(
        response, low, high, orbitals, matrix, lines, bounds, group_rows, width, blk
    )
    block_x = place(pieces_x, along, 1)
    block_z = place(pieces_z, across, 0)
    blocks_x = [block_x, *to(block_x, across)]
    pieces_z, base, padded = lax.optimization_barrier(
        ([block_z, *to(block_z, along)], base, pad_orbitals(orbitals, blk))
    )
    blocks = [*blocks_x, place(pieces_z, along, 1)]
    others = [swapped(part, count, core, 1) for part in blocks]
    sizes = (core, across, block, group_rows, blk)
    wide, keep = apply(blocks, projectors, base, padded, *sizes, False)
    others, keep = lax.optimization_barrier((others, keep))
    other_wide, part = apply(others, projectors, base, padded, *sizes, True)
    unprojected = (wide, other_wide)
    total, part = add_up(keep, to(part, core))
    total, part = add_up(total, to(part, across))
    own = finish(total, to(part, along), window_scale)
    weights = (own, *to(own, core))
    return project(weights, unprojected, padded, response, mask, core, group_rows, blk)


def solution(mesh):
    in_specs = (
        P("pert", "band"),
        P(None, "band"),
        P(None, "band"),
        P("band"),
        P(("pert", "band")),
        P(),
        P(),
        P(),
    )
    out_specs = (P("pert", "band"), P("pert", "band"))
    body = functools.partial(shards, mesh.shape["band"])
    return jax.shard_map(body, mesh=mesh, in_specs=in_specs, out_specs=out_specs, check_vma=False)
```

```python
import functools
import math

import jax
import jax.numpy as jnp
import ml_dtypes
import numpy as np
from jax import lax
from jax.experimental import pallas as pl
from jax.experimental.pallas import tpu as pltpu
from jax.sharding import PartitionSpec as P

GY = 8
GZ = 16
NBLK = 32
REACH = 4
GROUP_BLOCKS = 8
COEFFS = (
    -5369.0 / 1800.0,
    12.0 / 7.0,
    -15.0 / 56.0,
    10.0 / 189.0,
    -1.0 / 112.0,
    2.0 / 1925.0,
    -1.0 / 16632.0,
)
KINETIC = 0.125
STEP_SIZE = 0.3
MIB = 1024 * 1024
VMEM_BYTES = 24 * MIB
REDUCE_SHARE = 0.5
GATHER_SHARE = 0.5
BF16 = jnp.bfloat16
F32 = jnp.float32
NT = (((1,), (1,)), ((), ()))


def levels_of(count):
    chips = count // 2
    across = 2 ** (int(math.log2(chips)) // 3)
    return (2, 1), (across, 2), (chips // across, 2 * across)


def position(level):
    size, stride = level
    return lax.rem(lax.div(lax.axis_index("band"), jnp.int32(stride)), jnp.int32(size))


def neighbour(array, count, step):
    return lax.ppermute(array, "band", [(i, (i + step) % count) for i in range(count)])


def swapped(array, count, level, step):
    size, stride = level
    pairs = []
    for device in range(count):
        place = device // stride % size
        pairs.append((device, device + ((place ^ step) - place) * stride))
    return lax.ppermute(array, "band", pairs)


def plane_matrix():
    plane = GY * GZ
    matrix = 3.0 * COEFFS[0] * np.eye(plane)
    cells = np.arange(plane)
    y, z = cells // GZ, cells % GZ
    for offset in range(1, 7):
        for sign in (1, -1):
            np.add.at(matrix, ((y + sign * offset) % GY * GZ + z, cells), COEFFS[offset])
            np.add.at(matrix, (y * GZ + (z + sign * offset) % GZ, cells), COEFFS[offset])
    matrix = KINETIC * matrix
    high = matrix.astype(ml_dtypes.bfloat16)
    low = (matrix - high.astype(np.float64)).astype(ml_dtypes.bfloat16)
    return np.stack([high, low])


def whole():
    return pl.BlockSpec(memory_space=pltpu.VMEM)


def params(size=VMEM_BYTES):
    return pltpu.CompilerParams(vmem_limit_bytes=size)


def cost(flops, *arrays):
    moved = sum(math.prod(a.shape) * jnp.dtype(a.dtype).itemsize for a in arrays)
    return pl.CostEstimate(flops=int(flops), bytes_accessed=int(moved), transcendentals=0)


def local_call(body, outs, args, flops=0, scratch=()):
    return pl.pallas_call(
        body,
        out_shape=outs,
        in_specs=[whole() for _ in args],
        out_specs=jax.tree.map(lambda _: whole(), outs),
        scratch_shapes=scratch,
        compiler_params=params(),
        cost_estimate=cost(flops, *args, *jax.tree.leaves(outs)),
    )(*args)


def struct(shape, dtype):
    return jax.ShapeDtypeStruct(shape, dtype)


def cut(part, block, x_ref, z_ref, cols):
    size = part.shape[0] // block
    first, rest = x_ref.shape[0] // size, z_ref.shape[0] // size
    part = part.astype(x_ref.dtype)
    for i in range(size):
        x_ref[i * first : (i + 1) * first, cols] = part[i * block : i * block + first, :]
        z_ref[i * rest : (i + 1) * rest, cols] = part[i * block + first : (i + 1) * block, :]


def first_body(core, block, tile, r_ref, p_ref, *refs):
    sent_x, sent_z, keep_x, keep_z, r_held, p_held, r_sem, p_sem = refs
    rows = r_held.shape[0] // 2
    r_copy = pltpu.make_async_copy(r_ref, r_held, r_sem)
    r_copy.start()
    copies = []
    for t in range(p_held.shape[0] // tile):
        part = pl.ds(t * tile, tile)
        copies.append(pltpu.make_async_copy(p_ref.at[part, :], p_held.at[part, :], p_sem.at[t]))
        copies[-1].start()
    c = position(core)
    r_copy.wait()
    for t, copy in enumerate(copies):
        copy.wait()
        cols = slice(t * tile, (t + 1) * tile)
        for side, x_ref, z_ref in ((1 - c, sent_x, sent_z), (c, keep_x, keep_z)):
            part = lax.dot_general(
                r_held[pl.ds(pl.multiple_of(side * rows, rows), rows), :],
                p_held[cols, :],
                NT,
                preferred_element_type=F32,
            )
            cut(part, block, x_ref, z_ref, cols)


def first_sums(response, projectors, core, block, first):
    bands, cells = response.shape
    count = projectors.shape[0]
    rows = bands // 2
    tile = min(512, count)
    rows_x = rows // block * first
    outs = [struct((n, count), t) for t in (BF16, F32) for n in (rows_x, rows - rows_x)]
    return pl.pallas_call(
        functools.partial(first_body, core, block, tile),
        out_shape=outs,
        in_specs=[pl.BlockSpec(memory_space=pltpu.HBM)] * 2,
        out_specs=[whole() for _ in outs],
        scratch_shapes=[
            pltpu.VMEM((bands, cells), response.dtype),
            pltpu.VMEM((count, cells), projectors.dtype),
            pltpu.SemaphoreType.DMA,
            pltpu.SemaphoreType.DMA((count // tile,)),
        ],
        compiler_params=params(),
        cost_estimate=cost(2 * bands * cells * count, projectors, *outs),
    )(
        pltpu.with_memory_space_constraint(response, pltpu.HBM),
        pltpu.with_memory_space_constraint(projectors, pltpu.HBM),
    )


def rows_at(place, size):
    return pl.ds(pl.multiple_of(place * size, 16), size)


def cols_at(place, size):
    return pl.ds(pl.multiple_of(place * size, size), size)


def total_of(keep_ref, taken, part):
    total = keep_ref[part]
    for ref in taken:
        total = total + ref[part].astype(F32)
    return total


def split_body(received, level, along, *refs):
    keep_ref, taken, outs = refs[0], refs[1 : 1 + received], refs[1 + received :]
    me = position(level)
    rows, width = outs[0].shape
    for step, out in enumerate(outs):
        at = me ^ step
        if along == 0:
            part = (rows_at(at, rows), slice(None))
        else:
            part = (slice(None), cols_at(at, width))
        out[...] = total_of(keep_ref, taken, part).astype(out.dtype)


def shares_of(shape, count):
    return [struct(shape, F32)] + [struct(shape, BF16)] * (count - 1)


def split(keep, taken, level, along):
    shape = list(keep.shape)
    shape[along] //= level[0]
    return local_call(
        functools.partial(split_body, len(taken), level, along),
        shares_of(shape, level[0]),
        [keep, *taken],
    )


def finish_body(scale, keep_ref, *refs):
    *taken, out_ref = refs
    out_ref[...] = (total_of(keep_ref, taken, ...) * scale).astype(out_ref.dtype)


def finish(keep, taken, scale):
    return local_call(
        functools.partial(finish_body, scale), struct(keep.shape, BF16), [keep, *taken]
    )


def finish_both_body(scale, received, *refs):
    outs = refs[-2:]
    cut = outs[0].shape[0]
    row = 0
    for keep_ref, *taken in (refs[: 1 + received], refs[1 + received : -2]):
        low = (total_of(keep_ref, taken, ...) * scale).astype(BF16)
        end = row + keep_ref.shape[0]
        for out, first, last in ((outs[0], 0, cut), (outs[1], cut, cut + outs[1].shape[0])):
            top, bottom = max(row, first), min(end, last)
            if top < bottom:
                out[top - first : bottom - first, :] = low[top - row : bottom - row, :]
        row = end


def place_body(level, along, *refs):
    *parts, out_ref = refs
    me = position(level)
    width = parts[0].shape[along]
    for step, ref in enumerate(parts):
        at = pl.multiple_of((me ^ step) * width, width)
        if along == 0:
            out_ref[pl.ds(at, width), :] = ref[...]
        else:
            out_ref[:, pl.ds(at, width)] = ref[...]


def place(parts, level, along):
    shape = list(parts[0].shape)
    shape[along] *= level[0]
    return local_call(functools.partial(place_body, level, along), struct(shape, BF16), parts)


def turned(row, width):
    return jnp.transpose(jnp.broadcast_to(row, (width, row.shape[1])))


def local_body(depth, sizes, *refs):
    r_ref, l_ref, h_ref, o_ref, m_ref, pot_ref, v_ref, e_ref = refs[:8]
    first_ref, many_ref, out_ref, mask_ref = refs[8:]
    plane = GY * GZ
    reach = 6

    def plane_at(j):
        if j < 0:
            ref, k = l_ref, j + reach
        elif j < depth:
            ref, k = r_ref, j
        else:
            ref, k = h_ref, j - depth
        return ref[:, k * plane : (k + 1) * plane]

    group_rows, blk = sizes
    energy = turned(e_ref[...], plane)
    for j in range(depth):
        cols = slice(j * plane, (j + 1) * plane)
        low = plane_at(j)
        total = jnp.dot(low, m_ref[0], preferred_element_type=F32)
        total = total + jnp.dot(low, m_ref[1], preferred_element_type=F32)
        for offset in range(1, 7):
            pair = plane_at(j + offset).astype(F32) + plane_at(j - offset).astype(F32)
            total = total + (KINETIC * COEFFS[offset]) * pair
        total = total + (energy - pot_ref[:, cols]) * low.astype(F32)
        out_ref[:, cols] = total - v_ref[:, cols] * o_ref[:, cols].astype(F32)
    width = mask_ref.shape[1]
    block = lax.broadcasted_iota(jnp.int32, mask_ref.shape, 1) // blk
    block = (block + (pl.program_id(0) * (group_rows // blk) - REACH)).astype(F32)
    lowest = turned(first_ref[...].astype(F32), width)
    inside = (block >= lowest) & (block < lowest + turned(many_ref[...].astype(F32), width))
    mask_ref[...] = jnp.where(inside, 1.0, 0.0).astype(BF16)


def local_part(response, low, high, orbitals, matrix, lines, bounds, group_rows, width, blk):
    bands, cells = response.shape
    depth = cells // (GY * GZ)
    outs = [struct((bands, cells), F32), struct((bands, width), BF16)]
    here = pl.BlockSpec((group_rows, cells), lambda i: (i, 0))
    side = pl.BlockSpec((group_rows, low.shape[1]), lambda i: (i, 0))
    line = pl.BlockSpec((1, cells), lambda i: (0, 0))
    band = pl.BlockSpec((1, group_rows), lambda i: (0, i))
    return pl.pallas_call(
        functools.partial(local_body, depth, (group_rows, blk)),
        grid=(bands // group_rows,),
        out_shape=outs,
        in_specs=[
            here,
            side,
            side,
            here,
            pl.BlockSpec(matrix.shape, lambda i: (0, 0, 0)),
            line,
            line,
            band,
            band,
            band,
        ],
        out_specs=[here, pl.BlockSpec((group_rows, width), lambda i: (i, 0))],
        compiler_params=params(),
        cost_estimate=cost(2 * bands * cells * 300, low, high, low, low, *outs),
    )(response, low, high, orbitals, matrix, *lines, *bounds)


def pad_body(edge, o_ref, pad_ref):
    bands, cells = o_ref.shape
    pad_ref[:edge, :] = jnp.zeros((edge, cells), pad_ref.dtype)
    pad_ref[edge : edge + bands, :] = o_ref[...]
    pad_ref[edge + bands :, :] = jnp.zeros((edge, cells), pad_ref.dtype)


def pad_orbitals(orbitals, blk):
    bands, cells = orbitals.shape
    edge = REACH * blk
    return local_call(
        functools.partial(pad_body, edge),
        struct((bands + 2 * edge, cells), orbitals.dtype),
        [orbitals],
    )


def subgroup(shape, blk):
    return lax.broadcasted_iota(jnp.int32, shape, 1) // (2 * blk)


def packed(sums, blk):
    rows = sums.shape[0]
    sub = 2 * blk
    near, far = sums[:, :rows], sums[:, rows:]
    column = subgroup((rows, rows), blk)
    row = lax.broadcasted_iota(jnp.int32, (rows, rows), 0) // sub
    main = jnp.where(column >= row, near, far)
    rest = far[:sub, :]
    for k in range(1, rows // sub):
        rest = jnp.where(column[:sub, :] == k, far[k * sub : (k + 1) * sub, :], rest)
    return main, rest


def unpacked(main, rest, blk):
    rows = main.shape[0]
    sub = 2 * blk
    column = subgroup((rows, rows), blk)
    row = lax.broadcasted_iota(jnp.int32, (rows, rows), 0) // sub
    near = jnp.where(column >= row, main, 0.0)
    last = jnp.where(column == row, jnp.concatenate([rest] * (rows // sub), axis=0), 0.0)
    return near, jnp.where(column < row, main, last)


def apply_body(core, across, block, group_rows, blk, other, *refs):
    size = across[0]
    blocks = refs[: size + 1]
    p_ref, base_ref, pad_ref, u_ref, s_ref, c_ref = refs[size + 1 :]
    rows, cells = u_ref.shape
    c, x = position(core), position(across)
    side = 1 - c if other else c
    first = blocks[0].shape[0]
    for step, ref in enumerate(blocks[:size]):
        at = (x ^ step) * block
        c_ref[pl.ds(pl.multiple_of(at, 16), first), :] = ref[...]
    rest = block - first
    for i in range(size):
        there = slice(i * block + first, (i + 1) * block)
        c_ref[there, :] = blocks[size][i * rest : (i + 1) * rest, :]
    mine = pl.ds(pl.multiple_of(side * rows, rows), rows)
    tile = 256 if cells % 256 == 0 else 128
    for t in range(cells // tile):
        cols = slice(t * tile, (t + 1) * tile)
        u_ref[:, cols] = base_ref[mine, cols] + jnp.dot(
            c_ref[...], p_ref[:, cols], preferred_element_type=F32
        )
    height = group_rows + 2 * blk
    for g in range(rows // group_rows):
        start = pl.multiple_of(side * rows + g * group_rows, group_rows)
        sums = lax.dot_general(
            u_ref[g * group_rows : (g + 1) * group_rows, :].astype(BF16),
            pad_ref[pl.ds(start, 2 * group_rows), :],
            NT,
            preferred_element_type=F32,
        )
        main, rest_sums = packed(sums, blk)
        s_ref[g * height : g * height + group_rows, :] = main.astype(s_ref.dtype)
        s_ref[g * height + group_rows : (g + 1) * height, :] = rest_sums.astype(s_ref.dtype)


def apply(blocks, projectors, base, padded, core, across, block, group_rows, blk, other):
    bands, cells = base.shape
    rows = bands // 2
    count = projectors.shape[0]
    height = rows // group_rows * (group_rows + 2 * blk)
    return local_call(
        functools.partial(apply_body, core, across, block, group_rows, blk, other),
        [struct((rows, cells), F32), struct((height, group_rows), BF16 if other else F32)],
        [*blocks, projectors, base, padded],
        flops=2 * rows * cells * (count + 2 * group_rows),
        scratch=[pltpu.VMEM((rows, count), BF16)],
    )


def sum_body(keep_ref, *refs):
    *taken, total_ref, low_ref = refs
    total = total_of(keep_ref, taken, ...)
    total_ref[...] = total
    low_ref[...] = total.astype(BF16)


def add_up(keep, taken):
    outs = [struct(keep.shape, F32), struct(keep.shape, BF16)]
    return local_call(sum_body, outs, [keep, *taken])


def project_body(core, blk, *refs):
    w_own, w_other, u_own, u_other, pad_ref, r_ref, mask_ref = refs[:7]
    updated_ref, residual_ref, w_ref, u_ref = refs[7:]
    rows = u_ref.shape[0]
    height = w_ref.shape[0]
    per = u_own.shape[0] // rows
    g = pl.program_id(0)
    own = lax.div(g, jnp.int32(per)) == position(core)
    local = lax.rem(g, jnp.int32(per))
    w_rows = pl.ds(pl.multiple_of(local * height, 16), height)
    u_rows = pl.ds(pl.multiple_of(local * rows, rows), rows)

    @pl.when(own)
    def _():
        w_ref[...] = w_own[w_rows, :]
        u_ref[...] = u_own[u_rows, :]

    @pl.when(jnp.logical_not(own))
    def _():
        w_ref[...] = w_other[w_rows, :]
        u_ref[...] = u_other[u_rows, :]

    main, rest = w_ref[:rows, :].astype(F32), w_ref[rows:, :].astype(F32)
    start = pl.multiple_of(g * rows, rows)
    residual = u_ref[...]
    for k, part in enumerate(unpacked(main, rest, blk)):
        inside = mask_ref[:, k * rows : (k + 1) * rows].astype(F32) > 0.5
        weights = jnp.where(inside, part, 0.0).astype(BF16)
        window = pad_ref[pl.ds(pl.multiple_of(start + k * rows, rows), rows), :]
        residual = residual - jnp.dot(weights, window, preferred_element_type=F32)
    residual_ref[...] = residual.astype(BF16)
    updated_ref[...] = (r_ref[...].astype(F32) + STEP_SIZE * residual).astype(BF16)


def project(weights, unprojected, padded, response, mask, core, group_rows, blk):
    bands, cells = response.shape
    out = struct((bands, cells), BF16)
    here = pl.BlockSpec((group_rows, cells), lambda g: (g, 0))

    def full(a):
        return pl.BlockSpec(a.shape, lambda g: (0, 0))

    return pl.pallas_call(
        functools.partial(project_body, core, blk),
        grid=(bands // group_rows,),
        out_shape=(out, out),
        in_specs=[
            *[full(a) for a in (*weights, *unprojected, padded)],
            here,
            pl.BlockSpec((group_rows, mask.shape[1]), lambda g: (g, 0)),
        ],
        out_specs=(here, here),
        scratch_shapes=[
            pltpu.VMEM((group_rows + 2 * blk, group_rows), BF16),
            pltpu.VMEM((group_rows, cells), F32),
        ],
        compiler_params=params(),
        cost_estimate=cost(
            4 * bands * group_rows * cells, padded, *unprojected, response, out, out
        ),
    )(*weights, *unprojected, padded, response, mask)


def shards(
    count, response, orbitals, projectors, potential, perturbing, energies, window_start, block_count
):
    bands, local_cells = response.shape
    cells = local_cells * count
    projections = projectors.shape[0]
    halo = 6 * GY * GZ
    core, across, along = levels_of(count)
    ace_scale = 1.0 / math.sqrt(cells * projections)
    window_scale = 1.0 / math.sqrt(cells * bands)
    blk = bands // NBLK
    group_rows = GROUP_BLOCKS * blk
    width = 2 * group_rows
    half = bands // 2
    block = half // across[0]
    first = max(16, round(REDUCE_SHARE * block / 16) * 16)
    gather_first = max(16, round(GATHER_SHARE * block / 16) * 16)
    matrix = jnp.asarray(plane_matrix())
    lines = (potential[None, :], perturbing[None, :])
    bounds = tuple(a[None, :] for a in (energies, window_start, block_count))

    def to(array, level):
        return [swapped(array, count, level, k) for k in range(1, level[0])]

    def parts_to(parts, level):
        return [swapped(part, count, level, k + 1) for k, part in enumerate(parts)]

    low = neighbour(response[:, local_cells - halo :], count, 1)
    high = neighbour(response[:, :halo], count, -1)

    sent_x, sent_z, keep_x, keep_z = first_sums(response, projectors, core, block, first)
    sent_z = swapped(sent_z, count, core, 1)
    sent_x = swapped(sent_x, count, core, 1)
    keep_z, *parts_z = split(keep_z, [sent_z], along, 1)
    sent_x, parts_z[0] = lax.optimization_barrier((sent_x, parts_z[0]))
    keep_x, *parts_x = split(keep_x, [sent_x], across, 0)
    parts_z[-1], low = lax.optimization_barrier((parts_z[-1], low))
    taken_z, taken_x, low, high = lax.optimization_barrier(
        (parts_to(parts_z, along), parts_to(parts_x, across), low, high)
    )
    base, mask = local_part(
        response, low, high, orbitals, matrix, lines, bounds, group_rows, width, blk
    )
    padded = pad_orbitals(orbitals, blk)
    keep_x, *parts_x = split(keep_x, taken_x, along, 1)
    keep_z, *parts_z = split(keep_z, taken_z, across, 0)
    taken_x, taken_z, base, padded = lax.optimization_barrier(
        (parts_to(parts_x, along), parts_to(parts_z, across), base, padded)
    )
    share_x, share_z = local_call(
        functools.partial(finish_both_body, ace_scale, len(taken_x)),
        [
            struct((gather_first, projections // along[0]), BF16),
            struct((block - gather_first, projections // along[0]), BF16),
        ],
        [keep_x, *taken_x, keep_z, *taken_z],
    )

    pieces_x, pieces_z = lax.optimization_barrier(
        ([share_x, *to(share_x, along)], [share_z, *to(share_z, across)])
    )
    block_x = place(pieces_x, along, 1)
    block_z = place(pieces_z, across, 0)
    blocks_x = [block_x, *to(block_x, across)]
    pieces_z = [block_z, *to(block_z, along)]
    blocks = [*blocks_x, place(pieces_z, along, 1)]
    others = [swapped(part, count, core, 1) for part in blocks]
    sizes = (core, across, block, group_rows, blk)
    wide, keep = apply(blocks, projectors, base, padded, *sizes, False)
    others, keep = lax.optimization_barrier((others, keep))
    other_wide, part = apply(others, projectors, base, padded, *sizes, True)
    unprojected = (wide, other_wide)
    total, part = add_up(keep, to(part, core))
    total, part = add_up(total, to(part, across))
    own = finish(total, to(part, along), window_scale)
    weights = (own, *to(own, core))
    return project(weights, unprojected, padded, response, mask, core, group_rows, blk)


def solution(mesh):
    in_specs = (
        P("pert", "band"),
        P(None, "band"),
        P(None, "band"),
        P("band"),
        P(("pert", "band")),
        P(),
        P(),
        P(),
    )
    out_specs = (P("pert", "band"), P("pert", "band"))
    body = functools.partial(shards, mesh.shape["band"])
    return jax.shard_map(body, mesh=mesh, in_specs=in_specs, out_specs=out_specs, check_vma=False)
```

```python
import functools
import math

import jax
import jax.numpy as jnp
import ml_dtypes
import numpy as np
from jax import lax
from jax.experimental import pallas as pl
from jax.experimental.pallas import tpu as pltpu
from jax.sharding import PartitionSpec as P

GY = 8
GZ = 16
NBLK = 32
REACH = 4
GROUP_BLOCKS = 8
COEFFS = (
    -5369.0 / 1800.0,
    12.0 / 7.0,
    -15.0 / 56.0,
    10.0 / 189.0,
    -1.0 / 112.0,
    2.0 / 1925.0,
    -1.0 / 16632.0,
)
KINETIC = 0.125
STEP_SIZE = 0.3
MIB = 1024 * 1024
VMEM_BYTES = 24 * MIB
REDUCE_SHARE = 0.5
GATHER_SHARE = 0.5
BF16 = jnp.bfloat16
F32 = jnp.float32
NT = (((1,), (1,)), ((), ()))


def levels_of(count):
    chips = count // 2
    across = 2 ** (int(math.log2(chips)) // 3)
    return (2, 1), (across, 2), (chips // across, 2 * across)


def position(level):
    size, stride = level
    return lax.rem(lax.div(lax.axis_index("band"), jnp.int32(stride)), jnp.int32(size))


def neighbour(array, count, step):
    return lax.ppermute(array, "band", [(i, (i + step) % count) for i in range(count)])


def swapped(array, count, level, step):
    size, stride = level
    pairs = []
    for device in range(count):
        place = device // stride % size
        pairs.append((device, device + ((place ^ step) - place) * stride))
    return lax.ppermute(array, "band", pairs)


def plane_matrix():
    plane = GY * GZ
    matrix = 3.0 * COEFFS[0] * np.eye(plane)
    cells = np.arange(plane)
    y, z = cells // GZ, cells % GZ
    for offset in range(1, 7):
        for sign in (1, -1):
            np.add.at(matrix, ((y + sign * offset) % GY * GZ + z, cells), COEFFS[offset])
            np.add.at(matrix, (y * GZ + (z + sign * offset) % GZ, cells), COEFFS[offset])
    matrix = KINETIC * matrix
    high = matrix.astype(ml_dtypes.bfloat16)
    low = (matrix - high.astype(np.float64)).astype(ml_dtypes.bfloat16)
    return np.stack([high, low])


def whole():
    return pl.BlockSpec(memory_space=pltpu.VMEM)


def params(size=VMEM_BYTES):
    return pltpu.CompilerParams(vmem_limit_bytes=size)


def cost(flops, *arrays):
    moved = sum(math.prod(a.shape) * jnp.dtype(a.dtype).itemsize for a in arrays)
    return pl.CostEstimate(flops=int(flops), bytes_accessed=int(moved), transcendentals=0)


def local_call(body, outs, args, flops=0, scratch=()):
    return pl.pallas_call(
        body,
        out_shape=outs,
        in_specs=[whole() for _ in args],
        out_specs=jax.tree.map(lambda _: whole(), outs),
        scratch_shapes=scratch,
        compiler_params=params(),
        cost_estimate=cost(flops, *args, *jax.tree.leaves(outs)),
    )(*args)


def struct(shape, dtype):
    return jax.ShapeDtypeStruct(shape, dtype)


def cut(part, block, x_ref, z_ref, cols):
    size = part.shape[0] // block
    first, rest = x_ref.shape[0] // size, z_ref.shape[0] // size
    part = part.astype(x_ref.dtype)
    for i in range(size):
        x_ref[i * first : (i + 1) * first, cols] = part[i * block : i * block + first, :]
        z_ref[i * rest : (i + 1) * rest, cols] = part[i * block + first : (i + 1) * block, :]


def first_body(core, block, tile, r_ref, p_ref, *refs):
    sent_x, sent_z, keep_x, keep_z, r_held, p_held, r_sem, p_sem = refs
    rows = r_held.shape[0] // 2
    r_copy = pltpu.make_async_copy(r_ref, r_held, r_sem)
    r_copy.start()
    copies = []
    for t in range(p_held.shape[0] // tile):
        part = pl.ds(t * tile, tile)
        copies.append(pltpu.make_async_copy(p_ref.at[part, :], p_held.at[part, :], p_sem.at[t]))
        copies[-1].start()
    c = position(core)
    r_copy.wait()
    for t, copy in enumerate(copies):
        copy.wait()
        cols = slice(t * tile, (t + 1) * tile)
        for side, x_ref, z_ref in ((1 - c, sent_x, sent_z), (c, keep_x, keep_z)):
            part = lax.dot_general(
                r_held[pl.ds(pl.multiple_of(side * rows, rows), rows), :],
                p_held[cols, :],
                NT,
                preferred_element_type=F32,
            )
            cut(part, block, x_ref, z_ref, cols)


def first_sums(response, projectors, core, block, first):
    bands, cells = response.shape
    count = projectors.shape[0]
    rows = bands // 2
    tile = min(512, count)
    rows_x = rows // block * first
    outs = [struct((n, count), t) for t in (BF16, F32) for n in (rows_x, rows - rows_x)]
    return pl.pallas_call(
        functools.partial(first_body, core, block, tile),
        out_shape=outs,
        in_specs=[pl.BlockSpec(memory_space=pltpu.HBM)] * 2,
        out_specs=[whole() for _ in outs],
        scratch_shapes=[
            pltpu.VMEM((bands, cells), response.dtype),
            pltpu.VMEM((count, cells), projectors.dtype),
            pltpu.SemaphoreType.DMA,
            pltpu.SemaphoreType.DMA((count // tile,)),
        ],
        compiler_params=params(),
        cost_estimate=cost(2 * bands * cells * count, projectors, *outs),
    )(
        pltpu.with_memory_space_constraint(response, pltpu.HBM),
        pltpu.with_memory_space_constraint(projectors, pltpu.HBM),
    )


def reversed_bits(place, level):
    bits = int(math.log2(level[0]))
    return sum(((place >> bit) & 1) << (bits - 1 - bit) for bit in range(bits))


def rows_at(place, size):
    return pl.ds(pl.multiple_of(place * size, 16), size)


def cols_at(place, size):
    return pl.ds(pl.multiple_of(place * size, size), size)


def total_of(keep_ref, taken, part):
    total = keep_ref[part]
    for ref in taken:
        total = total + ref[part].astype(F32)
    return total


def split_body(received, level, along, *refs):
    keep_ref, taken, outs = refs[0], refs[1 : 1 + received], refs[1 + received :]
    me = position(level)
    rows, width = outs[0].shape
    for step, out in enumerate(outs):
        at = me ^ step
        if along == 0:
            part = (rows_at(at, rows), slice(None))
        else:
            part = (slice(None), cols_at(reversed_bits(at, level), width))
        out[...] = total_of(keep_ref, taken, part).astype(out.dtype)


def halve_body(level, bit, keep_ref, taken_ref, own_ref, send_ref):
    mine = (position(level) >> bit) & 1
    width = own_ref.shape[1]
    for out, half in ((own_ref, mine), (send_ref, 1 - mine)):
        part = (slice(None), cols_at(half, width))
        out[...] = total_of(keep_ref, [taken_ref], part).astype(out.dtype)


def halve(keep, taken, level, bit):
    rows, width = keep.shape
    return local_call(
        functools.partial(halve_body, level, bit), shares_of((rows, width // 2), 2), [keep, taken]
    )


def shares_of(shape, count):
    return [struct(shape, F32)] + [struct(shape, BF16)] * (count - 1)


def split(keep, taken, level, along):
    shape = list(keep.shape)
    shape[along] //= level[0]
    return local_call(
        functools.partial(split_body, len(taken), level, along),
        shares_of(shape, level[0]),
        [keep, *taken],
    )


def finish_body(scale, keep_ref, *refs):
    *taken, out_ref = refs
    out_ref[...] = (total_of(keep_ref, taken, ...) * scale).astype(out_ref.dtype)


def finish(keep, taken, scale):
    return local_call(
        functools.partial(finish_body, scale), struct(keep.shape, BF16), [keep, *taken]
    )


def finish_both_body(scale, received, *refs):
    outs = refs[-2:]
    cut = outs[0].shape[0]
    row = 0
    for keep_ref, *taken in (refs[: 1 + received], refs[1 + received : -2]):
        low = (total_of(keep_ref, taken, ...) * scale).astype(BF16)
        end = row + keep_ref.shape[0]
        for out, first, last in ((outs[0], 0, cut), (outs[1], cut, cut + outs[1].shape[0])):
            top, bottom = max(row, first), min(end, last)
            if top < bottom:
                out[top - first : bottom - first, :] = low[top - row : bottom - row, :]
        row = end


def place_body(level, along, *refs):
    *parts, out_ref = refs
    me = position(level)
    width = parts[0].shape[along]
    for step, ref in enumerate(parts):
        at = me ^ step
        if along == 0:
            out_ref[pl.ds(pl.multiple_of(at * width, width), width), :] = ref[...]
        else:
            out_ref[:, cols_at(reversed_bits(at, level), width)] = ref[...]


def place(parts, level, along):
    shape = list(parts[0].shape)
    shape[along] *= level[0]
    return local_call(functools.partial(place_body, level, along), struct(shape, BF16), parts)


def turned(row, width):
    return jnp.transpose(jnp.broadcast_to(row, (width, row.shape[1])))


def local_body(depth, sizes, *refs):
    r_ref, l_ref, h_ref, o_ref, m_ref, pot_ref, v_ref, e_ref = refs[:8]
    first_ref, many_ref, out_ref, mask_ref = refs[8:]
    plane = GY * GZ
    reach = 6

    def plane_at(j):
        if j < 0:
            ref, k = l_ref, j + reach
        elif j < depth:
            ref, k = r_ref, j
        else:
            ref, k = h_ref, j - depth
        return ref[:, k * plane : (k + 1) * plane]

    group_rows, blk = sizes
    energy = turned(e_ref[...], plane)
    for j in range(depth):
        cols = slice(j * plane, (j + 1) * plane)
        low = plane_at(j)
        total = jnp.dot(low, m_ref[0], preferred_element_type=F32)
        total = total + jnp.dot(low, m_ref[1], preferred_element_type=F32)
        for offset in range(1, 7):
            pair = plane_at(j + offset).astype(F32) + plane_at(j - offset).astype(F32)
            total = total + (KINETIC * COEFFS[offset]) * pair
        total = total + (energy - pot_ref[:, cols]) * low.astype(F32)
        out_ref[:, cols] = total - v_ref[:, cols] * o_ref[:, cols].astype(F32)
    width = mask_ref.shape[1]
    block = lax.broadcasted_iota(jnp.int32, mask_ref.shape, 1) // blk
    block = (block + (pl.program_id(0) * (group_rows // blk) - REACH)).astype(F32)
    lowest = turned(first_ref[...].astype(F32), width)
    inside = (block >= lowest) & (block < lowest + turned(many_ref[...].astype(F32), width))
    mask_ref[...] = jnp.where(inside, 1.0, 0.0).astype(BF16)


def local_part(response, low, high, orbitals, matrix, lines, bounds, group_rows, width, blk):
    bands, cells = response.shape
    depth = cells // (GY * GZ)
    outs = [struct((bands, cells), F32), struct((bands, width), BF16)]
    here = pl.BlockSpec((group_rows, cells), lambda i: (i, 0))
    side = pl.BlockSpec((group_rows, low.shape[1]), lambda i: (i, 0))
    line = pl.BlockSpec((1, cells), lambda i: (0, 0))
    band = pl.BlockSpec((1, group_rows), lambda i: (0, i))
    return pl.pallas_call(
        functools.partial(local_body, depth, (group_rows, blk)),
        grid=(bands // group_rows,),
        out_shape=outs,
        in_specs=[
            here,
            side,
            side,
            here,
            pl.BlockSpec(matrix.shape, lambda i: (0, 0, 0)),
            line,
            line,
            band,
            band,
            band,
        ],
        out_specs=[here, pl.BlockSpec((group_rows, width), lambda i: (i, 0))],
        compiler_params=params(),
        cost_estimate=cost(2 * bands * cells * 300, low, high, low, low, *outs),
    )(response, low, high, orbitals, matrix, *lines, *bounds)


def pad_body(core, edge, o_ref, pad_ref, sides_ref):
    bands, cells = o_ref.shape
    pad_ref[:edge, :] = jnp.zeros((edge, cells), pad_ref.dtype)
    pad_ref[edge : edge + bands, :] = o_ref[...]
    pad_ref[edge + bands :, :] = jnp.zeros((edge, cells), pad_ref.dtype)
    c = position(core)
    sides_ref[0] = c
    sides_ref[1] = 1 - c


def pad_orbitals(orbitals, core, blk):
    bands, cells = orbitals.shape
    edge = REACH * blk
    padded, sides = struct((bands + 2 * edge, cells), orbitals.dtype), struct((2,), jnp.int32)
    return pl.pallas_call(
        functools.partial(pad_body, core, edge),
        out_shape=[padded, sides],
        in_specs=[whole()],
        out_specs=[whole(), pl.BlockSpec(memory_space=pltpu.SMEM)],
        compiler_params=params(),
        cost_estimate=cost(0, orbitals, padded),
    )(orbitals)


def subgroup(shape, blk):
    return lax.broadcasted_iota(jnp.int32, shape, 1) // (2 * blk)


def packed(sums, blk):
    rows = sums.shape[0]
    sub = 2 * blk
    near, far = sums[:, :rows], sums[:, rows:]
    column = subgroup((rows, rows), blk)
    row = lax.broadcasted_iota(jnp.int32, (rows, rows), 0) // sub
    main = jnp.where(column >= row, near, far)
    rest = far[:sub, :]
    for k in range(1, rows // sub):
        rest = jnp.where(column[:sub, :] == k, far[k * sub : (k + 1) * sub, :], rest)
    return main, rest


def unpacked(main, rest, blk):
    rows = main.shape[0]
    sub = 2 * blk
    column = subgroup((rows, rows), blk)
    row = lax.broadcasted_iota(jnp.int32, (rows, rows), 0) // sub
    near = jnp.where(column >= row, main, 0.0)
    last = jnp.where(column == row, jnp.concatenate([rest] * (rows // sub), axis=0), 0.0)
    return near, jnp.where(column < row, main, last)


def apply_body(core, across, block, group_rows, blk, other, *refs):
    size = across[0]
    blocks = refs[: size + 1]
    p_ref, base_ref, pad_ref, u_ref, s_ref, c_ref = refs[size + 1 :]
    rows, cells = u_ref.shape
    c, x = position(core), position(across)
    side = 1 - c if other else c
    first = blocks[0].shape[0]
    for step, ref in enumerate(blocks[:size]):
        at = (x ^ step) * block
        c_ref[pl.ds(pl.multiple_of(at, 16), first), :] = ref[...]
    rest = block - first
    for i in range(size):
        there = slice(i * block + first, (i + 1) * block)
        c_ref[there, :] = blocks[size][i * rest : (i + 1) * rest, :]
    mine = pl.ds(pl.multiple_of(side * rows, rows), rows)
    tile = 256 if cells % 256 == 0 else 128
    for t in range(cells // tile):
        cols = slice(t * tile, (t + 1) * tile)
        u_ref[:, cols] = base_ref[mine, cols] + jnp.dot(
            c_ref[...], p_ref[:, cols], preferred_element_type=F32
        )
    height = group_rows + 2 * blk
    for g in range(rows // group_rows):
        start = pl.multiple_of(side * rows + g * group_rows, group_rows)
        sums = lax.dot_general(
            u_ref[g * group_rows : (g + 1) * group_rows, :].astype(BF16),
            pad_ref[pl.ds(start, 2 * group_rows), :],
            NT,
            preferred_element_type=F32,
        )
        main, rest_sums = packed(sums, blk)
        s_ref[g * height : g * height + group_rows, :] = main.astype(s_ref.dtype)
        s_ref[g * height + group_rows : (g + 1) * height, :] = rest_sums.astype(s_ref.dtype)


def apply(blocks, projectors, base, padded, core, across, block, group_rows, blk, other):
    bands, cells = base.shape
    rows = bands // 2
    count = projectors.shape[0]
    height = rows // group_rows * (group_rows + 2 * blk)
    return local_call(
        functools.partial(apply_body, core, across, block, group_rows, blk, other),
        [struct((rows, cells), F32), struct((height, group_rows), BF16 if other else F32)],
        [*blocks, projectors, base, padded],
        flops=2 * rows * cells * (count + 2 * group_rows),
        scratch=[pltpu.VMEM((rows, count), BF16)],
    )


def sum_body(keep_ref, *refs):
    *taken, total_ref, low_ref = refs
    total = total_of(keep_ref, taken, ...)
    total_ref[...] = total
    low_ref[...] = total.astype(BF16)


def add_up(keep, taken):
    outs = [struct(keep.shape, F32), struct(keep.shape, BF16)]
    return local_call(sum_body, outs, [keep, *taken])


def project_body(core, blk, other, *refs):
    w_ref, u_ref, pad_ref, r_ref, mask_ref = refs[:5]
    updated_ref, residual_ref = refs[-2:]
    rows = u_ref.shape[0]
    main, rest = w_ref[:rows, :].astype(F32), w_ref[rows:, :].astype(F32)
    start = pl.multiple_of(group_of(core, other) * rows, rows)
    residual = u_ref[...]
    for k, part in enumerate(unpacked(main, rest, blk)):
        inside = mask_ref[:, k * rows : (k + 1) * rows].astype(F32) > 0.5
        weights = jnp.where(inside, part, 0.0).astype(BF16)
        window = pad_ref[pl.ds(pl.multiple_of(start + k * rows, rows), rows), :]
        residual = residual - jnp.dot(weights, window, preferred_element_type=F32)
    residual_ref[...] = residual.astype(BF16)
    updated_ref[...] = (r_ref[...].astype(F32) + STEP_SIZE * residual).astype(BF16)


def group_of(core, other):
    c = position(core)
    return (1 - c if other else c) * pl.num_programs(0) + pl.program_id(0)


def project(weights, unprojected, padded, response, mask, sides, core, group_rows, blk, other, before):
    bands, cells = response.shape
    rows = unprojected.shape[0]
    per = rows // group_rows
    height = weights.shape[0] // per
    out = struct((bands, cells), BF16)

    def there(g, sides):
        return (sides[1 if other else 0] * per + g, 0)

    here = pl.BlockSpec((group_rows, cells), there)
    return pl.pallas_call(
        lambda sides_ref, *refs: project_body(core, blk, other, *refs),
        grid_spec=pltpu.PrefetchScalarGridSpec(
            num_scalar_prefetch=1,
            grid=(per,),
            in_specs=[
                pl.BlockSpec((height, group_rows), lambda g, sides: (g, 0)),
                pl.BlockSpec((group_rows, cells), lambda g, sides: (g, 0)),
                pl.BlockSpec(padded.shape, lambda g, sides: (0, 0)),
                here,
                pl.BlockSpec((group_rows, mask.shape[1]), there),
                *[pl.BlockSpec(memory_space=pl.ANY)] * len(before),
            ],
            out_specs=(here, here),
        ),
        out_shape=(out, out),
        input_output_aliases={6: 0, 7: 1} if before else {},
        compiler_params=params(),
        cost_estimate=cost(4 * rows * group_rows * cells, padded, unprojected, unprojected),
    )(sides, weights, unprojected, padded, response, mask, *before)


def shards(
    count, response, orbitals, projectors, potential, perturbing, energies, window_start, block_count
):
    bands, local_cells = response.shape
    cells = local_cells * count
    projections = projectors.shape[0]
    halo = 6 * GY * GZ
    core, across, along = levels_of(count)
    ace_scale = 1.0 / math.sqrt(cells * projections)
    window_scale = 1.0 / math.sqrt(cells * bands)
    blk = bands // NBLK
    group_rows = GROUP_BLOCKS * blk
    width = 2 * group_rows
    half = bands // 2
    block = half // across[0]
    first = max(16, round(REDUCE_SHARE * block / 16) * 16)
    gather_first = max(16, round(GATHER_SHARE * block / 16) * 16)
    matrix = jnp.asarray(plane_matrix())
    lines = (potential[None, :], perturbing[None, :])
    bounds = tuple(a[None, :] for a in (energies, window_start, block_count))

    def to(array, level):
        return [swapped(array, count, level, k) for k in range(1, level[0])]

    def parts_to(parts, level):
        return [swapped(part, count, level, k + 1) for k, part in enumerate(parts)]

    low = neighbour(response[:, local_cells - halo :], count, 1)
    high = neighbour(response[:, :halo], count, -1)

    sent_x, sent_z, keep_x, keep_z = first_sums(response, projectors, core, block, first)
    sent_z = swapped(sent_z, count, core, 1)
    sent_x = swapped(sent_x, count, core, 1)
    keep_z, part_z = halve(keep_z, sent_z, along, 0)
    keep_x, *parts_x = split(keep_x, [sent_x], across, 0)
    parts_x, low = lax.optimization_barrier((parts_x, low))
    for bit in range(1, int(math.log2(along[0]))):
        keep_z, part_z = halve(keep_z, swapped(part_z, count, along, 1 << (bit - 1)), along, bit)
    taken_z = [swapped(part_z, count, along, along[0] // 2)]
    taken_z, taken_x, low, high = lax.optimization_barrier(
        (taken_z, parts_to(parts_x, across), low, high)
    )
    base, mask = local_part(
        response, low, high, orbitals, matrix, lines, bounds, group_rows, width, blk
    )
    padded, sides = pad_orbitals(orbitals, core, blk)
    keep_x, *parts_x = split(keep_x, taken_x, along, 1)
    keep_z, *parts_z = split(keep_z, taken_z, across, 0)
    taken_x, taken_z, base, padded = lax.optimization_barrier(
        (parts_to(parts_x, along), parts_to(parts_z, across), base, padded)
    )
    share_x, share_z = local_call(
        functools.partial(finish_both_body, ace_scale, len(taken_x)),
        [
            struct((gather_first, projections // along[0]), BF16),
            struct((block - gather_first, projections // along[0]), BF16),
        ],
        [keep_x, *taken_x, keep_z, *taken_z],
    )

    pieces_x, pieces_z = lax.optimization_barrier(
        ([share_x, *to(share_x, along)], [share_z, *to(share_z, across)])
    )
    block_x = place(pieces_x, along, 1)
    block_z = place(pieces_z, across, 0)
    blocks_x = [block_x, *to(block_x, across)]
    pieces_z = [block_z, *to(block_z, along)]
    blocks = [*blocks_x, place(pieces_z, along, 1)]
    others = [swapped(part, count, core, 1) for part in blocks]
    sizes = (core, across, block, group_rows, blk)
    wide, keep = apply(blocks, projectors, base, padded, *sizes, False)
    others, keep = lax.optimization_barrier((others, keep))
    other_wide, part = apply(others, projectors, base, padded, *sizes, True)
    total, part = add_up(keep, to(part, core))
    total, part = add_up(total, to(part, across))
    own = finish(total, to(part, along), window_scale)
    (theirs,) = to(own, core)
    sizes = (core, group_rows, blk)
    outs = project(own, wide, padded, response, mask, sides, *sizes, False, ())
    return project(theirs, other_wide, padded, response, mask, sides, *sizes, True, outs)


def solution(mesh):
    in_specs = (
        P("pert", "band"),
        P(None, "band"),
        P(None, "band"),
        P("band"),
        P(("pert", "band")),
        P(),
        P(),
        P(),
    )
    out_specs = (P("pert", "band"), P("pert", "band"))
    body = functools.partial(shards, mesh.shape["band"])
    return jax.shard_map(body, mesh=mesh, in_specs=in_specs, out_specs=out_specs, check_vma=False)
```

```python
import functools
import math

import jax
import jax.numpy as jnp
import ml_dtypes
import numpy as np
from jax import lax
from jax.experimental import pallas as pl
from jax.experimental.pallas import tpu as pltpu
from jax.sharding import PartitionSpec as P

GY = 8
GZ = 16
NBLK = 32
REACH = 4
GROUP_BLOCKS = 8
COEFFS = (
    -5369.0 / 1800.0,
    12.0 / 7.0,
    -15.0 / 56.0,
    10.0 / 189.0,
    -1.0 / 112.0,
    2.0 / 1925.0,
    -1.0 / 16632.0,
)
KINETIC = 0.125
STEP_SIZE = 0.3
MIB = 1024 * 1024
VMEM_BYTES = 24 * MIB
REDUCE_SHARE = 0.5
GATHER_SHARE = 0.5
BF16 = jnp.bfloat16
F32 = jnp.float32
NT = (((1,), (1,)), ((), ()))


def levels_of(count):
    chips = count // 2
    across = 2 ** (int(math.log2(chips)) // 3)
    return (2, 1), (across, 2), (chips // across, 2 * across)


def position(level):
    size, stride = level
    return lax.rem(lax.div(lax.axis_index("band"), jnp.int32(stride)), jnp.int32(size))


def neighbour(array, count, step):
    return lax.ppermute(array, "band", [(i, (i + step) % count) for i in range(count)])


def swapped(array, count, level, step):
    size, stride = level
    pairs = []
    for device in range(count):
        place = device // stride % size
        pairs.append((device, device + ((place ^ step) - place) * stride))
    return lax.ppermute(array, "band", pairs)


def plane_matrix():
    plane = GY * GZ
    matrix = 3.0 * COEFFS[0] * np.eye(plane)
    cells = np.arange(plane)
    y, z = cells // GZ, cells % GZ
    for offset in range(1, 7):
        for sign in (1, -1):
            np.add.at(matrix, ((y + sign * offset) % GY * GZ + z, cells), COEFFS[offset])
            np.add.at(matrix, (y * GZ + (z + sign * offset) % GZ, cells), COEFFS[offset])
    matrix = KINETIC * matrix
    high = matrix.astype(ml_dtypes.bfloat16)
    low = (matrix - high.astype(np.float64)).astype(ml_dtypes.bfloat16)
    return np.stack([high, low])


def whole():
    return pl.BlockSpec(memory_space=pltpu.VMEM)


def params(size=VMEM_BYTES):
    return pltpu.CompilerParams(vmem_limit_bytes=size)


def cost(flops, *arrays):
    moved = sum(math.prod(a.shape) * jnp.dtype(a.dtype).itemsize for a in arrays)
    return pl.CostEstimate(flops=int(flops), bytes_accessed=int(moved), transcendentals=0)


def local_call(body, outs, args, flops=0, scratch=()):
    return pl.pallas_call(
        body,
        out_shape=outs,
        in_specs=[whole() for _ in args],
        out_specs=jax.tree.map(lambda _: whole(), outs),
        scratch_shapes=scratch,
        compiler_params=params(),
        cost_estimate=cost(flops, *args, *jax.tree.leaves(outs)),
    )(*args)


def struct(shape, dtype):
    return jax.ShapeDtypeStruct(shape, dtype)


def cut(part, block, x_ref, z_ref, cols):
    size = part.shape[0] // block
    first, rest = x_ref.shape[0] // size, z_ref.shape[0] // size
    part = part.astype(x_ref.dtype)
    for i in range(size):
        x_ref[i * first : (i + 1) * first, cols] = part[i * block : i * block + first, :]
        z_ref[i * rest : (i + 1) * rest, cols] = part[i * block + first : (i + 1) * block, :]


def first_body(core, block, tile, r_ref, p_ref, *refs):
    sent_x, sent_z, keep_x, keep_z, r_held, p_held, r_sem, p_sem = refs
    rows = r_held.shape[0] // 2
    c = position(core)
    r_copies = []
    for k, side in enumerate((1 - c, c)):
        there = pl.ds(pl.multiple_of(side * rows, rows), rows)
        here = pl.ds(k * rows, rows)
        r_copies.append(pltpu.make_async_copy(r_ref.at[there, :], r_held.at[here, :], r_sem.at[k]))
        r_copies[-1].start()
    copies = []
    for t in range(p_held.shape[0] // tile):
        part = pl.ds(t * tile, tile)
        copies.append(pltpu.make_async_copy(p_ref.at[part, :], p_held.at[part, :], p_sem.at[t]))
        copies[-1].start()
    for copy in r_copies:
        copy.wait()
    for t, copy in enumerate(copies):
        copy.wait()
        cols = slice(t * tile, (t + 1) * tile)
        part = lax.dot_general(r_held[...], p_held[cols, :], NT, preferred_element_type=F32)
        cut(part[:rows, :], block, sent_x, sent_z, cols)
        cut(part[rows:, :], block, keep_x, keep_z, cols)


def first_sums(response, projectors, core, block, first):
    bands, cells = response.shape
    count = projectors.shape[0]
    rows = bands // 2
    tile = min(512, count)
    rows_x = rows // block * first
    outs = [struct((n, count), t) for t in (BF16, F32) for n in (rows_x, rows - rows_x)]
    return pl.pallas_call(
        functools.partial(first_body, core, block, tile),
        out_shape=outs,
        in_specs=[pl.BlockSpec(memory_space=pltpu.HBM)] * 2,
        out_specs=[whole() for _ in outs],
        scratch_shapes=[
            pltpu.VMEM((bands, cells), response.dtype),
            pltpu.VMEM((count, cells), projectors.dtype),
            pltpu.SemaphoreType.DMA((2,)),
            pltpu.SemaphoreType.DMA((count // tile,)),
        ],
        compiler_params=params(),
        cost_estimate=cost(2 * bands * cells * count, projectors, *outs),
    )(
        pltpu.with_memory_space_constraint(response, pltpu.HBM),
        pltpu.with_memory_space_constraint(projectors, pltpu.HBM),
    )


def rows_at(place, size):
    return pl.ds(pl.multiple_of(place * size, 16), size)


def cols_at(place, size):
    return pl.ds(pl.multiple_of(place * size, size), size)


def total_of(keep_ref, taken, part):
    total = keep_ref[part]
    for ref in taken:
        total = total + ref[part].astype(F32)
    return total


def split_body(received, level, along, *refs):
    keep_ref, taken, outs = refs[0], refs[1 : 1 + received], refs[1 + received :]
    me = position(level)
    rows, width = outs[0].shape
    for step, out in enumerate(outs):
        at = me ^ step
        if along == 0:
            part = (rows_at(at, rows), slice(None))
        else:
            part = (slice(None), cols_at(at, width))
        out[...] = total_of(keep_ref, taken, part).astype(out.dtype)


def shares_of(shape, count):
    return [struct(shape, F32)] + [struct(shape, BF16)] * (count - 1)


def split(keep, taken, level, along):
    shape = list(keep.shape)
    shape[along] //= level[0]
    return local_call(
        functools.partial(split_body, len(taken), level, along),
        shares_of(shape, level[0]),
        [keep, *taken],
    )


def finish_body(scale, keep_ref, *refs):
    *taken, out_ref = refs
    out_ref[...] = (total_of(keep_ref, taken, ...) * scale).astype(out_ref.dtype)


def finish(keep, taken, scale):
    return local_call(
        functools.partial(finish_body, scale), struct(keep.shape, BF16), [keep, *taken]
    )


def finish_both_body(scale, received, *refs):
    outs = refs[-2:]
    cut = outs[0].shape[0]
    row = 0
    for keep_ref, *taken in (refs[: 1 + received], refs[1 + received : -2]):
        low = (total_of(keep_ref, taken, ...) * scale).astype(BF16)
        end = row + keep_ref.shape[0]
        for out, first, last in ((outs[0], 0, cut), (outs[1], cut, cut + outs[1].shape[0])):
            top, bottom = max(row, first), min(end, last)
            if top < bottom:
                out[top - first : bottom - first, :] = low[top - row : bottom - row, :]
        row = end


def place_body(level, along, *refs):
    *parts, out_ref = refs
    me = position(level)
    width = parts[0].shape[along]
    for step, ref in enumerate(parts):
        at = pl.multiple_of((me ^ step) * width, width)
        if along == 0:
            out_ref[pl.ds(at, width), :] = ref[...]
        else:
            out_ref[:, pl.ds(at, width)] = ref[...]


def place(parts, level, along):
    shape = list(parts[0].shape)
    shape[along] *= level[0]
    return local_call(functools.partial(place_body, level, along), struct(shape, BF16), parts)


def turned(row, width):
    return jnp.transpose(jnp.broadcast_to(row, (width, row.shape[1])))


def local_body(depth, sizes, *refs):
    r_ref, l_ref, h_ref, o_ref, m_ref, pot_ref, v_ref, e_ref = refs[:8]
    first_ref, many_ref, out_ref, mask_ref = refs[8:]
    plane = GY * GZ
    reach = 6

    def plane_at(j):
        if j < 0:
            ref, k = l_ref, j + reach
        elif j < depth:
            ref, k = r_ref, j
        else:
            ref, k = h_ref, j - depth
        return ref[:, k * plane : (k + 1) * plane]

    group_rows, blk = sizes
    energy = turned(e_ref[...], plane)
    for j in range(depth):
        cols = slice(j * plane, (j + 1) * plane)
        low = plane_at(j)
        total = jnp.dot(low, m_ref[0], preferred_element_type=F32)
        total = total + jnp.dot(low, m_ref[1], preferred_element_type=F32)
        for offset in range(1, 7):
            pair = plane_at(j + offset).astype(F32) + plane_at(j - offset).astype(F32)
            total = total + (KINETIC * COEFFS[offset]) * pair
        total = total + (energy - pot_ref[:, cols]) * low.astype(F32)
        out_ref[:, cols] = total - v_ref[:, cols] * o_ref[:, cols].astype(F32)
    width = mask_ref.shape[1]
    block = lax.broadcasted_iota(jnp.int32, mask_ref.shape, 1) // blk
    block = (block + (pl.program_id(0) * (group_rows // blk) - REACH)).astype(F32)
    lowest = turned(first_ref[...].astype(F32), width)
    inside = (block >= lowest) & (block < lowest + turned(many_ref[...].astype(F32), width))
    mask_ref[...] = jnp.where(inside, 1.0, 0.0).astype(BF16)


def local_part(response, low, high, orbitals, matrix, lines, bounds, group_rows, width, blk):
    bands, cells = response.shape
    depth = cells // (GY * GZ)
    outs = [struct((bands, cells), F32), struct((bands, width), BF16)]
    here = pl.BlockSpec((group_rows, cells), lambda i: (i, 0))
    side = pl.BlockSpec((group_rows, low.shape[1]), lambda i: (i, 0))
    line = pl.BlockSpec((1, cells), lambda i: (0, 0))
    band = pl.BlockSpec((1, group_rows), lambda i: (0, i))
    return pl.pallas_call(
        functools.partial(local_body, depth, (group_rows, blk)),
        grid=(bands // group_rows,),
        out_shape=outs,
        in_specs=[
            here,
            side,
            side,
            here,
            pl.BlockSpec(matrix.shape, lambda i: (0, 0, 0)),
            line,
            line,
            band,
            band,
            band,
        ],
        out_specs=[here, pl.BlockSpec((group_rows, width), lambda i: (i, 0))],
        compiler_params=params(),
        cost_estimate=cost(2 * bands * cells * 300, low, high, low, low, *outs),
    )(response, low, high, orbitals, matrix, *lines, *bounds)


def pad_body(edge, o_ref, pad_ref):
    bands, cells = o_ref.shape
    pad_ref[:edge, :] = jnp.zeros((edge, cells), pad_ref.dtype)
    pad_ref[edge : edge + bands, :] = o_ref[...]
    pad_ref[edge + bands :, :] = jnp.zeros((edge, cells), pad_ref.dtype)


def pad_orbitals(orbitals, blk):
    bands, cells = orbitals.shape
    edge = REACH * blk
    return local_call(
        functools.partial(pad_body, edge),
        struct((bands + 2 * edge, cells), orbitals.dtype),
        [orbitals],
    )


def subgroup(shape, blk):
    return lax.broadcasted_iota(jnp.int32, shape, 1) // (2 * blk)


def packed(sums, blk):
    rows = sums.shape[0]
    sub = 2 * blk
    near, far = sums[:, :rows], sums[:, rows:]
    column = subgroup((rows, rows), blk)
    row = lax.broadcasted_iota(jnp.int32, (rows, rows), 0) // sub
    main = jnp.where(column >= row, near, far)
    rest = far[:sub, :]
    for k in range(1, rows // sub):
        rest = jnp.where(column[:sub, :] == k, far[k * sub : (k + 1) * sub, :], rest)
    return main, rest


def unpacked(main, rest, blk):
    rows = main.shape[0]
    sub = 2 * blk
    column = subgroup((rows, rows), blk)
    row = lax.broadcasted_iota(jnp.int32, (rows, rows), 0) // sub
    near = jnp.where(column >= row, main, 0.0)
    last = jnp.where(column == row, jnp.concatenate([rest] * (rows // sub), axis=0), 0.0)
    return near, jnp.where(column < row, main, last)


def apply_body(core, across, block, group_rows, blk, other, *refs):
    size = across[0]
    blocks = refs[: size + 1]
    p_ref, base_ref, pad_ref, u_ref, s_ref, c_ref = refs[size + 1 :]
    rows, cells = u_ref.shape
    c, x = position(core), position(across)
    side = 1 - c if other else c
    first = blocks[0].shape[0]
    for step, ref in enumerate(blocks[:size]):
        at = (x ^ step) * block
        c_ref[pl.ds(pl.multiple_of(at, 16), first), :] = ref[...]
    rest = block - first
    for i in range(size):
        there = slice(i * block + first, (i + 1) * block)
        c_ref[there, :] = blocks[size][i * rest : (i + 1) * rest, :]
    mine = pl.ds(pl.multiple_of(side * rows, rows), rows)
    tile = 256 if cells % 256 == 0 else 128
    for t in range(cells // tile):
        cols = slice(t * tile, (t + 1) * tile)
        u_ref[:, cols] = base_ref[mine, cols] + jnp.dot(
            c_ref[...], p_ref[:, cols], preferred_element_type=F32
        )
    height = group_rows + 2 * blk
    for g in range(rows // group_rows):
        start = pl.multiple_of(side * rows + g * group_rows, group_rows)
        sums = lax.dot_general(
            u_ref[g * group_rows : (g + 1) * group_rows, :].astype(BF16),
            pad_ref[pl.ds(start, 2 * group_rows), :],
            NT,
            preferred_element_type=F32,
        )
        main, rest_sums = packed(sums, blk)
        s_ref[g * height : g * height + group_rows, :] = main.astype(s_ref.dtype)
        s_ref[g * height + group_rows : (g + 1) * height, :] = rest_sums.astype(s_ref.dtype)


def apply(blocks, projectors, base, padded, core, across, block, group_rows, blk, other):
    bands, cells = base.shape
    rows = bands // 2
    count = projectors.shape[0]
    height = rows // group_rows * (group_rows + 2 * blk)
    return local_call(
        functools.partial(apply_body, core, across, block, group_rows, blk, other),
        [struct((rows, cells), F32), struct((height, group_rows), BF16 if other else F32)],
        [*blocks, projectors, base, padded],
        flops=2 * rows * cells * (count + 2 * group_rows),
        scratch=[pltpu.VMEM((rows, count), BF16)],
    )


def sum_body(keep_ref, *refs):
    *taken, total_ref, low_ref = refs
    total = total_of(keep_ref, taken, ...)
    total_ref[...] = total
    low_ref[...] = total.astype(BF16)


def add_up(keep, taken):
    outs = [struct(keep.shape, F32), struct(keep.shape, BF16)]
    return local_call(sum_body, outs, [keep, *taken])


def project_body(core, blk, *refs):
    w_own, w_other, u_own, u_other, pad_ref, r_ref, mask_ref = refs[:7]
    updated_ref, residual_ref, w_ref, u_ref = refs[7:]
    rows = u_ref.shape[0]
    height = w_ref.shape[0]
    per = u_own.shape[0] // rows
    g = pl.program_id(0)
    own = lax.div(g, jnp.int32(per)) == position(core)
    local = lax.rem(g, jnp.int32(per))
    w_rows = pl.ds(pl.multiple_of(local * height, 16), height)
    u_rows = pl.ds(pl.multiple_of(local * rows, rows), rows)

    @pl.when(own)
    def _():
        w_ref[...] = w_own[w_rows, :]
        u_ref[...] = u_own[u_rows, :]

    @pl.when(jnp.logical_not(own))
    def _():
        w_ref[...] = w_other[w_rows, :]
        u_ref[...] = u_other[u_rows, :]

    main, rest = w_ref[:rows, :].astype(F32), w_ref[rows:, :].astype(F32)
    start = pl.multiple_of(g * rows, rows)
    residual = u_ref[...]
    for k, part in enumerate(unpacked(main, rest, blk)):
        inside = mask_ref[:, k * rows : (k + 1) * rows].astype(F32) > 0.5
        weights = jnp.where(inside, part, 0.0).astype(BF16)
        window = pad_ref[pl.ds(pl.multiple_of(start + k * rows, rows), rows), :]
        residual = residual - jnp.dot(weights, window, preferred_element_type=F32)
    residual_ref[...] = residual.astype(BF16)
    updated_ref[...] = (r_ref[...].astype(F32) + STEP_SIZE * residual).astype(BF16)


def project(weights, unprojected, padded, response, mask, core, group_rows, blk):
    bands, cells = response.shape
    out = struct((bands, cells), BF16)
    here = pl.BlockSpec((group_rows, cells), lambda g: (g, 0))

    def full(a):
        return pl.BlockSpec(a.shape, lambda g: (0, 0))

    return pl.pallas_call(
        functools.partial(project_body, core, blk),
        grid=(bands // group_rows,),
        out_shape=(out, out),
        in_specs=[
            *[full(a) for a in (*weights, *unprojected, padded)],
            here,
            pl.BlockSpec((group_rows, mask.shape[1]), lambda g: (g, 0)),
        ],
        out_specs=(here, here),
        scratch_shapes=[
            pltpu.VMEM((group_rows + 2 * blk, group_rows), BF16),
            pltpu.VMEM((group_rows, cells), F32),
        ],
        compiler_params=params(),
        cost_estimate=cost(
            4 * bands * group_rows * cells, padded, *unprojected, response, out, out
        ),
    )(*weights, *unprojected, padded, response, mask)


def shards(
    count, response, orbitals, projectors, potential, perturbing, energies, window_start, block_count
):
    bands, local_cells = response.shape
    cells = local_cells * count
    projections = projectors.shape[0]
    halo = 6 * GY * GZ
    core, across, along = levels_of(count)
    ace_scale = 1.0 / math.sqrt(cells * projections)
    window_scale = 1.0 / math.sqrt(cells * bands)
    blk = bands // NBLK
    group_rows = GROUP_BLOCKS * blk
    width = 2 * group_rows
    half = bands // 2
    block = half // across[0]
    first = max(16, round(REDUCE_SHARE * block / 16) * 16)
    gather_first = max(16, round(GATHER_SHARE * block / 16) * 16)
    matrix = jnp.asarray(plane_matrix())
    lines = (potential[None, :], perturbing[None, :])
    bounds = tuple(a[None, :] for a in (energies, window_start, block_count))

    def to(array, level):
        return [swapped(array, count, level, k) for k in range(1, level[0])]

    def parts_to(parts, level):
        return [swapped(part, count, level, k + 1) for k, part in enumerate(parts)]

    low = neighbour(response[:, local_cells - halo :], count, 1)
    high = neighbour(response[:, :halo], count, -1)

    sent_x, sent_z, keep_x, keep_z = first_sums(response, projectors, core, block, first)
    sent_z = swapped(sent_z, count, core, 1)
    sent_x = swapped(sent_x, count, core, 1)
    keep_z, *parts_z = split(keep_z, [sent_z], along, 1)
    sent_x, parts_z[0] = lax.optimization_barrier((sent_x, parts_z[0]))
    keep_x, *parts_x = split(keep_x, [sent_x], across, 0)
    parts_z[-1], low = lax.optimization_barrier((parts_z[-1], low))
    taken_z, taken_x, low, high = lax.optimization_barrier(
        (parts_to(parts_z, along), parts_to(parts_x, across), low, high)
    )
    base, mask = local_part(
        response, low, high, orbitals, matrix, lines, bounds, group_rows, width, blk
    )
    padded = pad_orbitals(orbitals, blk)
    keep_x, *parts_x = split(keep_x, taken_x, along, 1)
    keep_z, *parts_z = split(keep_z, taken_z, across, 0)
    taken_x, taken_z, base, padded = lax.optimization_barrier(
        (parts_to(parts_x, along), parts_to(parts_z, across), base, padded)
    )
    share_x, share_z = local_call(
        functools.partial(finish_both_body, ace_scale, len(taken_x)),
        [
            struct((gather_first, projections // along[0]), BF16),
            struct((block - gather_first, projections // along[0]), BF16),
        ],
        [keep_x, *taken_x, keep_z, *taken_z],
    )

    pieces_x, pieces_z = lax.optimization_barrier(
        ([share_x, *to(share_x, along)], [share_z, *to(share_z, across)])
    )
    block_x = place(pieces_x, along, 1)
    block_z = place(pieces_z, across, 0)
    blocks_x = [block_x, *to(block_x, across)]
    pieces_z = [block_z, *to(block_z, along)]
    blocks = [*blocks_x, place(pieces_z, along, 1)]
    others = [swapped(part, count, core, 1) for part in blocks]
    sizes = (core, across, block, group_rows, blk)
    wide, keep = apply(blocks, projectors, base, padded, *sizes, False)
    others, keep = lax.optimization_barrier((others, keep))
    other_wide, part = apply(others, projectors, base, padded, *sizes, True)
    unprojected = (wide, other_wide)
    total, part = add_up(keep, to(part, core))
    total, part = add_up(total, to(part, across))
    own = finish(total, to(part, along), window_scale)
    weights = (own, *to(own, core))
    return project(weights, unprojected, padded, response, mask, core, group_rows, blk)


def solution(mesh):
    in_specs = (
        P("pert", "band"),
        P(None, "band"),
        P(None, "band"),
        P("band"),
        P(("pert", "band")),
        P(),
        P(),
        P(),
    )
    out_specs = (P("pert", "band"), P("pert", "band"))
    body = functools.partial(shards, mesh.shape["band"])
    return jax.shard_map(body, mesh=mesh, in_specs=in_specs, out_specs=out_specs, check_vma=False)
```

```python
import functools
import math

import jax
import jax.numpy as jnp
import ml_dtypes
import numpy as np
from jax import lax
from jax.experimental import pallas as pl
from jax.experimental.pallas import tpu as pltpu
from jax.sharding import PartitionSpec as P

GY = 8
GZ = 16
NBLK = 32
REACH = 4
GROUP_BLOCKS = 8
COEFFS = (
    -5369.0 / 1800.0,
    12.0 / 7.0,
    -15.0 / 56.0,
    10.0 / 189.0,
    -1.0 / 112.0,
    2.0 / 1925.0,
    -1.0 / 16632.0,
)
KINETIC = 0.125
STEP_SIZE = 0.3
MIB = 1024 * 1024
VMEM_BYTES = 24 * MIB
REDUCE_SHARE = 0.625
GATHER_SHARE = 0.5
BF16 = jnp.bfloat16
F32 = jnp.float32
NT = (((1,), (1,)), ((), ()))


def levels_of(count):
    chips = count // 2
    across = 2 ** (int(math.log2(chips)) // 3)
    return (2, 1), (across, 2), (chips // across, 2 * across)


def position(level):
    size, stride = level
    return lax.rem(lax.div(lax.axis_index("band"), jnp.int32(stride)), jnp.int32(size))


def neighbour(array, count, step):
    return lax.ppermute(array, "band", [(i, (i + step) % count) for i in range(count)])


def swapped(array, count, level, step):
    size, stride = level
    pairs = []
    for device in range(count):
        place = device // stride % size
        pairs.append((device, device + ((place ^ step) - place) * stride))
    return lax.ppermute(array, "band", pairs)


def plane_matrix():
    plane = GY * GZ
    matrix = 3.0 * COEFFS[0] * np.eye(plane)
    cells = np.arange(plane)
    y, z = cells // GZ, cells % GZ
    for offset in range(1, 7):
        for sign in (1, -1):
            np.add.at(matrix, ((y + sign * offset) % GY * GZ + z, cells), COEFFS[offset])
            np.add.at(matrix, (y * GZ + (z + sign * offset) % GZ, cells), COEFFS[offset])
    matrix = KINETIC * matrix
    high = matrix.astype(ml_dtypes.bfloat16)
    low = (matrix - high.astype(np.float64)).astype(ml_dtypes.bfloat16)
    return np.stack([high, low])


def whole():
    return pl.BlockSpec(memory_space=pltpu.VMEM)


def params(size=VMEM_BYTES):
    return pltpu.CompilerParams(vmem_limit_bytes=size)


def cost(flops, *arrays):
    moved = sum(math.prod(a.shape) * jnp.dtype(a.dtype).itemsize for a in arrays)
    return pl.CostEstimate(flops=int(flops), bytes_accessed=int(moved), transcendentals=0)


def local_call(body, outs, args, flops=0, scratch=()):
    return pl.pallas_call(
        body,
        out_shape=outs,
        in_specs=[whole() for _ in args],
        out_specs=jax.tree.map(lambda _: whole(), outs),
        scratch_shapes=scratch,
        compiler_params=params(),
        cost_estimate=cost(flops, *args, *jax.tree.leaves(outs)),
    )(*args)


def struct(shape, dtype):
    return jax.ShapeDtypeStruct(shape, dtype)


def cut(part, block, x_ref, z_ref, cols):
    size = part.shape[0] // block
    first, rest = x_ref.shape[0] // size, z_ref.shape[0] // size
    part = part.astype(x_ref.dtype)
    for i in range(size):
        x_ref[i * first : (i + 1) * first, cols] = part[i * block : i * block + first, :]
        z_ref[i * rest : (i + 1) * rest, cols] = part[i * block + first : (i + 1) * block, :]


def first_body(core, block, tile, r_ref, p_ref, *refs):
    sent_low, sent_high, keep_x, keep_z, r_held, p_held, r_sem, p_sem = refs
    width = sent_low.shape[1]
    rows = r_held.shape[0] // 2
    r_copy = pltpu.make_async_copy(r_ref, r_held, r_sem)
    r_copy.start()
    copies = []
    for t in range(p_held.shape[0] // tile):
        part = pl.ds(t * tile, tile)
        copies.append(pltpu.make_async_copy(p_ref.at[part, :], p_held.at[part, :], p_sem.at[t]))
        copies[-1].start()
    c = position(core)
    r_copy.wait()
    for t, copy in enumerate(copies):
        copy.wait()
        cols = slice(t * tile, (t + 1) * tile)
        for side in (1 - c, c):
            part = lax.dot_general(
                r_held[pl.ds(pl.multiple_of(side * rows, rows), rows), :],
                p_held[cols, :],
                NT,
                preferred_element_type=F32,
            )
            if side is c:
                cut(part, block, keep_x, keep_z, cols)
            else:
                ref, first = (sent_low, 0) if t * tile < width else (sent_high, width)
                ref[:, t * tile - first : (t + 1) * tile - first] = part.astype(BF16)


def first_sums(response, projectors, core, block, first):
    bands, cells = response.shape
    count = projectors.shape[0]
    rows = bands // 2
    tile = min(512, count // 2)
    rows_x = rows // block * first
    outs = [struct((rows, count // 2), BF16)] * 2
    outs += [struct((n, count), F32) for n in (rows_x, rows - rows_x)]
    return pl.pallas_call(
        functools.partial(first_body, core, block, tile),
        out_shape=outs,
        in_specs=[pl.BlockSpec(memory_space=pltpu.HBM)] * 2,
        out_specs=[whole() for _ in outs],
        scratch_shapes=[
            pltpu.VMEM((bands, cells), response.dtype),
            pltpu.VMEM((count, cells), projectors.dtype),
            pltpu.SemaphoreType.DMA,
            pltpu.SemaphoreType.DMA((count // tile,)),
        ],
        compiler_params=params(),
        cost_estimate=cost(2 * bands * cells * count, projectors, *outs),
    )(
        pltpu.with_memory_space_constraint(response, pltpu.HBM),
        pltpu.with_memory_space_constraint(projectors, pltpu.HBM),
    )


def rows_at(place, size):
    return pl.ds(pl.multiple_of(place * size, 16), size)


def cols_at(place, size):
    return pl.ds(pl.multiple_of(place * size, size), size)


def total_of(keep_ref, taken, part):
    total = keep_ref[part]
    for ref in taken:
        total = total + ref[part].astype(F32)
    return total


def first_x_body(level, block, keep_ref, low_ref, high_ref, *outs):
    me = position(level)
    rows = outs[0].shape[0]
    half = low_ref.shape[1]
    for step, out in enumerate(outs):
        at = me ^ step
        mine = rows_at(at, rows)
        theirs = pl.ds(pl.multiple_of(at * block, 16), rows)
        for k, ref in enumerate((low_ref, high_ref)):
            cols = slice(k * half, (k + 1) * half)
            out[:, cols] = (keep_ref[mine, cols] + ref[theirs, :].astype(F32)).astype(out.dtype)


def first_z_body(level, block, first, keep_ref, low_ref, high_ref, *outs):
    me = position(level)
    rows = block - first
    width = outs[0].shape[1]
    per = low_ref.shape[1] // width
    for step, out in enumerate(outs):
        at = me ^ step
        cols = cols_at(at, width)
        near = cols_at(lax.rem(at, jnp.int32(per)), width)
        for i in range(out.shape[0] // rows):
            mine = slice(i * rows, (i + 1) * rows)
            theirs = slice(i * block + first, (i + 1) * block)
            taken = jnp.where(at < per, low_ref[theirs, near], high_ref[theirs, near])
            out[mine, :] = (keep_ref[mine, cols] + taken.astype(F32)).astype(out.dtype)


def split_body(received, level, along, *refs):
    keep_ref, taken, outs = refs[0], refs[1 : 1 + received], refs[1 + received :]
    me = position(level)
    rows, width = outs[0].shape
    for step, out in enumerate(outs):
        at = me ^ step
        if along == 0:
            part = (rows_at(at, rows), slice(None))
        else:
            part = (slice(None), cols_at(at, width))
        out[...] = total_of(keep_ref, taken, part).astype(out.dtype)


def shares_of(shape, count):
    return [struct(shape, F32)] + [struct(shape, BF16)] * (count - 1)


def split(keep, taken, level, along):
    shape = list(keep.shape)
    shape[along] //= level[0]
    return local_call(
        functools.partial(split_body, len(taken), level, along),
        shares_of(shape, level[0]),
        [keep, *taken],
    )


def finish_body(scale, keep_ref, *refs):
    *taken, out_ref = refs
    out_ref[...] = (total_of(keep_ref, taken, ...) * scale).astype(out_ref.dtype)


def finish(keep, taken, scale):
    return local_call(
        functools.partial(finish_body, scale), struct(keep.shape, BF16), [keep, *taken]
    )


def finish_both_body(scale, received, *refs):
    outs = refs[-2:]
    cut = outs[0].shape[0]
    row = 0
    for keep_ref, *taken in (refs[: 1 + received], refs[1 + received : -2]):
        low = (total_of(keep_ref, taken, ...) * scale).astype(BF16)
        end = row + keep_ref.shape[0]
        for out, first, last in ((outs[0], 0, cut), (outs[1], cut, cut + outs[1].shape[0])):
            top, bottom = max(row, first), min(end, last)
            if top < bottom:
                out[top - first : bottom - first, :] = low[top - row : bottom - row, :]
        row = end


def place_body(level, along, *refs):
    *parts, out_ref = refs
    me = position(level)
    width = parts[0].shape[along]
    for step, ref in enumerate(parts):
        at = pl.multiple_of((me ^ step) * width, width)
        if along == 0:
            out_ref[pl.ds(at, width), :] = ref[...]
        else:
            out_ref[:, pl.ds(at, width)] = ref[...]


def place(parts, level, along):
    shape = list(parts[0].shape)
    shape[along] *= level[0]
    return local_call(functools.partial(place_body, level, along), struct(shape, BF16), parts)


def turned(row, width):
    return jnp.transpose(jnp.broadcast_to(row, (width, row.shape[1])))


def local_body(depth, sizes, *refs):
    r_ref, l_ref, h_ref, o_ref, m_ref, pot_ref, v_ref, e_ref = refs[:8]
    first_ref, many_ref, out_ref, mask_ref = refs[8:]
    plane = GY * GZ
    reach = 6

    def plane_at(j):
        if j < 0:
            ref, k = l_ref, j + reach
        elif j < depth:
            ref, k = r_ref, j
        else:
            ref, k = h_ref, j - depth
        return ref[:, k * plane : (k + 1) * plane]

    group_rows, blk = sizes
    energy = turned(e_ref[...], plane)
    for j in range(depth):
        cols = slice(j * plane, (j + 1) * plane)
        low = plane_at(j)
        total = jnp.dot(low, m_ref[0], preferred_element_type=F32)
        total = total + jnp.dot(low, m_ref[1], preferred_element_type=F32)
        for offset in range(1, 7):
            pair = plane_at(j + offset).astype(F32) + plane_at(j - offset).astype(F32)
            total = total + (KINETIC * COEFFS[offset]) * pair
        total = total + (energy - pot_ref[:, cols]) * low.astype(F32)
        out_ref[:, cols] = total - v_ref[:, cols] * o_ref[:, cols].astype(F32)
    width = mask_ref.shape[1]
    block = lax.broadcasted_iota(jnp.int32, mask_ref.shape, 1) // blk
    block = (block + (pl.program_id(0) * (group_rows // blk) - REACH)).astype(F32)
    lowest = turned(first_ref[...].astype(F32), width)
    inside = (block >= lowest) & (block < lowest + turned(many_ref[...].astype(F32), width))
    mask_ref[...] = jnp.where(inside, 1.0, 0.0).astype(BF16)


def local_part(response, low, high, orbitals, matrix, lines, bounds, group_rows, width, blk):
    bands, cells = response.shape
    depth = cells // (GY * GZ)
    outs = [struct((bands, cells), F32), struct((bands, width), BF16)]
    here = pl.BlockSpec((group_rows, cells), lambda i: (i, 0))
    side = pl.BlockSpec((group_rows, low.shape[1]), lambda i: (i, 0))
    line = pl.BlockSpec((1, cells), lambda i: (0, 0))
    band = pl.BlockSpec((1, group_rows), lambda i: (0, i))
    return pl.pallas_call(
        functools.partial(local_body, depth, (group_rows, blk)),
        grid=(bands // group_rows,),
        out_shape=outs,
        in_specs=[
            here,
            side,
            side,
            here,
            pl.BlockSpec(matrix.shape, lambda i: (0, 0, 0)),
            line,
            line,
            band,
            band,
            band,
        ],
        out_specs=[here, pl.BlockSpec((group_rows, width), lambda i: (i, 0))],
        compiler_params=params(),
        cost_estimate=cost(2 * bands * cells * 300, low, high, low, low, *outs),
    )(response, low, high, orbitals, matrix, *lines, *bounds)


def pad_body(edge, o_ref, pad_ref):
    bands, cells = o_ref.shape
    pad_ref[:edge, :] = jnp.zeros((edge, cells), pad_ref.dtype)
    pad_ref[edge : edge + bands, :] = o_ref[...]
    pad_ref[edge + bands :, :] = jnp.zeros((edge, cells), pad_ref.dtype)


def pad_orbitals(orbitals, blk):
    bands, cells = orbitals.shape
    edge = REACH * blk
    return local_call(
        functools.partial(pad_body, edge),
        struct((bands + 2 * edge, cells), orbitals.dtype),
        [orbitals],
    )


def subgroup(shape, blk):
    return lax.broadcasted_iota(jnp.int32, shape, 1) // (2 * blk)


def packed(sums, blk):
    rows = sums.shape[0]
    sub = 2 * blk
    near, far = sums[:, :rows], sums[:, rows:]
    column = subgroup((rows, rows), blk)
    row = lax.broadcasted_iota(jnp.int32, (rows, rows), 0) // sub
    main = jnp.where(column >= row, near, far)
    rest = far[:sub, :]
    for k in range(1, rows // sub):
        rest = jnp.where(column[:sub, :] == k, far[k * sub : (k + 1) * sub, :], rest)
    return main, rest


def unpacked(main, rest, blk):
    rows = main.shape[0]
    sub = 2 * blk
    column = subgroup((rows, rows), blk)
    row = lax.broadcasted_iota(jnp.int32, (rows, rows), 0) // sub
    near = jnp.where(column >= row, main, 0.0)
    last = jnp.where(column == row, jnp.concatenate([rest] * (rows // sub), axis=0), 0.0)
    return near, jnp.where(column < row, main, last)


def apply_body(core, across, block, group_rows, blk, other, *refs):
    size = across[0]
    blocks = refs[: size + 1]
    p_ref, base_ref, pad_ref, u_ref, s_ref, c_ref = refs[size + 1 :]
    rows, cells = u_ref.shape
    c, x = position(core), position(across)
    side = 1 - c if other else c
    first = blocks[0].shape[0]
    for step, ref in enumerate(blocks[:size]):
        at = (x ^ step) * block
        c_ref[pl.ds(pl.multiple_of(at, 16), first), :] = ref[...]
    rest = block - first
    for i in range(size):
        there = slice(i * block + first, (i + 1) * block)
        c_ref[there, :] = blocks[size][i * rest : (i + 1) * rest, :]
    mine = pl.ds(pl.multiple_of(side * rows, rows), rows)
    tile = 256 if cells % 256 == 0 else 128
    for t in range(cells // tile):
        cols = slice(t * tile, (t + 1) * tile)
        u_ref[:, cols] = base_ref[mine, cols] + jnp.dot(
            c_ref[...], p_ref[:, cols], preferred_element_type=F32
        )
    height = group_rows + 2 * blk
    for g in range(rows // group_rows):
        start = pl.multiple_of(side * rows + g * group_rows, group_rows)
        sums = lax.dot_general(
            u_ref[g * group_rows : (g + 1) * group_rows, :].astype(BF16),
            pad_ref[pl.ds(start, 2 * group_rows), :],
            NT,
            preferred_element_type=F32,
        )
        main, rest_sums = packed(sums, blk)
        s_ref[g * height : g * height + group_rows, :] = main.astype(s_ref.dtype)
        s_ref[g * height + group_rows : (g + 1) * height, :] = rest_sums.astype(s_ref.dtype)


def apply(blocks, projectors, base, padded, core, across, block, group_rows, blk, other):
    bands, cells = base.shape
    rows = bands // 2
    count = projectors.shape[0]
    height = rows // group_rows * (group_rows + 2 * blk)
    return local_call(
        functools.partial(apply_body, core, across, block, group_rows, blk, other),
        [struct((rows, cells), F32), struct((height, group_rows), BF16 if other else F32)],
        [*blocks, projectors, base, padded],
        flops=2 * rows * cells * (count + 2 * group_rows),
        scratch=[pltpu.VMEM((rows, count), BF16)],
    )


def sum_body(keep_ref, *refs):
    *taken, total_ref, low_ref = refs
    total = total_of(keep_ref, taken, ...)
    total_ref[...] = total
    low_ref[...] = total.astype(BF16)


def add_up(keep, taken):
    outs = [struct(keep.shape, F32), struct(keep.shape, BF16)]
    return local_call(sum_body, outs, [keep, *taken])


def project_body(core, blk, *refs):
    w_own, w_other, u_own, u_other, pad_ref, r_ref, mask_ref = refs[:7]
    updated_ref, residual_ref, w_ref, u_ref = refs[7:]
    rows = u_ref.shape[0]
    height = w_ref.shape[0]
    per = u_own.shape[0] // rows
    g = pl.program_id(0)
    own = lax.div(g, jnp.int32(per)) == position(core)
    local = lax.rem(g, jnp.int32(per))
    w_rows = pl.ds(pl.multiple_of(local * height, 16), height)
    u_rows = pl.ds(pl.multiple_of(local * rows, rows), rows)

    @pl.when(own)
    def _():
        w_ref[...] = w_own[w_rows, :]
        u_ref[...] = u_own[u_rows, :]

    @pl.when(jnp.logical_not(own))
    def _():
        w_ref[...] = w_other[w_rows, :]
        u_ref[...] = u_other[u_rows, :]

    main, rest = w_ref[:rows, :].astype(F32), w_ref[rows:, :].astype(F32)
    start = pl.multiple_of(g * rows, rows)
    residual = u_ref[...]
    for k, part in enumerate(unpacked(main, rest, blk)):
        inside = mask_ref[:, k * rows : (k + 1) * rows].astype(F32) > 0.5
        weights = jnp.where(inside, part, 0.0).astype(BF16)
        window = pad_ref[pl.ds(pl.multiple_of(start + k * rows, rows), rows), :]
        residual = residual - jnp.dot(weights, window, preferred_element_type=F32)
    residual_ref[...] = residual.astype(BF16)
    updated_ref[...] = (r_ref[...].astype(F32) + STEP_SIZE * residual).astype(BF16)


def project(weights, unprojected, padded, response, mask, core, group_rows, blk):
    bands, cells = response.shape
    out = struct((bands, cells), BF16)
    here = pl.BlockSpec((group_rows, cells), lambda g: (g, 0))

    def full(a):
        return pl.BlockSpec(a.shape, lambda g: (0, 0))

    return pl.pallas_call(
        functools.partial(project_body, core, blk),
        grid=(bands // group_rows,),
        out_shape=(out, out),
        in_specs=[
            *[full(a) for a in (*weights, *unprojected, padded)],
            here,
            pl.BlockSpec((group_rows, mask.shape[1]), lambda g: (g, 0)),
        ],
        out_specs=(here, here),
        scratch_shapes=[
            pltpu.VMEM((group_rows + 2 * blk, group_rows), BF16),
            pltpu.VMEM((group_rows, cells), F32),
        ],
        compiler_params=params(),
        cost_estimate=cost(
            4 * bands * group_rows * cells, padded, *unprojected, response, out, out
        ),
    )(*weights, *unprojected, padded, response, mask)


def shards(
    count, response, orbitals, projectors, potential, perturbing, energies, window_start, block_count
):
    bands, local_cells = response.shape
    cells = local_cells * count
    projections = projectors.shape[0]
    halo = 6 * GY * GZ
    core, across, along = levels_of(count)
    ace_scale = 1.0 / math.sqrt(cells * projections)
    window_scale = 1.0 / math.sqrt(cells * bands)
    blk = bands // NBLK
    group_rows = GROUP_BLOCKS * blk
    width = 2 * group_rows
    half = bands // 2
    block = half // across[0]
    first = max(16, round(REDUCE_SHARE * block / 16) * 16)
    gather_first = max(16, round(GATHER_SHARE * block / 16) * 16)
    matrix = jnp.asarray(plane_matrix())
    lines = (potential[None, :], perturbing[None, :])
    bounds = tuple(a[None, :] for a in (energies, window_start, block_count))

    def to(array, level):
        return [swapped(array, count, level, k) for k in range(1, level[0])]

    def parts_to(parts, level):
        return [swapped(part, count, level, k + 1) for k, part in enumerate(parts)]

    low = neighbour(response[:, local_cells - halo :], count, 1)
    high = neighbour(response[:, :halo], count, -1)

    *sent, keep_x, keep_z = first_sums(response, projectors, core, block, first)
    sent = [swapped(part, count, core, 1) for part in sent]
    keep_z, *parts_z = local_call(
        functools.partial(first_z_body, along, block, first),
        shares_of((keep_z.shape[0], projections // along[0]), along[0]),
        [keep_z, *sent],
    )
    keep_x, parts_z[0] = lax.optimization_barrier((keep_x, parts_z[0]))
    keep_x, *parts_x = local_call(
        functools.partial(first_x_body, across, block),
        shares_of((first, projections), across[0]),
        [keep_x, *sent],
    )
    parts_z[-1], low = lax.optimization_barrier((parts_z[-1], low))
    taken_z, taken_x, low, high = lax.optimization_barrier(
        (parts_to(parts_z, along), parts_to(parts_x, across), low, high)
    )
    keep_x, *parts_x = split(keep_x, taken_x, along, 1)
    keep_z, *parts_z = split(keep_z, taken_z, across, 0)
    taken_x, taken_z = lax.optimization_barrier(
        (parts_to(parts_x, along), parts_to(parts_z, across))
    )
    share_x, share_z = local_call(
        functools.partial(finish_both_body, ace_scale, len(taken_x)),
        [
            struct((gather_first, projections // along[0]), BF16),
            struct((block - gather_first, projections // along[0]), BF16),
        ],
        [keep_x, *taken_x, keep_z, *taken_z],
    )

    pieces_x, pieces_z, bounds = lax.optimization_barrier(
        ([share_x, *to(share_x, along)], [share_z, *to(share_z, across)], bounds)
    )
    base, mask = local_part(
        response, low, high, orbitals, matrix, lines, bounds, group_rows, width, blk
    )
    block_x = place(pieces_x, along, 1)
    block_z = place(pieces_z, across, 0)
    blocks_x = [block_x, *to(block_x, across)]
    pieces_z, base, padded = lax.optimization_barrier(
        ([block_z, *to(block_z, along)], base, pad_orbitals(orbitals, blk))
    )
    blocks = [*blocks_x, place(pieces_z, along, 1)]
    others = [swapped(part, count, core, 1) for part in blocks]
    sizes = (core, across, block, group_rows, blk)
    wide, keep = apply(blocks, projectors, base, padded, *sizes, False)
    others, keep = lax.optimization_barrier((others, keep))
    other_wide, part = apply(others, projectors, base, padded, *sizes, True)
    unprojected = (wide, other_wide)
    total, part = add_up(keep, to(part, core))
    total, part = add_up(total, to(part, across))
    own = finish(total, to(part, along), window_scale)
    weights = (own, *to(own, core))
    return project(weights, unprojected, padded, response, mask, core, group_rows, blk)


def solution(mesh):
    in_specs = (
        P("pert", "band"),
        P(None, "band"),
        P(None, "band"),
        P("band"),
        P(("pert", "band")),
        P(),
        P(),
        P(),
    )
    out_specs = (P("pert", "band"), P("pert", "band"))
    body = functools.partial(shards, mesh.shape["band"])
    return jax.shard_map(body, mesh=mesh, in_specs=in_specs, out_specs=out_specs, check_vma=False)
```

```python
import functools
import math

import jax
import jax.numpy as jnp
import ml_dtypes
import numpy as np
from jax import lax
from jax.experimental import pallas as pl
from jax.experimental.pallas import tpu as pltpu
from jax.sharding import PartitionSpec as P

GY = 8
GZ = 16
NBLK = 32
REACH = 4
GROUP_BLOCKS = 8
COEFFS = (
    -5369.0 / 1800.0,
    12.0 / 7.0,
    -15.0 / 56.0,
    10.0 / 189.0,
    -1.0 / 112.0,
    2.0 / 1925.0,
    -1.0 / 16632.0,
)
KINETIC = 0.125
STEP_SIZE = 0.3
MIB = 1024 * 1024
VMEM_BYTES = 24 * MIB
REDUCE_SHARE = 0.625
GATHER_SHARE = 0.5
BF16 = jnp.bfloat16
F32 = jnp.float32
NT = (((1,), (1,)), ((), ()))


def levels_of(count):
    chips = count // 2
    across = 2 ** (int(math.log2(chips)) // 3)
    return (2, 1), (across, 2), (chips // across, 2 * across)


def position(level):
    size, stride = level
    return lax.rem(lax.div(lax.axis_index("band"), jnp.int32(stride)), jnp.int32(size))


def neighbour(array, count, step):
    return lax.ppermute(array, "band", [(i, (i + step) % count) for i in range(count)])


def swapped(array, count, level, step):
    size, stride = level
    pairs = []
    for device in range(count):
        place = device // stride % size
        pairs.append((device, device + ((place ^ step) - place) * stride))
    return lax.ppermute(array, "band", pairs)


def plane_matrix():
    plane = GY * GZ
    matrix = 3.0 * COEFFS[0] * np.eye(plane)
    cells = np.arange(plane)
    y, z = cells // GZ, cells % GZ
    for offset in range(1, 7):
        for sign in (1, -1):
            np.add.at(matrix, ((y + sign * offset) % GY * GZ + z, cells), COEFFS[offset])
            np.add.at(matrix, (y * GZ + (z + sign * offset) % GZ, cells), COEFFS[offset])
    matrix = KINETIC * matrix
    high = matrix.astype(ml_dtypes.bfloat16)
    low = (matrix - high.astype(np.float64)).astype(ml_dtypes.bfloat16)
    return np.stack([high, low])


def whole():
    return pl.BlockSpec(memory_space=pltpu.VMEM)


def params(size=VMEM_BYTES):
    return pltpu.CompilerParams(vmem_limit_bytes=size)


def cost(flops, *arrays):
    moved = sum(math.prod(a.shape) * jnp.dtype(a.dtype).itemsize for a in arrays)
    return pl.CostEstimate(flops=int(flops), bytes_accessed=int(moved), transcendentals=0)


def local_call(body, outs, args, flops=0, scratch=()):
    return pl.pallas_call(
        body,
        out_shape=outs,
        in_specs=[whole() for _ in args],
        out_specs=jax.tree.map(lambda _: whole(), outs),
        scratch_shapes=scratch,
        compiler_params=params(),
        cost_estimate=cost(flops, *args, *jax.tree.leaves(outs)),
    )(*args)


def struct(shape, dtype):
    return jax.ShapeDtypeStruct(shape, dtype)


def cut(part, block, x_ref, z_ref, cols):
    size = part.shape[0] // block
    first, rest = x_ref.shape[0] // size, z_ref.shape[0] // size
    part = part.astype(x_ref.dtype)
    for i in range(size):
        x_ref[i * first : (i + 1) * first, cols] = part[i * block : i * block + first, :]
        z_ref[i * rest : (i + 1) * rest, cols] = part[i * block + first : (i + 1) * block, :]


def first_body(core, block, tile, r_ref, p_ref, *refs):
    sent_low, sent_high, keep_x, keep_z, r_held, p_held, r_sem, p_sem = refs
    width = sent_low.shape[1]
    rows = r_held.shape[0] // 2
    r_copy = pltpu.make_async_copy(r_ref, r_held, r_sem)
    r_copy.start()
    copies = []
    for t in range(p_held.shape[0] // tile):
        part = pl.ds(t * tile, tile)
        copies.append(pltpu.make_async_copy(p_ref.at[part, :], p_held.at[part, :], p_sem.at[t]))
        copies[-1].start()
    c = position(core)
    r_copy.wait()
    for t, copy in enumerate(copies):
        copy.wait()
        cols = slice(t * tile, (t + 1) * tile)
        for side in (1 - c, c):
            part = lax.dot_general(
                r_held[pl.ds(pl.multiple_of(side * rows, rows), rows), :],
                p_held[cols, :],
                NT,
                preferred_element_type=F32,
            )
            if side is c:
                cut(part, block, keep_x, keep_z, cols)
            else:
                ref, first = (sent_low, 0) if t * tile < width else (sent_high, width)
                ref[:, t * tile - first : (t + 1) * tile - first] = part.astype(BF16)


def first_sums(response, projectors, core, block, first):
    bands, cells = response.shape
    count = projectors.shape[0]
    rows = bands // 2
    tile = min(512, count // 2)
    rows_x = rows // block * first
    outs = [struct((rows, count // 2), BF16)] * 2
    outs += [struct((n, count), F32) for n in (rows_x, rows - rows_x)]
    return pl.pallas_call(
        functools.partial(first_body, core, block, tile),
        out_shape=outs,
        in_specs=[pl.BlockSpec(memory_space=pltpu.HBM)] * 2,
        out_specs=[whole() for _ in outs],
        scratch_shapes=[
            pltpu.VMEM((bands, cells), response.dtype),
            pltpu.VMEM((count, cells), projectors.dtype),
            pltpu.SemaphoreType.DMA,
            pltpu.SemaphoreType.DMA((count // tile,)),
        ],
        compiler_params=params(),
        cost_estimate=cost(2 * bands * cells * count, projectors, *outs),
    )(
        pltpu.with_memory_space_constraint(response, pltpu.HBM),
        pltpu.with_memory_space_constraint(projectors, pltpu.HBM),
    )


def rows_at(place, size):
    return pl.ds(pl.multiple_of(place * size, 16), size)


def cols_at(place, size):
    return pl.ds(pl.multiple_of(place * size, size), size)


def total_of(keep_ref, taken, part):
    total = keep_ref[part]
    for ref in taken:
        total = total + ref[part].astype(F32)
    return total


def first_x_body(level, block, keep_ref, low_ref, high_ref, *outs):
    me = position(level)
    rows = outs[0].shape[0]
    half = low_ref.shape[1]
    for step, out in enumerate(outs):
        at = me ^ step
        mine = rows_at(at, rows)
        theirs = pl.ds(pl.multiple_of(at * block, 16), rows)
        for k, ref in enumerate((low_ref, high_ref)):
            cols = slice(k * half, (k + 1) * half)
            out[:, cols] = (keep_ref[mine, cols] + ref[theirs, :].astype(F32)).astype(out.dtype)


def first_z_body(level, block, first, keep_ref, low_ref, high_ref, *outs):
    me = position(level)
    rows = block - first
    width = outs[0].shape[1]
    per = low_ref.shape[1] // width
    for step, out in enumerate(outs):
        at = me ^ step
        cols = cols_at(at, width)
        near = cols_at(lax.rem(at, jnp.int32(per)), width)
        for i in range(out.shape[0] // rows):
            mine = slice(i * rows, (i + 1) * rows)
            theirs = slice(i * block + first, (i + 1) * block)
            taken = jnp.where(at < per, low_ref[theirs, near], high_ref[theirs, near])
            out[mine, :] = (keep_ref[mine, cols] + taken.astype(F32)).astype(out.dtype)


def split_body(received, level, along, *refs):
    keep_ref, taken, outs = refs[0], refs[1 : 1 + received], refs[1 + received :]
    me = position(level)
    rows, width = outs[0].shape
    for step, out in enumerate(outs):
        at = me ^ step
        if along == 0:
            part = (rows_at(at, rows), slice(None))
        else:
            part = (slice(None), cols_at(at, width))
        out[...] = total_of(keep_ref, taken, part).astype(out.dtype)


def shares_of(shape, count):
    return [struct(shape, F32)] + [struct(shape, BF16)] * (count - 1)


def split(keep, taken, level, along):
    shape = list(keep.shape)
    shape[along] //= level[0]
    return local_call(
        functools.partial(split_body, len(taken), level, along),
        shares_of(shape, level[0]),
        [keep, *taken],
    )


def finish_body(scale, keep_ref, *refs):
    *taken, out_ref = refs
    out_ref[...] = (total_of(keep_ref, taken, ...) * scale).astype(out_ref.dtype)


def finish(keep, taken, scale):
    return local_call(
        functools.partial(finish_body, scale), struct(keep.shape, BF16), [keep, *taken]
    )


def finish_both_body(scale, received, *refs):
    outs = refs[-2:]
    cut = outs[0].shape[0]
    row = 0
    for keep_ref, *taken in (refs[: 1 + received], refs[1 + received : -2]):
        low = (total_of(keep_ref, taken, ...) * scale).astype(BF16)
        end = row + keep_ref.shape[0]
        for out, first, last in ((outs[0], 0, cut), (outs[1], cut, cut + outs[1].shape[0])):
            top, bottom = max(row, first), min(end, last)
            if top < bottom:
                out[top - first : bottom - first, :] = low[top - row : bottom - row, :]
        row = end


def place_body(level, along, *refs):
    *parts, out_ref = refs
    me = position(level)
    width = parts[0].shape[along]
    for step, ref in enumerate(parts):
        at = pl.multiple_of((me ^ step) * width, width)
        if along == 0:
            out_ref[pl.ds(at, width), :] = ref[...]
        else:
            out_ref[:, pl.ds(at, width)] = ref[...]


def place(parts, level, along):
    shape = list(parts[0].shape)
    shape[along] *= level[0]
    return local_call(functools.partial(place_body, level, along), struct(shape, BF16), parts)


def turned(row, width):
    return jnp.transpose(jnp.broadcast_to(row, (width, row.shape[1])))


def local_body(depth, sizes, *refs):
    r_ref, l_ref, h_ref, o_ref, m_ref, pot_ref, v_ref, e_ref = refs[:8]
    first_ref, many_ref, out_ref, mask_ref = refs[8:]
    plane = GY * GZ
    reach = 6

    def plane_at(j):
        if j < 0:
            ref, k = l_ref, j + reach
        elif j < depth:
            ref, k = r_ref, j
        else:
            ref, k = h_ref, j - depth
        return ref[:, k * plane : (k + 1) * plane]

    group_rows, blk = sizes
    energy = turned(e_ref[...], plane)
    for j in range(depth):
        cols = slice(j * plane, (j + 1) * plane)
        low = plane_at(j)
        total = jnp.dot(low, m_ref[0], preferred_element_type=F32)
        total = total + jnp.dot(low, m_ref[1], preferred_element_type=F32)
        for offset in range(1, 7):
            pair = plane_at(j + offset).astype(F32) + plane_at(j - offset).astype(F32)
            total = total + (KINETIC * COEFFS[offset]) * pair
        total = total + (energy - pot_ref[:, cols]) * low.astype(F32)
        out_ref[:, cols] = total - v_ref[:, cols] * o_ref[:, cols].astype(F32)
    width = mask_ref.shape[1]
    block = lax.broadcasted_iota(jnp.int32, mask_ref.shape, 1) // blk
    block = (block + (pl.program_id(0) * (group_rows // blk) - REACH)).astype(F32)
    lowest = turned(first_ref[...].astype(F32), width)
    inside = (block >= lowest) & (block < lowest + turned(many_ref[...].astype(F32), width))
    mask_ref[...] = jnp.where(inside, 1.0, 0.0).astype(BF16)


def local_part(response, low, high, orbitals, matrix, lines, bounds, group_rows, width, blk):
    bands, cells = response.shape
    depth = cells // (GY * GZ)
    outs = [struct((bands, cells), F32), struct((bands, width), BF16)]
    here = pl.BlockSpec((group_rows, cells), lambda i: (i, 0))
    side = pl.BlockSpec((group_rows, low.shape[1]), lambda i: (i, 0))
    line = pl.BlockSpec((1, cells), lambda i: (0, 0))
    band = pl.BlockSpec((1, group_rows), lambda i: (0, i))
    return pl.pallas_call(
        functools.partial(local_body, depth, (group_rows, blk)),
        grid=(bands // group_rows,),
        out_shape=outs,
        in_specs=[
            here,
            side,
            side,
            here,
            pl.BlockSpec(matrix.shape, lambda i: (0, 0, 0)),
            line,
            line,
            band,
            band,
            band,
        ],
        out_specs=[here, pl.BlockSpec((group_rows, width), lambda i: (i, 0))],
        compiler_params=params(),
        cost_estimate=cost(2 * bands * cells * 300, low, high, low, low, *outs),
    )(response, low, high, orbitals, matrix, *lines, *bounds)


def pad_body(edge, o_ref, pad_ref):
    bands, cells = o_ref.shape
    pad_ref[:edge, :] = jnp.zeros((edge, cells), pad_ref.dtype)
    pad_ref[edge : edge + bands, :] = o_ref[...]
    pad_ref[edge + bands :, :] = jnp.zeros((edge, cells), pad_ref.dtype)


def pad_orbitals(orbitals, blk):
    bands, cells = orbitals.shape
    edge = REACH * blk
    return local_call(
        functools.partial(pad_body, edge),
        struct((bands + 2 * edge, cells), orbitals.dtype),
        [orbitals],
    )


def subgroup(shape, blk):
    return lax.broadcasted_iota(jnp.int32, shape, 1) // (2 * blk)


def packed(sums, blk):
    rows = sums.shape[0]
    sub = 2 * blk
    near, far = sums[:, :rows], sums[:, rows:]
    column = subgroup((rows, rows), blk)
    row = lax.broadcasted_iota(jnp.int32, (rows, rows), 0) // sub
    main = jnp.where(column >= row, near, far)
    rest = far[:sub, :]
    for k in range(1, rows // sub):
        rest = jnp.where(column[:sub, :] == k, far[k * sub : (k + 1) * sub, :], rest)
    return main, rest


def unpacked(main, rest, blk):
    rows = main.shape[0]
    sub = 2 * blk
    column = subgroup((rows, rows), blk)
    row = lax.broadcasted_iota(jnp.int32, (rows, rows), 0) // sub
    near = jnp.where(column >= row, main, 0.0)
    last = jnp.where(column == row, jnp.concatenate([rest] * (rows // sub), axis=0), 0.0)
    return near, jnp.where(column < row, main, last)


def apply_body(core, across, block, group_rows, blk, other, *refs):
    size = across[0]
    blocks = refs[: size + 1]
    p_ref, base_ref, pad_ref, u_ref, s_ref, c_ref = refs[size + 1 :]
    rows, cells = u_ref.shape
    c, x = position(core), position(across)
    side = 1 - c if other else c
    first = blocks[0].shape[0]
    for step, ref in enumerate(blocks[:size]):
        at = (x ^ step) * block
        c_ref[pl.ds(pl.multiple_of(at, 16), first), :] = ref[...]
    rest = block - first
    for i in range(size):
        there = slice(i * block + first, (i + 1) * block)
        c_ref[there, :] = blocks[size][i * rest : (i + 1) * rest, :]
    mine = pl.ds(pl.multiple_of(side * rows, rows), rows)
    tile = 256 if cells % 256 == 0 else 128
    for t in range(cells // tile):
        cols = slice(t * tile, (t + 1) * tile)
        u_ref[:, cols] = base_ref[mine, cols] + jnp.dot(
            c_ref[...], p_ref[:, cols], preferred_element_type=F32
        )
    height = group_rows + 2 * blk
    for g in range(rows // group_rows):
        start = pl.multiple_of(side * rows + g * group_rows, group_rows)
        sums = lax.dot_general(
            u_ref[g * group_rows : (g + 1) * group_rows, :].astype(BF16),
            pad_ref[pl.ds(start, 2 * group_rows), :],
            NT,
            preferred_element_type=F32,
        )
        main, rest_sums = packed(sums, blk)
        s_ref[g * height : g * height + group_rows, :] = main.astype(s_ref.dtype)
        s_ref[g * height + group_rows : (g + 1) * height, :] = rest_sums.astype(s_ref.dtype)


def apply(blocks, projectors, base, padded, core, across, block, group_rows, blk, other):
    bands, cells = base.shape
    rows = bands // 2
    count = projectors.shape[0]
    height = rows // group_rows * (group_rows + 2 * blk)
    return local_call(
        functools.partial(apply_body, core, across, block, group_rows, blk, other),
        [struct((rows, cells), F32), struct((height, group_rows), BF16 if other else F32)],
        [*blocks, projectors, base, padded],
        flops=2 * rows * cells * (count + 2 * group_rows),
        scratch=[pltpu.VMEM((rows, count), BF16)],
    )


def sum_body(keep_ref, *refs):
    *taken, total_ref, low_ref = refs
    total = total_of(keep_ref, taken, ...)
    total_ref[...] = total
    low_ref[...] = total.astype(BF16)


def add_up(keep, taken):
    outs = [struct(keep.shape, F32), struct(keep.shape, BF16)]
    return local_call(sum_body, outs, [keep, *taken])


def project_body(core, blk, other, *refs):
    w_ref, u_ref, pad_ref, r_ref, mask_ref = refs[:5]
    outs, helds, sems = refs[-5:-3], refs[-3:-1], refs[-1]
    rows = mask_ref.shape[1] // 2
    per = u_ref.shape[0] // rows
    height = w_ref.shape[0] // per
    c = position(core)
    copies = []
    for g in range(per):
        mine = slice(g * rows, (g + 1) * rows)
        start = pl.multiple_of(((1 - c if other else c) * per + g) * rows, rows)
        there = pl.ds(start, rows)
        main = w_ref[g * height : g * height + rows, :].astype(F32)
        rest = w_ref[g * height + rows : (g + 1) * height, :].astype(F32)
        residual = u_ref[mine, :]
        for k, part in enumerate(unpacked(main, rest, blk)):
            inside = mask_ref[there, k * rows : (k + 1) * rows].astype(F32) > 0.5
            weights = jnp.where(inside, part, 0.0).astype(BF16)
            window = pad_ref[pl.ds(pl.multiple_of(start + k * rows, rows), rows), :]
            residual = residual - jnp.dot(weights, window, preferred_element_type=F32)
        updated = r_ref[there, :].astype(F32) + STEP_SIZE * residual
        for k, value in enumerate((updated, residual)):
            helds[k][mine, :] = value.astype(BF16)
            copies.append(
                pltpu.make_async_copy(
                    helds[k].at[pl.ds(g * rows, rows), :], outs[k].at[there, :], sems.at[k, g]
                )
            )
            copies[-1].start()
    for copy in copies:
        copy.wait()


def project(weights, unprojected, padded, response, mask, core, blk, other, before):
    rows, cells = unprojected.shape
    per = rows // (mask.shape[1] // 2)
    out = struct(response.shape, BF16)
    args = [weights, unprojected, padded, response, mask]
    anywhere = pl.BlockSpec(memory_space=pl.ANY)
    return pl.pallas_call(
        functools.partial(project_body, core, blk, other),
        out_shape=(out, out),
        in_specs=[whole() for _ in args] + [anywhere for _ in before],
        out_specs=(anywhere, anywhere),
        scratch_shapes=[
            pltpu.VMEM((rows, cells), BF16),
            pltpu.VMEM((rows, cells), BF16),
            pltpu.SemaphoreType.DMA((2, per)),
        ],
        input_output_aliases={5: 0, 6: 1} if before else {},
        compiler_params=params(),
        cost_estimate=cost(2 * rows * mask.shape[1] * cells, padded, unprojected, unprojected),
    )(*args, *before)


def shards(
    count, response, orbitals, projectors, potential, perturbing, energies, window_start, block_count
):
    bands, local_cells = response.shape
    cells = local_cells * count
    projections = projectors.shape[0]
    halo = 6 * GY * GZ
    core, across, along = levels_of(count)
    ace_scale = 1.0 / math.sqrt(cells * projections)
    window_scale = 1.0 / math.sqrt(cells * bands)
    blk = bands // NBLK
    group_rows = GROUP_BLOCKS * blk
    width = 2 * group_rows
    half = bands // 2
    block = half // across[0]
    first = max(16, round(REDUCE_SHARE * block / 16) * 16)
    gather_first = max(16, round(GATHER_SHARE * block / 16) * 16)
    matrix = jnp.asarray(plane_matrix())
    lines = (potential[None, :], perturbing[None, :])
    bounds = tuple(a[None, :] for a in (energies, window_start, block_count))

    def to(array, level):
        return [swapped(array, count, level, k) for k in range(1, level[0])]

    def parts_to(parts, level):
        return [swapped(part, count, level, k + 1) for k, part in enumerate(parts)]

    low = neighbour(response[:, local_cells - halo :], count, 1)
    high = neighbour(response[:, :halo], count, -1)

    *sent, keep_x, keep_z = first_sums(response, projectors, core, block, first)
    sent = [swapped(part, count, core, 1) for part in sent]
    keep_z, *parts_z = local_call(
        functools.partial(first_z_body, along, block, first),
        shares_of((keep_z.shape[0], projections // along[0]), along[0]),
        [keep_z, *sent],
    )
    keep_x, parts_z[0] = lax.optimization_barrier((keep_x, parts_z[0]))
    keep_x, *parts_x = local_call(
        functools.partial(first_x_body, across, block),
        shares_of((first, projections), across[0]),
        [keep_x, *sent],
    )
    parts_z[-1], low = lax.optimization_barrier((parts_z[-1], low))
    taken_z, taken_x, low, high = lax.optimization_barrier(
        (parts_to(parts_z, along), parts_to(parts_x, across), low, high)
    )
    keep_x, *parts_x = split(keep_x, taken_x, along, 1)
    keep_z, *parts_z = split(keep_z, taken_z, across, 0)
    base, mask = local_part(
        response, low, high, orbitals, matrix, lines, bounds, group_rows, width, blk
    )
    padded = pad_orbitals(orbitals, blk)
    taken_x, taken_z, base, padded = lax.optimization_barrier(
        (parts_to(parts_x, along), parts_to(parts_z, across), base, padded)
    )
    share_x, share_z = local_call(
        functools.partial(finish_both_body, ace_scale, len(taken_x)),
        [
            struct((gather_first, projections // along[0]), BF16),
            struct((block - gather_first, projections // along[0]), BF16),
        ],
        [keep_x, *taken_x, keep_z, *taken_z],
    )

    pieces_x, pieces_z = lax.optimization_barrier(
        ([share_x, *to(share_x, along)], [share_z, *to(share_z, across)])
    )
    block_x = place(pieces_x, along, 1)
    block_z = place(pieces_z, across, 0)
    blocks_x = [block_x, *to(block_x, across)]
    pieces_z = [block_z, *to(block_z, along)]
    blocks = [*blocks_x, place(pieces_z, along, 1)]
    others = [swapped(part, count, core, 1) for part in blocks]
    sizes = (core, across, block, group_rows, blk)
    wide, keep = apply(blocks, projectors, base, padded, *sizes, False)
    others, keep = lax.optimization_barrier((others, keep))
    other_wide, part = apply(others, projectors, base, padded, *sizes, True)
    total, part = add_up(keep, to(part, core))
    total, part = add_up(total, to(part, across))
    own = finish(total, to(part, along), window_scale)
    (theirs,) = to(own, core)
    outs = project(own, wide, padded, response, mask, core, blk, False, ())
    return project(theirs, other_wide, padded, response, mask, core, blk, True, outs)


def solution(mesh):
    in_specs = (
        P("pert", "band"),
        P(None, "band"),
        P(None, "band"),
        P("band"),
        P(("pert", "band")),
        P(),
        P(),
        P(),
    )
    out_specs = (P("pert", "band"), P("pert", "band"))
    body = functools.partial(shards, mesh.shape["band"])
    return jax.shard_map(body, mesh=mesh, in_specs=in_specs, out_specs=out_specs, check_vma=False)
```

```python
import functools
import math

import jax
import jax.numpy as jnp
import ml_dtypes
import numpy as np
from jax import lax
from jax.experimental import pallas as pl
from jax.experimental.pallas import tpu as pltpu
from jax.sharding import PartitionSpec as P

GY = 8
GZ = 16
NBLK = 32
REACH = 4
GROUP_BLOCKS = 8
COEFFS = (
    -5369.0 / 1800.0,
    12.0 / 7.0,
    -15.0 / 56.0,
    10.0 / 189.0,
    -1.0 / 112.0,
    2.0 / 1925.0,
    -1.0 / 16632.0,
)
KINETIC = 0.125
STEP_SIZE = 0.3
MIB = 1024 * 1024
VMEM_BYTES = 24 * MIB
REDUCE_SHARE = 0.625
GATHER_SHARE = 0.625
BF16 = jnp.bfloat16
F32 = jnp.float32
NT = (((1,), (1,)), ((), ()))


def levels_of(count):
    chips = count // 2
    across = 2 ** (int(math.log2(chips)) // 3)
    return (2, 1), (across, 2), (chips // across, 2 * across)


def position(level):
    size, stride = level
    return lax.rem(lax.div(lax.axis_index("band"), jnp.int32(stride)), jnp.int32(size))


def neighbour(array, count, step):
    return lax.ppermute(array, "band", [(i, (i + step) % count) for i in range(count)])


def swapped(array, count, level, step):
    size, stride = level
    pairs = []
    for device in range(count):
        place = device // stride % size
        pairs.append((device, device + ((place ^ step) - place) * stride))
    return lax.ppermute(array, "band", pairs)


def plane_matrix():
    plane = GY * GZ
    matrix = 3.0 * COEFFS[0] * np.eye(plane)
    cells = np.arange(plane)
    y, z = cells // GZ, cells % GZ
    for offset in range(1, 7):
        for sign in (1, -1):
            np.add.at(matrix, ((y + sign * offset) % GY * GZ + z, cells), COEFFS[offset])
            np.add.at(matrix, (y * GZ + (z + sign * offset) % GZ, cells), COEFFS[offset])
    matrix = KINETIC * matrix
    high = matrix.astype(ml_dtypes.bfloat16)
    low = (matrix - high.astype(np.float64)).astype(ml_dtypes.bfloat16)
    return np.stack([high, low])


def whole():
    return pl.BlockSpec(memory_space=pltpu.VMEM)


def params(size=VMEM_BYTES):
    return pltpu.CompilerParams(vmem_limit_bytes=size)


def cost(flops, *arrays):
    moved = sum(math.prod(a.shape) * jnp.dtype(a.dtype).itemsize for a in arrays)
    return pl.CostEstimate(flops=int(flops), bytes_accessed=int(moved), transcendentals=0)


def local_call(body, outs, args, flops=0, scratch=()):
    return pl.pallas_call(
        body,
        out_shape=outs,
        in_specs=[whole() for _ in args],
        out_specs=jax.tree.map(lambda _: whole(), outs),
        scratch_shapes=scratch,
        compiler_params=params(),
        cost_estimate=cost(flops, *args, *jax.tree.leaves(outs)),
    )(*args)


def struct(shape, dtype):
    return jax.ShapeDtypeStruct(shape, dtype)


def cut(part, block, x_ref, z_ref, cols):
    size = part.shape[0] // block
    first, rest = x_ref.shape[0] // size, z_ref.shape[0] // size
    part = part.astype(x_ref.dtype)
    for i in range(size):
        x_ref[i * first : (i + 1) * first, cols] = part[i * block : i * block + first, :]
        z_ref[i * rest : (i + 1) * rest, cols] = part[i * block + first : (i + 1) * block, :]


def first_body(core, block, tile, r_ref, p_ref, *refs):
    sent_low, sent_high, keep_x, keep_z, r_held, p_held, r_sem, p_sem = refs
    width = sent_low.shape[1]
    rows = r_held.shape[0] // 2
    r_copy = pltpu.make_async_copy(r_ref, r_held, r_sem)
    r_copy.start()
    copies = []
    for t in range(p_held.shape[0] // tile):
        part = pl.ds(t * tile, tile)
        copies.append(pltpu.make_async_copy(p_ref.at[part, :], p_held.at[part, :], p_sem.at[t]))
        copies[-1].start()
    c = position(core)
    r_copy.wait()
    for t, copy in enumerate(copies):
        copy.wait()
        cols = slice(t * tile, (t + 1) * tile)
        for side in (1 - c, c):
            part = lax.dot_general(
                r_held[pl.ds(pl.multiple_of(side * rows, rows), rows), :],
                p_held[cols, :],
                NT,
                preferred_element_type=F32,
            )
            if side is c:
                cut(part, block, keep_x, keep_z, cols)
            else:
                ref, first = (sent_low, 0) if t * tile < width else (sent_high, width)
                ref[:, t * tile - first : (t + 1) * tile - first] = part.astype(BF16)


def first_sums(response, projectors, core, block, first):
    bands, cells = response.shape
    count = projectors.shape[0]
    rows = bands // 2
    tile = min(512, count // 2)
    rows_x = rows // block * first
    outs = [struct((rows, count // 2), BF16)] * 2
    outs += [struct((n, count), F32) for n in (rows_x, rows - rows_x)]
    return pl.pallas_call(
        functools.partial(first_body, core, block, tile),
        out_shape=outs,
        in_specs=[pl.BlockSpec(memory_space=pltpu.HBM)] * 2,
        out_specs=[whole() for _ in outs],
        scratch_shapes=[
            pltpu.VMEM((bands, cells), response.dtype),
            pltpu.VMEM((count, cells), projectors.dtype),
            pltpu.SemaphoreType.DMA,
            pltpu.SemaphoreType.DMA((count // tile,)),
        ],
        compiler_params=params(),
        cost_estimate=cost(2 * bands * cells * count, projectors, *outs),
    )(
        pltpu.with_memory_space_constraint(response, pltpu.HBM),
        pltpu.with_memory_space_constraint(projectors, pltpu.HBM),
    )


def rows_at(place, size):
    return pl.ds(pl.multiple_of(place * size, 16), size)


def cols_at(place, size):
    return pl.ds(pl.multiple_of(place * size, size), size)


def total_of(keep_ref, taken, part):
    total = keep_ref[part]
    for ref in taken:
        total = total + ref[part].astype(F32)
    return total


def first_x_body(level, block, keep_ref, low_ref, high_ref, *outs):
    me = position(level)
    rows = outs[0].shape[0]
    half = low_ref.shape[1]
    for step, out in enumerate(outs):
        at = me ^ step
        mine = rows_at(at, rows)
        theirs = pl.ds(pl.multiple_of(at * block, 16), rows)
        for k, ref in enumerate((low_ref, high_ref)):
            cols = slice(k * half, (k + 1) * half)
            out[:, cols] = (keep_ref[mine, cols] + ref[theirs, :].astype(F32)).astype(out.dtype)


def first_z_body(level, block, first, keep_ref, low_ref, high_ref, *outs):
    me = position(level)
    rows = block - first
    width = outs[0].shape[1]
    per = low_ref.shape[1] // width
    for step, out in enumerate(outs):
        at = me ^ step
        cols = cols_at(at, width)
        near = cols_at(lax.rem(at, jnp.int32(per)), width)
        for i in range(out.shape[0] // rows):
            mine = slice(i * rows, (i + 1) * rows)
            theirs = slice(i * block + first, (i + 1) * block)
            taken = jnp.where(at < per, low_ref[theirs, near], high_ref[theirs, near])
            out[mine, :] = (keep_ref[mine, cols] + taken.astype(F32)).astype(out.dtype)


def split_body(received, level, along, *refs):
    keep_ref, taken, outs = refs[0], refs[1 : 1 + received], refs[1 + received :]
    me = position(level)
    rows, width = outs[0].shape
    for step, out in enumerate(outs):
        at = me ^ step
        if along == 0:
            part = (rows_at(at, rows), slice(None))
        else:
            part = (slice(None), cols_at(at, width))
        out[...] = total_of(keep_ref, taken, part).astype(out.dtype)


def shares_of(shape, count):
    return [struct(shape, F32)] + [struct(shape, BF16)] * (count - 1)


def split(keep, taken, level, along):
    shape = list(keep.shape)
    shape[along] //= level[0]
    return local_call(
        functools.partial(split_body, len(taken), level, along),
        shares_of(shape, level[0]),
        [keep, *taken],
    )


def finish_body(scale, keep_ref, *refs):
    *taken, out_ref = refs
    out_ref[...] = (total_of(keep_ref, taken, ...) * scale).astype(out_ref.dtype)


def finish(keep, taken, scale):
    return local_call(
        functools.partial(finish_body, scale), struct(keep.shape, BF16), [keep, *taken]
    )


def finish_both_body(scale, received, *refs):
    outs = refs[-2:]
    cut = outs[0].shape[0]
    row = 0
    for keep_ref, *taken in (refs[: 1 + received], refs[1 + received : -2]):
        low = (total_of(keep_ref, taken, ...) * scale).astype(BF16)
        end = row + keep_ref.shape[0]
        for out, first, last in ((outs[0], 0, cut), (outs[1], cut, cut + outs[1].shape[0])):
            top, bottom = max(row, first), min(end, last)
            if top < bottom:
                out[top - first : bottom - first, :] = low[top - row : bottom - row, :]
        row = end


def place_body(level, along, *refs):
    *parts, out_ref = refs
    me = position(level)
    width = parts[0].shape[along]
    for step, ref in enumerate(parts):
        at = (me ^ step) * width
        if along == 0:
            out_ref[pl.ds(pl.multiple_of(at, 16), width), :] = ref[...]
        else:
            out_ref[:, pl.ds(pl.multiple_of(at, 128), width)] = ref[...]


def place(parts, level, along):
    shape = list(parts[0].shape)
    shape[along] *= level[0]
    return local_call(functools.partial(place_body, level, along), struct(shape, BF16), parts)


def turned(row, width):
    return jnp.transpose(jnp.broadcast_to(row, (width, row.shape[1])))


def local_body(depth, sizes, *refs):
    r_ref, l_ref, h_ref, o_ref, m_ref, pot_ref, v_ref, e_ref = refs[:8]
    first_ref, many_ref, out_ref, mask_ref = refs[8:]
    plane = GY * GZ
    reach = 6

    def plane_at(j):
        if j < 0:
            ref, k = l_ref, j + reach
        elif j < depth:
            ref, k = r_ref, j
        else:
            ref, k = h_ref, j - depth
        return ref[:, k * plane : (k + 1) * plane]

    group_rows, blk = sizes
    energy = turned(e_ref[...], plane)
    for j in range(depth):
        cols = slice(j * plane, (j + 1) * plane)
        low = plane_at(j)
        total = jnp.dot(low, m_ref[0], preferred_element_type=F32)
        total = total + jnp.dot(low, m_ref[1], preferred_element_type=F32)
        for offset in range(1, 7):
            pair = plane_at(j + offset).astype(F32) + plane_at(j - offset).astype(F32)
            total = total + (KINETIC * COEFFS[offset]) * pair
        total = total + (energy - pot_ref[:, cols]) * low.astype(F32)
        out_ref[:, cols] = total - v_ref[:, cols] * o_ref[:, cols].astype(F32)
    width = mask_ref.shape[1]
    block = lax.broadcasted_iota(jnp.int32, mask_ref.shape, 1) // blk
    block = (block + (pl.program_id(0) * (group_rows // blk) - REACH)).astype(F32)
    lowest = turned(first_ref[...].astype(F32), width)
    inside = (block >= lowest) & (block < lowest + turned(many_ref[...].astype(F32), width))
    mask_ref[...] = jnp.where(inside, 1.0, 0.0).astype(BF16)


def local_part(response, low, high, orbitals, matrix, lines, bounds, group_rows, width, blk):
    bands, cells = response.shape
    depth = cells // (GY * GZ)
    outs = [struct((bands, cells), F32), struct((bands, width), BF16)]
    here = pl.BlockSpec((group_rows, cells), lambda i: (i, 0))
    side = pl.BlockSpec((group_rows, low.shape[1]), lambda i: (i, 0))
    line = pl.BlockSpec((1, cells), lambda i: (0, 0))
    band = pl.BlockSpec((1, group_rows), lambda i: (0, i))
    return pl.pallas_call(
        functools.partial(local_body, depth, (group_rows, blk)),
        grid=(bands // group_rows,),
        out_shape=outs,
        in_specs=[
            here,
            side,
            side,
            here,
            pl.BlockSpec(matrix.shape, lambda i: (0, 0, 0)),
            line,
            line,
            band,
            band,
            band,
        ],
        out_specs=[here, pl.BlockSpec((group_rows, width), lambda i: (i, 0))],
        compiler_params=params(),
        cost_estimate=cost(2 * bands * cells * 300, low, high, low, low, *outs),
    )(response, low, high, orbitals, matrix, *lines, *bounds)


def pad_body(edge, o_ref, pad_ref):
    bands, cells = o_ref.shape
    pad_ref[:edge, :] = jnp.zeros((edge, cells), pad_ref.dtype)
    pad_ref[edge : edge + bands, :] = o_ref[...]
    pad_ref[edge + bands :, :] = jnp.zeros((edge, cells), pad_ref.dtype)


def pad_orbitals(orbitals, blk):
    bands, cells = orbitals.shape
    edge = REACH * blk
    return local_call(
        functools.partial(pad_body, edge),
        struct((bands + 2 * edge, cells), orbitals.dtype),
        [orbitals],
    )


def subgroup(shape, blk):
    return lax.broadcasted_iota(jnp.int32, shape, 1) // (2 * blk)


def packed(sums, blk):
    rows = sums.shape[0]
    sub = 2 * blk
    near, far = sums[:, :rows], sums[:, rows:]
    column = subgroup((rows, rows), blk)
    row = lax.broadcasted_iota(jnp.int32, (rows, rows), 0) // sub
    main = jnp.where(column >= row, near, far)
    rest = far[:sub, :]
    for k in range(1, rows // sub):
        rest = jnp.where(column[:sub, :] == k, far[k * sub : (k + 1) * sub, :], rest)
    return main, rest


def unpacked(main, rest, blk):
    rows = main.shape[0]
    sub = 2 * blk
    column = subgroup((rows, rows), blk)
    row = lax.broadcasted_iota(jnp.int32, (rows, rows), 0) // sub
    near = jnp.where(column >= row, main, 0.0)
    last = jnp.where(column == row, jnp.concatenate([rest] * (rows // sub), axis=0), 0.0)
    return near, jnp.where(column < row, main, last)


def apply_body(core, across, block, group_rows, blk, other, *refs):
    size = across[0]
    blocks = refs[: size + 1]
    p_ref, base_ref, pad_ref, u_ref, s_ref, c_ref = refs[size + 1 :]
    rows, cells = u_ref.shape
    c, x = position(core), position(across)
    side = 1 - c if other else c
    first = blocks[0].shape[0]
    for step, ref in enumerate(blocks[:size]):
        at = (x ^ step) * block
        c_ref[pl.ds(pl.multiple_of(at, 16), first), :] = ref[...]
    rest = block - first
    for i in range(size):
        there = slice(i * block + first, (i + 1) * block)
        c_ref[there, :] = blocks[size][i * rest : (i + 1) * rest, :]
    mine = pl.ds(pl.multiple_of(side * rows, rows), rows)
    tile = 256 if cells % 256 == 0 else 128
    for t in range(cells // tile):
        cols = slice(t * tile, (t + 1) * tile)
        u_ref[:, cols] = base_ref[mine, cols] + jnp.dot(
            c_ref[...], p_ref[:, cols], preferred_element_type=F32
        )
    height = group_rows + 2 * blk
    for g in range(rows // group_rows):
        start = pl.multiple_of(side * rows + g * group_rows, group_rows)
        sums = lax.dot_general(
            u_ref[g * group_rows : (g + 1) * group_rows, :].astype(BF16),
            pad_ref[pl.ds(start, 2 * group_rows), :],
            NT,
            preferred_element_type=F32,
        )
        main, rest_sums = packed(sums, blk)
        s_ref[g * height : g * height + group_rows, :] = main.astype(s_ref.dtype)
        s_ref[g * height + group_rows : (g + 1) * height, :] = rest_sums.astype(s_ref.dtype)


def apply(blocks, projectors, base, padded, core, across, block, group_rows, blk, other):
    bands, cells = base.shape
    rows = bands // 2
    count = projectors.shape[0]
    height = rows // group_rows * (group_rows + 2 * blk)
    return local_call(
        functools.partial(apply_body, core, across, block, group_rows, blk, other),
        [struct((rows, cells), F32), struct((height, group_rows), BF16 if other else F32)],
        [*blocks, projectors, base, padded],
        flops=2 * rows * cells * (count + 2 * group_rows),
        scratch=[pltpu.VMEM((rows, count), BF16)],
    )


def sum_body(keep_ref, *refs):
    *taken, total_ref, low_ref = refs
    total = total_of(keep_ref, taken, ...)
    total_ref[...] = total
    low_ref[...] = total.astype(BF16)


def add_up(keep, taken):
    outs = [struct(keep.shape, F32), struct(keep.shape, BF16)]
    return local_call(sum_body, outs, [keep, *taken])


def project_body(core, blk, other, *refs):
    w_ref, u_ref, pad_ref, r_ref, mask_ref = refs[:5]
    outs, helds, sems = refs[-5:-3], refs[-3:-1], refs[-1]
    rows = mask_ref.shape[1] // 2
    per = u_ref.shape[0] // rows
    height = w_ref.shape[0] // per
    c = position(core)
    copies = []
    for g in range(per):
        mine = slice(g * rows, (g + 1) * rows)
        start = pl.multiple_of(((1 - c if other else c) * per + g) * rows, rows)
        there = pl.ds(start, rows)
        main = w_ref[g * height : g * height + rows, :].astype(F32)
        rest = w_ref[g * height + rows : (g + 1) * height, :].astype(F32)
        residual = u_ref[mine, :]
        for k, part in enumerate(unpacked(main, rest, blk)):
            inside = mask_ref[there, k * rows : (k + 1) * rows].astype(F32) > 0.5
            weights = jnp.where(inside, part, 0.0).astype(BF16)
            window = pad_ref[pl.ds(pl.multiple_of(start + k * rows, rows), rows), :]
            residual = residual - jnp.dot(weights, window, preferred_element_type=F32)
        updated = r_ref[there, :].astype(F32) + STEP_SIZE * residual
        for k, value in enumerate((updated, residual)):
            helds[k][mine, :] = value.astype(BF16)
            copies.append(
                pltpu.make_async_copy(
                    helds[k].at[pl.ds(g * rows, rows), :], outs[k].at[there, :], sems.at[k, g]
                )
            )
            copies[-1].start()
    for copy in copies:
        copy.wait()


def project(weights, unprojected, padded, response, mask, core, blk, other, before):
    rows, cells = unprojected.shape
    per = rows // (mask.shape[1] // 2)
    out = struct(response.shape, BF16)
    args = [weights, unprojected, padded, response, mask]
    anywhere = pl.BlockSpec(memory_space=pl.ANY)
    return pl.pallas_call(
        functools.partial(project_body, core, blk, other),
        out_shape=(out, out),
        in_specs=[whole() for _ in args] + [anywhere for _ in before],
        out_specs=(anywhere, anywhere),
        scratch_shapes=[
            pltpu.VMEM((rows, cells), BF16),
            pltpu.VMEM((rows, cells), BF16),
            pltpu.SemaphoreType.DMA((2, per)),
        ],
        input_output_aliases={5: 0, 6: 1} if before else {},
        compiler_params=params(),
        cost_estimate=cost(2 * rows * mask.shape[1] * cells, padded, unprojected, unprojected),
    )(*args, *before)


def shards(
    count, response, orbitals, projectors, potential, perturbing, energies, window_start, block_count
):
    bands, local_cells = response.shape
    cells = local_cells * count
    projections = projectors.shape[0]
    halo = 6 * GY * GZ
    core, across, along = levels_of(count)
    ace_scale = 1.0 / math.sqrt(cells * projections)
    window_scale = 1.0 / math.sqrt(cells * bands)
    blk = bands // NBLK
    group_rows = GROUP_BLOCKS * blk
    width = 2 * group_rows
    half = bands // 2
    block = half // across[0]
    first = max(16, round(REDUCE_SHARE * block / 16) * 16)
    gather_first = max(16, round(GATHER_SHARE * block / 16) * 16)
    matrix = jnp.asarray(plane_matrix())
    lines = (potential[None, :], perturbing[None, :])
    bounds = tuple(a[None, :] for a in (energies, window_start, block_count))

    def to(array, level):
        return [swapped(array, count, level, k) for k in range(1, level[0])]

    def parts_to(parts, level):
        return [swapped(part, count, level, k + 1) for k, part in enumerate(parts)]

    low = neighbour(response[:, local_cells - halo :], count, 1)
    high = neighbour(response[:, :halo], count, -1)

    *sent, keep_x, keep_z = first_sums(response, projectors, core, block, first)
    sent = [swapped(part, count, core, 1) for part in sent]
    keep_z, *parts_z = local_call(
        functools.partial(first_z_body, along, block, first),
        shares_of((keep_z.shape[0], projections // along[0]), along[0]),
        [keep_z, *sent],
    )
    keep_x, parts_z[0] = lax.optimization_barrier((keep_x, parts_z[0]))
    keep_x, *parts_x = local_call(
        functools.partial(first_x_body, across, block),
        shares_of((first, projections), across[0]),
        [keep_x, *sent],
    )
    parts_z[-1], low = lax.optimization_barrier((parts_z[-1], low))
    taken_z, taken_x, low, high = lax.optimization_barrier(
        (parts_to(parts_z, along), parts_to(parts_x, across), low, high)
    )
    keep_x, *parts_x = split(keep_x, taken_x, along, 1)
    keep_z, *parts_z = split(keep_z, taken_z, across, 0)
    base, mask = local_part(
        response, low, high, orbitals, matrix, lines, bounds, group_rows, width, blk
    )
    padded = pad_orbitals(orbitals, blk)
    taken_x, taken_z, base, padded = lax.optimization_barrier(
        (parts_to(parts_x, along), parts_to(parts_z, across), base, padded)
    )
    share_x, share_z = local_call(
        functools.partial(finish_both_body, ace_scale, len(taken_x)),
        [
            struct((gather_first, projections // along[0]), BF16),
            struct((block - gather_first, projections // along[0]), BF16),
        ],
        [keep_x, *taken_x, keep_z, *taken_z],
    )

    pieces_x, pieces_z = lax.optimization_barrier(
        ([share_x, *to(share_x, along)], [share_z, *to(share_z, across)])
    )
    block_x = place(pieces_x, along, 1)
    block_z = place(pieces_z, across, 0)
    blocks_x = [block_x, *to(block_x, across)]
    pieces_z = [block_z, *to(block_z, along)]
    blocks = [*blocks_x, place(pieces_z, along, 1)]
    others = [swapped(part, count, core, 1) for part in blocks]
    sizes = (core, across, block, group_rows, blk)
    wide, keep = apply(blocks, projectors, base, padded, *sizes, False)
    others, keep = lax.optimization_barrier((others, keep))
    other_wide, part = apply(others, projectors, base, padded, *sizes, True)
    total, part = add_up(keep, to(part, core))
    total, part = add_up(total, to(part, across))
    own = finish(total, to(part, along), window_scale)
    (theirs,) = to(own, core)
    outs = project(own, wide, padded, response, mask, core, blk, False, ())
    return project(theirs, other_wide, padded, response, mask, core, blk, True, outs)


def solution(mesh):
    in_specs = (
        P("pert", "band"),
        P(None, "band"),
        P(None, "band"),
        P("band"),
        P(("pert", "band")),
        P(),
        P(),
        P(),
    )
    out_specs = (P("pert", "band"), P("pert", "band"))
    body = functools.partial(shards, mesh.shape["band"])
    return jax.shard_map(body, mesh=mesh, in_specs=in_specs, out_specs=out_specs, check_vma=False)
```

```python
import functools
import math

import jax
import jax.numpy as jnp
import ml_dtypes
import numpy as np
from jax import lax
from jax.experimental import pallas as pl
from jax.experimental.pallas import tpu as pltpu
from jax.sharding import PartitionSpec as P

GY = 8
GZ = 16
NBLK = 32
REACH = 4
GROUP_BLOCKS = 8
COEFFS = (
    -5369.0 / 1800.0,
    12.0 / 7.0,
    -15.0 / 56.0,
    10.0 / 189.0,
    -1.0 / 112.0,
    2.0 / 1925.0,
    -1.0 / 16632.0,
)
KINETIC = 0.125
STEP_SIZE = 0.3
MIB = 1024 * 1024
VMEM_BYTES = 24 * MIB
REDUCE_SHARE = 0.625
GATHER_SHARE = 0.625
BF16 = jnp.bfloat16
F32 = jnp.float32
NT = (((1,), (1,)), ((), ()))


def levels_of(count):
    chips = count // 2
    across = 2 ** (int(math.log2(chips)) // 3)
    return (2, 1), (across, 2), (chips // across, 2 * across)


def position(level):
    size, stride = level
    return lax.rem(lax.div(lax.axis_index("band"), jnp.int32(stride)), jnp.int32(size))


def neighbour(array, count, step):
    return lax.ppermute(array, "band", [(i, (i + step) % count) for i in range(count)])


def swapped(array, count, level, step):
    size, stride = level
    pairs = []
    for device in range(count):
        place = device // stride % size
        pairs.append((device, device + ((place ^ step) - place) * stride))
    return lax.ppermute(array, "band", pairs)


def plane_matrix():
    plane = GY * GZ
    matrix = 3.0 * COEFFS[0] * np.eye(plane)
    cells = np.arange(plane)
    y, z = cells // GZ, cells % GZ
    for offset in range(1, 7):
        for sign in (1, -1):
            np.add.at(matrix, ((y + sign * offset) % GY * GZ + z, cells), COEFFS[offset])
            np.add.at(matrix, (y * GZ + (z + sign * offset) % GZ, cells), COEFFS[offset])
    matrix = KINETIC * matrix
    high = matrix.astype(ml_dtypes.bfloat16)
    low = (matrix - high.astype(np.float64)).astype(ml_dtypes.bfloat16)
    return np.stack([high, low])


def whole():
    return pl.BlockSpec(memory_space=pltpu.VMEM)


def params(size=VMEM_BYTES):
    return pltpu.CompilerParams(vmem_limit_bytes=size)


def cost(flops, *arrays):
    moved = sum(math.prod(a.shape) * jnp.dtype(a.dtype).itemsize for a in arrays)
    return pl.CostEstimate(flops=int(flops), bytes_accessed=int(moved), transcendentals=0)


def local_call(body, outs, args, flops=0, scratch=()):
    return pl.pallas_call(
        body,
        out_shape=outs,
        in_specs=[whole() for _ in args],
        out_specs=jax.tree.map(lambda _: whole(), outs),
        scratch_shapes=scratch,
        compiler_params=params(),
        cost_estimate=cost(flops, *args, *jax.tree.leaves(outs)),
    )(*args)


def struct(shape, dtype):
    return jax.ShapeDtypeStruct(shape, dtype)


def cut(part, block, x_ref, z_ref, cols):
    size = part.shape[0] // block
    first, rest = x_ref.shape[0] // size, z_ref.shape[0] // size
    part = part.astype(x_ref.dtype)
    for i in range(size):
        x_ref[i * first : (i + 1) * first, cols] = part[i * block : i * block + first, :]
        z_ref[i * rest : (i + 1) * rest, cols] = part[i * block + first : (i + 1) * block, :]


def first_body(core, block, tile, r_ref, p_ref, *refs):
    sent_low, sent_high, keep_x, keep_z, r_held, p_held, r_sem, p_sem = refs
    width = sent_low.shape[1]
    rows = r_held.shape[0] // 2
    r_copy = pltpu.make_async_copy(r_ref, r_held, r_sem)
    r_copy.start()
    copies = []
    for t in range(p_held.shape[0] // tile):
        part = pl.ds(t * tile, tile)
        copies.append(pltpu.make_async_copy(p_ref.at[part, :], p_held.at[part, :], p_sem.at[t]))
        copies[-1].start()
    c = position(core)
    r_copy.wait()
    for t, copy in enumerate(copies):
        copy.wait()
        cols = slice(t * tile, (t + 1) * tile)
        for side in (1 - c, c):
            part = lax.dot_general(
                r_held[pl.ds(pl.multiple_of(side * rows, rows), rows), :],
                p_held[cols, :],
                NT,
                preferred_element_type=F32,
            )
            if side is c:
                cut(part, block, keep_x, keep_z, cols)
            else:
                ref, first = (sent_low, 0) if t * tile < width else (sent_high, width)
                ref[:, t * tile - first : (t + 1) * tile - first] = part.astype(BF16)


def first_sums(response, projectors, core, block, first):
    bands, cells = response.shape
    count = projectors.shape[0]
    rows = bands // 2
    tile = min(512, count // 2)
    rows_x = rows // block * first
    outs = [struct((rows, count // 2), BF16)] * 2
    outs += [struct((n, count), F32) for n in (rows_x, rows - rows_x)]
    return pl.pallas_call(
        functools.partial(first_body, core, block, tile),
        out_shape=outs,
        in_specs=[pl.BlockSpec(memory_space=pltpu.HBM)] * 2,
        out_specs=[whole() for _ in outs],
        scratch_shapes=[
            pltpu.VMEM((bands, cells), response.dtype),
            pltpu.VMEM((count, cells), projectors.dtype),
            pltpu.SemaphoreType.DMA,
            pltpu.SemaphoreType.DMA((count // tile,)),
        ],
        compiler_params=params(),
        cost_estimate=cost(2 * bands * cells * count, projectors, *outs),
    )(
        pltpu.with_memory_space_constraint(response, pltpu.HBM),
        pltpu.with_memory_space_constraint(projectors, pltpu.HBM),
    )


def rows_at(place, size):
    return pl.ds(pl.multiple_of(place * size, 16), size)


def cols_at(place, size):
    return pl.ds(pl.multiple_of(place * size, size), size)


def total_of(keep_ref, taken, part):
    total = keep_ref[part]
    for ref in taken:
        total = total + ref[part].astype(F32)
    return total


def first_x_body(level, block, keep_ref, low_ref, high_ref, *outs):
    me = position(level)
    rows = outs[0].shape[0]
    half = low_ref.shape[1]
    for step, out in enumerate(outs):
        at = me ^ step
        mine = rows_at(at, rows)
        theirs = pl.ds(pl.multiple_of(at * block, 16), rows)
        for k, ref in enumerate((low_ref, high_ref)):
            cols = slice(k * half, (k + 1) * half)
            out[:, cols] = (keep_ref[mine, cols] + ref[theirs, :].astype(F32)).astype(out.dtype)


def first_z_body(level, block, first, keep_ref, low_ref, high_ref, *outs):
    me = position(level)
    rows = block - first
    width = outs[0].shape[1]
    per = low_ref.shape[1] // width
    for step, out in enumerate(outs):
        at = me ^ step
        cols = cols_at(at, width)
        near = cols_at(lax.rem(at, jnp.int32(per)), width)
        for i in range(out.shape[0] // rows):
            mine = slice(i * rows, (i + 1) * rows)
            theirs = slice(i * block + first, (i + 1) * block)
            taken = jnp.where(at < per, low_ref[theirs, near], high_ref[theirs, near])
            out[mine, :] = (keep_ref[mine, cols] + taken.astype(F32)).astype(out.dtype)


def split_body(received, level, along, *refs):
    keep_ref, taken, outs = refs[0], refs[1 : 1 + received], refs[1 + received :]
    me = position(level)
    rows, width = outs[0].shape
    for step, out in enumerate(outs):
        at = me ^ step
        if along == 0:
            part = (rows_at(at, rows), slice(None))
        else:
            part = (slice(None), cols_at(at, width))
        out[...] = total_of(keep_ref, taken, part).astype(out.dtype)


def shares_of(shape, count):
    return [struct(shape, F32)] + [struct(shape, BF16)] * (count - 1)


def split(keep, taken, level, along):
    shape = list(keep.shape)
    shape[along] //= level[0]
    return local_call(
        functools.partial(split_body, len(taken), level, along),
        shares_of(shape, level[0]),
        [keep, *taken],
    )


def finish_body(scale, keep_ref, *refs):
    *taken, out_ref = refs
    out_ref[...] = (total_of(keep_ref, taken, ...) * scale).astype(out_ref.dtype)


def finish(keep, taken, scale):
    return local_call(
        functools.partial(finish_body, scale), struct(keep.shape, BF16), [keep, *taken]
    )


def finish_both_body(scale, received, *refs):
    outs = refs[-2:]
    cut = outs[0].shape[0]
    row = 0
    for keep_ref, *taken in (refs[: 1 + received], refs[1 + received : -2]):
        low = (total_of(keep_ref, taken, ...) * scale).astype(BF16)
        end = row + keep_ref.shape[0]
        for out, first, last in ((outs[0], 0, cut), (outs[1], cut, cut + outs[1].shape[0])):
            top, bottom = max(row, first), min(end, last)
            if top < bottom:
                out[top - first : bottom - first, :] = low[top - row : bottom - row, :]
        row = end


def place_body(level, along, *refs):
    *parts, out_ref = refs
    me = position(level)
    width = parts[0].shape[along]
    for step, ref in enumerate(parts):
        at = (me ^ (level[0] - step) % level[0]) * width
        if along == 0:
            out_ref[pl.ds(pl.multiple_of(at, 16), width), :] = ref[...]
        else:
            out_ref[:, pl.ds(pl.multiple_of(at, 128), width)] = ref[...]


def place(parts, level, along):
    shape = list(parts[0].shape)
    shape[along] *= level[0]
    return local_call(functools.partial(place_body, level, along), struct(shape, BF16), parts)


def turned(row, width):
    return jnp.transpose(jnp.broadcast_to(row, (width, row.shape[1])))


def local_body(depth, sizes, *refs):
    r_ref, l_ref, h_ref, o_ref, m_ref, pot_ref, v_ref, e_ref = refs[:8]
    first_ref, many_ref, out_ref, mask_ref = refs[8:]
    plane = GY * GZ
    reach = 6

    def plane_at(j):
        if j < 0:
            ref, k = l_ref, j + reach
        elif j < depth:
            ref, k = r_ref, j
        else:
            ref, k = h_ref, j - depth
        return ref[:, k * plane : (k + 1) * plane]

    group_rows, blk = sizes
    energy = turned(e_ref[...], plane)
    for j in range(depth):
        cols = slice(j * plane, (j + 1) * plane)
        low = plane_at(j)
        total = jnp.dot(low, m_ref[0], preferred_element_type=F32)
        total = total + jnp.dot(low, m_ref[1], preferred_element_type=F32)
        for offset in range(1, 7):
            pair = plane_at(j + offset).astype(F32) + plane_at(j - offset).astype(F32)
            total = total + (KINETIC * COEFFS[offset]) * pair
        total = total + (energy - pot_ref[:, cols]) * low.astype(F32)
        out_ref[:, cols] = total - v_ref[:, cols] * o_ref[:, cols].astype(F32)
    width = mask_ref.shape[1]
    block = lax.broadcasted_iota(jnp.int32, mask_ref.shape, 1) // blk
    block = (block + (pl.program_id(0) * (group_rows // blk) - REACH)).astype(F32)
    lowest = turned(first_ref[...].astype(F32), width)
    inside = (block >= lowest) & (block < lowest + turned(many_ref[...].astype(F32), width))
    mask_ref[...] = jnp.where(inside, 1.0, 0.0).astype(BF16)


def local_part(response, low, high, orbitals, matrix, lines, bounds, group_rows, width, blk):
    bands, cells = response.shape
    depth = cells // (GY * GZ)
    outs = [struct((bands, cells), F32), struct((bands, width), BF16)]
    here = pl.BlockSpec((group_rows, cells), lambda i: (i, 0))
    side = pl.BlockSpec((group_rows, low.shape[1]), lambda i: (i, 0))
    line = pl.BlockSpec((1, cells), lambda i: (0, 0))
    band = pl.BlockSpec((1, group_rows), lambda i: (0, i))
    return pl.pallas_call(
        functools.partial(local_body, depth, (group_rows, blk)),
        grid=(bands // group_rows,),
        out_shape=outs,
        in_specs=[
            here,
            side,
            side,
            here,
            pl.BlockSpec(matrix.shape, lambda i: (0, 0, 0)),
            line,
            line,
            band,
            band,
            band,
        ],
        out_specs=[here, pl.BlockSpec((group_rows, width), lambda i: (i, 0))],
        compiler_params=params(),
        cost_estimate=cost(2 * bands * cells * 300, low, high, low, low, *outs),
    )(response, low, high, orbitals, matrix, *lines, *bounds)


def pad_body(edge, o_ref, pad_ref):
    bands, cells = o_ref.shape
    pad_ref[:edge, :] = jnp.zeros((edge, cells), pad_ref.dtype)
    pad_ref[edge : edge + bands, :] = o_ref[...]
    pad_ref[edge + bands :, :] = jnp.zeros((edge, cells), pad_ref.dtype)


def pad_orbitals(orbitals, blk):
    bands, cells = orbitals.shape
    edge = REACH * blk
    return local_call(
        functools.partial(pad_body, edge),
        struct((bands + 2 * edge, cells), orbitals.dtype),
        [orbitals],
    )


def subgroup(shape, blk):
    return lax.broadcasted_iota(jnp.int32, shape, 1) // (2 * blk)


def packed(sums, blk):
    rows = sums.shape[0]
    sub = 2 * blk
    near, far = sums[:, :rows], sums[:, rows:]
    column = subgroup((rows, rows), blk)
    row = lax.broadcasted_iota(jnp.int32, (rows, rows), 0) // sub
    main = jnp.where(column >= row, near, far)
    rest = far[:sub, :]
    for k in range(1, rows // sub):
        rest = jnp.where(column[:sub, :] == k, far[k * sub : (k + 1) * sub, :], rest)
    return main, rest


def unpacked(main, rest, blk):
    rows = main.shape[0]
    sub = 2 * blk
    column = subgroup((rows, rows), blk)
    row = lax.broadcasted_iota(jnp.int32, (rows, rows), 0) // sub
    near = jnp.where(column >= row, main, 0.0)
    last = jnp.where(column == row, jnp.concatenate([rest] * (rows // sub), axis=0), 0.0)
    return near, jnp.where(column < row, main, last)


def apply_body(core, across, block, group_rows, blk, other, *refs):
    size = across[0]
    blocks = refs[: size + 1]
    p_ref, base_ref, pad_ref, u_ref, s_ref, c_ref = refs[size + 1 :]
    rows, cells = u_ref.shape
    c, x = position(core), position(across)
    side = 1 - c if other else c
    first = blocks[0].shape[0]
    for step, ref in enumerate(blocks[:size]):
        at = (x ^ (size - step) % size) * block
        c_ref[pl.ds(pl.multiple_of(at, 16), first), :] = ref[...]
    rest = block - first
    for i in range(size):
        there = slice(i * block + first, (i + 1) * block)
        c_ref[there, :] = blocks[size][i * rest : (i + 1) * rest, :]
    mine = pl.ds(pl.multiple_of(side * rows, rows), rows)
    tile = 256 if cells % 256 == 0 else 128
    for t in range(cells // tile):
        cols = slice(t * tile, (t + 1) * tile)
        u_ref[:, cols] = base_ref[mine, cols] + jnp.dot(
            c_ref[...], p_ref[:, cols], preferred_element_type=F32
        )
    height = group_rows + 2 * blk
    for g in range(rows // group_rows):
        start = pl.multiple_of(side * rows + g * group_rows, group_rows)
        sums = lax.dot_general(
            u_ref[g * group_rows : (g + 1) * group_rows, :].astype(BF16),
            pad_ref[pl.ds(start, 2 * group_rows), :],
            NT,
            preferred_element_type=F32,
        )
        main, rest_sums = packed(sums, blk)
        s_ref[g * height : g * height + group_rows, :] = main.astype(s_ref.dtype)
        s_ref[g * height + group_rows : (g + 1) * height, :] = rest_sums.astype(s_ref.dtype)


def apply(blocks, projectors, base, padded, core, across, block, group_rows, blk, other):
    bands, cells = base.shape
    rows = bands // 2
    count = projectors.shape[0]
    height = rows // group_rows * (group_rows + 2 * blk)
    return local_call(
        functools.partial(apply_body, core, across, block, group_rows, blk, other),
        [struct((rows, cells), F32), struct((height, group_rows), BF16 if other else F32)],
        [*blocks, projectors, base, padded],
        flops=2 * rows * cells * (count + 2 * group_rows),
        scratch=[pltpu.VMEM((rows, count), BF16)],
    )


def sum_body(keep_ref, *refs):
    *taken, total_ref, low_ref = refs
    total = total_of(keep_ref, taken, ...)
    total_ref[...] = total
    low_ref[...] = total.astype(BF16)


def add_up(keep, taken):
    outs = [struct(keep.shape, F32), struct(keep.shape, BF16)]
    return local_call(sum_body, outs, [keep, *taken])


def project_body(core, blk, other, *refs):
    w_ref, u_ref, pad_ref, r_ref, mask_ref = refs[:5]
    outs, helds, sems = refs[-5:-3], refs[-3:-1], refs[-1]
    rows = mask_ref.shape[1] // 2
    per = u_ref.shape[0] // rows
    height = w_ref.shape[0] // per
    c = position(core)
    copies = []
    for g in range(per):
        mine = slice(g * rows, (g + 1) * rows)
        start = pl.multiple_of(((1 - c if other else c) * per + g) * rows, rows)
        there = pl.ds(start, rows)
        main = w_ref[g * height : g * height + rows, :].astype(F32)
        rest = w_ref[g * height + rows : (g + 1) * height, :].astype(F32)
        residual = u_ref[mine, :]
        for k, part in enumerate(unpacked(main, rest, blk)):
            inside = mask_ref[there, k * rows : (k + 1) * rows].astype(F32) > 0.5
            weights = jnp.where(inside, part, 0.0).astype(BF16)
            window = pad_ref[pl.ds(pl.multiple_of(start + k * rows, rows), rows), :]
            residual = residual - jnp.dot(weights, window, preferred_element_type=F32)
        updated = r_ref[there, :].astype(F32) + STEP_SIZE * residual
        for k, value in enumerate((updated, residual)):
            helds[k][mine, :] = value.astype(BF16)
            copies.append(
                pltpu.make_async_copy(
                    helds[k].at[pl.ds(g * rows, rows), :], outs[k].at[there, :], sems.at[k, g]
                )
            )
            copies[-1].start()
    for copy in copies:
        copy.wait()


def project(weights, unprojected, padded, response, mask, core, blk, other, before):
    rows, cells = unprojected.shape
    per = rows // (mask.shape[1] // 2)
    out = struct(response.shape, BF16)
    args = [weights, unprojected, padded, response, mask]
    anywhere = pl.BlockSpec(memory_space=pl.ANY)
    return pl.pallas_call(
        functools.partial(project_body, core, blk, other),
        out_shape=(out, out),
        in_specs=[whole() for _ in args] + [anywhere for _ in before],
        out_specs=(anywhere, anywhere),
        scratch_shapes=[
            pltpu.VMEM((rows, cells), BF16),
            pltpu.VMEM((rows, cells), BF16),
            pltpu.SemaphoreType.DMA((2, per)),
        ],
        input_output_aliases={5: 0, 6: 1} if before else {},
        compiler_params=params(),
        cost_estimate=cost(2 * rows * mask.shape[1] * cells, padded, unprojected, unprojected),
    )(*args, *before)


def shards(
    count, response, orbitals, projectors, potential, perturbing, energies, window_start, block_count
):
    bands, local_cells = response.shape
    cells = local_cells * count
    projections = projectors.shape[0]
    halo = 6 * GY * GZ
    core, across, along = levels_of(count)
    ace_scale = 1.0 / math.sqrt(cells * projections)
    window_scale = 1.0 / math.sqrt(cells * bands)
    blk = bands // NBLK
    group_rows = GROUP_BLOCKS * blk
    width = 2 * group_rows
    half = bands // 2
    block = half // across[0]
    first = max(16, round(REDUCE_SHARE * block / 16) * 16)
    gather_first = max(16, round(GATHER_SHARE * block / 16) * 16)
    matrix = jnp.asarray(plane_matrix())
    lines = (potential[None, :], perturbing[None, :])
    bounds = tuple(a[None, :] for a in (energies, window_start, block_count))

    def to(array, level):
        return [swapped(array, count, level, k) for k in reversed(range(1, level[0]))]

    def parts_to(parts, level):
        order = reversed(list(enumerate(parts)))
        return [swapped(part, count, level, k + 1) for k, part in order]

    low = neighbour(response[:, local_cells - halo :], count, 1)
    high = neighbour(response[:, :halo], count, -1)

    *sent, keep_x, keep_z = first_sums(response, projectors, core, block, first)
    sent = [swapped(part, count, core, 1) for part in sent]
    keep_z, *parts_z = local_call(
        functools.partial(first_z_body, along, block, first),
        shares_of((keep_z.shape[0], projections // along[0]), along[0]),
        [keep_z, *sent],
    )
    keep_x, parts_z[0] = lax.optimization_barrier((keep_x, parts_z[0]))
    keep_x, *parts_x = local_call(
        functools.partial(first_x_body, across, block),
        shares_of((first, projections), across[0]),
        [keep_x, *sent],
    )
    parts_z[0], low = lax.optimization_barrier((parts_z[0], low))
    taken_z, taken_x, low, high = lax.optimization_barrier(
        (parts_to(parts_z, along), parts_to(parts_x, across), low, high)
    )
    keep_x, *parts_x = split(keep_x, taken_x, along, 1)
    keep_z, *parts_z = split(keep_z, taken_z, across, 0)
    base, mask = local_part(
        response, low, high, orbitals, matrix, lines, bounds, group_rows, width, blk
    )
    padded = pad_orbitals(orbitals, blk)
    taken_x, taken_z, base, padded = lax.optimization_barrier(
        (parts_to(parts_x, along), parts_to(parts_z, across), base, padded)
    )
    share_x, share_z = local_call(
        functools.partial(finish_both_body, ace_scale, len(taken_x)),
        [
            struct((gather_first, projections // along[0]), BF16),
            struct((block - gather_first, projections // along[0]), BF16),
        ],
        [keep_x, *taken_x, keep_z, *taken_z],
    )

    pieces_x, pieces_z = lax.optimization_barrier(
        ([share_x, *to(share_x, along)], [share_z, *to(share_z, across)])
    )
    block_x = place(pieces_x, along, 1)
    block_z = place(pieces_z, across, 0)
    blocks_x = [block_x, *to(block_x, across)]
    pieces_z = [block_z, *to(block_z, along)]
    blocks = [*blocks_x, place(pieces_z, along, 1)]
    others = [swapped(part, count, core, 1) for part in blocks]
    sizes = (core, across, block, group_rows, blk)
    wide, keep = apply(blocks, projectors, base, padded, *sizes, False)
    others, keep = lax.optimization_barrier((others, keep))
    other_wide, part = apply(others, projectors, base, padded, *sizes, True)
    total, part = add_up(keep, to(part, core))
    total, part = add_up(total, to(part, across))
    own = finish(total, to(part, along), window_scale)
    (theirs,) = to(own, core)
    outs = project(own, wide, padded, response, mask, core, blk, False, ())
    return project(theirs, other_wide, padded, response, mask, core, blk, True, outs)


def solution(mesh):
    in_specs = (
        P("pert", "band"),
        P(None, "band"),
        P(None, "band"),
        P("band"),
        P(("pert", "band")),
        P(),
        P(),
        P(),
    )
    out_specs = (P("pert", "band"), P("pert", "band"))
    body = functools.partial(shards, mesh.shape["band"])
    return jax.shard_map(body, mesh=mesh, in_specs=in_specs, out_specs=out_specs, check_vma=False)
```

```python
import functools
import math

import jax
import jax.numpy as jnp
import ml_dtypes
import numpy as np
from jax import lax
from jax.experimental import pallas as pl
from jax.experimental.pallas import tpu as pltpu
from jax.sharding import PartitionSpec as P

GY = 8
GZ = 16
NBLK = 32
REACH = 4
GROUP_BLOCKS = 8
COEFFS = (
    -5369.0 / 1800.0,
    12.0 / 7.0,
    -15.0 / 56.0,
    10.0 / 189.0,
    -1.0 / 112.0,
    2.0 / 1925.0,
    -1.0 / 16632.0,
)
KINETIC = 0.125
STEP_SIZE = 0.3
MIB = 1024 * 1024
VMEM_BYTES = 24 * MIB
REDUCE_SHARE = 0.625
GATHER_SHARE = 0.625
BF16 = jnp.bfloat16
F32 = jnp.float32
NT = (((1,), (1,)), ((), ()))


def levels_of(count):
    chips = count // 2
    across = 2 ** (int(math.log2(chips)) // 3)
    return (2, 1), (across, 2), (chips // across, 2 * across)


def position(level):
    size, stride = level
    return lax.rem(lax.div(lax.axis_index("band"), jnp.int32(stride)), jnp.int32(size))


def neighbour(array, count, step):
    return lax.ppermute(array, "band", [(i, (i + step) % count) for i in range(count)])


def swapped(array, count, level, step):
    size, stride = level
    pairs = []
    for device in range(count):
        place = device // stride % size
        pairs.append((device, device + ((place ^ step) - place) * stride))
    return lax.ppermute(array, "band", pairs)


def plane_matrix():
    plane = GY * GZ
    matrix = 3.0 * COEFFS[0] * np.eye(plane)
    cells = np.arange(plane)
    y, z = cells // GZ, cells % GZ
    for offset in range(1, 7):
        for sign in (1, -1):
            np.add.at(matrix, ((y + sign * offset) % GY * GZ + z, cells), COEFFS[offset])
            np.add.at(matrix, (y * GZ + (z + sign * offset) % GZ, cells), COEFFS[offset])
    matrix = KINETIC * matrix
    high = matrix.astype(ml_dtypes.bfloat16)
    low = (matrix - high.astype(np.float64)).astype(ml_dtypes.bfloat16)
    return np.stack([high, low])


def whole():
    return pl.BlockSpec(memory_space=pltpu.VMEM)


def params(size=VMEM_BYTES):
    return pltpu.CompilerParams(vmem_limit_bytes=size)


def cost(flops, *arrays):
    moved = sum(math.prod(a.shape) * jnp.dtype(a.dtype).itemsize for a in arrays)
    return pl.CostEstimate(flops=int(flops), bytes_accessed=int(moved), transcendentals=0)


def local_call(body, outs, args, flops=0, scratch=()):
    return pl.pallas_call(
        body,
        out_shape=outs,
        in_specs=[whole() for _ in args],
        out_specs=jax.tree.map(lambda _: whole(), outs),
        scratch_shapes=scratch,
        compiler_params=params(),
        cost_estimate=cost(flops, *args, *jax.tree.leaves(outs)),
    )(*args)


def struct(shape, dtype):
    return jax.ShapeDtypeStruct(shape, dtype)


def cut(part, block, x_ref, z_ref, cols):
    size = part.shape[0] // block
    first, rest = x_ref.shape[0] // size, z_ref.shape[0] // size
    part = part.astype(x_ref.dtype)
    for i in range(size):
        x_ref[i * first : (i + 1) * first, cols] = part[i * block : i * block + first, :]
        z_ref[i * rest : (i + 1) * rest, cols] = part[i * block + first : (i + 1) * block, :]


def first_body(core, block, tile, r_ref, p_ref, *refs):
    sent_low, sent_high, keep_x, keep_z, r_held, p_held, r_sem, p_sem = refs
    width = sent_low.shape[1]
    rows = r_held.shape[0] // 2
    r_copy = pltpu.make_async_copy(r_ref, r_held, r_sem)
    r_copy.start()
    copies = []
    for t in range(p_held.shape[0] // tile):
        part = pl.ds(t * tile, tile)
        copies.append(pltpu.make_async_copy(p_ref.at[part, :], p_held.at[part, :], p_sem.at[t]))
        copies[-1].start()
    c = position(core)
    r_copy.wait()
    for t, copy in enumerate(copies):
        copy.wait()
        cols = slice(t * tile, (t + 1) * tile)
        for side in (1 - c, c):
            part = lax.dot_general(
                r_held[pl.ds(pl.multiple_of(side * rows, rows), rows), :],
                p_held[cols, :],
                NT,
                preferred_element_type=F32,
            )
            if side is c:
                cut(part, block, keep_x, keep_z, cols)
            else:
                ref, first = (sent_low, 0) if t * tile < width else (sent_high, width)
                ref[:, t * tile - first : (t + 1) * tile - first] = part.astype(BF16)


def first_sums(response, projectors, core, block, first):
    bands, cells = response.shape
    count = projectors.shape[0]
    rows = bands // 2
    tile = min(512, count // 2)
    rows_x = rows // block * first
    outs = [struct((rows, count // 2), BF16)] * 2
    outs += [struct((n, count), F32) for n in (rows_x, rows - rows_x)]
    return pl.pallas_call(
        functools.partial(first_body, core, block, tile),
        out_shape=outs,
        in_specs=[pl.BlockSpec(memory_space=pltpu.HBM)] * 2,
        out_specs=[whole() for _ in outs],
        scratch_shapes=[
            pltpu.VMEM((bands, cells), response.dtype),
            pltpu.VMEM((count, cells), projectors.dtype),
            pltpu.SemaphoreType.DMA,
            pltpu.SemaphoreType.DMA((count // tile,)),
        ],
        compiler_params=params(),
        cost_estimate=cost(2 * bands * cells * count, projectors, *outs),
    )(
        pltpu.with_memory_space_constraint(response, pltpu.HBM),
        pltpu.with_memory_space_constraint(projectors, pltpu.HBM),
    )


def rows_at(place, size):
    return pl.ds(pl.multiple_of(place * size, 16), size)


def cols_at(place, size):
    return pl.ds(pl.multiple_of(place * size, size), size)


def total_of(keep_ref, taken, part):
    total = keep_ref[part]
    for ref in taken:
        total = total + ref[part].astype(F32)
    return total


def first_x_body(level, block, keep_ref, low_ref, high_ref, *outs):
    me = position(level)
    rows = outs[0].shape[0]
    half = low_ref.shape[1]
    for step, out in enumerate(outs):
        at = me ^ step
        mine = rows_at(at, rows)
        theirs = pl.ds(pl.multiple_of(at * block, 16), rows)
        for k, ref in enumerate((low_ref, high_ref)):
            cols = slice(k * half, (k + 1) * half)
            out[:, cols] = (keep_ref[mine, cols] + ref[theirs, :].astype(F32)).astype(out.dtype)


def first_z_body(level, block, first, keep_ref, low_ref, high_ref, *outs):
    me = position(level)
    rows = block - first
    width = outs[0].shape[1]
    per = low_ref.shape[1] // width
    for step, out in enumerate(outs):
        at = me ^ step
        cols = cols_at(at, width)
        near = cols_at(lax.rem(at, jnp.int32(per)), width)
        for i in range(out.shape[0] // rows):
            mine = slice(i * rows, (i + 1) * rows)
            theirs = slice(i * block + first, (i + 1) * block)
            taken = jnp.where(at < per, low_ref[theirs, near], high_ref[theirs, near])
            out[mine, :] = (keep_ref[mine, cols] + taken.astype(F32)).astype(out.dtype)


def split_body(received, level, along, *refs):
    keep_ref, taken, outs = refs[0], refs[1 : 1 + received], refs[1 + received :]
    me = position(level)
    rows, width = outs[0].shape
    for step, out in enumerate(outs):
        at = me ^ step
        if along == 0:
            part = (rows_at(at, rows), slice(None))
        else:
            part = (slice(None), cols_at(at, width))
        out[...] = total_of(keep_ref, taken, part).astype(out.dtype)


def shares_of(shape, count):
    return [struct(shape, F32)] + [struct(shape, BF16)] * (count - 1)


def split(keep, taken, level, along):
    shape = list(keep.shape)
    shape[along] //= level[0]
    return local_call(
        functools.partial(split_body, len(taken), level, along),
        shares_of(shape, level[0]),
        [keep, *taken],
    )


def finish_body(scale, keep_ref, *refs):
    *taken, out_ref = refs
    out_ref[...] = (total_of(keep_ref, taken, ...) * scale).astype(out_ref.dtype)


def finish(keep, taken, scale):
    return local_call(
        functools.partial(finish_body, scale), struct(keep.shape, BF16), [keep, *taken]
    )


def finish_both_body(scale, received, *refs):
    outs = refs[-2:]
    cut = outs[0].shape[0]
    row = 0
    for keep_ref, *taken in (refs[: 1 + received], refs[1 + received : -2]):
        low = (total_of(keep_ref, taken, ...) * scale).astype(BF16)
        end = row + keep_ref.shape[0]
        for out, first, last in ((outs[0], 0, cut), (outs[1], cut, cut + outs[1].shape[0])):
            top, bottom = max(row, first), min(end, last)
            if top < bottom:
                out[top - first : bottom - first, :] = low[top - row : bottom - row, :]
        row = end


def place_body(level, along, *refs):
    *parts, out_ref = refs
    me = position(level)
    width = parts[0].shape[along]
    for step, ref in enumerate(parts):
        at = (me ^ step) * width
        if along == 0:
            out_ref[pl.ds(pl.multiple_of(at, 16), width), :] = ref[...]
        else:
            out_ref[:, pl.ds(pl.multiple_of(at, 128), width)] = ref[...]


def place(parts, level, along):
    shape = list(parts[0].shape)
    shape[along] *= level[0]
    return local_call(functools.partial(place_body, level, along), struct(shape, BF16), parts)


def turned(row, width):
    return jnp.transpose(jnp.broadcast_to(row, (width, row.shape[1])))


def local_body(depth, sizes, *refs):
    r_ref, l_ref, h_ref, o_ref, m_ref, pot_ref, v_ref, e_ref = refs[:8]
    first_ref, many_ref, out_ref, mask_ref = refs[8:]
    plane = GY * GZ
    reach = 6

    def plane_at(j):
        if j < 0:
            ref, k = l_ref, j + reach
        elif j < depth:
            ref, k = r_ref, j
        else:
            ref, k = h_ref, j - depth
        return ref[:, k * plane : (k + 1) * plane]

    group_rows, blk = sizes
    energy = turned(e_ref[...], plane)
    for j in range(depth):
        cols = slice(j * plane, (j + 1) * plane)
        low = plane_at(j)
        total = jnp.dot(low, m_ref[0], preferred_element_type=F32)
        total = total + jnp.dot(low, m_ref[1], preferred_element_type=F32)
        for offset in range(1, 7):
            pair = plane_at(j + offset).astype(F32) + plane_at(j - offset).astype(F32)
            total = total + (KINETIC * COEFFS[offset]) * pair
        total = total + (energy - pot_ref[:, cols]) * low.astype(F32)
        out_ref[:, cols] = total - v_ref[:, cols] * o_ref[:, cols].astype(F32)
    width = mask_ref.shape[1]
    block = lax.broadcasted_iota(jnp.int32, mask_ref.shape, 1) // blk
    block = (block + (pl.program_id(0) * (group_rows // blk) - REACH)).astype(F32)
    lowest = turned(first_ref[...].astype(F32), width)
    inside = (block >= lowest) & (block < lowest + turned(many_ref[...].astype(F32), width))
    mask_ref[...] = jnp.where(inside, 1.0, 0.0).astype(BF16)


def local_part(response, low, high, orbitals, matrix, lines, bounds, group_rows, width, blk):
    bands, cells = response.shape
    depth = cells // (GY * GZ)
    outs = [struct((bands, cells), F32), struct((bands, width), BF16)]
    here = pl.BlockSpec((group_rows, cells), lambda i: (i, 0))
    side = pl.BlockSpec((group_rows, low.shape[1]), lambda i: (i, 0))
    line = pl.BlockSpec((1, cells), lambda i: (0, 0))
    band = pl.BlockSpec((1, group_rows), lambda i: (0, i))
    return pl.pallas_call(
        functools.partial(local_body, depth, (group_rows, blk)),
        grid=(bands // group_rows,),
        out_shape=outs,
        in_specs=[
            here,
            side,
            side,
            here,
            pl.BlockSpec(matrix.shape, lambda i: (0, 0, 0)),
            line,
            line,
            band,
            band,
            band,
        ],
        out_specs=[here, pl.BlockSpec((group_rows, width), lambda i: (i, 0))],
        compiler_params=params(),
        cost_estimate=cost(2 * bands * cells * 300, low, high, low, low, *outs),
    )(response, low, high, orbitals, matrix, *lines, *bounds)


def pad_body(edge, o_ref, pad_ref):
    bands, cells = o_ref.shape
    pad_ref[:edge, :] = jnp.zeros((edge, cells), pad_ref.dtype)
    pad_ref[edge : edge + bands, :] = o_ref[...]
    pad_ref[edge + bands :, :] = jnp.zeros((edge, cells), pad_ref.dtype)


def pad_orbitals(orbitals, blk):
    bands, cells = orbitals.shape
    edge = REACH * blk
    return local_call(
        functools.partial(pad_body, edge),
        struct((bands + 2 * edge, cells), orbitals.dtype),
        [orbitals],
    )


def subgroup(shape, blk):
    return lax.broadcasted_iota(jnp.int32, shape, 1) // (2 * blk)


def packed(sums, blk):
    rows = sums.shape[0]
    sub = 2 * blk
    near, far = sums[:, :rows], sums[:, rows:]
    column = subgroup((rows, rows), blk)
    row = lax.broadcasted_iota(jnp.int32, (rows, rows), 0) // sub
    main = jnp.where(column >= row, near, far)
    rest = far[:sub, :]
    for k in range(1, rows // sub):
        rest = jnp.where(column[:sub, :] == k, far[k * sub : (k + 1) * sub, :], rest)
    return main, rest


def unpacked(main, rest, blk):
    rows = main.shape[0]
    sub = 2 * blk
    column = subgroup((rows, rows), blk)
    row = lax.broadcasted_iota(jnp.int32, (rows, rows), 0) // sub
    near = jnp.where(column >= row, main, 0.0)
    last = jnp.where(column == row, jnp.concatenate([rest] * (rows // sub), axis=0), 0.0)
    return near, jnp.where(column < row, main, last)


def apply_body(core, across, block, group_rows, blk, other, *refs):
    size = across[0]
    blocks = refs[: size + 1]
    p_ref, base_ref, pad_ref, u_ref, s_ref, c_ref = refs[size + 1 :]
    rows, cells = u_ref.shape
    c, x = position(core), position(across)
    side = 1 - c if other else c
    first = blocks[0].shape[0]
    for step, ref in enumerate(blocks[:size]):
        at = (x ^ step) * block
        c_ref[pl.ds(pl.multiple_of(at, 16), first), :] = ref[...]
    rest = block - first
    for i in range(size):
        there = slice(i * block + first, (i + 1) * block)
        c_ref[there, :] = blocks[size][i * rest : (i + 1) * rest, :]
    mine = pl.ds(pl.multiple_of(side * rows, rows), rows)
    tile = 256 if cells % 256 == 0 else 128
    for t in range(cells // tile):
        cols = slice(t * tile, (t + 1) * tile)
        u_ref[:, cols] = base_ref[mine, cols] + jnp.dot(
            c_ref[...], p_ref[:, cols], preferred_element_type=F32
        )
    height = group_rows + 2 * blk
    for g in range(rows // group_rows):
        start = pl.multiple_of(side * rows + g * group_rows, group_rows)
        sums = lax.dot_general(
            u_ref[g * group_rows : (g + 1) * group_rows, :].astype(BF16),
            pad_ref[pl.ds(start, 2 * group_rows), :],
            NT,
            preferred_element_type=F32,
        )
        main, rest_sums = packed(sums, blk)
        s_ref[g * height : g * height + group_rows, :] = main.astype(s_ref.dtype)
        s_ref[g * height + group_rows : (g + 1) * height, :] = rest_sums.astype(s_ref.dtype)


def apply(blocks, projectors, base, padded, core, across, block, group_rows, blk, other):
    bands, cells = base.shape
    rows = bands // 2
    count = projectors.shape[0]
    height = rows // group_rows * (group_rows + 2 * blk)
    return local_call(
        functools.partial(apply_body, core, across, block, group_rows, blk, other),
        [struct((rows, cells), F32), struct((height, group_rows), BF16 if other else F32)],
        [*blocks, projectors, base, padded],
        flops=2 * rows * cells * (count + 2 * group_rows),
        scratch=[pltpu.VMEM((rows, count), BF16)],
    )


def sum_body(keep_ref, *refs):
    *taken, total_ref, low_ref = refs
    total = total_of(keep_ref, taken, ...)
    total_ref[...] = total
    low_ref[...] = total.astype(BF16)


def add_up(keep, taken):
    outs = [struct(keep.shape, F32), struct(keep.shape, BF16)]
    return local_call(sum_body, outs, [keep, *taken])


def project_body(core, blk, other, *refs):
    w_ref, u_ref, pad_ref, r_ref, mask_ref = refs[:5]
    outs, helds, sems = refs[-5:-3], refs[-3:-1], refs[-1]
    rows = mask_ref.shape[1] // 2
    per = u_ref.shape[0] // rows
    height = w_ref.shape[0] // per
    c = position(core)
    copies = []
    for g in range(per):
        mine = slice(g * rows, (g + 1) * rows)
        start = pl.multiple_of(((1 - c if other else c) * per + g) * rows, rows)
        there = pl.ds(start, rows)
        main = w_ref[g * height : g * height + rows, :].astype(F32)
        rest = w_ref[g * height + rows : (g + 1) * height, :].astype(F32)
        residual = u_ref[mine, :]
        for k, part in enumerate(unpacked(main, rest, blk)):
            inside = mask_ref[there, k * rows : (k + 1) * rows].astype(F32) > 0.5
            weights = jnp.where(inside, part, 0.0).astype(BF16)
            window = pad_ref[pl.ds(pl.multiple_of(start + k * rows, rows), rows), :]
            residual = residual - jnp.dot(weights, window, preferred_element_type=F32)
        updated = r_ref[there, :].astype(F32) + STEP_SIZE * residual
        for k, value in enumerate((updated, residual)):
            helds[k][mine, :] = value.astype(BF16)
            copies.append(
                pltpu.make_async_copy(
                    helds[k].at[pl.ds(g * rows, rows), :], outs[k].at[there, :], sems.at[k, g]
                )
            )
            copies[-1].start()
    for copy in copies:
        copy.wait()


def project(weights, unprojected, padded, response, mask, core, blk, other, before):
    rows, cells = unprojected.shape
    per = rows // (mask.shape[1] // 2)
    out = struct(response.shape, BF16)
    args = [weights, unprojected, padded, response, mask]
    anywhere = pl.BlockSpec(memory_space=pl.ANY)
    return pl.pallas_call(
        functools.partial(project_body, core, blk, other),
        out_shape=(out, out),
        in_specs=[whole() for _ in args] + [anywhere for _ in before],
        out_specs=(anywhere, anywhere),
        scratch_shapes=[
            pltpu.VMEM((rows, cells), BF16),
            pltpu.VMEM((rows, cells), BF16),
            pltpu.SemaphoreType.DMA((2, per)),
        ],
        input_output_aliases={5: 0, 6: 1} if before else {},
        compiler_params=params(),
        cost_estimate=cost(2 * rows * mask.shape[1] * cells, padded, unprojected, unprojected),
    )(*args, *before)


def shards(
    count, response, orbitals, projectors, potential, perturbing, energies, window_start, block_count
):
    bands, local_cells = response.shape
    cells = local_cells * count
    projections = projectors.shape[0]
    halo = 6 * GY * GZ
    core, across, along = levels_of(count)
    ace_scale = 1.0 / math.sqrt(cells * projections)
    window_scale = 1.0 / math.sqrt(cells * bands)
    blk = bands // NBLK
    group_rows = GROUP_BLOCKS * blk
    width = 2 * group_rows
    half = bands // 2
    block = half // across[0]
    first = max(16, round(REDUCE_SHARE * block / 16) * 16)
    gather_first = max(16, round(GATHER_SHARE * block / 16) * 16)
    matrix = jnp.asarray(plane_matrix())
    lines = (potential[None, :], perturbing[None, :])
    bounds = tuple(a[None, :] for a in (energies, window_start, block_count))

    def to(array, level):
        return [swapped(array, count, level, k) for k in range(1, level[0])]

    def parts_to(parts, level):
        return [swapped(part, count, level, k + 1) for k, part in enumerate(parts)]

    low = neighbour(response[:, local_cells - halo :], count, 1)
    high = neighbour(response[:, :halo], count, -1)

    *sent, keep_x, keep_z = first_sums(response, projectors, core, block, first)
    sent = [swapped(part, count, core, 1) for part in sent]
    keep_z, *parts_z = local_call(
        functools.partial(first_z_body, along, block, first),
        shares_of((keep_z.shape[0], projections // along[0]), along[0]),
        [keep_z, *sent],
    )
    keep_x, parts_z[0] = lax.optimization_barrier((keep_x, parts_z[0]))
    keep_x, *parts_x = local_call(
        functools.partial(first_x_body, across, block),
        shares_of((first, projections), across[0]),
        [keep_x, *sent],
    )
    parts_z[-1], low = lax.optimization_barrier((parts_z[-1], low))
    taken_z, taken_x, low, high = lax.optimization_barrier(
        (parts_to(parts_z, along), parts_to(parts_x, across), low, high)
    )
    keep_x, *parts_x = split(keep_x, taken_x, along, 1)
    keep_z, *parts_z = split(keep_z, taken_z, across, 0)
    base, mask = local_part(
        response, low, high, orbitals, matrix, lines, bounds, group_rows, width, blk
    )
    padded = pad_orbitals(orbitals, blk)
    taken_x, taken_z, base, padded = lax.optimization_barrier(
        (parts_to(parts_x, along), parts_to(parts_z, across), base, padded)
    )
    share_x, share_z = local_call(
        functools.partial(finish_both_body, ace_scale, len(taken_x)),
        [
            struct((gather_first, projections // along[0]), BF16),
            struct((block - gather_first, projections // along[0]), BF16),
        ],
        [keep_x, *taken_x, keep_z, *taken_z],
    )

    pieces_x, pieces_z = lax.optimization_barrier(
        ([share_x, *to(share_x, along)], [share_z, *to(share_z, across)])
    )
    block_x = place(pieces_x, along, 1)
    block_z = place(pieces_z, across, 0)
    blocks_x = [block_x, *to(block_x, across)]
    pieces_z = [block_z, *to(block_z, along)]
    blocks = [*blocks_x, place(pieces_z, along, 1)]
    others = [swapped(part, count, core, 1) for part in blocks]
    sizes = (core, across, block, group_rows, blk)
    wide, keep = apply(blocks, projectors, base, padded, *sizes, False)
    others, keep = lax.optimization_barrier((others, keep))
    other_wide, part = apply(others, projectors, base, padded, *sizes, True)
    total, part = add_up(keep, to(part, core))
    total, part = add_up(total, to(part, across))
    far_first = [swapped(part, count, along, k) for k in reversed(range(1, along[0]))]
    own = finish(total, far_first, window_scale)
    (theirs,) = to(own, core)
    outs = project(own, wide, padded, response, mask, core, blk, False, ())
    return project(theirs, other_wide, padded, response, mask, core, blk, True, outs)


def solution(mesh):
    in_specs = (
        P("pert", "band"),
        P(None, "band"),
        P(None, "band"),
        P("band"),
        P(("pert", "band")),
        P(),
        P(),
        P(),
    )
    out_specs = (P("pert", "band"), P("pert", "band"))
    body = functools.partial(shards, mesh.shape["band"])
    return jax.shard_map(body, mesh=mesh, in_specs=in_specs, out_specs=out_specs, check_vma=False)
```

```python
import functools
import math

import jax
import jax.numpy as jnp
import ml_dtypes
import numpy as np
from jax import lax
from jax.experimental import pallas as pl
from jax.experimental.pallas import tpu as pltpu
from jax.sharding import PartitionSpec as P

GY = 8
GZ = 16
NBLK = 32
REACH = 4
GROUP_BLOCKS = 8
COEFFS = (
    -5369.0 / 1800.0,
    12.0 / 7.0,
    -15.0 / 56.0,
    10.0 / 189.0,
    -1.0 / 112.0,
    2.0 / 1925.0,
    -1.0 / 16632.0,
)
KINETIC = 0.125
STEP_SIZE = 0.3
MIB = 1024 * 1024
VMEM_BYTES = 24 * MIB
REDUCE_SHARE = 0.5
GATHER_SHARE = 0.5
BF16 = jnp.bfloat16
F32 = jnp.float32
NT = (((1,), (1,)), ((), ()))


def levels_of(count):
    chips = count // 2
    across = 2 ** (int(math.log2(chips)) // 3)
    return (2, 1), (across, 2), (chips // across, 2 * across)


def position(level):
    size, stride = level
    return lax.rem(lax.div(lax.axis_index("band"), jnp.int32(stride)), jnp.int32(size))


def neighbour(array, count, step):
    return lax.ppermute(array, "band", [(i, (i + step) % count) for i in range(count)])


def swapped(array, count, level, step):
    size, stride = level
    pairs = []
    for device in range(count):
        place = device // stride % size
        pairs.append((device, device + ((place ^ step) - place) * stride))
    return lax.ppermute(array, "band", pairs)


def plane_matrix():
    plane = GY * GZ
    matrix = 3.0 * COEFFS[0] * np.eye(plane)
    cells = np.arange(plane)
    y, z = cells // GZ, cells % GZ
    for offset in range(1, 7):
        for sign in (1, -1):
            np.add.at(matrix, ((y + sign * offset) % GY * GZ + z, cells), COEFFS[offset])
            np.add.at(matrix, (y * GZ + (z + sign * offset) % GZ, cells), COEFFS[offset])
    matrix = KINETIC * matrix
    high = matrix.astype(ml_dtypes.bfloat16)
    low = (matrix - high.astype(np.float64)).astype(ml_dtypes.bfloat16)
    return np.stack([high, low])


def whole():
    return pl.BlockSpec(memory_space=pltpu.VMEM)


def params(size=VMEM_BYTES):
    return pltpu.CompilerParams(vmem_limit_bytes=size)


def cost(flops, *arrays):
    moved = sum(math.prod(a.shape) * jnp.dtype(a.dtype).itemsize for a in arrays)
    return pl.CostEstimate(flops=int(flops), bytes_accessed=int(moved), transcendentals=0)


def local_call(body, outs, args, flops=0, scratch=()):
    return pl.pallas_call(
        body,
        out_shape=outs,
        in_specs=[whole() for _ in args],
        out_specs=jax.tree.map(lambda _: whole(), outs),
        scratch_shapes=scratch,
        compiler_params=params(),
        cost_estimate=cost(flops, *args, *jax.tree.leaves(outs)),
    )(*args)


def struct(shape, dtype):
    return jax.ShapeDtypeStruct(shape, dtype)


def cut(part, block, x_ref, z_ref, cols):
    size = part.shape[0] // block
    first, rest = x_ref.shape[0] // size, z_ref.shape[0] // size
    part = part.astype(x_ref.dtype)
    for i in range(size):
        x_ref[i * first : (i + 1) * first, cols] = part[i * block : i * block + first, :]
        z_ref[i * rest : (i + 1) * rest, cols] = part[i * block + first : (i + 1) * block, :]


def first_body(core, block, tile, r_ref, p_ref, *refs):
    sent_x, sent_z, keep_x, keep_z, r_held, p_held, r_sem, p_sem = refs
    rows = r_held.shape[0] // 2
    r_copy = pltpu.make_async_copy(r_ref, r_held, r_sem)
    r_copy.start()
    copies = []
    for t in range(p_held.shape[0] // tile):
        part = pl.ds(t * tile, tile)
        copies.append(pltpu.make_async_copy(p_ref.at[part, :], p_held.at[part, :], p_sem.at[t]))
        copies[-1].start()
    c = position(core)
    r_copy.wait()
    for t, copy in enumerate(copies):
        copy.wait()
        cols = slice(t * tile, (t + 1) * tile)
        for side, x_ref, z_ref in ((1 - c, sent_x, sent_z), (c, keep_x, keep_z)):
            part = lax.dot_general(
                r_held[pl.ds(pl.multiple_of(side * rows, rows), rows), :],
                p_held[cols, :],
                NT,
                preferred_element_type=F32,
            )
            cut(part, block, x_ref, z_ref, cols)


def first_sums(response, projectors, core, block, first):
    bands, cells = response.shape
    count = projectors.shape[0]
    rows = bands // 2
    tile = min(512, count)
    rows_x = rows // block * first
    outs = [struct((n, count), t) for t in (BF16, F32) for n in (rows_x, rows - rows_x)]
    return pl.pallas_call(
        functools.partial(first_body, core, block, tile),
        out_shape=outs,
        in_specs=[pl.BlockSpec(memory_space=pltpu.HBM)] * 2,
        out_specs=[whole() for _ in outs],
        scratch_shapes=[
            pltpu.VMEM((bands, cells), response.dtype),
            pltpu.VMEM((count, cells), projectors.dtype),
            pltpu.SemaphoreType.DMA,
            pltpu.SemaphoreType.DMA((count // tile,)),
        ],
        compiler_params=params(),
        cost_estimate=cost(2 * bands * cells * count, projectors, *outs),
    )(
        pltpu.with_memory_space_constraint(response, pltpu.HBM),
        pltpu.with_memory_space_constraint(projectors, pltpu.HBM),
    )


def rows_at(place, size):
    return pl.ds(pl.multiple_of(place * size, 16), size)


def cols_at(place, size):
    return pl.ds(pl.multiple_of(place * size, size), size)


def total_of(keep_ref, taken, part):
    total = keep_ref[part]
    for ref in taken:
        total = total + ref[part].astype(F32)
    return total


def split_body(received, level, along, *refs):
    keep_ref, taken, outs = refs[0], refs[1 : 1 + received], refs[1 + received :]
    me = position(level)
    rows, width = outs[0].shape
    for step, out in enumerate(outs):
        at = me ^ step
        if along == 0:
            part = (rows_at(at, rows), slice(None))
        else:
            part = (slice(None), cols_at(at, width))
        out[...] = total_of(keep_ref, taken, part).astype(out.dtype)


def shares_of(shape, count):
    return [struct(shape, F32)] + [struct(shape, BF16)] * (count - 1)


def split(keep, taken, level, along):
    shape = list(keep.shape)
    shape[along] //= level[0]
    return local_call(
        functools.partial(split_body, len(taken), level, along),
        shares_of(shape, level[0]),
        [keep, *taken],
    )


def finish_body(scale, keep_ref, *refs):
    *taken, out_ref = refs
    out_ref[...] = (total_of(keep_ref, taken, ...) * scale).astype(out_ref.dtype)


def finish(keep, taken, scale):
    return local_call(
        functools.partial(finish_body, scale), struct(keep.shape, BF16), [keep, *taken]
    )


def finish_both_body(scale, received, *refs):
    outs = refs[-2:]
    cut = outs[0].shape[0]
    row = 0
    for keep_ref, *taken in (refs[: 1 + received], refs[1 + received : -2]):
        low = (total_of(keep_ref, taken, ...) * scale).astype(BF16)
        end = row + keep_ref.shape[0]
        for out, first, last in ((outs[0], 0, cut), (outs[1], cut, cut + outs[1].shape[0])):
            top, bottom = max(row, first), min(end, last)
            if top < bottom:
                out[top - first : bottom - first, :] = low[top - row : bottom - row, :]
        row = end


def place_body(level, along, *refs):
    *parts, out_ref = refs
    me = position(level)
    width = parts[0].shape[along]
    for step, ref in enumerate(parts):
        at = pl.multiple_of((me ^ step) * width, width)
        if along == 0:
            out_ref[pl.ds(at, width), :] = ref[...]
        else:
            out_ref[:, pl.ds(at, width)] = ref[...]


def place(parts, level, along):
    shape = list(parts[0].shape)
    shape[along] *= level[0]
    return local_call(functools.partial(place_body, level, along), struct(shape, BF16), parts)


def turned(row, width):
    return jnp.transpose(jnp.broadcast_to(row, (width, row.shape[1])))


def local_body(depth, sizes, *refs):
    r_ref, l_ref, h_ref, o_ref, m_ref, pot_ref, v_ref, e_ref = refs[:8]
    first_ref, many_ref, out_ref, mask_ref = refs[8:]
    plane = GY * GZ
    reach = 6

    def plane_at(j):
        if j < 0:
            ref, k = l_ref, j + reach
        elif j < depth:
            ref, k = r_ref, j
        else:
            ref, k = h_ref, j - depth
        return ref[:, k * plane : (k + 1) * plane]

    group_rows, blk = sizes
    energy = turned(e_ref[...], plane)
    for j in range(depth):
        cols = slice(j * plane, (j + 1) * plane)
        low = plane_at(j)
        total = jnp.dot(low, m_ref[0], preferred_element_type=F32)
        total = total + jnp.dot(low, m_ref[1], preferred_element_type=F32)
        for offset in range(1, 7):
            pair = plane_at(j + offset).astype(F32) + plane_at(j - offset).astype(F32)
            total = total + (KINETIC * COEFFS[offset]) * pair
        total = total + (energy - pot_ref[:, cols]) * low.astype(F32)
        out_ref[:, cols] = total - v_ref[:, cols] * o_ref[:, cols].astype(F32)
    width = mask_ref.shape[1]
    block = lax.broadcasted_iota(jnp.int32, mask_ref.shape, 1) // blk
    block = (block + (pl.program_id(0) * (group_rows // blk) - REACH)).astype(F32)
    lowest = turned(first_ref[...].astype(F32), width)
    inside = (block >= lowest) & (block < lowest + turned(many_ref[...].astype(F32), width))
    mask_ref[...] = jnp.where(inside, 1.0, 0.0).astype(BF16)


def local_part(response, low, high, orbitals, matrix, lines, bounds, group_rows, width, blk):
    bands, cells = response.shape
    depth = cells // (GY * GZ)
    outs = [struct((bands, cells), F32), struct((bands, width), BF16)]
    here = pl.BlockSpec((group_rows, cells), lambda i: (i, 0))
    side = pl.BlockSpec((group_rows, low.shape[1]), lambda i: (i, 0))
    line = pl.BlockSpec((1, cells), lambda i: (0, 0))
    band = pl.BlockSpec((1, group_rows), lambda i: (0, i))
    return pl.pallas_call(
        functools.partial(local_body, depth, (group_rows, blk)),
        grid=(bands // group_rows,),
        out_shape=outs,
        in_specs=[
            here,
            side,
            side,
            here,
            pl.BlockSpec(matrix.shape, lambda i: (0, 0, 0)),
            line,
            line,
            band,
            band,
            band,
        ],
        out_specs=[here, pl.BlockSpec((group_rows, width), lambda i: (i, 0))],
        compiler_params=params(),
        cost_estimate=cost(2 * bands * cells * 300, low, high, low, low, *outs),
    )(response, low, high, orbitals, matrix, *lines, *bounds)


def pad_body(edge, o_ref, pad_ref):
    bands, cells = o_ref.shape
    pad_ref[:edge, :] = jnp.zeros((edge, cells), pad_ref.dtype)
    pad_ref[edge : edge + bands, :] = o_ref[...]
    pad_ref[edge + bands :, :] = jnp.zeros((edge, cells), pad_ref.dtype)


def pad_orbitals(orbitals, blk):
    bands, cells = orbitals.shape
    edge = REACH * blk
    return local_call(
        functools.partial(pad_body, edge),
        struct((bands + 2 * edge, cells), orbitals.dtype),
        [orbitals],
    )


def subgroup(shape, blk):
    return lax.broadcasted_iota(jnp.int32, shape, 1) // (2 * blk)


def packed(sums, blk):
    rows = sums.shape[0]
    sub = 2 * blk
    near, far = sums[:, :rows], sums[:, rows:]
    column = subgroup((rows, rows), blk)
    row = lax.broadcasted_iota(jnp.int32, (rows, rows), 0) // sub
    main = jnp.where(column >= row, near, far)
    rest = far[:sub, :]
    for k in range(1, rows // sub):
        rest = jnp.where(column[:sub, :] == k, far[k * sub : (k + 1) * sub, :], rest)
    return main, rest


def unpacked(main, rest, blk):
    rows = main.shape[0]
    sub = 2 * blk
    column = subgroup((rows, rows), blk)
    row = lax.broadcasted_iota(jnp.int32, (rows, rows), 0) // sub
    near = jnp.where(column >= row, main, 0.0)
    last = jnp.where(column == row, jnp.concatenate([rest] * (rows // sub), axis=0), 0.0)
    return near, jnp.where(column < row, main, last)


def apply_body(core, across, block, group_rows, blk, other, *refs):
    size = across[0]
    blocks = refs[: size + 1]
    p_ref, base_ref, pad_ref, u_ref, s_ref, c_ref = refs[size + 1 :]
    rows, cells = u_ref.shape
    c, x = position(core), position(across)
    side = 1 - c if other else c
    first = blocks[0].shape[0]
    for step, ref in enumerate(blocks[:size]):
        at = (x ^ step) * block
        c_ref[pl.ds(pl.multiple_of(at, 16), first), :] = ref[...]
    rest = block - first
    for i in range(size):
        there = slice(i * block + first, (i + 1) * block)
        c_ref[there, :] = blocks[size][i * rest : (i + 1) * rest, :]
    mine = pl.ds(pl.multiple_of(side * rows, rows), rows)
    tile = 256 if cells % 256 == 0 else 128
    for t in range(cells // tile):
        cols = slice(t * tile, (t + 1) * tile)
        u_ref[:, cols] = base_ref[mine, cols] + jnp.dot(
            c_ref[...], p_ref[:, cols], preferred_element_type=F32
        )
    height = group_rows + 2 * blk
    for g in range(rows // group_rows):
        start = pl.multiple_of(side * rows + g * group_rows, group_rows)
        sums = lax.dot_general(
            u_ref[g * group_rows : (g + 1) * group_rows, :].astype(BF16),
            pad_ref[pl.ds(start, 2 * group_rows), :],
            NT,
            preferred_element_type=F32,
        )
        main, rest_sums = packed(sums, blk)
        s_ref[g * height : g * height + group_rows, :] = main.astype(s_ref.dtype)
        s_ref[g * height + group_rows : (g + 1) * height, :] = rest_sums.astype(s_ref.dtype)


def apply(blocks, projectors, base, padded, core, across, block, group_rows, blk, other):
    bands, cells = base.shape
    rows = bands // 2
    count = projectors.shape[0]
    height = rows // group_rows * (group_rows + 2 * blk)
    return local_call(
        functools.partial(apply_body, core, across, block, group_rows, blk, other),
        [struct((rows, cells), F32), struct((height, group_rows), BF16 if other else F32)],
        [*blocks, projectors, base, padded],
        flops=2 * rows * cells * (count + 2 * group_rows),
        scratch=[pltpu.VMEM((rows, count), BF16)],
    )


def sum_body(keep_ref, *refs):
    *taken, total_ref, low_ref = refs
    total = total_of(keep_ref, taken, ...)
    total_ref[...] = total
    low_ref[...] = total.astype(BF16)


def add_up(keep, taken):
    outs = [struct(keep.shape, F32), struct(keep.shape, BF16)]
    return local_call(sum_body, outs, [keep, *taken])


def project_body(core, blk, other, *refs):
    w_ref, u_ref, pad_ref, r_ref, mask_ref = refs[:5]
    outs, helds, sems = refs[-5:-3], refs[-3:-1], refs[-1]
    rows = mask_ref.shape[1] // 2
    per = u_ref.shape[0] // rows
    height = w_ref.shape[0] // per
    c = position(core)
    copies = []
    for g in range(per):
        mine = slice(g * rows, (g + 1) * rows)
        start = pl.multiple_of(((1 - c if other else c) * per + g) * rows, rows)
        there = pl.ds(start, rows)
        main = w_ref[g * height : g * height + rows, :].astype(F32)
        rest = w_ref[g * height + rows : (g + 1) * height, :].astype(F32)
        residual = u_ref[mine, :]
        for k, part in enumerate(unpacked(main, rest, blk)):
            inside = mask_ref[there, k * rows : (k + 1) * rows].astype(F32) > 0.5
            weights = jnp.where(inside, part, 0.0).astype(BF16)
            window = pad_ref[pl.ds(pl.multiple_of(start + k * rows, rows), rows), :]
            residual = residual - jnp.dot(weights, window, preferred_element_type=F32)
        updated = r_ref[there, :].astype(F32) + STEP_SIZE * residual
        for k, value in enumerate((updated, residual)):
            helds[k][mine, :] = value.astype(BF16)
            copies.append(
                pltpu.make_async_copy(
                    helds[k].at[pl.ds(g * rows, rows), :], outs[k].at[there, :], sems.at[k, g]
                )
            )
            copies[-1].start()
    for copy in copies:
        copy.wait()


def project(weights, unprojected, padded, response, mask, core, blk, other, before):
    rows, cells = unprojected.shape
    per = rows // (mask.shape[1] // 2)
    out = struct(response.shape, BF16)
    args = [weights, unprojected, padded, response, mask]
    anywhere = pl.BlockSpec(memory_space=pl.ANY)
    return pl.pallas_call(
        functools.partial(project_body, core, blk, other),
        out_shape=(out, out),
        in_specs=[whole() for _ in args] + [anywhere for _ in before],
        out_specs=(anywhere, anywhere),
        scratch_shapes=[
            pltpu.VMEM((rows, cells), BF16),
            pltpu.VMEM((rows, cells), BF16),
            pltpu.SemaphoreType.DMA((2, per)),
        ],
        input_output_aliases={5: 0, 6: 1} if before else {},
        compiler_params=params(),
        cost_estimate=cost(2 * rows * mask.shape[1] * cells, padded, unprojected, unprojected),
    )(*args, *before)


def shards(
    count, response, orbitals, projectors, potential, perturbing, energies, window_start, block_count
):
    bands, local_cells = response.shape
    cells = local_cells * count
    projections = projectors.shape[0]
    halo = 6 * GY * GZ
    core, across, along = levels_of(count)
    ace_scale = 1.0 / math.sqrt(cells * projections)
    window_scale = 1.0 / math.sqrt(cells * bands)
    blk = bands // NBLK
    group_rows = GROUP_BLOCKS * blk
    width = 2 * group_rows
    half = bands // 2
    block = half // across[0]
    first = max(16, round(REDUCE_SHARE * block / 16) * 16)
    gather_first = max(16, round(GATHER_SHARE * block / 16) * 16)
    matrix = jnp.asarray(plane_matrix())
    lines = (potential[None, :], perturbing[None, :])
    bounds = tuple(a[None, :] for a in (energies, window_start, block_count))

    def to(array, level):
        return [swapped(array, count, level, k) for k in range(1, level[0])]

    def parts_to(parts, level):
        return [swapped(part, count, level, k + 1) for k, part in enumerate(parts)]

    low = neighbour(response[:, local_cells - halo :], count, 1)
    high = neighbour(response[:, :halo], count, -1)

    sent_x, sent_z, keep_x, keep_z = first_sums(response, projectors, core, block, first)
    sent_z = swapped(sent_z, count, core, 1)
    sent_x = swapped(sent_x, count, core, 1)
    keep_z, *parts_z = split(keep_z, [sent_z], along, 1)
    sent_x, parts_z[0] = lax.optimization_barrier((sent_x, parts_z[0]))
    keep_x, *parts_x = split(keep_x, [sent_x], across, 0)
    parts_z[-1], low = lax.optimization_barrier((parts_z[-1], low))
    taken_z, taken_x, low, high = lax.optimization_barrier(
        (parts_to(parts_z, along), parts_to(parts_x, across), low, high)
    )
    base, mask = local_part(
        response, low, high, orbitals, matrix, lines, bounds, group_rows, width, blk
    )
    padded = pad_orbitals(orbitals, blk)
    keep_x, *parts_x = split(keep_x, taken_x, along, 1)
    keep_z, *parts_z = split(keep_z, taken_z, across, 0)
    taken_x, taken_z, base, padded = lax.optimization_barrier(
        (parts_to(parts_x, along), parts_to(parts_z, across), base, padded)
    )
    share_x, share_z = local_call(
        functools.partial(finish_both_body, ace_scale, len(taken_x)),
        [
            struct((gather_first, projections // along[0]), BF16),
            struct((block - gather_first, projections // along[0]), BF16),
        ],
        [keep_x, *taken_x, keep_z, *taken_z],
    )

    pieces_x, pieces_z = lax.optimization_barrier(
        ([share_x, *to(share_x, along)], [share_z, *to(share_z, across)])
    )
    block_x = place(pieces_x, along, 1)
    block_z = place(pieces_z, across, 0)
    blocks_x = [block_x, *to(block_x, across)]
    pieces_z = [block_z, *to(block_z, along)]
    blocks = [*blocks_x, place(pieces_z, along, 1)]
    others = [swapped(part, count, core, 1) for part in blocks]
    sizes = (core, across, block, group_rows, blk)
    wide, keep = apply(blocks, projectors, base, padded, *sizes, False)
    others, keep = lax.optimization_barrier((others, keep))
    other_wide, part = apply(others, projectors, base, padded, *sizes, True)
    total, part = add_up(keep, to(part, core))
    total, part = add_up(total, to(part, across))
    far_first = [swapped(part, count, along, k) for k in reversed(range(1, along[0]))]
    own = finish(total, far_first, window_scale)
    (theirs,) = to(own, core)
    outs = project(own, wide, padded, response, mask, core, blk, False, ())
    return project(theirs, other_wide, padded, response, mask, core, blk, True, outs)


def solution(mesh):
    in_specs = (
        P("pert", "band"),
        P(None, "band"),
        P(None, "band"),
        P("band"),
        P(("pert", "band")),
        P(),
        P(),
        P(),
    )
    out_specs = (P("pert", "band"), P("pert", "band"))
    body = functools.partial(shards, mesh.shape["band"])
    return jax.shard_map(body, mesh=mesh, in_specs=in_specs, out_specs=out_specs, check_vma=False)
```

```python
import functools
import math

import jax
import jax.numpy as jnp
import ml_dtypes
import numpy as np
from jax import lax
from jax.experimental import pallas as pl
from jax.experimental.pallas import tpu as pltpu
from jax.sharding import PartitionSpec as P

GY = 8
GZ = 16
NBLK = 32
REACH = 4
GROUP_BLOCKS = 8
COEFFS = (
    -5369.0 / 1800.0,
    12.0 / 7.0,
    -15.0 / 56.0,
    10.0 / 189.0,
    -1.0 / 112.0,
    2.0 / 1925.0,
    -1.0 / 16632.0,
)
KINETIC = 0.125
STEP_SIZE = 0.3
MIB = 1024 * 1024
VMEM_BYTES = 24 * MIB
REDUCE_SHARE = 0.625
GATHER_SHARE = 0.625
BF16 = jnp.bfloat16
F32 = jnp.float32
NT = (((1,), (1,)), ((), ()))


def levels_of(count):
    chips = count // 2
    across = 2 ** (int(math.log2(chips)) // 3)
    return (2, 1), (across, 2), (chips // across, 2 * across)


def position(level):
    size, stride = level
    return lax.rem(lax.div(lax.axis_index("band"), jnp.int32(stride)), jnp.int32(size))


def neighbour(array, count, step):
    return lax.ppermute(array, "band", [(i, (i + step) % count) for i in range(count)])


def swapped(array, count, level, step):
    size, stride = level
    pairs = []
    for device in range(count):
        place = device // stride % size
        pairs.append((device, device + ((place ^ step) - place) * stride))
    return lax.ppermute(array, "band", pairs)


def plane_matrix():
    plane = GY * GZ
    matrix = 3.0 * COEFFS[0] * np.eye(plane)
    cells = np.arange(plane)
    y, z = cells // GZ, cells % GZ
    for offset in range(1, 7):
        for sign in (1, -1):
            np.add.at(matrix, ((y + sign * offset) % GY * GZ + z, cells), COEFFS[offset])
            np.add.at(matrix, (y * GZ + (z + sign * offset) % GZ, cells), COEFFS[offset])
    matrix = KINETIC * matrix
    high = matrix.astype(ml_dtypes.bfloat16)
    low = (matrix - high.astype(np.float64)).astype(ml_dtypes.bfloat16)
    return np.stack([high, low])


def whole():
    return pl.BlockSpec(memory_space=pltpu.VMEM)


def params(size=VMEM_BYTES):
    return pltpu.CompilerParams(vmem_limit_bytes=size)


def cost(flops, *arrays):
    moved = sum(math.prod(a.shape) * jnp.dtype(a.dtype).itemsize for a in arrays)
    return pl.CostEstimate(flops=int(flops), bytes_accessed=int(moved), transcendentals=0)


def local_call(body, outs, args, flops=0, scratch=()):
    return pl.pallas_call(
        body,
        out_shape=outs,
        in_specs=[whole() for _ in args],
        out_specs=jax.tree.map(lambda _: whole(), outs),
        scratch_shapes=scratch,
        compiler_params=params(),
        cost_estimate=cost(flops, *args, *jax.tree.leaves(outs)),
    )(*args)


def struct(shape, dtype):
    return jax.ShapeDtypeStruct(shape, dtype)


def cut(part, block, x_ref, z_ref, cols):
    size = part.shape[0] // block
    first, rest = x_ref.shape[0] // size, z_ref.shape[0] // size
    part = part.astype(x_ref.dtype)
    for i in range(size):
        x_ref[i * first : (i + 1) * first, cols] = part[i * block : i * block + first, :]
        z_ref[i * rest : (i + 1) * rest, cols] = part[i * block + first : (i + 1) * block, :]


def first_body(core, block, tile, r_ref, p_ref, *refs):
    sent_low, sent_high, keep_x, keep_z, r_held, p_held, r_sem, p_sem = refs
    width = sent_low.shape[1]
    rows = r_held.shape[0] // 2
    r_copy = pltpu.make_async_copy(r_ref, r_held, r_sem)
    r_copy.start()
    copies = []
    for t in range(p_held.shape[0] // tile):
        part = pl.ds(t * tile, tile)
        copies.append(pltpu.make_async_copy(p_ref.at[part, :], p_held.at[part, :], p_sem.at[t]))
        copies[-1].start()
    c = position(core)
    r_copy.wait()
    for t, copy in enumerate(copies):
        copy.wait()
        cols = slice(t * tile, (t + 1) * tile)
        for side in (1 - c, c):
            part = lax.dot_general(
                r_held[pl.ds(pl.multiple_of(side * rows, rows), rows), :],
                p_held[cols, :],
                NT,
                preferred_element_type=F32,
            )
            if side is c:
                cut(part, block, keep_x, keep_z, cols)
            else:
                ref, first = (sent_low, 0) if t * tile < width else (sent_high, width)
                ref[:, t * tile - first : (t + 1) * tile - first] = part.astype(BF16)


def first_sums(response, projectors, core, block, first):
    bands, cells = response.shape
    count = projectors.shape[0]
    rows = bands // 2
    tile = min(512, count // 2)
    rows_x = rows // block * first
    outs = [struct((rows, count // 2), BF16)] * 2
    outs += [struct((n, count), F32) for n in (rows_x, rows - rows_x)]
    return pl.pallas_call(
        functools.partial(first_body, core, block, tile),
        out_shape=outs,
        in_specs=[pl.BlockSpec(memory_space=pltpu.HBM)] * 2,
        out_specs=[whole() for _ in outs],
        scratch_shapes=[
            pltpu.VMEM((bands, cells), response.dtype),
            pltpu.VMEM((count, cells), projectors.dtype),
            pltpu.SemaphoreType.DMA,
            pltpu.SemaphoreType.DMA((count // tile,)),
        ],
        compiler_params=params(),
        cost_estimate=cost(2 * bands * cells * count, projectors, *outs),
    )(
        pltpu.with_memory_space_constraint(response, pltpu.HBM),
        pltpu.with_memory_space_constraint(projectors, pltpu.HBM),
    )


def rows_at(place, size):
    return pl.ds(pl.multiple_of(place * size, 16), size)


def cols_at(place, size):
    return pl.ds(pl.multiple_of(place * size, size), size)


def total_of(keep_ref, taken, part):
    total = keep_ref[part]
    for ref in taken:
        total = total + ref[part].astype(F32)
    return total


def first_x_body(level, block, keep_ref, low_ref, high_ref, *outs):
    me = position(level)
    rows = outs[0].shape[0]
    half = low_ref.shape[1]
    for step, out in enumerate(outs):
        at = me ^ step
        mine = rows_at(at, rows)
        theirs = pl.ds(pl.multiple_of(at * block, 16), rows)
        for k, ref in enumerate((low_ref, high_ref)):
            cols = slice(k * half, (k + 1) * half)
            out[:, cols] = (keep_ref[mine, cols] + ref[theirs, :].astype(F32)).astype(out.dtype)


def first_z_body(level, block, first, keep_ref, low_ref, high_ref, *outs):
    me = position(level)
    rows = block - first
    width = outs[0].shape[1]
    per = low_ref.shape[1] // width
    for step, out in enumerate(outs):
        at = me ^ step
        cols = cols_at(at, width)
        near = cols_at(lax.rem(at, jnp.int32(per)), width)
        for i in range(out.shape[0] // rows):
            mine = slice(i * rows, (i + 1) * rows)
            theirs = slice(i * block + first, (i + 1) * block)
            taken = jnp.where(at < per, low_ref[theirs, near], high_ref[theirs, near])
            out[mine, :] = (keep_ref[mine, cols] + taken.astype(F32)).astype(out.dtype)


def split_body(received, level, along, *refs):
    keep_ref, taken, outs = refs[0], refs[1 : 1 + received], refs[1 + received :]
    me = position(level)
    rows, width = outs[0].shape
    for step, out in enumerate(outs):
        at = me ^ step
        if along == 0:
            part = (rows_at(at, rows), slice(None))
        else:
            part = (slice(None), cols_at(at, width))
        out[...] = total_of(keep_ref, taken, part).astype(out.dtype)


def shares_of(shape, count):
    return [struct(shape, F32)] + [struct(shape, BF16)] * (count - 1)


def split(keep, taken, level, along):
    shape = list(keep.shape)
    shape[along] //= level[0]
    return local_call(
        functools.partial(split_body, len(taken), level, along),
        shares_of(shape, level[0]),
        [keep, *taken],
    )


def finish_body(scale, keep_ref, *refs):
    *taken, out_ref = refs
    out_ref[...] = (total_of(keep_ref, taken, ...) * scale).astype(out_ref.dtype)


def finish(keep, taken, scale):
    return local_call(
        functools.partial(finish_body, scale), struct(keep.shape, BF16), [keep, *taken]
    )


def finish_both_body(scale, received, *refs):
    outs = refs[-2:]
    cut = outs[0].shape[0]
    row = 0
    for keep_ref, *taken in (refs[: 1 + received], refs[1 + received : -2]):
        low = (total_of(keep_ref, taken, ...) * scale).astype(BF16)
        end = row + keep_ref.shape[0]
        for out, first, last in ((outs[0], 0, cut), (outs[1], cut, cut + outs[1].shape[0])):
            top, bottom = max(row, first), min(end, last)
            if top < bottom:
                out[top - first : bottom - first, :] = low[top - row : bottom - row, :]
        row = end


def place_body(level, along, *refs):
    *parts, out_ref = refs
    me = position(level)
    width = parts[0].shape[along]
    for step, ref in enumerate(parts):
        at = (me ^ (level[0] - step) % level[0]) * width
        if along == 0:
            out_ref[pl.ds(pl.multiple_of(at, 16), width), :] = ref[...]
        else:
            out_ref[:, pl.ds(pl.multiple_of(at, 128), width)] = ref[...]


def place(parts, level, along):
    shape = list(parts[0].shape)
    shape[along] *= level[0]
    return local_call(functools.partial(place_body, level, along), struct(shape, BF16), parts)


def turned(row, width):
    return jnp.transpose(jnp.broadcast_to(row, (width, row.shape[1])))


def local_body(depth, sizes, *refs):
    r_ref, l_ref, h_ref, o_ref, m_ref, pot_ref, v_ref, e_ref = refs[:8]
    first_ref, many_ref, out_ref, mask_ref = refs[8:]
    plane = GY * GZ
    reach = 6

    def plane_at(j):
        if j < 0:
            ref, k = l_ref, j + reach
        elif j < depth:
            ref, k = r_ref, j
        else:
            ref, k = h_ref, j - depth
        return ref[:, k * plane : (k + 1) * plane]

    group_rows, blk = sizes
    energy = turned(e_ref[...], plane)
    for j in range(depth):
        cols = slice(j * plane, (j + 1) * plane)
        low = plane_at(j)
        total = jnp.dot(low, m_ref[0], preferred_element_type=F32)
        total = total + jnp.dot(low, m_ref[1], preferred_element_type=F32)
        for offset in range(1, 7):
            pair = plane_at(j + offset).astype(F32) + plane_at(j - offset).astype(F32)
            total = total + (KINETIC * COEFFS[offset]) * pair
        total = total + (energy - pot_ref[:, cols]) * low.astype(F32)
        out_ref[:, cols] = total - v_ref[:, cols] * o_ref[:, cols].astype(F32)
    width = mask_ref.shape[1]
    block = lax.broadcasted_iota(jnp.int32, mask_ref.shape, 1) // blk
    block = (block + (pl.program_id(0) * (group_rows // blk) - REACH)).astype(F32)
    lowest = turned(first_ref[...].astype(F32), width)
    inside = (block >= lowest) & (block < lowest + turned(many_ref[...].astype(F32), width))
    mask_ref[...] = jnp.where(inside, 1.0, 0.0).astype(BF16)


def local_part(response, low, high, orbitals, matrix, lines, bounds, group_rows, width, blk):
    bands, cells = response.shape
    depth = cells // (GY * GZ)
    outs = [struct((bands, cells), F32), struct((bands, width), BF16)]
    here = pl.BlockSpec((group_rows, cells), lambda i: (i, 0))
    side = pl.BlockSpec((group_rows, low.shape[1]), lambda i: (i, 0))
    line = pl.BlockSpec((1, cells), lambda i: (0, 0))
    band = pl.BlockSpec((1, group_rows), lambda i: (0, i))
    return pl.pallas_call(
        functools.partial(local_body, depth, (group_rows, blk)),
        grid=(bands // group_rows,),
        out_shape=outs,
        in_specs=[
            here,
            side,
            side,
            here,
            pl.BlockSpec(matrix.shape, lambda i: (0, 0, 0)),
            line,
            line,
            band,
            band,
            band,
        ],
        out_specs=[here, pl.BlockSpec((group_rows, width), lambda i: (i, 0))],
        compiler_params=params(),
        cost_estimate=cost(2 * bands * cells * 300, low, high, low, low, *outs),
    )(response, low, high, orbitals, matrix, *lines, *bounds)


def pad_body(edge, o_ref, pad_ref):
    bands, cells = o_ref.shape
    pad_ref[:edge, :] = jnp.zeros((edge, cells), pad_ref.dtype)
    pad_ref[edge : edge + bands, :] = o_ref[...]
    pad_ref[edge + bands :, :] = jnp.zeros((edge, cells), pad_ref.dtype)


def pad_orbitals(orbitals, blk):
    bands, cells = orbitals.shape
    edge = REACH * blk
    return local_call(
        functools.partial(pad_body, edge),
        struct((bands + 2 * edge, cells), orbitals.dtype),
        [orbitals],
    )


def subgroup(shape, blk):
    return lax.broadcasted_iota(jnp.int32, shape, 1) // (2 * blk)


def packed(sums, blk):
    rows = sums.shape[0]
    sub = 2 * blk
    near, far = sums[:, :rows], sums[:, rows:]
    column = subgroup((rows, rows), blk)
    row = lax.broadcasted_iota(jnp.int32, (rows, rows), 0) // sub
    main = jnp.where(column >= row, near, far)
    rest = far[:sub, :]
    for k in range(1, rows // sub):
        rest = jnp.where(column[:sub, :] == k, far[k * sub : (k + 1) * sub, :], rest)
    return main, rest


def unpacked(main, rest, blk):
    rows = main.shape[0]
    sub = 2 * blk
    column = subgroup((rows, rows), blk)
    row = lax.broadcasted_iota(jnp.int32, (rows, rows), 0) // sub
    near = jnp.where(column >= row, main, 0.0)
    last = jnp.where(column == row, jnp.concatenate([rest] * (rows // sub), axis=0), 0.0)
    return near, jnp.where(column < row, main, last)


def apply_body(core, across, block, group_rows, blk, other, *refs):
    size = across[0]
    blocks = refs[: size + 1]
    p_ref, base_ref, pad_ref, u_ref, s_ref, c_ref = refs[size + 1 :]
    rows, cells = u_ref.shape
    c, x = position(core), position(across)
    side = 1 - c if other else c
    first = blocks[0].shape[0]
    for step, ref in enumerate(blocks[:size]):
        at = (x ^ (size - step) % size) * block
        c_ref[pl.ds(pl.multiple_of(at, 16), first), :] = ref[...]
    rest = block - first
    for i in range(size):
        there = slice(i * block + first, (i + 1) * block)
        c_ref[there, :] = blocks[size][i * rest : (i + 1) * rest, :]
    mine = pl.ds(pl.multiple_of(side * rows, rows), rows)
    tile = 256 if cells % 256 == 0 else 128
    for t in range(cells // tile):
        cols = slice(t * tile, (t + 1) * tile)
        u_ref[:, cols] = base_ref[mine, cols] + jnp.dot(
            c_ref[...], p_ref[:, cols], preferred_element_type=F32
        )
    height = group_rows + 2 * blk
    for g in range(rows // group_rows):
        start = pl.multiple_of(side * rows + g * group_rows, group_rows)
        sums = lax.dot_general(
            u_ref[g * group_rows : (g + 1) * group_rows, :].astype(BF16),
            pad_ref[pl.ds(start, 2 * group_rows), :],
            NT,
            preferred_element_type=F32,
        )
        main, rest_sums = packed(sums, blk)
        s_ref[g * height : g * height + group_rows, :] = main.astype(s_ref.dtype)
        s_ref[g * height + group_rows : (g + 1) * height, :] = rest_sums.astype(s_ref.dtype)


def apply(blocks, projectors, base, padded, core, across, block, group_rows, blk, other):
    bands, cells = base.shape
    rows = bands // 2
    count = projectors.shape[0]
    height = rows // group_rows * (group_rows + 2 * blk)
    return local_call(
        functools.partial(apply_body, core, across, block, group_rows, blk, other),
        [struct((rows, cells), F32), struct((height, group_rows), BF16 if other else F32)],
        [*blocks, projectors, base, padded],
        flops=2 * rows * cells * (count + 2 * group_rows),
        scratch=[pltpu.VMEM((rows, count), BF16)],
    )


def sum_body(keep_ref, *refs):
    *taken, total_ref, low_ref = refs
    total = total_of(keep_ref, taken, ...)
    total_ref[...] = total
    low_ref[...] = total.astype(BF16)


def add_up(keep, taken):
    outs = [struct(keep.shape, F32), struct(keep.shape, BF16)]
    return local_call(sum_body, outs, [keep, *taken])


def project_body(core, blk, other, *refs):
    w_ref, u_ref, pad_ref, r_ref, mask_ref = refs[:5]
    outs, helds, sems = refs[-5:-3], refs[-3:-1], refs[-1]
    rows = mask_ref.shape[1] // 2
    per = u_ref.shape[0] // rows
    height = w_ref.shape[0] // per
    c = position(core)
    copies = []
    for g in range(per):
        mine = slice(g * rows, (g + 1) * rows)
        start = pl.multiple_of(((1 - c if other else c) * per + g) * rows, rows)
        there = pl.ds(start, rows)
        main = w_ref[g * height : g * height + rows, :].astype(F32)
        rest = w_ref[g * height + rows : (g + 1) * height, :].astype(F32)
        residual = u_ref[mine, :]
        for k, part in enumerate(unpacked(main, rest, blk)):
            inside = mask_ref[there, k * rows : (k + 1) * rows].astype(F32) > 0.5
            weights = jnp.where(inside, part, 0.0).astype(BF16)
            window = pad_ref[pl.ds(pl.multiple_of(start + k * rows, rows), rows), :]
            residual = residual - jnp.dot(weights, window, preferred_element_type=F32)
        updated = r_ref[there, :].astype(F32) + STEP_SIZE * residual
        for k, value in enumerate((updated, residual)):
            helds[k][mine, :] = value.astype(BF16)
            copies.append(
                pltpu.make_async_copy(
                    helds[k].at[pl.ds(g * rows, rows), :], outs[k].at[there, :], sems.at[k, g]
                )
            )
            copies[-1].start()
    for copy in copies:
        copy.wait()


def project(weights, unprojected, padded, response, mask, core, blk, other, before):
    rows, cells = unprojected.shape
    per = rows // (mask.shape[1] // 2)
    out = struct(response.shape, BF16)
    args = [weights, unprojected, padded, response, mask]
    anywhere = pl.BlockSpec(memory_space=pl.ANY)
    return pl.pallas_call(
        functools.partial(project_body, core, blk, other),
        out_shape=(out, out),
        in_specs=[whole() for _ in args] + [anywhere for _ in before],
        out_specs=(anywhere, anywhere),
        scratch_shapes=[
            pltpu.VMEM((rows, cells), BF16),
            pltpu.VMEM((rows, cells), BF16),
            pltpu.SemaphoreType.DMA((2, per)),
        ],
        input_output_aliases={5: 0, 6: 1} if before else {},
        compiler_params=params(),
        cost_estimate=cost(2 * rows * mask.shape[1] * cells, padded, unprojected, unprojected),
    )(*args, *before)


def shards(
    count, response, orbitals, projectors, potential, perturbing, energies, window_start, block_count
):
    bands, local_cells = response.shape
    cells = local_cells * count
    projections = projectors.shape[0]
    halo = 6 * GY * GZ
    core, across, along = levels_of(count)
    ace_scale = 1.0 / math.sqrt(cells * projections)
    window_scale = 1.0 / math.sqrt(cells * bands)
    blk = bands // NBLK
    group_rows = GROUP_BLOCKS * blk
    width = 2 * group_rows
    half = bands // 2
    block = half // across[0]
    first = max(16, round(REDUCE_SHARE * block / 16) * 16)
    gather_first = max(16, round(GATHER_SHARE * block / 16) * 16)
    matrix = jnp.asarray(plane_matrix())
    lines = (potential[None, :], perturbing[None, :])
    bounds = tuple(a[None, :] for a in (energies, window_start, block_count))

    def to(array, level):
        return [swapped(array, count, level, k) for k in reversed(range(1, level[0]))]

    def parts_to(parts, level):
        order = reversed(list(enumerate(parts)))
        return [swapped(part, count, level, k + 1) for k, part in order]

    low = neighbour(response[:, local_cells - halo :], count, 1)
    high = neighbour(response[:, :halo], count, -1)

    *sent, keep_x, keep_z = first_sums(response, projectors, core, block, first)
    sent = [swapped(part, count, core, 1) for part in sent]
    keep_z, *parts_z = local_call(
        functools.partial(first_z_body, along, block, first),
        shares_of((keep_z.shape[0], projections // along[0]), along[0]),
        [keep_z, *sent],
    )
    keep_x, parts_z[0] = lax.optimization_barrier((keep_x, parts_z[0]))
    keep_x, *parts_x = local_call(
        functools.partial(first_x_body, across, block),
        shares_of((first, projections), across[0]),
        [keep_x, *sent],
    )
    parts_z[0], low = lax.optimization_barrier((parts_z[0], low))
    taken_z, taken_x, low, high = lax.optimization_barrier(
        (parts_to(parts_z, along), parts_to(parts_x, across), low, high)
    )
    keep_x, *parts_x = split(keep_x, taken_x, along, 1)
    keep_z, *parts_z = split(keep_z, taken_z, across, 0)
    base, mask = local_part(
        response, low, high, orbitals, matrix, lines, bounds, group_rows, width, blk
    )
    padded = pad_orbitals(orbitals, blk)
    taken_x, taken_z, base, padded = lax.optimization_barrier(
        (
            [swapped(part, count, along, k + 1) for k, part in enumerate(parts_x)],
            parts_to(parts_z, across),
            base,
            padded,
        )
    )
    share_x, share_z = local_call(
        functools.partial(finish_both_body, ace_scale, len(taken_x)),
        [
            struct((gather_first, projections // along[0]), BF16),
            struct((block - gather_first, projections // along[0]), BF16),
        ],
        [keep_x, *taken_x, keep_z, *taken_z],
    )

    pieces_x, pieces_z = lax.optimization_barrier(
        ([share_x, *to(share_x, along)], [share_z, *to(share_z, across)])
    )
    block_x = place(pieces_x, along, 1)
    block_z = place(pieces_z, across, 0)
    blocks_x = [block_x, *to(block_x, across)]
    pieces_z = [block_z, *to(block_z, along)]
    blocks = [*blocks_x, place(pieces_z, along, 1)]
    others = [swapped(part, count, core, 1) for part in blocks]
    sizes = (core, across, block, group_rows, blk)
    wide, keep = apply(blocks, projectors, base, padded, *sizes, False)
    others, keep = lax.optimization_barrier((others, keep))
    other_wide, part = apply(others, projectors, base, padded, *sizes, True)
    total, part = add_up(keep, to(part, core))
    total, part = add_up(total, to(part, across))
    own = finish(total, to(part, along), window_scale)
    (theirs,) = to(own, core)
    outs = project(own, wide, padded, response, mask, core, blk, False, ())
    return project(theirs, other_wide, padded, response, mask, core, blk, True, outs)


def solution(mesh):
    in_specs = (
        P("pert", "band"),
        P(None, "band"),
        P(None, "band"),
        P("band"),
        P(("pert", "band")),
        P(),
        P(),
        P(),
    )
    out_specs = (P("pert", "band"), P("pert", "band"))
    body = functools.partial(shards, mesh.shape["band"])
    return jax.shard_map(body, mesh=mesh, in_specs=in_specs, out_specs=out_specs, check_vma=False)
```

```python
import functools
import math

import jax
import jax.numpy as jnp
import ml_dtypes
import numpy as np
from jax import lax
from jax.experimental import pallas as pl
from jax.experimental.pallas import tpu as pltpu
from jax.sharding import PartitionSpec as P

GY = 8
GZ = 16
NBLK = 32
REACH = 4
GROUP_BLOCKS = 8
COEFFS = (
    -5369.0 / 1800.0,
    12.0 / 7.0,
    -15.0 / 56.0,
    10.0 / 189.0,
    -1.0 / 112.0,
    2.0 / 1925.0,
    -1.0 / 16632.0,
)
KINETIC = 0.125
STEP_SIZE = 0.3
MIB = 1024 * 1024
VMEM_BYTES = 24 * MIB
REDUCE_SHARE = 0.625
GATHER_SHARE = 0.5
BF16 = jnp.bfloat16
F32 = jnp.float32
NT = (((1,), (1,)), ((), ()))


def levels_of(count):
    chips = count // 2
    across = 2 ** (int(math.log2(chips)) // 3)
    return (2, 1), (across, 2), (chips // across, 2 * across)


def position(level):
    size, stride = level
    return lax.rem(lax.div(lax.axis_index("band"), jnp.int32(stride)), jnp.int32(size))


def neighbour(array, count, step):
    return lax.ppermute(array, "band", [(i, (i + step) % count) for i in range(count)])


def swapped(array, count, level, step):
    size, stride = level
    pairs = []
    for device in range(count):
        place = device // stride % size
        pairs.append((device, device + ((place ^ step) - place) * stride))
    return lax.ppermute(array, "band", pairs)


def plane_matrix():
    plane = GY * GZ
    matrix = 3.0 * COEFFS[0] * np.eye(plane)
    cells = np.arange(plane)
    y, z = cells // GZ, cells % GZ
    for offset in range(1, 7):
        for sign in (1, -1):
            np.add.at(matrix, ((y + sign * offset) % GY * GZ + z, cells), COEFFS[offset])
            np.add.at(matrix, (y * GZ + (z + sign * offset) % GZ, cells), COEFFS[offset])
    matrix = KINETIC * matrix
    high = matrix.astype(ml_dtypes.bfloat16)
    low = (matrix - high.astype(np.float64)).astype(ml_dtypes.bfloat16)
    return np.stack([high, low])


def whole():
    return pl.BlockSpec(memory_space=pltpu.VMEM)


def params(size=VMEM_BYTES):
    return pltpu.CompilerParams(vmem_limit_bytes=size)


def cost(flops, *arrays):
    moved = sum(math.prod(a.shape) * jnp.dtype(a.dtype).itemsize for a in arrays)
    return pl.CostEstimate(flops=int(flops), bytes_accessed=int(moved), transcendentals=0)


def local_call(body, outs, args, flops=0, scratch=()):
    return pl.pallas_call(
        body,
        out_shape=outs,
        in_specs=[whole() for _ in args],
        out_specs=jax.tree.map(lambda _: whole(), outs),
        scratch_shapes=scratch,
        compiler_params=params(),
        cost_estimate=cost(flops, *args, *jax.tree.leaves(outs)),
    )(*args)


def struct(shape, dtype):
    return jax.ShapeDtypeStruct(shape, dtype)


def cut(part, block, x_ref, z_ref, cols):
    size = part.shape[0] // block
    first, rest = x_ref.shape[0] // size, z_ref.shape[0] // size
    part = part.astype(x_ref.dtype)
    for i in range(size):
        x_ref[i * first : (i + 1) * first, cols] = part[i * block : i * block + first, :]
        z_ref[i * rest : (i + 1) * rest, cols] = part[i * block + first : (i + 1) * block, :]


def first_body(core, block, tile, r_ref, p_ref, *refs):
    sent_low, sent_high, keep_x, keep_z, r_held, p_held, r_sem, p_sem = refs
    width = sent_low.shape[1]
    rows = r_held.shape[0] // 2
    r_copy = pltpu.make_async_copy(r_ref, r_held, r_sem)
    r_copy.start()
    copies = []
    for t in range(p_held.shape[0] // tile):
        part = pl.ds(t * tile, tile)
        copies.append(pltpu.make_async_copy(p_ref.at[part, :], p_held.at[part, :], p_sem.at[t]))
        copies[-1].start()
    c = position(core)
    r_copy.wait()
    for t, copy in enumerate(copies):
        copy.wait()
        cols = slice(t * tile, (t + 1) * tile)
        for side in (1 - c, c):
            part = lax.dot_general(
                r_held[pl.ds(pl.multiple_of(side * rows, rows), rows), :],
                p_held[cols, :],
                NT,
                preferred_element_type=F32,
            )
            if side is c:
                cut(part, block, keep_x, keep_z, cols)
            else:
                ref, first = (sent_low, 0) if t * tile < width else (sent_high, width)
                ref[:, t * tile - first : (t + 1) * tile - first] = part.astype(BF16)


def first_sums(response, projectors, core, block, first):
    bands, cells = response.shape
    count = projectors.shape[0]
    rows = bands // 2
    tile = min(512, count // 2)
    rows_x = rows // block * first
    outs = [struct((rows, count // 2), BF16)] * 2
    outs += [struct((n, count), F32) for n in (rows_x, rows - rows_x)]
    return pl.pallas_call(
        functools.partial(first_body, core, block, tile),
        out_shape=outs,
        in_specs=[pl.BlockSpec(memory_space=pltpu.HBM)] * 2,
        out_specs=[whole() for _ in outs],
        scratch_shapes=[
            pltpu.VMEM((bands, cells), response.dtype),
            pltpu.VMEM((count, cells), projectors.dtype),
            pltpu.SemaphoreType.DMA,
            pltpu.SemaphoreType.DMA((count // tile,)),
        ],
        compiler_params=params(),
        cost_estimate=cost(2 * bands * cells * count, projectors, *outs),
    )(
        pltpu.with_memory_space_constraint(response, pltpu.HBM),
        pltpu.with_memory_space_constraint(projectors, pltpu.HBM),
    )


def rows_at(place, size):
    return pl.ds(pl.multiple_of(place * size, 16), size)


def cols_at(place, size):
    return pl.ds(pl.multiple_of(place * size, size), size)


def total_of(keep_ref, taken, part):
    total = keep_ref[part]
    for ref in taken:
        total = total + ref[part].astype(F32)
    return total


def first_x_body(level, block, keep_ref, low_ref, high_ref, *outs):
    me = position(level)
    rows = outs[0].shape[0]
    half = low_ref.shape[1]
    for step, out in enumerate(outs):
        at = me ^ step
        mine = rows_at(at, rows)
        theirs = pl.ds(pl.multiple_of(at * block, 16), rows)
        for k, ref in enumerate((low_ref, high_ref)):
            cols = slice(k * half, (k + 1) * half)
            out[:, cols] = (keep_ref[mine, cols] + ref[theirs, :].astype(F32)).astype(out.dtype)


def first_z_body(level, block, first, keep_ref, low_ref, high_ref, *outs):
    me = position(level)
    rows = block - first
    width = outs[0].shape[1]
    per = low_ref.shape[1] // width
    for step, out in enumerate(outs):
        at = me ^ step
        cols = cols_at(at, width)
        near = cols_at(lax.rem(at, jnp.int32(per)), width)
        for i in range(out.shape[0] // rows):
            mine = slice(i * rows, (i + 1) * rows)
            theirs = slice(i * block + first, (i + 1) * block)
            taken = jnp.where(at < per, low_ref[theirs, near], high_ref[theirs, near])
            out[mine, :] = (keep_ref[mine, cols] + taken.astype(F32)).astype(out.dtype)


def split_body(received, level, along, *refs):
    keep_ref, taken, outs = refs[0], refs[1 : 1 + received], refs[1 + received :]
    me = position(level)
    rows, width = outs[0].shape
    for step, out in enumerate(outs):
        at = me ^ step
        if along == 0:
            part = (rows_at(at, rows), slice(None))
        else:
            part = (slice(None), cols_at(at, width))
        out[...] = total_of(keep_ref, taken, part).astype(out.dtype)


def shares_of(shape, count):
    return [struct(shape, F32)] + [struct(shape, BF16)] * (count - 1)


def split(keep, taken, level, along):
    shape = list(keep.shape)
    shape[along] //= level[0]
    return local_call(
        functools.partial(split_body, len(taken), level, along),
        shares_of(shape, level[0]),
        [keep, *taken],
    )


def finish_body(scale, keep_ref, *refs):
    *taken, out_ref = refs
    out_ref[...] = (total_of(keep_ref, taken, ...) * scale).astype(out_ref.dtype)


def finish(keep, taken, scale):
    return local_call(
        functools.partial(finish_body, scale), struct(keep.shape, BF16), [keep, *taken]
    )


def finish_both_body(scale, received, *refs):
    outs = refs[-2:]
    cut = outs[0].shape[0]
    row = 0
    for keep_ref, *taken in (refs[: 1 + received], refs[1 + received : -2]):
        low = (total_of(keep_ref, taken, ...) * scale).astype(BF16)
        end = row + keep_ref.shape[0]
        for out, first, last in ((outs[0], 0, cut), (outs[1], cut, cut + outs[1].shape[0])):
            top, bottom = max(row, first), min(end, last)
            if top < bottom:
                out[top - first : bottom - first, :] = low[top - row : bottom - row, :]
        row = end


def place_body(level, along, *refs):
    *parts, out_ref = refs
    me = position(level)
    width = parts[0].shape[along]
    for step, ref in enumerate(parts):
        at = (me ^ (level[0] - step) % level[0]) * width
        if along == 0:
            out_ref[pl.ds(pl.multiple_of(at, 16), width), :] = ref[...]
        else:
            out_ref[:, pl.ds(pl.multiple_of(at, 128), width)] = ref[...]


def place(parts, level, along):
    shape = list(parts[0].shape)
    shape[along] *= level[0]
    return local_call(functools.partial(place_body, level, along), struct(shape, BF16), parts)


def turned(row, width):
    return jnp.transpose(jnp.broadcast_to(row, (width, row.shape[1])))


def local_body(depth, sizes, *refs):
    r_ref, l_ref, h_ref, o_ref, m_ref, pot_ref, v_ref, e_ref = refs[:8]
    first_ref, many_ref, out_ref, mask_ref = refs[8:]
    plane = GY * GZ
    reach = 6

    def plane_at(j):
        if j < 0:
            ref, k = l_ref, j + reach
        elif j < depth:
            ref, k = r_ref, j
        else:
            ref, k = h_ref, j - depth
        return ref[:, k * plane : (k + 1) * plane]

    group_rows, blk = sizes
    energy = turned(e_ref[...], plane)
    for j in range(depth):
        cols = slice(j * plane, (j + 1) * plane)
        low = plane_at(j)
        total = jnp.dot(low, m_ref[0], preferred_element_type=F32)
        total = total + jnp.dot(low, m_ref[1], preferred_element_type=F32)
        for offset in range(1, 7):
            pair = plane_at(j + offset).astype(F32) + plane_at(j - offset).astype(F32)
            total = total + (KINETIC * COEFFS[offset]) * pair
        total = total + (energy - pot_ref[:, cols]) * low.astype(F32)
        out_ref[:, cols] = total - v_ref[:, cols] * o_ref[:, cols].astype(F32)
    width = mask_ref.shape[1]
    block = lax.broadcasted_iota(jnp.int32, mask_ref.shape, 1) // blk
    block = (block + (pl.program_id(0) * (group_rows // blk) - REACH)).astype(F32)
    lowest = turned(first_ref[...].astype(F32), width)
    inside = (block >= lowest) & (block < lowest + turned(many_ref[...].astype(F32), width))
    mask_ref[...] = jnp.where(inside, 1.0, 0.0).astype(BF16)


def local_part(response, low, high, orbitals, matrix, lines, bounds, group_rows, width, blk):
    bands, cells = response.shape
    depth = cells // (GY * GZ)
    outs = [struct((bands, cells), F32), struct((bands, width), BF16)]
    here = pl.BlockSpec((group_rows, cells), lambda i: (i, 0))
    side = pl.BlockSpec((group_rows, low.shape[1]), lambda i: (i, 0))
    line = pl.BlockSpec((1, cells), lambda i: (0, 0))
    band = pl.BlockSpec((1, group_rows), lambda i: (0, i))
    return pl.pallas_call(
        functools.partial(local_body, depth, (group_rows, blk)),
        grid=(bands // group_rows,),
        out_shape=outs,
        in_specs=[
            here,
            side,
            side,
            here,
            pl.BlockSpec(matrix.shape, lambda i: (0, 0, 0)),
            line,
            line,
            band,
            band,
            band,
        ],
        out_specs=[here, pl.BlockSpec((group_rows, width), lambda i: (i, 0))],
        compiler_params=params(),
        cost_estimate=cost(2 * bands * cells * 300, low, high, low, low, *outs),
    )(response, low, high, orbitals, matrix, *lines, *bounds)


def pad_body(edge, o_ref, pad_ref):
    bands, cells = o_ref.shape
    pad_ref[:edge, :] = jnp.zeros((edge, cells), pad_ref.dtype)
    pad_ref[edge : edge + bands, :] = o_ref[...]
    pad_ref[edge + bands :, :] = jnp.zeros((edge, cells), pad_ref.dtype)


def pad_orbitals(orbitals, blk):
    bands, cells = orbitals.shape
    edge = REACH * blk
    return local_call(
        functools.partial(pad_body, edge),
        struct((bands + 2 * edge, cells), orbitals.dtype),
        [orbitals],
    )


def subgroup(shape, blk):
    return lax.broadcasted_iota(jnp.int32, shape, 1) // (2 * blk)


def packed(sums, blk):
    rows = sums.shape[0]
    sub = 2 * blk
    near, far = sums[:, :rows], sums[:, rows:]
    column = subgroup((rows, rows), blk)
    row = lax.broadcasted_iota(jnp.int32, (rows, rows), 0) // sub
    main = jnp.where(column >= row, near, far)
    rest = far[:sub, :]
    for k in range(1, rows // sub):
        rest = jnp.where(column[:sub, :] == k, far[k * sub : (k + 1) * sub, :], rest)
    return main, rest


def unpacked(main, rest, blk):
    rows = main.shape[0]
    sub = 2 * blk
    column = subgroup((rows, rows), blk)
    row = lax.broadcasted_iota(jnp.int32, (rows, rows), 0) // sub
    near = jnp.where(column >= row, main, 0.0)
    last = jnp.where(column == row, jnp.concatenate([rest] * (rows // sub), axis=0), 0.0)
    return near, jnp.where(column < row, main, last)


def apply_body(core, across, block, group_rows, blk, other, *refs):
    size = across[0]
    blocks = refs[: size + 1]
    p_ref, base_ref, pad_ref, u_ref, s_ref, c_ref = refs[size + 1 :]
    rows, cells = u_ref.shape
    c, x = position(core), position(across)
    side = 1 - c if other else c
    first = blocks[0].shape[0]
    for step, ref in enumerate(blocks[:size]):
        at = (x ^ (size - step) % size) * block
        c_ref[pl.ds(pl.multiple_of(at, 16), first), :] = ref[...]
    rest = block - first
    for i in range(size):
        there = slice(i * block + first, (i + 1) * block)
        c_ref[there, :] = blocks[size][i * rest : (i + 1) * rest, :]
    mine = pl.ds(pl.multiple_of(side * rows, rows), rows)
    tile = 256 if cells % 256 == 0 else 128
    for t in range(cells // tile):
        cols = slice(t * tile, (t + 1) * tile)
        u_ref[:, cols] = base_ref[mine, cols] + jnp.dot(
            c_ref[...], p_ref[:, cols], preferred_element_type=F32
        )
    height = group_rows + 2 * blk
    for g in range(rows // group_rows):
        start = pl.multiple_of(side * rows + g * group_rows, group_rows)
        sums = lax.dot_general(
            u_ref[g * group_rows : (g + 1) * group_rows, :].astype(BF16),
            pad_ref[pl.ds(start, 2 * group_rows), :],
            NT,
            preferred_element_type=F32,
        )
        main, rest_sums = packed(sums, blk)
        s_ref[g * height : g * height + group_rows, :] = main.astype(s_ref.dtype)
        s_ref[g * height + group_rows : (g + 1) * height, :] = rest_sums.astype(s_ref.dtype)


def apply(blocks, projectors, base, padded, core, across, block, group_rows, blk, other):
    bands, cells = base.shape
    rows = bands // 2
    count = projectors.shape[0]
    height = rows // group_rows * (group_rows + 2 * blk)
    return local_call(
        functools.partial(apply_body, core, across, block, group_rows, blk, other),
        [struct((rows, cells), F32), struct((height, group_rows), BF16 if other else F32)],
        [*blocks, projectors, base, padded],
        flops=2 * rows * cells * (count + 2 * group_rows),
        scratch=[pltpu.VMEM((rows, count), BF16)],
    )


def sum_body(keep_ref, *refs):
    *taken, total_ref, low_ref = refs
    total = total_of(keep_ref, taken, ...)
    total_ref[...] = total
    low_ref[...] = total.astype(BF16)


def add_up(keep, taken):
    outs = [struct(keep.shape, F32), struct(keep.shape, BF16)]
    return local_call(sum_body, outs, [keep, *taken])


def project_body(core, blk, other, *refs):
    w_ref, u_ref, pad_ref, r_ref, mask_ref = refs[:5]
    outs, helds, sems = refs[-5:-3], refs[-3:-1], refs[-1]
    rows = mask_ref.shape[1] // 2
    per = u_ref.shape[0] // rows
    height = w_ref.shape[0] // per
    c = position(core)
    copies = []
    for g in range(per):
        mine = slice(g * rows, (g + 1) * rows)
        start = pl.multiple_of(((1 - c if other else c) * per + g) * rows, rows)
        there = pl.ds(start, rows)
        main = w_ref[g * height : g * height + rows, :].astype(F32)
        rest = w_ref[g * height + rows : (g + 1) * height, :].astype(F32)
        residual = u_ref[mine, :]
        for k, part in enumerate(unpacked(main, rest, blk)):
            inside = mask_ref[there, k * rows : (k + 1) * rows].astype(F32) > 0.5
            weights = jnp.where(inside, part, 0.0).astype(BF16)
            window = pad_ref[pl.ds(pl.multiple_of(start + k * rows, rows), rows), :]
            residual = residual - jnp.dot(weights, window, preferred_element_type=F32)
        updated = r_ref[there, :].astype(F32) + STEP_SIZE * residual
        for k, value in enumerate((updated, residual)):
            helds[k][mine, :] = value.astype(BF16)
            copies.append(
                pltpu.make_async_copy(
                    helds[k].at[pl.ds(g * rows, rows), :], outs[k].at[there, :], sems.at[k, g]
                )
            )
            copies[-1].start()
    for copy in copies:
        copy.wait()


def project(weights, unprojected, padded, response, mask, core, blk, other, before):
    rows, cells = unprojected.shape
    per = rows // (mask.shape[1] // 2)
    out = struct(response.shape, BF16)
    args = [weights, unprojected, padded, response, mask]
    anywhere = pl.BlockSpec(memory_space=pl.ANY)
    return pl.pallas_call(
        functools.partial(project_body, core, blk, other),
        out_shape=(out, out),
        in_specs=[whole() for _ in args] + [anywhere for _ in before],
        out_specs=(anywhere, anywhere),
        scratch_shapes=[
            pltpu.VMEM((rows, cells), BF16),
            pltpu.VMEM((rows, cells), BF16),
            pltpu.SemaphoreType.DMA((2, per)),
        ],
        input_output_aliases={5: 0, 6: 1} if before else {},
        compiler_params=params(),
        cost_estimate=cost(2 * rows * mask.shape[1] * cells, padded, unprojected, unprojected),
    )(*args, *before)


def shards(
    count, response, orbitals, projectors, potential, perturbing, energies, window_start, block_count
):
    bands, local_cells = response.shape
    cells = local_cells * count
    projections = projectors.shape[0]
    halo = 6 * GY * GZ
    core, across, along = levels_of(count)
    ace_scale = 1.0 / math.sqrt(cells * projections)
    window_scale = 1.0 / math.sqrt(cells * bands)
    blk = bands // NBLK
    group_rows = GROUP_BLOCKS * blk
    width = 2 * group_rows
    half = bands // 2
    block = half // across[0]
    first = max(16, round(REDUCE_SHARE * block / 16) * 16)
    gather_first = max(16, round(GATHER_SHARE * block / 16) * 16)
    matrix = jnp.asarray(plane_matrix())
    lines = (potential[None, :], perturbing[None, :])
    bounds = tuple(a[None, :] for a in (energies, window_start, block_count))

    def to(array, level):
        return [swapped(array, count, level, k) for k in reversed(range(1, level[0]))]

    def parts_to(parts, level):
        order = reversed(list(enumerate(parts)))
        return [swapped(part, count, level, k + 1) for k, part in order]

    low = neighbour(response[:, local_cells - halo :], count, 1)
    high = neighbour(response[:, :halo], count, -1)

    *sent, keep_x, keep_z = first_sums(response, projectors, core, block, first)
    sent = [swapped(part, count, core, 1) for part in sent]
    keep_z, *parts_z = local_call(
        functools.partial(first_z_body, along, block, first),
        shares_of((keep_z.shape[0], projections // along[0]), along[0]),
        [keep_z, *sent],
    )
    keep_x, parts_z[0] = lax.optimization_barrier((keep_x, parts_z[0]))
    keep_x, *parts_x = local_call(
        functools.partial(first_x_body, across, block),
        shares_of((first, projections), across[0]),
        [keep_x, *sent],
    )
    parts_z[0], low = lax.optimization_barrier((parts_z[0], low))
    taken_z, taken_x, low, high = lax.optimization_barrier(
        (parts_to(parts_z, along), parts_to(parts_x, across), low, high)
    )
    keep_x, *parts_x = split(keep_x, taken_x, along, 1)
    keep_z, *parts_z = split(keep_z, taken_z, across, 0)
    base, mask = local_part(
        response, low, high, orbitals, matrix, lines, bounds, group_rows, width, blk
    )
    padded = pad_orbitals(orbitals, blk)
    taken_x, taken_z, base, padded = lax.optimization_barrier(
        (
            [swapped(part, count, along, k + 1) for k, part in enumerate(parts_x)],
            parts_to(parts_z, across),
            base,
            padded,
        )
    )
    share_x, share_z = local_call(
        functools.partial(finish_both_body, ace_scale, len(taken_x)),
        [
            struct((gather_first, projections // along[0]), BF16),
            struct((block - gather_first, projections // along[0]), BF16),
        ],
        [keep_x, *taken_x, keep_z, *taken_z],
    )

    pieces_x, pieces_z = lax.optimization_barrier(
        ([share_x, *to(share_x, along)], [share_z, *to(share_z, across)])
    )
    block_x = place(pieces_x, along, 1)
    block_z = place(pieces_z, across, 0)
    blocks_x = [block_x, *to(block_x, across)]
    pieces_z = [block_z, *to(block_z, along)]
    blocks = [*blocks_x, place(pieces_z, along, 1)]
    others = [swapped(part, count, core, 1) for part in blocks]
    sizes = (core, across, block, group_rows, blk)
    wide, keep = apply(blocks, projectors, base, padded, *sizes, False)
    others, keep = lax.optimization_barrier((others, keep))
    other_wide, part = apply(others, projectors, base, padded, *sizes, True)
    total, part = add_up(keep, to(part, core))
    total, part = add_up(total, to(part, across))
    own = finish(total, to(part, along), window_scale)
    (theirs,) = to(own, core)
    outs = project(own, wide, padded, response, mask, core, blk, False, ())
    return project(theirs, other_wide, padded, response, mask, core, blk, True, outs)


def solution(mesh):
    in_specs = (
        P("pert", "band"),
        P(None, "band"),
        P(None, "band"),
        P("band"),
        P(("pert", "band")),
        P(),
        P(),
        P(),
    )
    out_specs = (P("pert", "band"), P("pert", "band"))
    body = functools.partial(shards, mesh.shape["band"])
    return jax.shard_map(body, mesh=mesh, in_specs=in_specs, out_specs=out_specs, check_vma=False)
```
